512 devices in a mesh: enc: 16 (over x_hi, y, core), dp: 32 (over z, x_lo).
Axes of the slice: x: 4 (x_hi: 2, x_lo: 2; x = x_hi * 2 + x_lo), y: 4, z: 16, core: 2. Of those that a mesh axis runs over, the one named last changes fastest.
Arguments:
- mel: bfloat16 [8192, 16, 128], P(('enc', 'dp')), may hold values from -6 to 6
- lengths: int32 [8192], P(('enc', 'dp')), may hold values from 1 to 16
- routes: int32 [8192, 1], P(('enc', 'dp')), may hold values from 0 to 15; in each aligned block of 16 rows (0 to 15, 16 to 31, ...) at most 2 rows name the same one
- conv1_weight: bfloat16 [384, 1280], replicated, may hold values from -0.3125 to 0.3125
- conv1_bias: float32 [1280], replicated, may hold values from -3 to 3
- conv2_weight: bfloat16 [1280, 1920], P('enc'), may hold values from -0.09375 to 0.09375
- conv2_bias: float32 [640], replicated, may hold values from -3 to 3
- out_grad: bfloat16 [8192, 8, 640], P(('enc', 'dp')), may hold values from -6 to 6
Outputs:
- packed_features: bfloat16 [16384, 8, 640], P(('enc', 'dp'))
- grad_conv1_weight: float32 [384, 1280], replicated
- grad_conv1_bias: float32 [1280], replicated
- grad_conv2_bias: float32 [640], replicated
- grad_conv2_weight: float32 [1280, 1920], P('enc')
The draws below stay inside these ranges and needn't reach their ends.
Inputs may be any that keep to these rules, and one draw needn't show every extreme that they name: `routes`: among the clips of one device at most 2 name the same owner.
All inputs are finite; a program needn't handle non-finite values.
Results may differ from the reference program's by a relative error of at most 0.007.
Values may be sent and summed in bfloat16 or wider, within the bound.
No kernel may reach another device: no remote copies, remote signals or barrier semaphores. Data moves between devices by JAX's collectives and lax.ppermute only.
A program may use at most 128 MiB of HBM per device.

```python
import math
import jax
import jax.numpy as jnp
import numpy as np
from jax import lax

MEL = 128
D = 1280
D2 = 640
FRAMES = 16
CLIPS_DEV = 16
HALF = 8
SLOTS = 2
CLIPS = 8192
ALL_SLOTS = 16384
N_ENC = 16
N_DP = 32


def touch_ends(result, key, smallest, high):
    dims = result.shape
    place = [jax.random.randint(jax.random.fold_in(key, axis), (), 0, dims[axis]) for axis in range(len(dims))]
    result = result.at[tuple(place)].set(smallest)
    longest = dims.index(max(dims))
    place[longest] = (place[longest] + 1) % dims[longest]
    return result.at[tuple(place)].set(high)


def shard_levels(key, dims, shards, least, high):
    factor_of, own = 1.0, jax.random.fold_in(key, 6)
    for dim, shards_of in shards:
        heights = jnp.exp(jax.random.uniform(jax.random.fold_in(own, dim), (shards_of,), jnp.float32, least / len(shards), high / len(shards)))
        factor_of = factor_of * jnp.repeat(heights, dims[dim] // shards_of).reshape([-1 if axis == dim else 1 for axis in range(len(dims))])
    return factor_of


def shared_out(stream_key, own, number, rows, count, top, reach, lean):
    order = jax.random.permutation(stream_key, count)
    crowded, usual = shares(count, rows * top, reach, lean, True), shares(count, rows * top, reach, lean, False)
    places = jnp.arange(count)

    def named(sizes, rotation):
        used = int((sizes > 0).sum())
        fixed = max(1, used // 4)
        shifted = fixed + (places - fixed + rotation * (used - fixed)) % max(1, count - fixed)
        return jnp.zeros((count,), jnp.int32).at[order[jnp.where(places < fixed, places, shifted)]].set(jnp.asarray(sizes, jnp.int32))

    sizes = jnp.where(number % 4 == 0, named(crowded, number // 4), named(usual, number - number // 4 - 1))
    mixed = jax.random.permutation(jax.random.fold_in(own, 3), count)
    source_of, receiver = mixed[0:count // 2 * 2:2], mixed[1:count // 2 * 2:2]
    slack = jnp.minimum(sizes[source_of] - 1, reach - sizes[receiver]) // 2
    slack = jnp.where((source_of == order[0]) | (receiver == order[0]) | (sizes[receiver] == 0), 0, jnp.maximum(slack, 0))
    shifted = jax.random.randint(jax.random.fold_in(own, 4), (count // 2,), 0, 1 << 20) % (slack + 1)
    sizes = sizes.at[source_of].add(-shifted).at[receiver].add(shifted)
    items = jnp.searchsorted(jnp.cumsum(sizes), jnp.arange(rows * top), side="right").astype(jnp.int32)
    grid = items.reshape(top, rows).T
    grid = grid[jax.random.permutation(jax.random.fold_in(own, 1), rows)]
    rotation = jax.random.randint(jax.random.fold_in(own, 2), (rows, 1), 0, top)
    return jnp.take_along_axis(grid, (jnp.arange(top)[None, :] + rotation) % top, axis=1)


def shares(amount, total, reach, skew, full):
    portions = [(1 << 20) // math.isqrt(grade ** skew) + 1 for grade in range(1, amount + 1)]
    largest = reach if full else min(reach, max(-(-total // amount), total * portions[0] // sum(portions)))
    least = 1 if total - largest >= amount - 1 else 0
    given, surplus = [largest] + [least] * (amount - 1), total - largest - least * (amount - 1)
    while surplus > 0:
        candidates = [i for i in range(1, amount) if given[i] < largest] or [i for i in range(1, amount) if given[i] < reach]
        whole, budget = sum([portions[i] for i in candidates]), surplus
        for i in candidates:
            extra = min(reach - given[i], max(1, budget * portions[i] // whole), surplus)
            given[i] = given[i] + extra
            surplus = surplus - extra
    return np.array(given)


def normal_values(rng, extent, scale, reach, split=(), kind=jnp.bfloat16):
    factor_of = shard_levels(rng, extent, split, -0.22, 0.18) if split else 1.0
    values = jax.random.normal(rng, extent, jnp.float32) * scale * factor_of
    return jnp.minimum(jnp.maximum(values, -reach), reach).astype(kind)


def setup_inputs(seed: int = 0) -> dict:
    key_list = jax.random.split(jax.random.key(seed), 9)
    mel = normal_values(key_list[0], (CLIPS, FRAMES, MEL), 1.0, 6.0, ((0, 512),))
    lengths = touch_ends(jax.random.randint(key_list[1], (CLIPS,), 1, FRAMES + 1), jax.random.fold_in(key_list[1], 1), 1, FRAMES).astype(jnp.int32)
    routes_keys = jax.random.split(jax.random.fold_in(key_list[2], 1), CLIPS // CLIPS_DEV)
    routes_turns = jax.random.permutation(jax.random.fold_in(key_list[2], 3), CLIPS // CLIPS_DEV)
    routes = jax.vmap(lambda own, number: shared_out(jax.random.fold_in(key_list[2], 2), own, number, CLIPS_DEV, N_ENC, 1, SLOTS, 2))(routes_keys, routes_turns).reshape((CLIPS, 1))
    conv1_weight = normal_values(key_list[3], (3 * MEL, D), (3 * MEL) ** -0.5, 0.3125)
    conv1_bias = normal_values(key_list[4], (D,), 0.5, 3.0, (), jnp.float32)
    conv2_weight = normal_values(key_list[5], (D, 3 * D2), (3 * D) ** -0.5, 0.09375, ((0, 16),))
    conv2_bias = normal_values(key_list[6], (D2,), 0.5, 3.0, (), jnp.float32)
    out_grad = normal_values(key_list[7], (CLIPS, HALF, D2), 1.0, 6.0, ((0, 512),))
    return {"mel": mel, "lengths": lengths, "routes": routes, "conv1_weight": conv1_weight, "conv1_bias": conv1_bias, "conv2_weight": conv2_weight, "conv2_bias": conv2_bias, "out_grad": out_grad}


inv_root_two = 0.7071067811865476
inv_root_tau = 0.3989422804014327


def gelu_value(values):
    return 0.5 * values * (1.0 + lax.erf(values * inv_root_two))


def gelu_slope(values):
    return 0.5 * (1.0 + lax.erf(values * inv_root_two)) + values * jnp.exp(-0.5 * values * values) * inv_root_tau


def tap_rows(second_grad):
    clip_count, half_frames, out_width = second_grad.shape
    later_grad = jnp.pad(second_grad[:, 1:], ((0, 0), (0, 1), (0, 0)))
    zero_rows = jnp.zeros_like(second_grad)
    even_rows = jnp.concatenate([zero_rows, second_grad, zero_rows], axis=2)
    odd_rows = jnp.concatenate([later_grad, zero_rows, second_grad], axis=2)
    return jnp.stack([even_rows, odd_rows], axis=2).reshape(clip_count * half_frames * 2, 3 * out_width)


def stem_block(mel, length_f, out_grad, first_weight, first_bias, second_weight, second_bias):
    clip_count, frames, mel_bins = mel.shape
    half_frames = frames // 2
    out_width = second_weight.shape[1] // 3
    live_first = (jnp.arange(frames, dtype=jnp.float32)[None, :] < length_f[:, None])
    masked = jnp.where(live_first[:, :, None], mel, jnp.zeros_like(mel))
    padded = jnp.pad(masked, ((0, 0), (1, 1), (0, 0)))
    columns = jnp.concatenate([padded[:, :frames], padded[:, 1:frames + 1], padded[:, 2:]], axis=2)
    columns = columns.reshape(clip_count * frames, 3 * mel_bins)
    live_rows = live_first.reshape(clip_count * frames, 1).astype(jnp.float32)
    first_pre = jnp.dot(columns, first_weight, preferred_element_type=jnp.float32) + first_bias
    first_act = (gelu_value(first_pre) * live_rows).astype(jnp.bfloat16)
    taps_out = jnp.dot(first_act, second_weight, preferred_element_type=jnp.float32)
    taps_out = taps_out.reshape(clip_count, half_frames, 2, 3, out_width)
    earlier = jnp.pad(taps_out[:, :-1, 1, 0], ((0, 0), (1, 0), (0, 0)))
    second_pre = earlier + taps_out[:, :, 0, 1] + taps_out[:, :, 1, 2] + second_bias
    live_second = (2.0 * jnp.arange(half_frames, dtype=jnp.float32)[None, :] < length_f[:, None]).astype(jnp.float32)[:, :, None]
    features = (gelu_value(second_pre) * live_second).astype(jnp.bfloat16)
    second_grad = (out_grad.astype(jnp.float32) * gelu_slope(second_pre) * live_second).astype(jnp.bfloat16)
    stacked = tap_rows(second_grad)
    act_grad = lax.dot_general(stacked, second_weight, (((1,), (1,)), ((), ())), preferred_element_type=jnp.float32)
    first_grad = (act_grad * gelu_slope(first_pre) * live_rows).astype(jnp.bfloat16)
    weight_grad = lax.dot_general(columns, first_grad, (((0,), (0,)), ((), ())), preferred_element_type=jnp.float32)
    bias_grad = jnp.sum(first_grad.astype(jnp.float32), axis=0)
    second_bias_grad = jnp.sum(second_grad.astype(jnp.float32), axis=(0, 1))
    second_weight_grad = lax.dot_general(first_act, stacked, (((0,), (0,)), ((), ())), preferred_element_type=jnp.float32)
    return features, weight_grad, bias_grad, second_bias_grad, second_weight_grad


def reference(mel, lengths, routes, conv1_weight, conv1_bias, conv2_weight, conv2_bias, out_grad):
    device_count = N_ENC * N_DP
    mel_blocks = mel.reshape(device_count, CLIPS_DEV, FRAMES, MEL)
    length_blocks = lengths.astype(jnp.float32).reshape(device_count, CLIPS_DEV)
    grad_blocks = out_grad.reshape(device_count, CLIPS_DEV, HALF, D2)

    def one_device(carry, device_block):
        features, weight_grad, bias_grad, second_bias_grad, second_weight_grad = stem_block(
            device_block[0], device_block[1], device_block[2], conv1_weight, conv1_bias, conv2_weight, conv2_bias)
        carry = (carry[0] + weight_grad, carry[1] + bias_grad, carry[2] + second_bias_grad, carry[3] + second_weight_grad)
        return carry, features

    start = (jnp.zeros((3 * MEL, D), jnp.float32), jnp.zeros((D,), jnp.float32),
             jnp.zeros((D2,), jnp.float32), jnp.zeros((D, 3 * D2), jnp.float32))
    sums, features = lax.scan(one_device, start, (mel_blocks, length_blocks, grad_blocks))
    owner_of = routes[:, 0].reshape(device_count, CLIPS_DEV)
    owner_hits = (owner_of[:, :, None] == jnp.arange(N_ENC, dtype=jnp.int32)[None, None, :]).astype(jnp.int32)
    slot_rank = jnp.sum((jnp.cumsum(owner_hits, axis=1) - owner_hits) * owner_hits, axis=2)
    device_ids = jnp.arange(device_count, dtype=jnp.int32)
    enc_ids = (device_ids // N_DP)[:, None]
    group_ids = (device_ids % N_DP)[:, None]
    target = (owner_of * N_DP + group_ids) * (N_ENC * SLOTS) + enc_ids * SLOTS + slot_rank
    packed = jnp.zeros((ALL_SLOTS, HALF, D2), jnp.bfloat16)
    packed = packed.at[target.reshape(-1).astype(jnp.int32)].set(features.reshape(CLIPS, HALF, D2))
    return packed, sums[0], sums[1], sums[2], sums[3]
```

```python
import functools

import jax
import jax.numpy as jnp
from jax import lax
from jax.experimental import pallas as pl
from jax.experimental.pallas import tpu as pltpu
from jax.sharding import Mesh
from jax.sharding import PartitionSpec as P

inv_root_two = 0.7071067811865476
inv_root_tau = 0.3989422804014327

MEL = 128
D2 = 640
ROWS = 80
LANES = 128
CHIPS = 8
CLIPS = 16
HALF = 8
STEPS = CLIPS * HALF
SLOTS = 2 * CLIPS
PACK = 1536
TILES = 19
VMEM = 56 * 1024 * 1024
ALL_AXES = ("xh", "y", "c", "z", "xl")
ENC = ("xh", "y", "c")
CHIP = ("xh", "y")
F32 = jnp.float32
BF16 = jnp.bfloat16


def gelu_both(values):
    cdf = 0.5 * (1.0 + lax.erf(values * inv_root_two))
    return values * cdf, cdf + values * jnp.exp(-0.5 * values * values) * inv_root_tau


def shift_down(values):
    rows, width = values.shape
    t = lax.broadcasted_iota(jnp.int32, (rows, width), 0) & (HALF - 1)
    clips = values.reshape(rows // HALF, HALF, width)
    moved = pltpu.roll(clips, 1, 1).reshape(rows, width)
    return jnp.where(t == 0, 0.0, moved)


def shift_up(values):
    rows, width = values.shape
    t = lax.broadcasted_iota(jnp.int32, (rows, width), 0) & (HALF - 1)
    clips = values.reshape(rows // HALF, HALF, width)
    moved = pltpu.roll(clips, HALF - 1, 1).reshape(rows, width)
    return jnp.where(t == HALF - 1, 0.0, moved)


def dot(left, right):
    return jnp.dot(left, right, preferred_element_type=F32)


def dot_nt(left, right):
    return lax.dot_general(left, right, (((1,), (1,)), ((), ())), preferred_element_type=F32)


def dot_tn(left, right):
    return lax.dot_general(left, right, (((0,), (0,)), ((), ())), preferred_element_type=F32)


def forward_kernel(pay_ref, w1_ref, b1_ref, w2_ref, part_ref, cols_ref, act_ref, slope_ref):
    spread = (
        lax.broadcasted_iota(jnp.int32, (STEPS, CLIPS), 0) >> 3
        == lax.broadcasted_iota(jnp.int32, (STEPS, CLIPS), 1)
    ).astype(F32).astype(BF16)
    length = dot(spread, pay_ref[0, STEPS : STEPS + CLIPS, :LANES])
    t = (lax.broadcasted_iota(jnp.int32, (STEPS, LANES), 0) & (HALF - 1)).astype(F32)
    live_even, live_odd = 2.0 * t < length, 2.0 * t + 1.0 < length
    even = jnp.where(live_even, pay_ref[0, :STEPS, :LANES].astype(F32), 0.0)
    odd = jnp.where(live_odd, pay_ref[0, :STEPS, LANES:].astype(F32), 0.0)
    cols_ref[0, :, :LANES] = shift_down(odd).astype(BF16)
    cols_ref[0, :, LANES : 2 * LANES] = even.astype(BF16)
    cols_ref[0, :, 2 * LANES : 3 * LANES] = odd.astype(BF16)
    cols_ref[0, :, 3 * LANES :] = shift_up(even).astype(BF16)
    bias = b1_ref[...]
    mask_even = jnp.where(live_even, 1.0, 0.0)
    mask_odd = jnp.where(live_odd, 1.0, 0.0)
    mask_even = jnp.concatenate([mask_even, mask_even], axis=1)
    mask_odd = jnp.concatenate([mask_odd, mask_odd], axis=1)
    act, slope = gelu_both(dot(cols_ref[0, :, : 3 * LANES], w1_ref[...]) + bias)
    act_even = (act * mask_even).astype(BF16)
    slope_ref[0, 0] = slope * mask_even
    act, slope = gelu_both(dot(cols_ref[0, :, LANES:], w1_ref[...]) + bias)
    act = act * mask_odd
    act_odd = act.astype(BF16)
    slope_ref[0, 1] = slope * mask_odd
    act_prior = shift_down(act).astype(BF16)
    act_ref[0, 0] = act_prior
    act_ref[0, 1] = act_even
    act_ref[0, 2] = act_odd
    total = dot(act_prior, w2_ref[:, :D2])
    total = total + dot(act_even, w2_ref[:, D2 : 2 * D2])
    total = total + dot(act_odd, w2_ref[:, 2 * D2 :])
    part_ref[0] = total.astype(BF16)


def middle_kernel(part_ref, grad_ref, b2_ref, length_ref, owner_col_ref, owner_row_ref, rep_ref, placed_ref):
    pre = part_ref[0].astype(F32)
    for source in range(1, CHIPS):
        pre = pre + part_ref[source].astype(F32)
    pre = pre + b2_ref[...]
    t = (lax.broadcasted_iota(jnp.int32, (STEPS, 1), 0) & (HALF - 1)).astype(F32)
    live = jnp.where(2.0 * t < length_ref[...], 1.0, 0.0)
    value, slope = gelu_both(pre)
    features = (value * live).astype(BF16)
    second_grad = (grad_ref[...].astype(F32) * slope * live).astype(BF16)
    for target in range(CHIPS):
        rep_ref[target] = second_grad
    here = lax.broadcasted_iota(jnp.int32, (STEPS, STEPS), 0)
    there = lax.broadcasted_iota(jnp.int32, (STEPS, STEPS), 1)
    same = (owner_col_ref[...] == owner_row_ref[...]) & ((here >> 3) < (there >> 3))
    same = same & ((here & (HALF - 1)) == 0)
    rank = jnp.sum(jnp.where(same, 1.0, 0.0), axis=0, keepdims=True).astype(jnp.int32)
    place = lax.broadcasted_iota(jnp.int32, (1, STEPS), 1) & (HALF - 1)
    place = (owner_row_ref[...] * 2 + rank) * HALF + place
    wanted = lax.broadcasted_iota(jnp.int32, (SLOTS * HALF, STEPS), 0) == place
    placed_ref[...] = dot(jnp.where(wanted, 1.0, 0.0).astype(BF16), features).astype(BF16)


def backward_kernel(
    where_ref, grad_ref, w2_ref, cols_ref, act_ref, slope_ref, pack_ref,
    conv2_sum, conv1_sum, bias1_sum, bias2_sum, bias2_col,
):
    step = pl.program_id(0)

    @pl.when(step == 0)
    def _():
        conv2_sum[...] = jnp.zeros_like(conv2_sum)
        conv1_sum[...] = jnp.zeros_like(conv1_sum)
        bias1_sum[...] = jnp.zeros_like(bias1_sum)
        bias2_sum[...] = jnp.zeros_like(bias2_sum)

    rows = 2 * STEPS
    grad = grad_ref[...].reshape(rows, D2)
    bias2_sum[...] += jnp.sum(grad.astype(F32), axis=0, keepdims=True)
    even = dot_nt(grad, w2_ref[:, D2 : 2 * D2])
    odd = dot_nt(grad, w2_ref[:, 2 * D2 :]) + shift_up(dot_nt(grad, w2_ref[:, :D2]))
    even = (even * slope_ref[:, 0].reshape(rows, 2 * LANES)).astype(BF16)
    odd = (odd * slope_ref[:, 1].reshape(rows, 2 * LANES)).astype(BF16)
    cols = cols_ref[...].reshape(rows, 4 * LANES)
    conv1_sum[...] += dot_tn(even, cols[:, : 3 * LANES]) + dot_tn(odd, cols[:, LANES:])
    ones = jnp.ones((rows, LANES), BF16)
    bias1_sum[...] += dot_tn(even, ones) + dot_tn(odd, ones)
    for tap in range(3):
        conv2_sum[:, tap * D2 : (tap + 1) * D2] += dot_tn(
            act_ref[:, tap].reshape(rows, 2 * LANES), grad
        )

    @pl.when(step == pl.num_programs(0) - 1)
    def _():
        core, place = where_ref[0], where_ref[1]
        for tile in range(D2 // LANES):
            block = bias2_sum[:, tile * LANES : (tile + 1) * LANES]
            bias2_col[tile * LANES : (tile + 1) * LANES, :] = jnp.broadcast_to(block, (LANES, LANES)).T
        lane = lax.broadcasted_iota(jnp.int32, (ROWS, LANES), 1)
        for side in range(2):
            target = core if side == 0 else 1 - core
            first = side * LANES
            for tile in range(15):
                block = conv2_sum[first : first + ROWS, tile * LANES : (tile + 1) * LANES]
                pack_ref[target, tile * ROWS : (tile + 1) * ROWS, :] = block.astype(BF16)
            for tile in range(3):
                block = conv1_sum[first : first + ROWS, tile * LANES : (tile + 1) * LANES]
                pack_ref[target, (15 + tile) * ROWS : (16 + tile) * ROWS, :] = block.astype(BF16)
            holder = 2 * place + target
            start = pl.multiple_of(jnp.minimum(holder, CHIPS - 1) * ROWS, 16)
            second = jnp.where(holder < CHIPS, bias2_col[pl.ds(start, ROWS), :], 0.0)
            block = jnp.where(lane == 0, bias1_sum[first : first + ROWS, :], jnp.where(lane == 1, second, 0.0))
            pack_ref[target, 18 * ROWS : 19 * ROWS, :] = block.astype(BF16)
            pack_ref[target, 19 * ROWS :, :] = jnp.zeros((PACK - 19 * ROWS, LANES), BF16)


def unpack_kernel(pack_ref, out_ref):
    for tile in range(15):
        out_ref[:, tile * LANES : (tile + 1) * LANES] = pack_ref[tile * ROWS : (tile + 1) * ROWS, :].astype(F32)


def last_kernel(got_ref, weight_ref, bias1_ref, bias2_ref, whole):
    for tile in range(4):
        for source in range(16):
            whole[source * ROWS : (source + 1) * ROWS, :] = got_ref[
                source, tile * ROWS : (tile + 1) * ROWS, :
            ].astype(F32)
        for block in range(10):
            turned = whole[block * LANES : (block + 1) * LANES, :].T
            if tile < 3:
                weight_ref[tile * LANES : (tile + 1) * LANES, block * LANES : (block + 1) * LANES] = turned
            else:
                bias1_ref[:, block * LANES : (block + 1) * LANES] = turned[0:1, :]
                if block < D2 // LANES:
                    bias2_ref[:, block * LANES : (block + 1) * LANES] = turned[1:2, :]


def exchange(values, axes):
    return lax.all_to_all(values, axes, split_axis=0, concat_axis=0, tiled=True)


def spread_to(values, count):
    return jnp.broadcast_to(values[None], (count,) + values.shape)


def vmem():
    return pl.BlockSpec(memory_space=pltpu.VMEM)


def params(*semantics):
    return pltpu.CompilerParams(vmem_limit_bytes=VMEM, dimension_semantics=semantics or None)


def local(mel, lengths, routes, conv1_weight, conv1_bias, conv2_weight, conv2_bias, out_grad):
    core = lax.axis_index("c")
    chip = lax.axis_index(CHIP)
    place = 2 * chip + core

    def shape(*dims, dtype=BF16):
        return jax.ShapeDtypeStruct(dims, dtype)

    other_weight = lax.ppermute(conv2_weight, "c", [(0, 1), (1, 0)])
    lengths_bf = lengths.astype(BF16)
    pay = jnp.concatenate(
        [mel.reshape(STEPS, 2 * MEL), jnp.broadcast_to(lengths_bf[:, None], (CLIPS, 2 * MEL))], axis=0
    )
    pay_rows = pay.shape[0]
    got_pay = exchange(spread_to(pay, CHIPS), CHIP)

    def side(index):
        weight = lax.dynamic_slice(conv1_weight, (0, index * ROWS), (3 * MEL, ROWS))
        bias = lax.dynamic_slice(conv1_bias, (index * ROWS,), (ROWS,))
        return jnp.pad(weight, ((0, 0), (0, LANES - ROWS))), jnp.pad(bias, (0, LANES - ROWS))

    own_w1, own_b1 = side(place)
    other_w1, other_b1 = side(2 * chip + 1 - core)
    w1 = jnp.concatenate([own_w1, other_w1], axis=1)
    b1 = jnp.concatenate([own_b1, other_b1])[None]
    gap = jnp.zeros((LANES - ROWS, 3 * D2), BF16)
    w2 = jnp.concatenate([conv2_weight, gap, other_weight, gap], axis=0)

    wide = 2 * LANES
    parts, cols, acts, slopes = pl.pallas_call(
        forward_kernel,
        grid=(CHIPS,),
        in_specs=[
            pl.BlockSpec((1, pay_rows, 2 * MEL), lambda i: (i, 0, 0)),
            pl.BlockSpec((3 * MEL, wide), lambda i: (0, 0)),
            pl.BlockSpec((1, wide), lambda i: (0, 0)),
            pl.BlockSpec((wide, 3 * D2), lambda i: (0, 0)),
        ],
        out_specs=[
            pl.BlockSpec((1, STEPS, D2), lambda i: (i, 0, 0)),
            pl.BlockSpec((1, STEPS, 4 * LANES), lambda i: (i, 0, 0)),
            pl.BlockSpec((1, 3, STEPS, wide), lambda i: (i, 0, 0, 0)),
            pl.BlockSpec((1, 2, STEPS, wide), lambda i: (i, 0, 0, 0)),
        ],
        out_shape=[
            shape(CHIPS, STEPS, D2),
            shape(CHIPS, STEPS, 4 * LANES),
            shape(CHIPS, 3, STEPS, wide),
            shape(CHIPS, 2, STEPS, wide, dtype=F32),
        ],
        compiler_params=params("arbitrary"),
        name="stem_forward",
    )(got_pay.reshape(CHIPS, pay_rows, 2 * MEL), w1, b1, w2)

    got_parts = exchange(parts, CHIP)
    owner = jnp.repeat(routes[:, 0], HALF)
    rep, placed = pl.pallas_call(
        middle_kernel,
        in_specs=[vmem()] * 6,
        out_specs=[vmem()] * 2,
        out_shape=[shape(CHIPS, STEPS, D2), shape(SLOTS * HALF, D2)],
        compiler_params=params(),
        name="stem_middle",
    )(
        got_parts,
        out_grad.reshape(STEPS, D2),
        conv2_bias[None],
        jnp.repeat(lengths.astype(F32), HALF)[:, None],
        owner[:, None],
        owner[None],
    )
    got_grad = exchange(rep, CHIP)
    packed = exchange(placed.reshape(16, 2 * HALF, D2), ENC).reshape(SLOTS, HALF, D2)

    pair = lambda i: (i, 0, 0)
    pair4 = lambda i: (i, 0, 0, 0)
    pack = pl.pallas_call(
        backward_kernel,
        grid=(CHIPS // 2,),
        in_specs=[
            pl.BlockSpec(memory_space=pltpu.SMEM),
            pl.BlockSpec((2, STEPS, D2), pair),
            pl.BlockSpec((wide, 3 * D2), lambda i: (0, 0)),
            pl.BlockSpec((2, STEPS, 4 * LANES), pair),
            pl.BlockSpec((2, 3, STEPS, wide), pair4),
            pl.BlockSpec((2, 2, STEPS, wide), pair4),
        ],
        out_specs=pl.BlockSpec((2, PACK, LANES), lambda i: (0, 0, 0)),
        out_shape=shape(2, PACK, LANES),
        scratch_shapes=[
            pltpu.VMEM((wide, 3 * D2), F32),
            pltpu.VMEM((wide, 3 * LANES), F32),
            pltpu.VMEM((wide, LANES), F32),
            pltpu.VMEM((1, D2), F32),
            pltpu.VMEM((D2, LANES), F32),
        ],
        compiler_params=params("arbitrary"),
        name="stem_backward",
    )(jnp.stack([core, chip]).astype(jnp.int32), got_grad, w2, cols, acts, slopes)

    quarters = exchange(pack.reshape(4, PACK // 2, LANES), ("c", "xl"))
    half = jnp.sum(quarters.astype(F32), axis=0).astype(BF16)
    pieces = exchange(half.reshape(16, PACK // 32, LANES), "z")
    piece = jnp.sum(pieces.astype(F32), axis=0).astype(BF16)
    half = exchange(spread_to(piece, 16), "z").reshape(PACK // 2, LANES)
    whole = exchange(spread_to(half, 2), "xl").reshape(PACK, LANES)
    conv2_rows_grad = pl.pallas_call(
        unpack_kernel,
        in_specs=[vmem()],
        out_specs=vmem(),
        out_shape=shape(ROWS, 3 * D2, dtype=F32),
        compiler_params=params(),
        name="conv2_unpack",
    )(whole)
    shares = exchange(spread_to(whole[15 * ROWS : 19 * ROWS], 16), ENC)
    weight_grad, bias_grad, second_bias_grad = pl.pallas_call(
        last_kernel,
        in_specs=[vmem()],
        out_specs=[vmem()] * 3,
        out_shape=[
            shape(3 * MEL, 16 * ROWS, dtype=F32),
            shape(1, 16 * ROWS, dtype=F32),
            shape(1, D2, dtype=F32),
        ],
        scratch_shapes=[pltpu.VMEM((16 * ROWS, LANES), F32)],
        compiler_params=params(),
        name="conv1_unpack",
    )(shares)
    return (packed, weight_grad, bias_grad[0], second_bias_grad[0], conv2_rows_grad)


def solution(mesh):
    fine = Mesh(mesh.devices.reshape(2, 4, 2, 16, 2), ALL_AXES)
    placed = (
        P(ALL_AXES, None, None),
        P(ALL_AXES),
        P(ALL_AXES, None),
        P(),
        P(),
        P(ENC, None),
        P(),
        P(ALL_AXES, None, None),
    )
    return jax.shard_map(
        local,
        mesh=fine,
        in_specs=placed,
        out_specs=(P(ALL_AXES, None, None), P(), P(), P(), P(ENC, None)),
        check_vma=False,
    )
```

```python
import functools

import jax
import jax.numpy as jnp
from jax import lax
from jax.experimental import pallas as pl
from jax.experimental.pallas import tpu as pltpu
from jax.sharding import Mesh
from jax.sharding import PartitionSpec as P

inv_root_two = 0.7071067811865476
inv_root_tau = 0.3989422804014327

MEL = 128
D2 = 640
ROWS = 80
LANES = 128
HOLDERS = 4
BLOCKS = 4
WIDE = 384
CLIPS = 16
HALF = 8
STEPS = CLIPS * HALF
SLOTS = 2 * CLIPS
PACK = 896
HALF_ROWS = 8 * ROWS
VMEM = 56 * 1024 * 1024
ALL_AXES = ("xh", "y", "c", "z", "xl")
ENC = ("xh", "y", "c")
F32 = jnp.float32
BF16 = jnp.bfloat16


def gelu_both(values):
    cdf = 0.5 * (1.0 + lax.erf(values * inv_root_two))
    return values * cdf, cdf + values * jnp.exp(-0.5 * values * values) * inv_root_tau


def shift_down(values):
    rows, width = values.shape
    t = lax.broadcasted_iota(jnp.int32, (rows, width), 0) & (HALF - 1)
    clips = values.reshape(rows // HALF, HALF, width)
    moved = pltpu.roll(clips, 1, 1).reshape(rows, width)
    return jnp.where(t == 0, 0.0, moved)


def shift_up(values):
    rows, width = values.shape
    t = lax.broadcasted_iota(jnp.int32, (rows, width), 0) & (HALF - 1)
    clips = values.reshape(rows // HALF, HALF, width)
    moved = pltpu.roll(clips, HALF - 1, 1).reshape(rows, width)
    return jnp.where(t == HALF - 1, 0.0, moved)


def dot(left, right):
    return jnp.dot(left, right, preferred_element_type=F32)


def dot_nt(left, right):
    return lax.dot_general(left, right, (((1,), (1,)), ((), ())), preferred_element_type=F32)


def dot_tn(left, right):
    return lax.dot_general(left, right, (((0,), (0,)), ((), ())), preferred_element_type=F32)


def stack_weights(refs, w2_ref):
    @pl.when(pl.program_id(0) == 0)
    def _():
        for block, ref in enumerate(refs):
            w2_ref[block * ROWS : (block + 1) * ROWS, :] = ref[...]
        w2_ref[BLOCKS * ROWS :, :] = jnp.zeros((WIDE - BLOCKS * ROWS, 3 * D2), BF16)


def forward_kernel(
    pay_ref, w1_ref, b1_ref, own_ref, side_ref, far_ref, both_ref, part_ref, cols_ref, act_ref, slope_ref, w2_ref
):
    stack_weights((own_ref, side_ref, far_ref, both_ref), w2_ref)
    spread = (
        lax.broadcasted_iota(jnp.int32, (STEPS, CLIPS), 0) >> 3
        == lax.broadcasted_iota(jnp.int32, (STEPS, CLIPS), 1)
    ).astype(F32).astype(BF16)
    length = dot(spread, pay_ref[0, STEPS : STEPS + CLIPS, :LANES])
    t = (lax.broadcasted_iota(jnp.int32, (STEPS, LANES), 0) & (HALF - 1)).astype(F32)
    live_even, live_odd = 2.0 * t < length, 2.0 * t + 1.0 < length
    even = jnp.where(live_even, pay_ref[0, :STEPS, :LANES].astype(F32), 0.0)
    odd = jnp.where(live_odd, pay_ref[0, :STEPS, LANES:].astype(F32), 0.0)
    cols_ref[0, :, :LANES] = shift_down(odd).astype(BF16)
    cols_ref[0, :, LANES : 2 * LANES] = even.astype(BF16)
    cols_ref[0, :, 2 * LANES : 3 * LANES] = odd.astype(BF16)
    cols_ref[0, :, 3 * LANES :] = shift_up(even).astype(BF16)
    bias = b1_ref[...]
    mask_even = jnp.where(live_even, 1.0, 0.0)
    mask_odd = jnp.where(live_odd, 1.0, 0.0)
    mask_even = jnp.concatenate([mask_even] * (WIDE // LANES), axis=1)
    mask_odd = jnp.concatenate([mask_odd] * (WIDE // LANES), axis=1)
    act, slope = gelu_both(dot(cols_ref[0, :, : 3 * LANES], w1_ref[...]) + bias)
    act_even = (act * mask_even).astype(BF16)
    slope_ref[0, 0] = slope * mask_even
    act, slope = gelu_both(dot(cols_ref[0, :, LANES:], w1_ref[...]) + bias)
    act = act * mask_odd
    act_odd = act.astype(BF16)
    slope_ref[0, 1] = slope * mask_odd
    act_prior = shift_down(act).astype(BF16)
    act_ref[0, 0] = act_prior
    act_ref[0, 1] = act_even
    act_ref[0, 2] = act_odd
    total = dot(act_prior, w2_ref[:, :D2])
    total = total + dot(act_even, w2_ref[:, D2 : 2 * D2])
    total = total + dot(act_odd, w2_ref[:, 2 * D2 :])
    part_ref[0] = total.astype(BF16)


def middle_kernel(part_ref, grad_ref, b2_ref, length_ref, owner_col_ref, owner_row_ref, rep_ref, placed_ref):
    pre = part_ref[0].astype(F32)
    for source in range(1, HOLDERS):
        pre = pre + part_ref[source].astype(F32)
    pre = pre + b2_ref[...]
    t = (lax.broadcasted_iota(jnp.int32, (STEPS, 1), 0) & (HALF - 1)).astype(F32)
    live = jnp.where(2.0 * t < length_ref[...], 1.0, 0.0)
    value, slope = gelu_both(pre)
    features = (value * live).astype(BF16)
    second_grad = (grad_ref[...].astype(F32) * slope * live).astype(BF16)
    for target in range(HOLDERS):
        rep_ref[target] = second_grad
    here = lax.broadcasted_iota(jnp.int32, (STEPS, STEPS), 0)
    there = lax.broadcasted_iota(jnp.int32, (STEPS, STEPS), 1)
    same = (owner_col_ref[...] == owner_row_ref[...]) & ((here >> 3) < (there >> 3))
    same = same & ((here & (HALF - 1)) == 0)
    rank = jnp.sum(jnp.where(same, 1.0, 0.0), axis=0, keepdims=True).astype(jnp.int32)
    place = lax.broadcasted_iota(jnp.int32, (1, STEPS), 1) & (HALF - 1)
    place = (owner_row_ref[...] * 2 + rank) * HALF + place
    wanted = lax.broadcasted_iota(jnp.int32, (SLOTS * HALF, STEPS), 0) == place
    placed_ref[...] = dot(jnp.where(wanted, 1.0, 0.0).astype(BF16), features).astype(BF16)


def backward_kernel(
    where_ref, grad_ref, own_ref, side_ref, far_ref, both_ref, cols_ref, act_ref, slope_ref, keep_ref, send_ref,
    w2_ref, conv2_sum, conv1_sum, bias1_sum, bias2_sum,
):
    stack_weights((own_ref, side_ref, far_ref, both_ref), w2_ref)
    step = pl.program_id(0)

    @pl.when(step == 0)
    def _():
        conv2_sum[...] = jnp.zeros_like(conv2_sum)
        conv1_sum[...] = jnp.zeros_like(conv1_sum)
        bias1_sum[...] = jnp.zeros_like(bias1_sum)
        bias2_sum[...] = jnp.zeros_like(bias2_sum)

    rows = 2 * STEPS
    grad = grad_ref[...].reshape(rows, D2)
    bias2_sum[...] += jnp.sum(grad.astype(F32), axis=0, keepdims=True)
    even = dot_nt(grad, w2_ref[:, D2 : 2 * D2])
    odd = dot_nt(grad, w2_ref[:, 2 * D2 :]) + shift_up(dot_nt(grad, w2_ref[:, :D2]))
    even = (even * slope_ref[:, 0].reshape(rows, WIDE)).astype(BF16)
    odd = (odd * slope_ref[:, 1].reshape(rows, WIDE)).astype(BF16)
    cols = cols_ref[...].reshape(rows, 4 * LANES)
    conv1_sum[...] += dot_tn(even, cols[:, : 3 * LANES]) + dot_tn(odd, cols[:, LANES:])
    bias1_sum[...] += jnp.sum(even.astype(F32) + odd.astype(F32), axis=0, keepdims=True)
    for tap in range(3):
        conv2_sum[:, tap * D2 : (tap + 1) * D2] += dot_tn(act_ref[:, tap].reshape(rows, WIDE), grad)

    @pl.when(step == pl.num_programs(0) - 1)
    def _():
        mine = where_ref[0]
        for block in range(BLOCKS):
            target = mine if block < 2 else 1 - mine
            out = keep_ref if block % 2 == 0 else send_ref
            first = block * ROWS
            for tile in range(15):
                half, spot = tile // 8, tile % 8
                piece = conv2_sum[first : first + ROWS, tile * LANES : (tile + 1) * LANES]
                out[target, half, spot * ROWS : (spot + 1) * ROWS, :] = piece.astype(out.dtype)
            out[target, 1, 7 * ROWS : 8 * ROWS, :] = jnp.zeros((ROWS, LANES), out.dtype)
            biases = [jnp.concatenate([bias1_sum[:, first : first + ROWS], jnp.zeros((1, LANES - ROWS), F32)], axis=1)]
            for tile in range(D2 // LANES):
                biases.append(bias2_sum[:, tile * LANES : (tile + 1) * LANES])
            biases.append(jnp.zeros((16 - len(biases), LANES), F32))
            biases = jnp.concatenate(biases, axis=0).astype(out.dtype)
            for half in range(2):
                for tile in range(3):
                    piece = conv1_sum[first : first + ROWS, tile * LANES : (tile + 1) * LANES]
                    out[target, half, (8 + tile) * ROWS : (9 + tile) * ROWS, :] = piece.astype(out.dtype)
                out[target, half, 11 * ROWS :, :] = biases


def sum_kernel(got_ref, out_ref):
    total = got_ref[0].astype(F32)
    for source in range(1, got_ref.shape[0]):
        total = total + got_ref[source].astype(F32)
    total = total.astype(BF16)
    if len(out_ref.shape) == 2:
        out_ref[...] = total
    else:
        for target in range(out_ref.shape[0]):
            out_ref[target] = total


def unpack_kernel(where_ref, own_ref, other_ref, out_ref):
    first = where_ref[1] == 0
    for tile in range(15):
        half, spot = tile // 8, tile % 8
        rows = slice(spot * ROWS, (spot + 1) * ROWS)
        own, other = own_ref[rows, :].astype(F32), other_ref[rows, :].astype(F32)
        picked = jnp.where(first, own, other) if half == 0 else jnp.where(first, other, own)
        out_ref[:, tile * LANES : (tile + 1) * LANES] = picked


def last_kernel(got_ref, weight_ref, bias1_ref, bias2_ref, whole):
    for tile in range(3):
        for source in range(16):
            whole[source * ROWS : (source + 1) * ROWS, :] = got_ref[
                source, tile * ROWS : (tile + 1) * ROWS, :
            ].astype(F32)
        for block in range(10):
            weight_ref[tile * LANES : (tile + 1) * LANES, block * LANES : (block + 1) * LANES] = whole[
                block * LANES : (block + 1) * LANES, :
            ].T
    pieces = [got_ref[source, 3 * ROWS :, :].astype(F32) for source in range(16)]
    bias1_ref[...] = jnp.concatenate([piece[0:1, :ROWS] for piece in pieces], axis=1)
    bias2_ref[...] = jnp.concatenate([pieces[0][1 + tile : 2 + tile, :] for tile in range(D2 // LANES)], axis=1)


def exchange(values, axes):
    return lax.all_to_all(values, axes, split_axis=0, concat_axis=0, tiled=True)


def spread_to(values, count):
    return jnp.broadcast_to(values[None], (count,) + values.shape)


def vmem():
    return pl.BlockSpec(memory_space=pltpu.VMEM)


def params(*semantics):
    return pltpu.CompilerParams(vmem_limit_bytes=VMEM, dimension_semantics=semantics or None)


def local(mel, lengths, routes, conv1_weight, conv1_bias, conv2_weight, conv2_bias, out_grad):
    x_hi, y, core = lax.axis_index("xh"), lax.axis_index("y"), lax.axis_index("c")
    where = jnp.stack([x_hi, lax.axis_index("xl")]).astype(jnp.int32)

    def shape(*dims, dtype=BF16):
        return jax.ShapeDtypeStruct(dims, dtype)

    weights = [
        conv2_weight,
        lax.ppermute(conv2_weight, "c", [(0, 1), (1, 0)]),
        lax.ppermute(conv2_weight, "xh", [(0, 1), (1, 0)]),
        lax.ppermute(conv2_weight, ("xh", "c"), [(0, 3), (3, 0), (1, 2), (2, 1)]),
    ]
    lengths_bf = lengths.astype(BF16)
    pay = jnp.concatenate(
        [mel.reshape(STEPS, 2 * MEL), jnp.broadcast_to(lengths_bf[:, None], (CLIPS, 2 * MEL))], axis=0
    )
    pay_rows = pay.shape[0]
    got_pay = exchange(spread_to(pay, HOLDERS), "y")

    w1, b1 = [], []
    for flip_x, flip_c in ((0, 0), (0, 1), (1, 0), (1, 1)):
        place = ((x_hi ^ flip_x) * HOLDERS + y) * 2 + (core ^ flip_c)
        w1.append(lax.dynamic_slice(conv1_weight, (0, place * ROWS), (3 * MEL, ROWS)))
        b1.append(lax.dynamic_slice(conv1_bias, (place * ROWS,), (ROWS,)))
    gap = WIDE - BLOCKS * ROWS
    w1 = jnp.concatenate(w1 + [jnp.zeros((3 * MEL, gap), BF16)], axis=1)
    b1 = jnp.concatenate(b1 + [jnp.zeros((gap,), F32)])[None]

    parts, cols, acts, slopes = pl.pallas_call(
        forward_kernel,
        grid=(HOLDERS,),
        in_specs=[
            pl.BlockSpec((1, pay_rows, 2 * MEL), lambda i: (i, 0, 0)),
            pl.BlockSpec((3 * MEL, WIDE), lambda i: (0, 0)),
            pl.BlockSpec((1, WIDE), lambda i: (0, 0)),
            *[pl.BlockSpec((ROWS, 3 * D2), lambda i: (0, 0))] * BLOCKS,
        ],
        out_specs=[
            pl.BlockSpec((1, STEPS, D2), lambda i: (i, 0, 0)),
            pl.BlockSpec((1, STEPS, 4 * LANES), lambda i: (i, 0, 0)),
            pl.BlockSpec((1, 3, STEPS, WIDE), lambda i: (i, 0, 0, 0)),
            pl.BlockSpec((1, 2, STEPS, WIDE), lambda i: (i, 0, 0, 0)),
        ],
        out_shape=[
            shape(HOLDERS, STEPS, D2),
            shape(HOLDERS, STEPS, 4 * LANES),
            shape(HOLDERS, 3, STEPS, WIDE),
            shape(HOLDERS, 2, STEPS, WIDE, dtype=F32),
        ],
        scratch_shapes=[pltpu.VMEM((WIDE, 3 * D2), BF16)],
        compiler_params=params("arbitrary"),
        name="stem_forward",
    )(got_pay.reshape(HOLDERS, pay_rows, 2 * MEL), w1, b1, *weights)

    got_parts = exchange(parts, "y")
    owner = jnp.repeat(routes[:, 0], HALF)
    rep, placed = pl.pallas_call(
        middle_kernel,
        in_specs=[vmem()] * 6,
        out_specs=[vmem()] * 2,
        out_shape=[shape(HOLDERS, STEPS, D2), shape(SLOTS * HALF, D2)],
        compiler_params=params(),
        name="stem_middle",
    )(
        got_parts,
        out_grad.reshape(STEPS, D2),
        conv2_bias[None],
        jnp.repeat(lengths.astype(F32), HALF)[:, None],
        owner[:, None],
        owner[None],
    )
    got_grad = exchange(rep, "y")
    packed = exchange(placed.reshape(16, 2 * HALF, D2), ENC)

    pair = lambda i: (i, 0, 0)
    pair4 = lambda i: (i, 0, 0, 0)
    whole = lambda i: (0, 0, 0, 0)
    keep, send = pl.pallas_call(
        backward_kernel,
        grid=(HOLDERS // 2,),
        in_specs=[
            pl.BlockSpec(memory_space=pltpu.SMEM),
            pl.BlockSpec((2, STEPS, D2), pair),
            *[pl.BlockSpec((ROWS, 3 * D2), lambda i: (0, 0))] * BLOCKS,
            pl.BlockSpec((2, STEPS, 4 * LANES), pair),
            pl.BlockSpec((2, 3, STEPS, WIDE), pair4),
            pl.BlockSpec((2, 2, STEPS, WIDE), pair4),
        ],
        out_specs=[pl.BlockSpec((2, 2, PACK, LANES), whole)] * 2,
        out_shape=[shape(2, 2, PACK, LANES, dtype=F32), shape(2, 2, PACK, LANES)],
        scratch_shapes=[
            pltpu.VMEM((WIDE, 3 * D2), BF16),
            pltpu.VMEM((WIDE, 3 * D2), F32),
            pltpu.VMEM((WIDE, 3 * LANES), F32),
            pltpu.VMEM((1, WIDE), F32),
            pltpu.VMEM((1, D2), F32),
        ],
        compiler_params=params("arbitrary"),
        cost_estimate=pl.CostEstimate(flops=24 * 10**8, bytes_accessed=8 * 10**6, transcendentals=0),
        name="stem_backward",
    )(where, got_grad, *weights, cols, acts, slopes)
    send, packed = lax.optimization_barrier((send, packed))
    got = lax.ppermute(send, "c", [(0, 1), (1, 0)])
    quarters = exchange((keep + got.astype(F32)).astype(BF16).reshape(4, PACK, LANES), ("xh", "xl"))

    def summed(values, *dims):
        return pl.pallas_call(
            sum_kernel,
            in_specs=[vmem()],
            out_specs=vmem(),
            out_shape=shape(*dims),
            compiler_params=params(),
            name="gradient_sum",
        )(values)

    half = summed(quarters, PACK, LANES)
    pieces = exchange(half.reshape(16, PACK // 16, LANES), "z")
    half = exchange(summed(pieces, 16, PACK // 16, LANES), "z").reshape(PACK, LANES)
    shares = exchange(spread_to(half[HALF_ROWS:], 16), ENC)
    own = half[:HALF_ROWS]
    conv2_rows_grad = pl.pallas_call(
        unpack_kernel,
        in_specs=[pl.BlockSpec(memory_space=pltpu.SMEM), vmem(), vmem()],
        out_specs=vmem(),
        out_shape=shape(ROWS, 3 * D2, dtype=F32),
        compiler_params=params(),
        name="conv2_unpack",
    )(where, own, lax.ppermute(own, "xl", [(0, 1), (1, 0)]))
    weight_grad, bias_grad, second_bias_grad = pl.pallas_call(
        last_kernel,
        in_specs=[vmem()],
        out_specs=[vmem()] * 3,
        out_shape=[
            shape(3 * MEL, 16 * ROWS, dtype=F32),
            shape(1, 16 * ROWS, dtype=F32),
            shape(1, D2, dtype=F32),
        ],
        scratch_shapes=[pltpu.VMEM((16 * ROWS, LANES), F32)],
        compiler_params=params(),
        name="conv1_unpack",
    )(shares)
    return (
        packed.reshape(SLOTS, HALF, D2),
        weight_grad,
        bias_grad[0],
        second_bias_grad[0],
        conv2_rows_grad,
    )


def solution(mesh):
    fine = Mesh(mesh.devices.reshape(2, 4, 2, 16, 2), ALL_AXES)
    placed = (
        P(ALL_AXES, None, None),
        P(ALL_AXES),
        P(ALL_AXES, None),
        P(),
        P(),
        P(ENC, None),
        P(),
        P(ALL_AXES, None, None),
    )
    return jax.shard_map(
        local,
        mesh=fine,
        in_specs=placed,
        out_specs=(P(ALL_AXES, None, None), P(), P(), P(), P(ENC, None)),
        check_vma=False,
    )
```

```python
import functools

import jax
import jax.numpy as jnp
from jax import lax
from jax.experimental import pallas as pl
from jax.experimental.pallas import tpu as pltpu
from jax.sharding import Mesh
from jax.sharding import PartitionSpec as P

inv_root_two = 0.7071067811865476
inv_root_tau = 0.3989422804014327

MEL = 128
D2 = 640
ROWS = 80
LANES = 128
HOLDERS = 4
BLOCKS = 4
WIDE = 384
CLIPS = 16
HALF = 8
STEPS = CLIPS * HALF
SLOTS = 2 * CLIPS
PACK = 896
HALF_ROWS = 8 * ROWS
VMEM = 56 * 1024 * 1024
ALL_AXES = ("xh", "y", "c", "zh", "zl", "xl")
ENC = ("xh", "y", "c")
F32 = jnp.float32
BF16 = jnp.bfloat16


def gelu_both(values):
    cdf = 0.5 * (1.0 + lax.erf(values * inv_root_two))
    return values * cdf, cdf + values * jnp.exp(-0.5 * values * values) * inv_root_tau


def shift_down(values):
    rows, width = values.shape
    t = lax.broadcasted_iota(jnp.int32, (rows, width), 0) & (HALF - 1)
    clips = values.reshape(rows // HALF, HALF, width)
    moved = pltpu.roll(clips, 1, 1).reshape(rows, width)
    return jnp.where(t == 0, 0.0, moved)


def shift_up(values):
    rows, width = values.shape
    t = lax.broadcasted_iota(jnp.int32, (rows, width), 0) & (HALF - 1)
    clips = values.reshape(rows // HALF, HALF, width)
    moved = pltpu.roll(clips, HALF - 1, 1).reshape(rows, width)
    return jnp.where(t == HALF - 1, 0.0, moved)


def dot(left, right):
    return jnp.dot(left, right, preferred_element_type=F32)


def dot_nt(left, right):
    return lax.dot_general(left, right, (((1,), (1,)), ((), ())), preferred_element_type=F32)


def dot_tn(left, right):
    return lax.dot_general(left, right, (((0,), (0,)), ((), ())), preferred_element_type=F32)


def stack_weights(refs, w2_ref):
    @pl.when(pl.program_id(0) == 0)
    def _():
        for block, ref in enumerate(refs):
            w2_ref[block * ROWS : (block + 1) * ROWS, :] = ref[...]
        w2_ref[BLOCKS * ROWS :, :] = jnp.zeros((WIDE - BLOCKS * ROWS, 3 * D2), BF16)


def prepare_kernel(length_ref, mel_ref, pay_ref):
    clip = lax.broadcasted_iota(jnp.int32, (CLIPS, MEL), 0)
    length = jnp.zeros((CLIPS, MEL), F32)
    for index in range(CLIPS):
        length = jnp.where(clip == index, length_ref[index].astype(F32), length)
    for target in range(HOLDERS):
        pay_ref[target, :CLIPS] = mel_ref[...]
        pay_ref[target, CLIPS] = length.astype(BF16)


def forward_kernel(
    pay_ref, w1_ref, b1_ref, own_ref, side_ref, far_ref, both_ref, part_ref, cols_ref, act_ref, slope_ref, w2_ref,
    frames_ref,
):
    stack_weights((own_ref, side_ref, far_ref, both_ref), w2_ref)
    spread = (
        lax.broadcasted_iota(jnp.int32, (STEPS, CLIPS), 0) >> 3
        == lax.broadcasted_iota(jnp.int32, (STEPS, CLIPS), 1)
    ).astype(F32).astype(BF16)
    length = dot(spread, pay_ref[0, CLIPS])
    frames_ref[...] = pay_ref[0, :CLIPS].astype(F32).reshape(2 * STEPS, MEL)
    t = (lax.broadcasted_iota(jnp.int32, (STEPS, LANES), 0) & (HALF - 1)).astype(F32)
    live_even, live_odd = 2.0 * t < length, 2.0 * t + 1.0 < length
    even = jnp.where(live_even, frames_ref[pl.ds(0, STEPS, 2), :], 0.0)
    odd = jnp.where(live_odd, frames_ref[pl.ds(1, STEPS, 2), :], 0.0)
    cols_ref[0, :, :LANES] = shift_down(odd).astype(BF16)
    cols_ref[0, :, LANES : 2 * LANES] = even.astype(BF16)
    cols_ref[0, :, 2 * LANES : 3 * LANES] = odd.astype(BF16)
    cols_ref[0, :, 3 * LANES :] = shift_up(even).astype(BF16)
    bias = b1_ref[...]
    mask_even = jnp.where(live_even, 1.0, 0.0)
    mask_odd = jnp.where(live_odd, 1.0, 0.0)
    mask_even = jnp.concatenate([mask_even] * (WIDE // LANES), axis=1)
    mask_odd = jnp.concatenate([mask_odd] * (WIDE // LANES), axis=1)
    act, slope = gelu_both(dot(cols_ref[0, :, : 3 * LANES], w1_ref[...]) + bias)
    act_even = (act * mask_even).astype(BF16)
    slope_ref[0, 0] = slope * mask_even
    act, slope = gelu_both(dot(cols_ref[0, :, LANES:], w1_ref[...]) + bias)
    act = act * mask_odd
    act_odd = act.astype(BF16)
    slope_ref[0, 1] = slope * mask_odd
    act_prior = shift_down(act).astype(BF16)
    act_ref[0, 0] = act_prior
    act_ref[0, 1] = act_even
    act_ref[0, 2] = act_odd
    total = dot(act_prior, w2_ref[:, :D2])
    total = total + dot(act_even, w2_ref[:, D2 : 2 * D2])
    total = total + dot(act_odd, w2_ref[:, 2 * D2 :])
    part_ref[0] = total.astype(BF16)


def middle_kernel(part_ref, grad_ref, b2_ref, length_ref, owner_col_ref, owner_row_ref, rep_ref, feature_ref):
    pre = part_ref[0].astype(F32)
    for source in range(1, HOLDERS):
        pre = pre + part_ref[source].astype(F32)
    pre = pre + b2_ref[...]
    t = (lax.broadcasted_iota(jnp.int32, (STEPS, 1), 0) & (HALF - 1)).astype(F32)
    live = jnp.where(2.0 * t < length_ref[...], 1.0, 0.0)
    value, slope = gelu_both(pre)
    features = (value * live).astype(BF16)
    second_grad = (grad_ref[...].astype(F32) * slope * live).astype(BF16)
    for target in range(HOLDERS):
        rep_ref[target] = second_grad
    here = lax.broadcasted_iota(jnp.int32, (STEPS, STEPS), 0)
    there = lax.broadcasted_iota(jnp.int32, (STEPS, STEPS), 1)
    same = (owner_col_ref[...] == owner_row_ref[...]) & ((here >> 3) < (there >> 3))
    same = same & ((here & (HALF - 1)) == 0)
    rank = jnp.sum(jnp.where(same, 1.0, 0.0), axis=0, keepdims=True)
    slot = owner_row_ref[...].astype(F32) * 2.0 + rank
    feature_ref[:STEPS, :] = features
    feature_ref[STEPS:, :] = jnp.zeros((16, D2), BF16)
    feature_ref[STEPS:, :LANES] = jnp.broadcast_to(slot, (16, LANES)).astype(BF16)


def place_kernel(where_ref, got_ref, out_ref):
    row = lax.broadcasted_iota(jnp.int32, (16, STEPS), 0)
    lane = lax.broadcasted_iota(jnp.int32, (16, STEPS), 1)
    same = (row & (HALF - 1)) == (lane & (HALF - 1))
    first = where_ref[2] * 2
    for source in range(16):
        start = source * (STEPS + 16)
        slot = got_ref[start + STEPS : start + STEPS + 16, :LANES].astype(F32).astype(jnp.int32)
        wanted = jnp.where(same & (slot == first + (row >> 3)), 1.0, 0.0).astype(BF16)
        out_ref[source * 16 : (source + 1) * 16, :] = dot(wanted, got_ref[start : start + STEPS, :]).astype(BF16)


def backward_kernel(
    where_ref, grad_ref, own_ref, side_ref, far_ref, both_ref, cols_ref, act_ref, slope_ref, keep_ref, send_ref,
    w2_ref, conv2_sum, conv1_sum, bias1_sum, bias2_sum,
):
    stack_weights((own_ref, side_ref, far_ref, both_ref), w2_ref)
    step = pl.program_id(0)

    @pl.when(step == 0)
    def _():
        conv2_sum[...] = jnp.zeros_like(conv2_sum)
        conv1_sum[...] = jnp.zeros_like(conv1_sum)
        bias1_sum[...] = jnp.zeros_like(bias1_sum)
        bias2_sum[...] = jnp.zeros_like(bias2_sum)

    rows = 2 * STEPS
    grad = grad_ref[...].reshape(rows, D2)
    bias2_sum[...] += jnp.sum(grad.astype(F32), axis=0, keepdims=True)
    even = dot_nt(grad, w2_ref[:, D2 : 2 * D2])
    odd = dot_nt(grad, w2_ref[:, 2 * D2 :]) + shift_up(dot_nt(grad, w2_ref[:, :D2]))
    even = (even * slope_ref[:, 0].reshape(rows, WIDE)).astype(BF16)
    odd = (odd * slope_ref[:, 1].reshape(rows, WIDE)).astype(BF16)
    cols = cols_ref[...].reshape(rows, 4 * LANES)
    conv1_sum[...] += dot_tn(even, cols[:, : 3 * LANES]) + dot_tn(odd, cols[:, LANES:])
    bias1_sum[...] += jnp.sum(even.astype(F32) + odd.astype(F32), axis=0, keepdims=True)
    for tap in range(3):
        conv2_sum[:, tap * D2 : (tap + 1) * D2] += dot_tn(act_ref[:, tap].reshape(rows, WIDE), grad)

    @pl.when(step == pl.num_programs(0) - 1)
    def _():
        mine = where_ref[0]
        for block in range(BLOCKS):
            target = mine if block < 2 else 1 - mine
            out = keep_ref if block % 2 == 0 else send_ref
            first = block * ROWS
            for tile in range(15):
                half, spot = tile // 8, tile % 8
                piece = conv2_sum[first : first + ROWS, tile * LANES : (tile + 1) * LANES]
                out[target, half, spot * ROWS : (spot + 1) * ROWS, :] = piece.astype(out.dtype)
            out[target, 1, 7 * ROWS : 8 * ROWS, :] = jnp.zeros((ROWS, LANES), out.dtype)
            biases = [jnp.concatenate([bias1_sum[:, first : first + ROWS], jnp.zeros((1, LANES - ROWS), F32)], axis=1)]
            for tile in range(D2 // LANES):
                biases.append(bias2_sum[:, tile * LANES : (tile + 1) * LANES])
            biases.append(jnp.zeros((16 - len(biases), LANES), F32))
            biases = jnp.concatenate(biases, axis=0).astype(out.dtype)
            for half in range(2):
                for tile in range(3):
                    piece = conv1_sum[first : first + ROWS, tile * LANES : (tile + 1) * LANES]
                    out[target, half, (8 + tile) * ROWS : (9 + tile) * ROWS, :] = piece.astype(out.dtype)
                out[target, half, 11 * ROWS :, :] = biases


def sum_kernel(got_ref, out_ref):
    total = got_ref[0].astype(F32)
    for source in range(1, got_ref.shape[0]):
        total = total + got_ref[source].astype(F32)
    total = total.astype(BF16)
    if len(out_ref.shape) == 2:
        out_ref[...] = total
    else:
        for target in range(out_ref.shape[0]):
            out_ref[target] = total


def last_kernel(
    where_ref, got_ref, bias_ref, own_ref, other_ref, weight_ref, bias1_ref, bias2_ref, conv2_ref, whole
):
    for source in range(16):
        whole[source * ROWS : (source + 1) * ROWS, :] = got_ref[source].astype(F32)
    for block in range(10):
        columns = slice(block * LANES, (block + 1) * LANES)
        weight_ref[:, columns] = whole[columns, :].T

    @pl.when(pl.program_id(0) == 0)
    def _():
        pieces = [bias_ref[source].astype(F32) for source in range(16)]
        bias1 = jnp.concatenate([piece[0:1, :ROWS] for piece in pieces], axis=1)
        bias1_ref[...] = bias1.reshape(16 * ROWS)
        bias2 = jnp.concatenate([pieces[0][1 + tile : 2 + tile, :] for tile in range(D2 // LANES)], axis=1)
        bias2_ref[...] = bias2.reshape(D2)
        first = where_ref[1] == 0
        for tile in range(15):
            half, spot = tile // 8, tile % 8
            rows = slice(spot * ROWS, (spot + 1) * ROWS)
            own, other = own_ref[rows, :].astype(F32), other_ref[rows, :].astype(F32)
            picked = jnp.where(first, own, other) if half == 0 else jnp.where(first, other, own)
            conv2_ref[:, tile * LANES : (tile + 1) * LANES] = picked


def exchange(values, axes):
    return lax.all_to_all(values, axes, split_axis=0, concat_axis=0, tiled=True)


def spread_to(values, count):
    return jnp.broadcast_to(values[None], (count,) + values.shape)


def vmem():
    return pl.BlockSpec(memory_space=pltpu.VMEM)


def params(*semantics):
    return pltpu.CompilerParams(vmem_limit_bytes=VMEM, dimension_semantics=semantics or None)


def local(mel, lengths, routes, conv1_weight, conv1_bias, conv2_weight, conv2_bias, out_grad):
    x_hi, y, core = lax.axis_index("xh"), lax.axis_index("y"), lax.axis_index("c")
    where = jnp.stack([x_hi, lax.axis_index("xl"), (x_hi * HOLDERS + y) * 2 + core]).astype(jnp.int32)

    def shape(*dims, dtype=BF16):
        return jax.ShapeDtypeStruct(dims, dtype)

    pay = pl.pallas_call(
        prepare_kernel,
        in_specs=[pl.BlockSpec(memory_space=pltpu.SMEM), vmem()],
        out_specs=vmem(),
        out_shape=shape(HOLDERS, CLIPS + 1, 2 * HALF, MEL),
        compiler_params=params(),
        name="mel_payload",
    )(lengths, mel)
    got_pay = exchange(pay, "y")
    weights = [
        conv2_weight,
        lax.ppermute(conv2_weight, "c", [(0, 1), (1, 0)]),
        lax.ppermute(conv2_weight, ("xh", "xl"), [(0, 3), (3, 0), (1, 2), (2, 1)]),
        lax.ppermute(conv2_weight, ("xh", "c", "xl"), [(i, 7 - i) for i in range(8)]),
    ]

    w1, b1 = [], []
    for flip_x, flip_c in ((0, 0), (0, 1), (1, 0), (1, 1)):
        place = ((x_hi ^ flip_x) * HOLDERS + y) * 2 + (core ^ flip_c)
        w1.append(lax.dynamic_slice(conv1_weight, (0, place * ROWS), (3 * MEL, ROWS)))
        b1.append(lax.dynamic_slice(conv1_bias, (place * ROWS,), (ROWS,)))
    gap = WIDE - BLOCKS * ROWS
    w1 = jnp.concatenate(w1 + [jnp.zeros((3 * MEL, gap), BF16)], axis=1)
    b1 = jnp.concatenate(b1 + [jnp.zeros((gap,), F32)])[None]

    parts, cols, acts, slopes = pl.pallas_call(
        forward_kernel,
        grid=(HOLDERS,),
        in_specs=[
            pl.BlockSpec((1, CLIPS + 1, 2 * HALF, MEL), lambda i: (i, 0, 0, 0)),
            pl.BlockSpec((3 * MEL, WIDE), lambda i: (0, 0)),
            pl.BlockSpec((1, WIDE), lambda i: (0, 0)),
            *[pl.BlockSpec((ROWS, 3 * D2), lambda i: (0, 0))] * BLOCKS,
        ],
        out_specs=[
            pl.BlockSpec((1, STEPS, D2), lambda i: (i, 0, 0)),
            pl.BlockSpec((1, STEPS, 4 * LANES), lambda i: (i, 0, 0)),
            pl.BlockSpec((1, 3, STEPS, WIDE), lambda i: (i, 0, 0, 0)),
            pl.BlockSpec((1, 2, STEPS, WIDE), lambda i: (i, 0, 0, 0)),
        ],
        out_shape=[
            shape(HOLDERS, STEPS, D2),
            shape(HOLDERS, STEPS, 4 * LANES),
            shape(HOLDERS, 3, STEPS, WIDE),
            shape(HOLDERS, 2, STEPS, WIDE, dtype=F32),
        ],
        scratch_shapes=[pltpu.VMEM((WIDE, 3 * D2), BF16), pltpu.VMEM((2 * STEPS, MEL), F32)],
        compiler_params=params("arbitrary"),
        name="stem_forward",
    )(got_pay, w1, b1, *weights)

    got_parts = exchange(parts, "y")
    owner = jnp.repeat(routes[:, 0], HALF)
    rep, features = pl.pallas_call(
        middle_kernel,
        in_specs=[vmem()] * 6,
        out_specs=[vmem()] * 2,
        out_shape=[shape(HOLDERS, STEPS, D2), shape(STEPS + 16, D2)],
        compiler_params=params(),
        name="stem_middle",
    )(
        got_parts,
        out_grad.reshape(STEPS, D2),
        conv2_bias[None],
        jnp.repeat(lengths.astype(F32), HALF)[:, None],
        owner[:, None],
        owner[None],
    )
    got_grad = exchange(rep, "y")

    pair = lambda i: (i, 0, 0)
    pair4 = lambda i: (i, 0, 0, 0)
    whole = lambda i: (0, 0, 0, 0)
    keep, send = pl.pallas_call(
        backward_kernel,
        grid=(HOLDERS // 2,),
        in_specs=[
            pl.BlockSpec(memory_space=pltpu.SMEM),
            pl.BlockSpec((2, STEPS, D2), pair),
            *[pl.BlockSpec((ROWS, 3 * D2), lambda i: (0, 0))] * BLOCKS,
            pl.BlockSpec((2, STEPS, 4 * LANES), pair),
            pl.BlockSpec((2, 3, STEPS, WIDE), pair4),
            pl.BlockSpec((2, 2, STEPS, WIDE), pair4),
        ],
        out_specs=[pl.BlockSpec((2, 2, PACK, LANES), whole)] * 2,
        out_shape=[shape(2, 2, PACK, LANES, dtype=F32), shape(2, 2, PACK, LANES)],
        scratch_shapes=[
            pltpu.VMEM((WIDE, 3 * D2), BF16),
            pltpu.VMEM((WIDE, 3 * D2), F32),
            pltpu.VMEM((WIDE, 3 * LANES), F32),
            pltpu.VMEM((1, WIDE), F32),
            pltpu.VMEM((1, D2), F32),
        ],
        compiler_params=params("arbitrary"),
        name="stem_backward",
    )(where, got_grad, *weights, cols, acts, slopes)
    got = lax.ppermute(send, "c", [(0, 1), (1, 0)])
    quarters = exchange((keep + got.astype(F32)).astype(BF16).reshape(4, PACK, LANES), ("xh", "xl"))

    def summed(values, *dims):
        return pl.pallas_call(
            sum_kernel,
            in_specs=[vmem()],
            out_specs=vmem(),
            out_shape=shape(*dims),
            compiler_params=params(),
            name="gradient_sum",
        )(values)

    half = summed(quarters, PACK, LANES)
    half, features = lax.optimization_barrier((half, features))
    got_features = lax.all_gather(features, ENC, axis=0, tiled=True)
    quarter = PACK // 4
    near = summed(exchange(half.reshape(4, quarter, LANES), "zl"), 4, quarter, LANES)
    far = summed(exchange(near, "zh"), 4, quarter, LANES)
    half = exchange(far, "zl").reshape(PACK, LANES)
    shares = exchange(spread_to(half[HALF_ROWS:], 16), ENC)
    own = half[:HALF_ROWS]
    other = lax.ppermute(own, "xl", [(0, 1), (1, 0)])
    packed = pl.pallas_call(
        place_kernel,
        in_specs=[pl.BlockSpec(memory_space=pltpu.SMEM), vmem()],
        out_specs=vmem(),
        out_shape=shape(SLOTS * HALF, D2),
        compiler_params=params(),
        name="features_place",
    )(where, got_features)
    shares, packed = lax.optimization_barrier((shares, packed))
    weight_grad, bias_grad, second_bias_grad, conv2_rows_grad = pl.pallas_call(
        last_kernel,
        grid=(3,),
        in_specs=[
            pl.BlockSpec(memory_space=pltpu.SMEM),
            pl.BlockSpec((16, ROWS, LANES), lambda i: (0, i, 0)),
            pl.BlockSpec((16, 16, LANES), lambda i: (0, 3 * ROWS // 16, 0)),
            pl.BlockSpec((HALF_ROWS, LANES), lambda i: (0, 0)),
            pl.BlockSpec((HALF_ROWS, LANES), lambda i: (0, 0)),
        ],
        out_specs=[
            pl.BlockSpec((LANES, 16 * ROWS), lambda i: (i, 0)),
            pl.BlockSpec((16 * ROWS,), lambda i: (0,)),
            pl.BlockSpec((D2,), lambda i: (0,)),
            pl.BlockSpec((ROWS, 3 * D2), lambda i: (0, 0)),
        ],
        out_shape=[
            shape(3 * MEL, 16 * ROWS, dtype=F32),
            shape(16 * ROWS, dtype=F32),
            shape(D2, dtype=F32),
            shape(ROWS, 3 * D2, dtype=F32),
        ],
        scratch_shapes=[pltpu.VMEM((16 * ROWS, LANES), F32)],
        compiler_params=params("arbitrary"),
        name="gradient_unpack",
    )(where, shares, shares, own, other)
    return packed.reshape(SLOTS, HALF, D2), weight_grad, bias_grad, second_bias_grad, conv2_rows_grad


def solution(mesh):
    fine = Mesh(mesh.devices.reshape(2, 4, 2, 4, 4, 2), ALL_AXES)
    placed = (
        P(ALL_AXES, None, None),
        P(ALL_AXES),
        P(ALL_AXES, None),
        P(),
        P(),
        P(ENC, None),
        P(),
        P(ALL_AXES, None, None),
    )
    return jax.shard_map(
        local,
        mesh=fine,
        in_specs=placed,
        out_specs=(P(ALL_AXES, None, None), P(), P(), P(), P(ENC, None)),
        check_vma=False,
    )
```

```python
import functools

import jax
import jax.numpy as jnp
from jax import lax
from jax.experimental import pallas as pl
from jax.experimental.pallas import tpu as pltpu
from jax.sharding import Mesh
from jax.sharding import PartitionSpec as P

inv_root_two = 0.7071067811865476
inv_root_tau = 0.3989422804014327

MEL = 128
D2 = 640
ROWS = 80
LANES = 128
HOLDERS = 4
BLOCKS = 4
WIDE = 384
CLIPS = 16
HALF = 8
STEPS = CLIPS * HALF
SLOTS = 2 * CLIPS
PACK = 896
HALF_ROWS = 8 * ROWS
VMEM = 56 * 1024 * 1024
ALL_AXES = ("xh", "y", "c", "zh", "zl", "xl")
ENC = ("xh", "y", "c")
F32 = jnp.float32
BF16 = jnp.bfloat16


def gelu_both(values):
    cdf = 0.5 * (1.0 + lax.erf(values * inv_root_two))
    return values * cdf, cdf + values * jnp.exp(-0.5 * values * values) * inv_root_tau


def shift_down(values):
    rows, width = values.shape
    t = lax.broadcasted_iota(jnp.int32, (rows, width), 0) & (HALF - 1)
    clips = values.reshape(rows // HALF, HALF, width)
    moved = pltpu.roll(clips, 1, 1).reshape(rows, width)
    return jnp.where(t == 0, 0.0, moved)


def shift_up(values):
    rows, width = values.shape
    t = lax.broadcasted_iota(jnp.int32, (rows, width), 0) & (HALF - 1)
    clips = values.reshape(rows // HALF, HALF, width)
    moved = pltpu.roll(clips, HALF - 1, 1).reshape(rows, width)
    return jnp.where(t == HALF - 1, 0.0, moved)


def dot(left, right):
    return jnp.dot(left, right, preferred_element_type=F32)


def dot_nt(left, right):
    return lax.dot_general(left, right, (((1,), (1,)), ((), ())), preferred_element_type=F32)


def dot_tn(left, right):
    return lax.dot_general(left, right, (((0,), (0,)), ((), ())), preferred_element_type=F32)


def stack_weights(refs, w2_ref):
    @pl.when(pl.program_id(0) == 0)
    def _():
        for block, ref in enumerate(refs):
            w2_ref[block * ROWS : (block + 1) * ROWS, :] = ref[...]
        w2_ref[BLOCKS * ROWS :, :] = jnp.zeros((WIDE - BLOCKS * ROWS, 3 * D2), BF16)


def prepare_kernel(length_ref, mel_ref, pay_ref):
    clip = lax.broadcasted_iota(jnp.int32, (CLIPS, MEL), 0)
    length = jnp.zeros((CLIPS, MEL), F32)
    for index in range(CLIPS):
        length = jnp.where(clip == index, length_ref[index].astype(F32), length)
    for target in range(HOLDERS):
        pay_ref[target, :CLIPS] = mel_ref[...]
        pay_ref[target, CLIPS] = length.astype(BF16)


def first_kernel(pay_ref, w1_ref, b1_ref, cols_ref, act_ref, slope_ref, frames_ref):
    spread = (
        lax.broadcasted_iota(jnp.int32, (STEPS, CLIPS), 0) >> 3
        == lax.broadcasted_iota(jnp.int32, (STEPS, CLIPS), 1)
    ).astype(F32).astype(BF16)
    length = dot(spread, pay_ref[0, CLIPS])
    frames_ref[...] = pay_ref[0, :CLIPS].astype(F32).reshape(2 * STEPS, MEL)
    t = (lax.broadcasted_iota(jnp.int32, (STEPS, LANES), 0) & (HALF - 1)).astype(F32)
    live_even, live_odd = 2.0 * t < length, 2.0 * t + 1.0 < length
    even = jnp.where(live_even, frames_ref[pl.ds(0, STEPS, 2), :], 0.0)
    odd = jnp.where(live_odd, frames_ref[pl.ds(1, STEPS, 2), :], 0.0)
    cols_ref[0, :, :LANES] = shift_down(odd).astype(BF16)
    cols_ref[0, :, LANES : 2 * LANES] = even.astype(BF16)
    cols_ref[0, :, 2 * LANES : 3 * LANES] = odd.astype(BF16)
    cols_ref[0, :, 3 * LANES :] = shift_up(even).astype(BF16)
    bias = b1_ref[...]
    mask_even = jnp.where(live_even, 1.0, 0.0)
    mask_odd = jnp.where(live_odd, 1.0, 0.0)
    mask_even = jnp.concatenate([mask_even] * (WIDE // LANES), axis=1)
    mask_odd = jnp.concatenate([mask_odd] * (WIDE // LANES), axis=1)
    act, slope = gelu_both(dot(cols_ref[0, :, : 3 * LANES], w1_ref[...]) + bias)
    act_even = (act * mask_even).astype(BF16)
    slope_ref[0, 0] = slope * mask_even
    act, slope = gelu_both(dot(cols_ref[0, :, LANES:], w1_ref[...]) + bias)
    act = act * mask_odd
    act_odd = act.astype(BF16)
    slope_ref[0, 1] = slope * mask_odd
    act_prior = shift_down(act).astype(BF16)
    act_ref[0, 0] = act_prior
    act_ref[0, 1] = act_even
    act_ref[0, 2] = act_odd


def second_kernel(act_ref, own_ref, side_ref, far_ref, both_ref, part_ref, w2_ref):
    stack_weights((own_ref, side_ref, far_ref, both_ref), w2_ref)
    rows = 2 * STEPS
    total = dot(act_ref[:, 0].reshape(rows, WIDE), w2_ref[:, :D2])
    total = total + dot(act_ref[:, 1].reshape(rows, WIDE), w2_ref[:, D2 : 2 * D2])
    total = total + dot(act_ref[:, 2].reshape(rows, WIDE), w2_ref[:, 2 * D2 :])
    part_ref[...] = total.astype(BF16).reshape(2, STEPS, D2)


def middle_kernel(part_ref, grad_ref, b2_ref, length_ref, owner_col_ref, owner_row_ref, rep_ref, feature_ref):
    pre = part_ref[0].astype(F32)
    for source in range(1, HOLDERS):
        pre = pre + part_ref[source].astype(F32)
    pre = pre + b2_ref[...]
    t = (lax.broadcasted_iota(jnp.int32, (STEPS, 1), 0) & (HALF - 1)).astype(F32)
    live = jnp.where(2.0 * t < length_ref[...], 1.0, 0.0)
    value, slope = gelu_both(pre)
    features = (value * live).astype(BF16)
    second_grad = (grad_ref[...].astype(F32) * slope * live).astype(BF16)
    for target in range(HOLDERS):
        rep_ref[target] = second_grad
    here = lax.broadcasted_iota(jnp.int32, (STEPS, STEPS), 0)
    there = lax.broadcasted_iota(jnp.int32, (STEPS, STEPS), 1)
    same = (owner_col_ref[...] == owner_row_ref[...]) & ((here >> 3) < (there >> 3))
    same = same & ((here & (HALF - 1)) == 0)
    rank = jnp.sum(jnp.where(same, 1.0, 0.0), axis=0, keepdims=True)
    place = lax.broadcasted_iota(jnp.int32, (1, STEPS), 1) & (HALF - 1)
    place = (owner_row_ref[...] * 2 + rank.astype(jnp.int32)) * HALF + place
    wanted = lax.broadcasted_iota(jnp.int32, (SLOTS * HALF, STEPS), 0) == place
    placed = dot(jnp.where(wanted, 1.0, 0.0).astype(BF16), features).astype(BF16)
    for target in range(16):
        for tile in range(D2 // LANES):
            feature_ref[target, tile * 16 : (tile + 1) * 16, :] = placed[
                target * 16 : (target + 1) * 16, tile * LANES : (tile + 1) * LANES
            ]


def backward_kernel(
    where_ref, grad_ref, own_ref, side_ref, far_ref, both_ref, cols_ref, act_ref, slope_ref, keep_ref, send_ref,
    w2_ref, conv2_sum, conv1_sum, bias1_sum, bias2_sum,
):
    stack_weights((own_ref, side_ref, far_ref, both_ref), w2_ref)
    step = pl.program_id(0)

    @pl.when(step == 0)
    def _():
        conv2_sum[...] = jnp.zeros_like(conv2_sum)
        conv1_sum[...] = jnp.zeros_like(conv1_sum)
        bias1_sum[...] = jnp.zeros_like(bias1_sum)
        bias2_sum[...] = jnp.zeros_like(bias2_sum)

    rows = 2 * STEPS
    grad = grad_ref[...].reshape(rows, D2)
    bias2_sum[...] += jnp.sum(grad.astype(F32), axis=0, keepdims=True)
    even = dot_nt(grad, w2_ref[:, D2 : 2 * D2])
    odd = dot_nt(grad, w2_ref[:, 2 * D2 :]) + shift_up(dot_nt(grad, w2_ref[:, :D2]))
    even = (even * slope_ref[:, 0].reshape(rows, WIDE)).astype(BF16)
    odd = (odd * slope_ref[:, 1].reshape(rows, WIDE)).astype(BF16)
    cols = cols_ref[...].reshape(rows, 4 * LANES)
    conv1_sum[...] += dot_tn(even, cols[:, : 3 * LANES]) + dot_tn(odd, cols[:, LANES:])
    bias1_sum[...] += jnp.sum(even.astype(F32) + odd.astype(F32), axis=0, keepdims=True)
    for tap in range(3):
        conv2_sum[:, tap * D2 : (tap + 1) * D2] += dot_tn(act_ref[:, tap].reshape(rows, WIDE), grad)

    @pl.when(step == pl.num_programs(0) - 1)
    def _():
        mine = where_ref[0]
        for block in range(BLOCKS):
            target = mine if block < 2 else 1 - mine
            out = keep_ref if block % 2 == 0 else send_ref
            first = block * ROWS
            for tile in range(15):
                half, spot = tile // 8, tile % 8
                piece = conv2_sum[first : first + ROWS, tile * LANES : (tile + 1) * LANES]
                out[target, half, spot * ROWS : (spot + 1) * ROWS, :] = piece.astype(out.dtype)
            out[target, 1, 7 * ROWS : 8 * ROWS, :] = jnp.zeros((ROWS, LANES), out.dtype)
            biases = [jnp.concatenate([bias1_sum[:, first : first + ROWS], jnp.zeros((1, LANES - ROWS), F32)], axis=1)]
            for tile in range(D2 // LANES):
                biases.append(bias2_sum[:, tile * LANES : (tile + 1) * LANES])
            biases.append(jnp.zeros((16 - len(biases), LANES), F32))
            biases = jnp.concatenate(biases, axis=0).astype(out.dtype)
            for half in range(2):
                for tile in range(3):
                    piece = conv1_sum[first : first + ROWS, tile * LANES : (tile + 1) * LANES]
                    out[target, half, (8 + tile) * ROWS : (9 + tile) * ROWS, :] = piece.astype(out.dtype)
                out[target, half, 11 * ROWS :, :] = biases


def sum_kernel(got_ref, out_ref):
    total = got_ref[0].astype(F32)
    for source in range(1, got_ref.shape[0]):
        total = total + got_ref[source].astype(F32)
    total = total.astype(BF16)
    if len(out_ref.shape) == 2:
        out_ref[...] = total
    else:
        for target in range(out_ref.shape[0]):
            out_ref[target] = total


def last_kernel(
    where_ref, got_ref, feature_ref, bias_ref, own_ref, other_ref,
    weight_ref, bias1_ref, bias2_ref, conv2_ref, packed_ref, whole,
):
    for source in range(16):
        whole[source * ROWS : (source + 1) * ROWS, :] = got_ref[source].astype(F32)
    for block in range(10):
        columns = slice(block * LANES, (block + 1) * LANES)
        weight_ref[:, columns] = whole[columns, :].T

    @pl.when(pl.program_id(0) == 0)
    def _():
        pieces = [bias_ref[source].astype(F32) for source in range(16)]
        bias1 = jnp.concatenate([piece[0:1, :ROWS] for piece in pieces], axis=1)
        bias1_ref[...] = bias1.reshape(16 * ROWS)
        bias2 = jnp.concatenate([pieces[0][1 + tile : 2 + tile, :] for tile in range(D2 // LANES)], axis=1)
        bias2_ref[...] = bias2.reshape(D2)
        for source in range(16):
            for tile in range(D2 // LANES):
                packed_ref[source * 16 : (source + 1) * 16, tile * LANES : (tile + 1) * LANES] = feature_ref[
                    source, tile * 16 : (tile + 1) * 16, :
                ]
        first = where_ref[1] == 0
        for tile in range(15):
            half, spot = tile // 8, tile % 8
            rows = slice(spot * ROWS, (spot + 1) * ROWS)
            own, other = own_ref[rows, :].astype(F32), other_ref[rows, :].astype(F32)
            picked = jnp.where(first, own, other) if half == 0 else jnp.where(first, other, own)
            conv2_ref[:, tile * LANES : (tile + 1) * LANES] = picked


def exchange(values, axes):
    return lax.all_to_all(values, axes, split_axis=0, concat_axis=0, tiled=True)


def spread_to(values, count):
    return jnp.broadcast_to(values[None], (count,) + values.shape)


def vmem():
    return pl.BlockSpec(memory_space=pltpu.VMEM)


def params(*semantics):
    return pltpu.CompilerParams(vmem_limit_bytes=VMEM, dimension_semantics=semantics or None)


def local(mel, lengths, routes, conv1_weight, conv1_bias, conv2_weight, conv2_bias, out_grad):
    x_hi, y, core = lax.axis_index("xh"), lax.axis_index("y"), lax.axis_index("c")
    where = jnp.stack([x_hi, lax.axis_index("xl"), (x_hi * HOLDERS + y) * 2 + core]).astype(jnp.int32)

    def shape(*dims, dtype=BF16):
        return jax.ShapeDtypeStruct(dims, dtype)

    pay = pl.pallas_call(
        prepare_kernel,
        in_specs=[pl.BlockSpec(memory_space=pltpu.SMEM), vmem()],
        out_specs=vmem(),
        out_shape=shape(HOLDERS, CLIPS + 1, 2 * HALF, MEL),
        compiler_params=params(),
        name="mel_payload",
    )(lengths, mel)
    got_pay = exchange(pay, "y")
    weights = [
        conv2_weight,
        lax.ppermute(conv2_weight, "c", [(0, 1), (1, 0)]),
        lax.ppermute(conv2_weight, ("xh", "xl"), [(0, 3), (3, 0), (1, 2), (2, 1)]),
        lax.ppermute(conv2_weight, ("xh", "c", "xl"), [(i, 7 - i) for i in range(8)]),
    ]

    w1, b1 = [], []
    for flip_x, flip_c in ((0, 0), (0, 1), (1, 0), (1, 1)):
        place = ((x_hi ^ flip_x) * HOLDERS + y) * 2 + (core ^ flip_c)
        w1.append(lax.dynamic_slice(conv1_weight, (0, place * ROWS), (3 * MEL, ROWS)))
        b1.append(lax.dynamic_slice(conv1_bias, (place * ROWS,), (ROWS,)))
    gap = WIDE - BLOCKS * ROWS
    w1 = jnp.concatenate(w1 + [jnp.zeros((3 * MEL, gap), BF16)], axis=1)
    b1 = jnp.concatenate(b1 + [jnp.zeros((gap,), F32)])[None]

    pair = lambda i: (i, 0, 0)
    pair4 = lambda i: (i, 0, 0, 0)
    weight_spec = pl.BlockSpec((ROWS, 3 * D2), lambda i: (0, 0))
    cols, acts, slopes = pl.pallas_call(
        first_kernel,
        grid=(HOLDERS,),
        in_specs=[
            pl.BlockSpec((1, CLIPS + 1, 2 * HALF, MEL), pair4),
            pl.BlockSpec((3 * MEL, WIDE), lambda i: (0, 0)),
            pl.BlockSpec((1, WIDE), lambda i: (0, 0)),
        ],
        out_specs=[
            pl.BlockSpec((1, STEPS, 4 * LANES), pair),
            pl.BlockSpec((1, 3, STEPS, WIDE), pair4),
            pl.BlockSpec((1, 2, STEPS, WIDE), pair4),
        ],
        out_shape=[
            shape(HOLDERS, STEPS, 4 * LANES),
            shape(HOLDERS, 3, STEPS, WIDE),
            shape(HOLDERS, 2, STEPS, WIDE, dtype=F32),
        ],
        scratch_shapes=[pltpu.VMEM((2 * STEPS, MEL), F32)],
        compiler_params=params("arbitrary"),
        cost_estimate=pl.CostEstimate(flops=302 * 10**6, bytes_accessed=10**7, transcendentals=8 * 10**5),
        name="stem_first",
    )(got_pay, w1, b1)
    parts = pl.pallas_call(
        second_kernel,
        grid=(HOLDERS // 2,),
        in_specs=[pl.BlockSpec((2, 3, STEPS, WIDE), pair4), *[weight_spec] * BLOCKS],
        out_specs=pl.BlockSpec((2, STEPS, D2), pair),
        out_shape=shape(HOLDERS, STEPS, D2),
        scratch_shapes=[pltpu.VMEM((WIDE, 3 * D2), BF16)],
        compiler_params=params("arbitrary"),
        name="stem_second",
    )(acts, *weights)

    got_parts = exchange(parts, "y")
    owner = jnp.repeat(routes[:, 0], HALF)
    rep, features = pl.pallas_call(
        middle_kernel,
        in_specs=[vmem()] * 6,
        out_specs=[vmem()] * 2,
        out_shape=[shape(HOLDERS, STEPS, D2), shape(16, ROWS, LANES)],
        compiler_params=params(),
        name="stem_middle",
    )(
        got_parts,
        out_grad.reshape(STEPS, D2),
        conv2_bias[None],
        jnp.repeat(lengths.astype(F32), HALF)[:, None],
        owner[:, None],
        owner[None],
    )
    got_grad = exchange(rep, "y")

    whole = lambda i: (0, 0, 0, 0)
    keep, send = pl.pallas_call(
        backward_kernel,
        grid=(HOLDERS // 2,),
        in_specs=[
            pl.BlockSpec(memory_space=pltpu.SMEM),
            pl.BlockSpec((2, STEPS, D2), pair),
            *[weight_spec] * BLOCKS,
            pl.BlockSpec((2, STEPS, 4 * LANES), pair),
            pl.BlockSpec((2, 3, STEPS, WIDE), pair4),
            pl.BlockSpec((2, 2, STEPS, WIDE), pair4),
        ],
        out_specs=[pl.BlockSpec((2, 2, PACK, LANES), whole)] * 2,
        out_shape=[shape(2, 2, PACK, LANES, dtype=F32), shape(2, 2, PACK, LANES)],
        scratch_shapes=[
            pltpu.VMEM((WIDE, 3 * D2), BF16),
            pltpu.VMEM((WIDE, 3 * D2), F32),
            pltpu.VMEM((WIDE, 3 * LANES), F32),
            pltpu.VMEM((1, WIDE), F32),
            pltpu.VMEM((1, D2), F32),
        ],
        compiler_params=params("arbitrary"),
        name="stem_backward",
    )(where, got_grad, *weights, cols, acts, slopes)
    got = lax.ppermute(send, "c", [(0, 1), (1, 0)])
    quarters = exchange((keep + got.astype(F32)).astype(BF16).reshape(4, PACK, LANES), ("xh", "xl"))

    def summed(values, *dims):
        return pl.pallas_call(
            sum_kernel,
            in_specs=[vmem()],
            out_specs=vmem(),
            out_shape=shape(*dims),
            compiler_params=params(),
            name="gradient_sum",
        )(values)

    half = summed(quarters, PACK, LANES)
    quarter = PACK // 4
    near = summed(exchange(half.reshape(4, quarter, LANES), "zl"), 4, quarter, LANES)
    far = summed(exchange(near, "zh"), 4, quarter, LANES)
    half = exchange(far, "zl").reshape(PACK, LANES)
    own = half[:HALF_ROWS]
    other = lax.ppermute(own, "xl", [(0, 1), (1, 0)])
    shares = exchange(jnp.concatenate([features, spread_to(half[HALF_ROWS:], 16)], axis=1), ENC)
    weight_grad, bias_grad, second_bias_grad, conv2_rows_grad, packed = pl.pallas_call(
        last_kernel,
        grid=(3,),
        in_specs=[
            pl.BlockSpec(memory_space=pltpu.SMEM),
            pl.BlockSpec((16, ROWS, LANES), lambda i: (0, i + 1, 0)),
            pl.BlockSpec((16, ROWS, LANES), lambda i: (0, 0, 0)),
            pl.BlockSpec((16, 16, LANES), lambda i: (0, 4 * ROWS // 16, 0)),
            pl.BlockSpec((HALF_ROWS, LANES), lambda i: (0, 0)),
            pl.BlockSpec((HALF_ROWS, LANES), lambda i: (0, 0)),
        ],
        out_specs=[
            pl.BlockSpec((LANES, 16 * ROWS), lambda i: (i, 0)),
            pl.BlockSpec((16 * ROWS,), lambda i: (0,)),
            pl.BlockSpec((D2,), lambda i: (0,)),
            pl.BlockSpec((ROWS, 3 * D2), lambda i: (0, 0)),
            pl.BlockSpec((SLOTS * HALF, D2), lambda i: (0, 0)),
        ],
        out_shape=[
            shape(3 * MEL, 16 * ROWS, dtype=F32),
            shape(16 * ROWS, dtype=F32),
            shape(D2, dtype=F32),
            shape(ROWS, 3 * D2, dtype=F32),
            shape(SLOTS * HALF, D2),
        ],
        scratch_shapes=[pltpu.VMEM((16 * ROWS, LANES), F32)],
        compiler_params=params("arbitrary"),
        name="gradient_unpack",
    )(where, shares, shares, shares, own, other)
    return packed.reshape(SLOTS, HALF, D2), weight_grad, bias_grad, second_bias_grad, conv2_rows_grad


def solution(mesh):
    fine = Mesh(mesh.devices.reshape(2, 4, 2, 4, 4, 2), ALL_AXES)
    placed = (
        P(ALL_AXES, None, None),
        P(ALL_AXES),
        P(ALL_AXES, None),
        P(),
        P(),
        P(ENC, None),
        P(),
        P(ALL_AXES, None, None),
    )
    return jax.shard_map(
        local,
        mesh=fine,
        in_specs=placed,
        out_specs=(P(ALL_AXES, None, None), P(), P(), P(), P(ENC, None)),
        check_vma=False,
    )
```

```python
import functools

import jax
import jax.numpy as jnp
from jax import lax
from jax.experimental import pallas as pl
from jax.experimental.pallas import tpu as pltpu
from jax.sharding import Mesh
from jax.sharding import PartitionSpec as P

inv_root_two = 0.7071067811865476
inv_root_tau = 0.3989422804014327

MEL = 128
D2 = 640
ROWS = 80
LANES = 128
HOLDERS = 4
BLOCKS = 4
WIDE = 384
CLIPS = 16
HALF = 8
STEPS = CLIPS * HALF
SLOTS = 2 * CLIPS
PACK = 896
HALF_ROWS = 8 * ROWS
MIB = 1024 * 1024
ALL_AXES = ("xh", "y", "c", "zh", "zl", "xl")
ENC = ("xh", "y", "c")
F32 = jnp.float32
BF16 = jnp.bfloat16


def gelu_both(values):
    cdf = 0.5 * (1.0 + lax.erf(values * inv_root_two))
    return values * cdf, cdf + values * jnp.exp(-0.5 * values * values) * inv_root_tau


def shift_down(values):
    rows, width = values.shape
    t = lax.broadcasted_iota(jnp.int32, (rows, width), 0) & (HALF - 1)
    clips = values.reshape(rows // HALF, HALF, width)
    moved = pltpu.roll(clips, 1, 1).reshape(rows, width)
    return jnp.where(t == 0, 0.0, moved)


def shift_up(values):
    rows, width = values.shape
    t = lax.broadcasted_iota(jnp.int32, (rows, width), 0) & (HALF - 1)
    clips = values.reshape(rows // HALF, HALF, width)
    moved = pltpu.roll(clips, HALF - 1, 1).reshape(rows, width)
    return jnp.where(t == HALF - 1, 0.0, moved)


def dot(left, right):
    return jnp.dot(left, right, preferred_element_type=F32)


def dot_nt(left, right):
    return lax.dot_general(left, right, (((1,), (1,)), ((), ())), preferred_element_type=F32)


def dot_tn(left, right):
    return lax.dot_general(left, right, (((0,), (0,)), ((), ())), preferred_element_type=F32)


def stack_weights(refs, w2_ref):
    @pl.when(pl.program_id(0) == 0)
    def _():
        for block, ref in enumerate(refs):
            w2_ref[block * ROWS : (block + 1) * ROWS, :] = ref[...]
        w2_ref[BLOCKS * ROWS :, :] = jnp.zeros((WIDE - BLOCKS * ROWS, 3 * D2), BF16)


def prepare_kernel(length_ref, mel_ref, pay_ref):
    clip = lax.broadcasted_iota(jnp.int32, (CLIPS, MEL), 0)
    length = jnp.zeros((CLIPS, MEL), F32)
    for index in range(CLIPS):
        length = jnp.where(clip == index, length_ref[index].astype(F32), length)
    for target in range(HOLDERS):
        pay_ref[target, :CLIPS] = mel_ref[...]
        pay_ref[target, CLIPS] = length.astype(BF16)


def forward_kernel(
    pay_ref, w1_ref, b1_ref, own_ref, side_ref, far_ref, both_ref, part_ref, cols_ref, act_ref, slope_ref, w2_ref,
    frames_ref,
):
    stack_weights((own_ref, side_ref, far_ref, both_ref), w2_ref)
    spread = (
        lax.broadcasted_iota(jnp.int32, (STEPS, CLIPS), 0) >> 3
        == lax.broadcasted_iota(jnp.int32, (STEPS, CLIPS), 1)
    ).astype(F32).astype(BF16)
    length = dot(spread, pay_ref[0, CLIPS])
    frames_ref[...] = pay_ref[0, :CLIPS].astype(F32).reshape(2 * STEPS, MEL)
    t = (lax.broadcasted_iota(jnp.int32, (STEPS, LANES), 0) & (HALF - 1)).astype(F32)
    live_even, live_odd = 2.0 * t < length, 2.0 * t + 1.0 < length
    even = jnp.where(live_even, frames_ref[pl.ds(0, STEPS, 2), :], 0.0)
    odd = jnp.where(live_odd, frames_ref[pl.ds(1, STEPS, 2), :], 0.0)
    cols_ref[0, :, :LANES] = shift_down(odd).astype(BF16)
    cols_ref[0, :, LANES : 2 * LANES] = even.astype(BF16)
    cols_ref[0, :, 2 * LANES : 3 * LANES] = odd.astype(BF16)
    cols_ref[0, :, 3 * LANES :] = shift_up(even).astype(BF16)
    bias = b1_ref[...]
    mask_even = jnp.where(live_even, 1.0, 0.0)
    mask_odd = jnp.where(live_odd, 1.0, 0.0)
    mask_even = jnp.concatenate([mask_even] * (WIDE // LANES), axis=1)
    mask_odd = jnp.concatenate([mask_odd] * (WIDE // LANES), axis=1)
    act, slope = gelu_both(dot(cols_ref[0, :, : 3 * LANES], w1_ref[...]) + bias)
    act_even = (act * mask_even).astype(BF16)
    slope_ref[0, 0] = slope * mask_even
    act, slope = gelu_both(dot(cols_ref[0, :, LANES:], w1_ref[...]) + bias)
    act = act * mask_odd
    act_odd = act.astype(BF16)
    slope_ref[0, 1] = slope * mask_odd
    act_prior = shift_down(act).astype(BF16)
    act_ref[0, 0] = act_prior
    act_ref[0, 1] = act_even
    act_ref[0, 2] = act_odd
    total = dot(act_prior, w2_ref[:, :D2])
    total = total + dot(act_even, w2_ref[:, D2 : 2 * D2])
    total = total + dot(act_odd, w2_ref[:, 2 * D2 :])
    part_ref[0] = total.astype(BF16)


def middle_kernel(part_ref, grad_ref, b2_ref, length_ref, owner_col_ref, owner_row_ref, rep_ref, feature_ref):
    pre = part_ref[0].astype(F32)
    for source in range(1, HOLDERS):
        pre = pre + part_ref[source].astype(F32)
    pre = pre + b2_ref[...]
    t = (lax.broadcasted_iota(jnp.int32, (STEPS, 1), 0) & (HALF - 1)).astype(F32)
    live = jnp.where(2.0 * t < length_ref[...], 1.0, 0.0)
    value, slope = gelu_both(pre)
    features = (value * live).astype(BF16)
    second_grad = (grad_ref[...].astype(F32) * slope * live).astype(BF16)
    for target in range(HOLDERS):
        rep_ref[target] = second_grad
    here = lax.broadcasted_iota(jnp.int32, (STEPS, STEPS), 0)
    there = lax.broadcasted_iota(jnp.int32, (STEPS, STEPS), 1)
    same = (owner_col_ref[...] == owner_row_ref[...]) & ((here >> 3) < (there >> 3))
    same = same & ((here & (HALF - 1)) == 0)
    rank = jnp.sum(jnp.where(same, 1.0, 0.0), axis=0, keepdims=True)
    place = lax.broadcasted_iota(jnp.int32, (1, STEPS), 1) & (HALF - 1)
    place = (owner_row_ref[...] * 2 + rank.astype(jnp.int32)) * HALF + place
    wanted = lax.broadcasted_iota(jnp.int32, (SLOTS * HALF, STEPS), 0) == place
    placed = dot(jnp.where(wanted, 1.0, 0.0).astype(BF16), features).astype(BF16)
    for target in range(16):
        for tile in range(D2 // LANES):
            feature_ref[target, tile * 16 : (tile + 1) * 16, :] = placed[
                target * 16 : (target + 1) * 16, tile * LANES : (tile + 1) * LANES
            ]


def backward_kernel(
    where_ref, grad_ref, own_ref, side_ref, far_ref, both_ref, cols_ref, act_ref, slope_ref, keep_ref, send_ref,
    w2_ref, conv2_sum, conv1_sum, bias1_sum, bias2_sum,
):
    stack_weights((own_ref, side_ref, far_ref, both_ref), w2_ref)
    step = pl.program_id(0)

    @pl.when(step == 0)
    def _():
        conv2_sum[...] = jnp.zeros_like(conv2_sum)
        conv1_sum[...] = jnp.zeros_like(conv1_sum)
        bias1_sum[...] = jnp.zeros_like(bias1_sum)
        bias2_sum[...] = jnp.zeros_like(bias2_sum)

    rows = 2 * STEPS
    grad = grad_ref[...].reshape(rows, D2)
    bias2_sum[...] += jnp.sum(grad.astype(F32), axis=0, keepdims=True)
    even = dot_nt(grad, w2_ref[:, D2 : 2 * D2])
    odd = dot_nt(grad, w2_ref[:, 2 * D2 :]) + shift_up(dot_nt(grad, w2_ref[:, :D2]))
    even = (even * slope_ref[:, 0].reshape(rows, WIDE)).astype(BF16)
    odd = (odd * slope_ref[:, 1].reshape(rows, WIDE)).astype(BF16)
    cols = cols_ref[...].reshape(rows, 4 * LANES)
    conv1_sum[...] += dot_tn(even, cols[:, : 3 * LANES]) + dot_tn(odd, cols[:, LANES:])
    bias1_sum[...] += jnp.sum(even.astype(F32) + odd.astype(F32), axis=0, keepdims=True)
    for tap in range(3):
        conv2_sum[:, tap * D2 : (tap + 1) * D2] += dot_tn(act_ref[:, tap].reshape(rows, WIDE), grad)

    @pl.when(step == pl.num_programs(0) - 1)
    def _():
        mine = where_ref[0]
        for block in range(BLOCKS):
            target = mine if block < 2 else 1 - mine
            out = keep_ref if block % 2 == 0 else send_ref
            first = block * ROWS
            for tile in range(15):
                half, spot = tile // 8, tile % 8
                piece = conv2_sum[first : first + ROWS, tile * LANES : (tile + 1) * LANES]
                out[target, half, spot * ROWS : (spot + 1) * ROWS, :] = piece.astype(out.dtype)
            out[target, 1, 7 * ROWS : 8 * ROWS, :] = jnp.zeros((ROWS, LANES), out.dtype)
            biases = [jnp.concatenate([bias1_sum[:, first : first + ROWS], jnp.zeros((1, LANES - ROWS), F32)], axis=1)]
            for tile in range(D2 // LANES):
                biases.append(bias2_sum[:, tile * LANES : (tile + 1) * LANES])
            biases.append(jnp.zeros((16 - len(biases), LANES), F32))
            biases = jnp.concatenate(biases, axis=0).astype(out.dtype)
            for half in range(2):
                for tile in range(3):
                    piece = conv1_sum[first : first + ROWS, tile * LANES : (tile + 1) * LANES]
                    out[target, half, (8 + tile) * ROWS : (9 + tile) * ROWS, :] = piece.astype(out.dtype)
                out[target, half, 11 * ROWS :, :] = biases


def sum_kernel(got_ref, out_ref):
    total = got_ref[0].astype(F32)
    for source in range(1, got_ref.shape[0]):
        total = total + got_ref[source].astype(F32)
    total = total.astype(BF16)
    if len(out_ref.shape) == 2:
        out_ref[...] = total
    else:
        for target in range(out_ref.shape[0]):
            out_ref[target] = total


def last_kernel(
    where_ref, got_ref, feature_ref, bias_ref, own_ref, other_ref,
    weight_ref, bias1_ref, bias2_ref, conv2_ref, packed_ref, whole,
):
    for source in range(16):
        whole[source * ROWS : (source + 1) * ROWS, :] = got_ref[source].astype(F32)
    for block in range(10):
        columns = slice(block * LANES, (block + 1) * LANES)
        weight_ref[:, columns] = whole[columns, :].T

    @pl.when(pl.program_id(0) == 0)
    def _():
        pieces = [bias_ref[source].astype(F32) for source in range(16)]
        bias1 = jnp.concatenate([piece[0:1, :ROWS] for piece in pieces], axis=1)
        bias1_ref[...] = bias1.reshape(16 * ROWS)
        bias2 = jnp.concatenate([pieces[0][1 + tile : 2 + tile, :] for tile in range(D2 // LANES)], axis=1)
        bias2_ref[...] = bias2.reshape(D2)
        for source in range(16):
            for tile in range(D2 // LANES):
                packed_ref[source * 16 : (source + 1) * 16, tile * LANES : (tile + 1) * LANES] = feature_ref[
                    source, tile * 16 : (tile + 1) * 16, :
                ]
        first = where_ref[1] == 0
        for tile in range(15):
            half, spot = tile // 8, tile % 8
            rows = slice(spot * ROWS, (spot + 1) * ROWS)
            own, other = own_ref[rows, :].astype(F32), other_ref[rows, :].astype(F32)
            picked = jnp.where(first, own, other) if half == 0 else jnp.where(first, other, own)
            conv2_ref[:, tile * LANES : (tile + 1) * LANES] = picked


def exchange(values, axes):
    return lax.all_to_all(values, axes, split_axis=0, concat_axis=0, tiled=True)


def spread_to(values, count):
    return jnp.broadcast_to(values[None], (count,) + values.shape)


def vmem():
    return pl.BlockSpec(memory_space=pltpu.VMEM)


def params(mib, *semantics):
    return pltpu.CompilerParams(vmem_limit_bytes=mib * MIB, dimension_semantics=semantics or None)


def local(mel, lengths, routes, conv1_weight, conv1_bias, conv2_weight, conv2_bias, out_grad):
    x_hi, y, core = lax.axis_index("xh"), lax.axis_index("y"), lax.axis_index("c")
    where = jnp.stack([x_hi, lax.axis_index("xl")]).astype(jnp.int32)

    def shape(*dims, dtype=BF16):
        return jax.ShapeDtypeStruct(dims, dtype)

    def from_hbm(values):
        return pltpu.with_memory_space_constraint(values, pltpu.HBM)

    def in_hbm(*dims, dtype=BF16):
        return pltpu.HBM(dims, dtype)

    pay = pl.pallas_call(
        prepare_kernel,
        in_specs=[pl.BlockSpec(memory_space=pltpu.SMEM), vmem()],
        out_specs=vmem(),
        out_shape=in_hbm(HOLDERS, CLIPS + 1, 2 * HALF, MEL),
        compiler_params=params(60),
        name="mel_payload",
    )(lengths, mel)
    got_pay = exchange(pay, "y")
    weights = [
        conv2_weight,
        lax.ppermute(conv2_weight, "c", [(0, 1), (1, 0)]),
        lax.ppermute(conv2_weight, ("xh", "xl"), [(0, 3), (3, 0), (1, 2), (2, 1)]),
        lax.ppermute(conv2_weight, ("xh", "c", "xl"), [(i, 7 - i) for i in range(8)]),
    ]

    w1, b1 = [], []
    for flip_x, flip_c in ((0, 0), (0, 1), (1, 0), (1, 1)):
        place = ((x_hi ^ flip_x) * HOLDERS + y) * 2 + (core ^ flip_c)
        w1.append(lax.dynamic_slice(conv1_weight, (0, place * ROWS), (3 * MEL, ROWS)))
        b1.append(lax.dynamic_slice(conv1_bias, (place * ROWS,), (ROWS,)))
    gap = WIDE - BLOCKS * ROWS
    w1 = jnp.concatenate(w1 + [jnp.zeros((3 * MEL, gap), BF16)], axis=1)
    b1 = jnp.concatenate(b1 + [jnp.zeros((gap,), F32)])[None]

    pair = lambda i: (i, 0, 0)
    pair4 = lambda i: (i, 0, 0, 0)
    weight_spec = pl.BlockSpec((ROWS, 3 * D2), lambda i: (0, 0))
    parts, cols, acts, slopes = pl.pallas_call(
        forward_kernel,
        grid=(HOLDERS,),
        in_specs=[
            pl.BlockSpec((1, CLIPS + 1, 2 * HALF, MEL), pair4),
            pl.BlockSpec((3 * MEL, WIDE), lambda i: (0, 0)),
            pl.BlockSpec((1, WIDE), lambda i: (0, 0)),
            *[weight_spec] * BLOCKS,
        ],
        out_specs=[
            pl.BlockSpec((1, STEPS, D2), pair),
            pl.BlockSpec((1, STEPS, 4 * LANES), pair),
            pl.BlockSpec((1, 3, STEPS, WIDE), pair4),
            pl.BlockSpec((1, 2, STEPS, WIDE), pair4),
        ],
        out_shape=[
            in_hbm(HOLDERS, STEPS, D2),
            in_hbm(HOLDERS, STEPS, 4 * LANES),
            in_hbm(HOLDERS, 3, STEPS, WIDE),
            in_hbm(HOLDERS, 2, STEPS, WIDE, dtype=F32),
        ],
        scratch_shapes=[pltpu.VMEM((WIDE, 3 * D2), BF16), pltpu.VMEM((2 * STEPS, MEL), F32)],
        compiler_params=params(20, "arbitrary"),
        name="stem_forward",
    )(got_pay, w1, b1, *weights)

    got_parts = exchange(parts, "y")
    owner = jnp.repeat(routes[:, 0], HALF)
    rep, features = pl.pallas_call(
        middle_kernel,
        in_specs=[vmem()] * 6,
        out_specs=[vmem()] * 2,
        out_shape=[in_hbm(HOLDERS, STEPS, D2), in_hbm(16, ROWS, LANES)],
        compiler_params=params(10),
        name="stem_middle",
    )(
        got_parts,
        from_hbm(out_grad.reshape(STEPS, D2)),
        conv2_bias[None],
        from_hbm(jnp.repeat(lengths.astype(F32), HALF)[:, None]),
        owner[:, None],
        owner[None],
    )
    got_grad = exchange(rep, "y")

    whole = lambda i: (0, 0, 0, 0)
    keep, send = pl.pallas_call(
        backward_kernel,
        grid=(HOLDERS // 2,),
        in_specs=[
            pl.BlockSpec(memory_space=pltpu.SMEM),
            pl.BlockSpec((2, STEPS, D2), pair),
            *[weight_spec] * BLOCKS,
            pl.BlockSpec((2, STEPS, 4 * LANES), pair),
            pl.BlockSpec((2, 3, STEPS, WIDE), pair4),
            pl.BlockSpec((2, 2, STEPS, WIDE), pair4),
        ],
        out_specs=[pl.BlockSpec((2, 2, PACK, LANES), whole)] * 2,
        out_shape=[shape(2, 2, PACK, LANES, dtype=F32), shape(2, 2, PACK, LANES)],
        scratch_shapes=[
            pltpu.VMEM((WIDE, 3 * D2), BF16),
            pltpu.VMEM((WIDE, 3 * D2), F32),
            pltpu.VMEM((WIDE, 3 * LANES), F32),
            pltpu.VMEM((1, WIDE), F32),
            pltpu.VMEM((1, D2), F32),
        ],
        compiler_params=params(32, "arbitrary"),
        name="stem_backward",
    )(where, got_grad, *weights, from_hbm(cols), from_hbm(acts), from_hbm(slopes))
    got = lax.ppermute(send, "c", [(0, 1), (1, 0)])
    quarters = exchange((keep + got.astype(F32)).astype(BF16).reshape(4, PACK, LANES), ("xh", "xl"))

    def summed(values, *dims):
        return pl.pallas_call(
            sum_kernel,
            in_specs=[vmem()],
            out_specs=vmem(),
            out_shape=shape(*dims),
            compiler_params=params(8),
            name="gradient_sum",
        )(values)

    half = summed(quarters, PACK, LANES)
    quarter = PACK // 4
    near = summed(exchange(half.reshape(4, quarter, LANES), "zl"), 4, quarter, LANES)
    far = summed(exchange(near, "zh"), 4, quarter, LANES)
    half = exchange(far, "zl").reshape(PACK, LANES)
    own = half[:HALF_ROWS]
    other = lax.ppermute(own, "xl", [(0, 1), (1, 0)])
    shares = exchange(jnp.concatenate([features, spread_to(half[HALF_ROWS:], 16)], axis=1), ENC)
    weight_grad, bias_grad, second_bias_grad, conv2_rows_grad, packed = pl.pallas_call(
        last_kernel,
        grid=(3,),
        in_specs=[
            pl.BlockSpec(memory_space=pltpu.SMEM),
            pl.BlockSpec((16, ROWS, LANES), lambda i: (0, i + 1, 0)),
            pl.BlockSpec((16, ROWS, LANES), lambda i: (0, 0, 0)),
            pl.BlockSpec((16, 16, LANES), lambda i: (0, 4 * ROWS // 16, 0)),
            pl.BlockSpec((HALF_ROWS, LANES), lambda i: (0, 0)),
            pl.BlockSpec((HALF_ROWS, LANES), lambda i: (0, 0)),
        ],
        out_specs=[
            pl.BlockSpec((LANES, 16 * ROWS), lambda i: (i, 0)),
            pl.BlockSpec((16 * ROWS,), lambda i: (0,)),
            pl.BlockSpec((D2,), lambda i: (0,)),
            pl.BlockSpec((ROWS, 3 * D2), lambda i: (0, 0)),
            pl.BlockSpec((SLOTS * HALF, D2), lambda i: (0, 0)),
        ],
        out_shape=[
            shape(3 * MEL, 16 * ROWS, dtype=F32),
            shape(16 * ROWS, dtype=F32),
            shape(D2, dtype=F32),
            shape(ROWS, 3 * D2, dtype=F32),
            shape(SLOTS * HALF, D2),
        ],
        scratch_shapes=[pltpu.VMEM((16 * ROWS, LANES), F32)],
        compiler_params=params(16, "arbitrary"),
        name="gradient_unpack",
    )(where, shares, shares, shares, own, other)
    return packed.reshape(SLOTS, HALF, D2), weight_grad, bias_grad, second_bias_grad, conv2_rows_grad


def solution(mesh):
    fine = Mesh(mesh.devices.reshape(2, 4, 2, 4, 4, 2), ALL_AXES)
    placed = (
        P(ALL_AXES, None, None),
        P(ALL_AXES),
        P(ALL_AXES, None),
        P(),
        P(),
        P(ENC, None),
        P(),
        P(ALL_AXES, None, None),
    )
    return jax.shard_map(
        local,
        mesh=fine,
        in_specs=placed,
        out_specs=(P(ALL_AXES, None, None), P(), P(), P(), P(ENC, None)),
        check_vma=False,
    )
```

```python
import functools

import jax
import jax.numpy as jnp
from jax import lax
from jax.experimental import pallas as pl
from jax.experimental.pallas import tpu as pltpu
from jax.sharding import Mesh
from jax.sharding import PartitionSpec as P

inv_root_two = 0.7071067811865476
inv_root_tau = 0.3989422804014327

MEL = 128
D2 = 640
ROWS = 80
LANES = 128
HOLDERS = 4
BLOCKS = 4
WIDE = 384
CLIPS = 16
HALF = 8
STEPS = CLIPS * HALF
SLOTS = 2 * CLIPS
PAY = 26
CHIPS = 8
PACK = 896
HALF_ROWS = 8 * ROWS
MIB = 1024 * 1024
ALL_AXES = ("xh", "y", "c", "zh", "zl", "xl")
ENC = ("xh", "y", "c")
F32 = jnp.float32
BF16 = jnp.bfloat16


def gelu_both(values):
    cdf = 0.5 * (1.0 + lax.erf(values * inv_root_two))
    return values * cdf, cdf + values * jnp.exp(-0.5 * values * values) * inv_root_tau


def shift_down(values):
    rows, width = values.shape
    t = lax.broadcasted_iota(jnp.int32, (rows, width), 0) & (HALF - 1)
    clips = values.reshape(rows // HALF, HALF, width)
    moved = pltpu.roll(clips, 1, 1).reshape(rows, width)
    return jnp.where(t == 0, 0.0, moved)


def shift_up(values):
    rows, width = values.shape
    t = lax.broadcasted_iota(jnp.int32, (rows, width), 0) & (HALF - 1)
    clips = values.reshape(rows // HALF, HALF, width)
    moved = pltpu.roll(clips, HALF - 1, 1).reshape(rows, width)
    return jnp.where(t == HALF - 1, 0.0, moved)


def dot(left, right):
    return jnp.dot(left, right, preferred_element_type=F32)


def dot_nt(left, right):
    return lax.dot_general(left, right, (((1,), (1,)), ((), ())), preferred_element_type=F32)


def dot_tn(left, right):
    return lax.dot_general(left, right, (((0,), (0,)), ((), ())), preferred_element_type=F32)


def stack_weights(refs, w2_ref):
    @pl.when(pl.program_id(0) == 0)
    def _():
        for block, ref in enumerate(refs):
            w2_ref[block * ROWS : (block + 1) * ROWS, :] = ref[...]
        w2_ref[BLOCKS * ROWS :, :] = jnp.zeros((WIDE - BLOCKS * ROWS, 3 * D2), BF16)


def prepare_kernel(length_ref, mel_ref, pay_ref):
    clip = lax.broadcasted_iota(jnp.int32, (CLIPS, MEL), 0)
    length = jnp.zeros((CLIPS, MEL), F32)
    for index in range(CLIPS):
        length = jnp.where(clip == index, length_ref[index].astype(F32), length)
    for target in range(HOLDERS):
        pay_ref[target, :CLIPS] = mel_ref[...]
        pay_ref[target, CLIPS] = length.astype(BF16)
        pay_ref[target, CLIPS + 1 :] = jnp.zeros((PAY - CLIPS - 1, 2 * HALF, MEL), BF16)


def forward_kernel(
    pay_ref, w1_ref, b1_ref, own_ref, side_ref, far_ref, both_ref, part_ref, cols_ref, act_ref, slope_ref, w2_ref,
    frames_ref,
):
    stack_weights((own_ref, side_ref, far_ref, both_ref), w2_ref)
    spread = (
        lax.broadcasted_iota(jnp.int32, (STEPS, CLIPS), 0) >> 3
        == lax.broadcasted_iota(jnp.int32, (STEPS, CLIPS), 1)
    ).astype(F32).astype(BF16)
    length = dot(spread, pay_ref[0, CLIPS])
    frames_ref[...] = pay_ref[0, :CLIPS].astype(F32).reshape(2 * STEPS, MEL)
    t = (lax.broadcasted_iota(jnp.int32, (STEPS, LANES), 0) & (HALF - 1)).astype(F32)
    live_even, live_odd = 2.0 * t < length, 2.0 * t + 1.0 < length
    even = jnp.where(live_even, frames_ref[pl.ds(0, STEPS, 2), :], 0.0)
    odd = jnp.where(live_odd, frames_ref[pl.ds(1, STEPS, 2), :], 0.0)
    cols_ref[0, :, :LANES] = shift_down(odd).astype(BF16)
    cols_ref[0, :, LANES : 2 * LANES] = even.astype(BF16)
    cols_ref[0, :, 2 * LANES : 3 * LANES] = odd.astype(BF16)
    cols_ref[0, :, 3 * LANES :] = shift_up(even).astype(BF16)
    bias = b1_ref[...]
    mask_even = jnp.where(live_even, 1.0, 0.0)
    mask_odd = jnp.where(live_odd, 1.0, 0.0)
    mask_even = jnp.concatenate([mask_even] * (WIDE // LANES), axis=1)
    mask_odd = jnp.concatenate([mask_odd] * (WIDE // LANES), axis=1)
    act, slope = gelu_both(dot(cols_ref[0, :, : 3 * LANES], w1_ref[...]) + bias)
    act_even = (act * mask_even).astype(BF16)
    slope_ref[0, 0] = slope * mask_even
    act, slope = gelu_both(dot(cols_ref[0, :, LANES:], w1_ref[...]) + bias)
    act = act * mask_odd
    act_odd = act.astype(BF16)
    slope_ref[0, 1] = slope * mask_odd
    act_prior = shift_down(act).astype(BF16)
    act_ref[0, 0] = act_prior
    act_ref[0, 1] = act_even
    act_ref[0, 2] = act_odd
    total = dot(act_prior, w2_ref[:, :D2])
    total = total + dot(act_even, w2_ref[:, D2 : 2 * D2])
    total = total + dot(act_odd, w2_ref[:, 2 * D2 :])
    part_ref[0] = total.astype(BF16)


def middle_kernel(
    where_ref, part_ref, grad_ref, b2_ref, length_ref, owner_col_ref, owner_row_ref, rep_ref, same_ref, cross_ref
):
    pre = part_ref[0].astype(F32)
    for source in range(1, HOLDERS):
        pre = pre + part_ref[source].astype(F32)
    pre = pre + b2_ref[...]
    t = (lax.broadcasted_iota(jnp.int32, (STEPS, 1), 0) & (HALF - 1)).astype(F32)
    live = jnp.where(2.0 * t < length_ref[...], 1.0, 0.0)
    value, slope = gelu_both(pre)
    features = (value * live).astype(BF16)
    second_grad = (grad_ref[...].astype(F32) * slope * live).astype(BF16)
    for target in range(HOLDERS):
        rep_ref[target] = second_grad
    here = lax.broadcasted_iota(jnp.int32, (STEPS, STEPS), 0)
    there = lax.broadcasted_iota(jnp.int32, (STEPS, STEPS), 1)
    same = (owner_col_ref[...] == owner_row_ref[...]) & ((here >> 3) < (there >> 3))
    same = same & ((here & (HALF - 1)) == 0)
    rank = jnp.sum(jnp.where(same, 1.0, 0.0), axis=0, keepdims=True)
    place = lax.broadcasted_iota(jnp.int32, (1, STEPS), 1) & (HALF - 1)
    place = (owner_row_ref[...] * 2 + rank.astype(jnp.int32)) * HALF + place
    wanted = lax.broadcasted_iota(jnp.int32, (SLOTS * HALF, STEPS), 0) == place
    placed = dot(jnp.where(wanted, 1.0, 0.0).astype(BF16), features)
    first = where_ref[2] == 0
    for chip in range(CHIPS):
        for tile in range(D2 // LANES):
            rows, columns = slice(tile * 16, (tile + 1) * 16), slice(tile * LANES, (tile + 1) * LANES)
            left = placed[chip * 32 : chip * 32 + 16, columns]
            right = placed[chip * 32 + 16 : chip * 32 + 32, columns]
            same_ref[chip, rows, :] = jnp.where(first, left, right).astype(BF16)
            cross_ref[chip, rows, :] = jnp.where(first, right, left).astype(BF16)


def backward_kernel(
    where_ref, grad_ref, own_ref, side_ref, far_ref, both_ref, cols_ref, act_ref, slope_ref, keep_ref, send_ref,
    w2_ref, conv2_sum, conv1_sum, bias1_sum, bias2_sum,
):
    stack_weights((own_ref, side_ref, far_ref, both_ref), w2_ref)
    step = pl.program_id(0)

    @pl.when(step == 0)
    def _():
        conv2_sum[...] = jnp.zeros_like(conv2_sum)
        conv1_sum[...] = jnp.zeros_like(conv1_sum)
        bias1_sum[...] = jnp.zeros_like(bias1_sum)
        bias2_sum[...] = jnp.zeros_like(bias2_sum)

    rows = 2 * STEPS
    grad = grad_ref[...].reshape(rows, D2)
    bias2_sum[...] += jnp.sum(grad.astype(F32), axis=0, keepdims=True)
    even = dot_nt(grad, w2_ref[:, D2 : 2 * D2])
    odd = dot_nt(grad, w2_ref[:, 2 * D2 :]) + shift_up(dot_nt(grad, w2_ref[:, :D2]))
    even = (even * slope_ref[:, 0].reshape(rows, WIDE)).astype(BF16)
    odd = (odd * slope_ref[:, 1].reshape(rows, WIDE)).astype(BF16)
    cols = cols_ref[...].reshape(rows, 4 * LANES)
    conv1_sum[...] += dot_tn(even, cols[:, : 3 * LANES]) + dot_tn(odd, cols[:, LANES:])
    bias1_sum[...] += jnp.sum(even.astype(F32) + odd.astype(F32), axis=0, keepdims=True)
    for tap in range(3):
        conv2_sum[:, tap * D2 : (tap + 1) * D2] += dot_tn(act_ref[:, tap].reshape(rows, WIDE), grad)

    @pl.when(step == pl.num_programs(0) - 1)
    def _():
        mine = where_ref[0]
        for block in range(BLOCKS):
            target = mine if block < 2 else 1 - mine
            out = keep_ref if block % 2 == 0 else send_ref
            first = block * ROWS
            for tile in range(15):
                half, spot = tile // 8, tile % 8
                piece = conv2_sum[first : first + ROWS, tile * LANES : (tile + 1) * LANES]
                out[target, half, spot * ROWS : (spot + 1) * ROWS, :] = piece.astype(out.dtype)
            out[target, 1, 7 * ROWS : 8 * ROWS, :] = jnp.zeros((ROWS, LANES), out.dtype)
            biases = [jnp.concatenate([bias1_sum[:, first : first + ROWS], jnp.zeros((1, LANES - ROWS), F32)], axis=1)]
            for tile in range(D2 // LANES):
                biases.append(bias2_sum[:, tile * LANES : (tile + 1) * LANES])
            biases.append(jnp.zeros((16 - len(biases), LANES), F32))
            biases = jnp.concatenate(biases, axis=0).astype(out.dtype)
            for half in range(2):
                for tile in range(3):
                    piece = conv1_sum[first : first + ROWS, tile * LANES : (tile + 1) * LANES]
                    out[target, half, (8 + tile) * ROWS : (9 + tile) * ROWS, :] = piece.astype(out.dtype)
                out[target, half, 11 * ROWS :, :] = biases


def sum_kernel(got_ref, out_ref):
    total = got_ref[0].astype(F32)
    for source in range(1, got_ref.shape[0]):
        total = total + got_ref[source].astype(F32)
    total = total.astype(BF16)
    if len(out_ref.shape) == 2:
        out_ref[...] = total
    else:
        for target in range(out_ref.shape[0]):
            out_ref[target] = total


def last_kernel(
    where_ref, got_ref, got_cross_ref, feature_ref, feature_cross_ref, bias_ref, bias_cross_ref, own_ref, other_ref,
    weight_ref, bias1_ref, bias2_ref, conv2_ref, packed_ref, whole,
):
    first = where_ref[2] == 0

    def in_order(here, there):
        here, there = here.astype(F32), there.astype(F32)
        return jnp.where(first, here, there), jnp.where(first, there, here)

    for chip in range(CHIPS):
        start = 2 * chip * ROWS
        left, right = in_order(got_ref[chip], got_cross_ref[chip])
        whole[start : start + ROWS, :] = left
        whole[start + ROWS : start + 2 * ROWS, :] = right
    for block in range(10):
        columns = slice(block * LANES, (block + 1) * LANES)
        weight_ref[:, columns] = whole[columns, :].T

    @pl.when(pl.program_id(0) == 0)
    def _():
        pieces = []
        for chip in range(CHIPS):
            pieces.extend(in_order(bias_ref[chip], bias_cross_ref[chip]))
        bias1 = jnp.concatenate([piece[0:1, :ROWS] for piece in pieces], axis=1)
        bias1_ref[...] = bias1.reshape(16 * ROWS)
        bias2 = jnp.concatenate([pieces[0][1 + tile : 2 + tile, :] for tile in range(D2 // LANES)], axis=1)
        bias2_ref[...] = bias2.reshape(D2)
        for chip in range(CHIPS):
            left, right = in_order(feature_ref[chip], feature_cross_ref[chip])
            for tile in range(D2 // LANES):
                rows, columns = slice(tile * 16, (tile + 1) * 16), slice(tile * LANES, (tile + 1) * LANES)
                packed_ref[chip * 32 : chip * 32 + 16, columns] = left[rows, :].astype(BF16)
                packed_ref[chip * 32 + 16 : chip * 32 + 32, columns] = right[rows, :].astype(BF16)
        lower = where_ref[1] == 0
        for tile in range(15):
            half, spot = tile // 8, tile % 8
            rows = slice(spot * ROWS, (spot + 1) * ROWS)
            own, other = own_ref[rows, :].astype(F32), other_ref[rows, :].astype(F32)
            picked = jnp.where(lower, own, other) if half == 0 else jnp.where(lower, other, own)
            conv2_ref[:, tile * LANES : (tile + 1) * LANES] = picked


def exchange(values, axes):
    return lax.all_to_all(values, axes, split_axis=0, concat_axis=0, tiled=True)


def spread_to(values, count):
    return jnp.broadcast_to(values[None], (count,) + values.shape)


def vmem():
    return pl.BlockSpec(memory_space=pltpu.VMEM)


def params(mib, *semantics):
    return pltpu.CompilerParams(vmem_limit_bytes=mib * MIB, dimension_semantics=semantics or None)


def local(mel, lengths, routes, conv1_weight, conv1_bias, conv2_weight, conv2_bias, out_grad):
    x_hi, y, core = lax.axis_index("xh"), lax.axis_index("y"), lax.axis_index("c")
    where = jnp.stack([x_hi, lax.axis_index("xl"), core]).astype(jnp.int32)

    def shape(*dims, dtype=BF16):
        return jax.ShapeDtypeStruct(dims, dtype)

    def from_hbm(values):
        return pltpu.with_memory_space_constraint(values, pltpu.HBM)

    def in_hbm(*dims, dtype=BF16):
        return pltpu.HBM(dims, dtype)

    pay = pl.pallas_call(
        prepare_kernel,
        in_specs=[pl.BlockSpec(memory_space=pltpu.SMEM), vmem()],
        out_specs=vmem(),
        out_shape=in_hbm(HOLDERS, PAY, 2 * HALF, MEL),
        compiler_params=params(60),
        name="mel_payload",
    )(lengths, mel)
    got_pay = exchange(pay, "y")
    cores = [(0, 1), (1, 0)]
    far_weight = lax.ppermute(conv2_weight, ("xh", "xl"), [(0, 3), (3, 0), (1, 2), (2, 1)])
    pay = pl.pallas_call(
        prepare_kernel,
        in_specs=[pl.BlockSpec(memory_space=pltpu.SMEM), vmem()],
        out_specs=vmem(),
        out_shape=in_hbm(HOLDERS, PAY, 2 * HALF, MEL),
        compiler_params=params(60),
        name="mel_payload",
    )(lengths, mel)
    got_pay = exchange(pay, "y")
    weights = [
        conv2_weight,
        lax.ppermute(conv2_weight, "c", [(0, 1), (1, 0)]),
        lax.ppermute(conv2_weight, ("xh", "xl"), [(0, 3), (3, 0), (1, 2), (2, 1)]),
        lax.ppermute(conv2_weight, ("xh", "c", "xl"), [(i, 7 - i) for i in range(8)]),
    ]

    w1, b1 = [], []
    for flip_x, flip_c in ((0, 0), (0, 1), (1, 0), (1, 1)):
        place = ((x_hi ^ flip_x) * HOLDERS + y) * 2 + (core ^ flip_c)
        w1.append(lax.dynamic_slice(conv1_weight, (0, place * ROWS), (3 * MEL, ROWS)))
        b1.append(lax.dynamic_slice(conv1_bias, (place * ROWS,), (ROWS,)))
    gap = WIDE - BLOCKS * ROWS
    w1 = jnp.concatenate(w1 + [jnp.zeros((3 * MEL, gap), BF16)], axis=1)
    b1 = jnp.concatenate(b1 + [jnp.zeros((gap,), F32)])[None]
    own_weight, b1 = lax.optimization_barrier((conv2_weight, b1))
    far_weight, b1 = lax.optimization_barrier((far_weight, b1))
    weights = [
        conv2_weight,
        lax.ppermute(own_weight, "c", cores),
        far_weight,
        lax.ppermute(far_weight, "c", cores),
    ]

    pair = lambda i: (i, 0, 0)
    pair4 = lambda i: (i, 0, 0, 0)
    weight_spec = pl.BlockSpec((ROWS, 3 * D2), lambda i: (0, 0))
    parts, cols, acts, slopes = pl.pallas_call(
        forward_kernel,
        grid=(HOLDERS,),
        in_specs=[
            pl.BlockSpec((1, PAY, 2 * HALF, MEL), pair4),
            pl.BlockSpec((3 * MEL, WIDE), lambda i: (0, 0)),
            pl.BlockSpec((1, WIDE), lambda i: (0, 0)),
            *[weight_spec] * BLOCKS,
        ],
        out_specs=[
            pl.BlockSpec((1, STEPS, D2), pair),
            pl.BlockSpec((1, STEPS, 4 * LANES), pair),
            pl.BlockSpec((1, 3, STEPS, WIDE), pair4),
            pl.BlockSpec((1, 2, STEPS, WIDE), pair4),
        ],
        out_shape=[
            in_hbm(HOLDERS, STEPS, D2),
            in_hbm(HOLDERS, STEPS, 4 * LANES),
            in_hbm(HOLDERS, 3, STEPS, WIDE),
            in_hbm(HOLDERS, 2, STEPS, WIDE, dtype=F32),
        ],
        scratch_shapes=[pltpu.VMEM((WIDE, 3 * D2), BF16), pltpu.VMEM((2 * STEPS, MEL), F32)],
        compiler_params=params(20, "arbitrary"),
        name="stem_forward",
    )(got_pay, w1, b1, *weights)

    got_parts = exchange(parts, "y")
    owner = jnp.repeat(routes[:, 0], HALF)
    rep, same, cross = pl.pallas_call(
        middle_kernel,
        in_specs=[pl.BlockSpec(memory_space=pltpu.SMEM)] + [vmem()] * 6,
        out_specs=[vmem()] * 3,
        out_shape=[in_hbm(HOLDERS, STEPS, D2), shape(CHIPS, ROWS, LANES), shape(CHIPS, ROWS, LANES)],
        compiler_params=params(10),
        name="stem_middle",
    )(
        where,
        got_parts,
        from_hbm(out_grad.reshape(STEPS, D2)),
        conv2_bias[None],
        from_hbm(jnp.repeat(lengths.astype(F32), HALF)[:, None]),
        owner[:, None],
        owner[None],
    )
    got_grad = exchange(rep, "y")

    whole = lambda i: (0, 0, 0, 0)
    keep, send = pl.pallas_call(
        backward_kernel,
        grid=(HOLDERS // 2,),
        in_specs=[
            pl.BlockSpec(memory_space=pltpu.SMEM),
            pl.BlockSpec((2, STEPS, D2), pair),
            *[weight_spec] * BLOCKS,
            pl.BlockSpec((2, STEPS, 4 * LANES), pair),
            pl.BlockSpec((2, 3, STEPS, WIDE), pair4),
            pl.BlockSpec((2, 2, STEPS, WIDE), pair4),
        ],
        out_specs=[pl.BlockSpec((2, 2, PACK, LANES), whole)] * 2,
        out_shape=[shape(2, 2, PACK, LANES, dtype=F32), shape(2, 2, PACK, LANES)],
        scratch_shapes=[
            pltpu.VMEM((WIDE, 3 * D2), BF16),
            pltpu.VMEM((WIDE, 3 * D2), F32),
            pltpu.VMEM((WIDE, 3 * LANES), F32),
            pltpu.VMEM((1, WIDE), F32),
            pltpu.VMEM((1, D2), F32),
        ],
        compiler_params=params(32, "arbitrary"),
        name="stem_backward",
    )(where, got_grad, *weights, from_hbm(cols), from_hbm(acts), from_hbm(slopes))
    got = lax.ppermute(send, "c", cores)
    quarters = exchange((keep + got.astype(F32)).astype(BF16).reshape(4, PACK, LANES), ("xh", "xl"))

    def summed(values, *dims):
        return pl.pallas_call(
            sum_kernel,
            in_specs=[vmem()],
            out_specs=vmem(),
            out_shape=shape(*dims),
            compiler_params=params(8),
            name="gradient_sum",
        )(values)

    half = summed(quarters, PACK, LANES)
    quarter = PACK // 4
    near = summed(exchange(half.reshape(4, quarter, LANES), "zl"), 4, quarter, LANES)
    far = summed(exchange(near, "zh"), 4, quarter, LANES)
    half = exchange(far, "zl").reshape(PACK, LANES)
    own = half[:HALF_ROWS]
    other = lax.ppermute(own, "xl", [(0, 1), (1, 0)])
    conv1 = spread_to(half[HALF_ROWS:], CHIPS)
    got = exchange(jnp.concatenate([same, conv1[:, : 3 * ROWS], cross, conv1[:, 3 * ROWS :]], axis=1), ("xh", "y"))
    got, other = lax.optimization_barrier((got, other))
    got_cross = lax.ppermute(got, "c", cores)
    weight_grad, bias_grad, second_bias_grad, conv2_rows_grad, packed = pl.pallas_call(
        last_kernel,
        grid=(3,),
        in_specs=[
            pl.BlockSpec(memory_space=pltpu.SMEM),
            pl.BlockSpec((CHIPS, ROWS, LANES), lambda i: (0, i + 1, 0)),
            pl.BlockSpec((CHIPS, ROWS, LANES), lambda i: (0, i + 1, 0)),
            pl.BlockSpec((CHIPS, ROWS, LANES), lambda i: (0, 0, 0)),
            pl.BlockSpec((CHIPS, ROWS, LANES), lambda i: (0, 4, 0)),
            pl.BlockSpec((CHIPS, 16, LANES), lambda i: (0, 5 * ROWS // 16, 0)),
            pl.BlockSpec((CHIPS, 16, LANES), lambda i: (0, 5 * ROWS // 16, 0)),
            pl.BlockSpec((HALF_ROWS, LANES), lambda i: (0, 0)),
            pl.BlockSpec((HALF_ROWS, LANES), lambda i: (0, 0)),
        ],
        out_specs=[
            pl.BlockSpec((LANES, 16 * ROWS), lambda i: (i, 0)),
            pl.BlockSpec((16 * ROWS,), lambda i: (0,)),
            pl.BlockSpec((D2,), lambda i: (0,)),
            pl.BlockSpec((ROWS, 3 * D2), lambda i: (0, 0)),
            pl.BlockSpec((SLOTS * HALF, D2), lambda i: (0, 0)),
        ],
        out_shape=[
            shape(3 * MEL, 16 * ROWS, dtype=F32),
            shape(16 * ROWS, dtype=F32),
            shape(D2, dtype=F32),
            shape(ROWS, 3 * D2, dtype=F32),
            shape(SLOTS * HALF, D2),
        ],
        scratch_shapes=[pltpu.VMEM((16 * ROWS, LANES), F32)],
        compiler_params=params(16, "arbitrary"),
        name="gradient_unpack",
    )(where, got, got_cross, got, got_cross, got, got_cross, own, other)
    return packed.reshape(SLOTS, HALF, D2), weight_grad, bias_grad, second_bias_grad, conv2_rows_grad


def solution(mesh):
    fine = Mesh(mesh.devices.reshape(2, 4, 2, 4, 4, 2), ALL_AXES)
    placed = (
        P(ALL_AXES, None, None),
        P(ALL_AXES),
        P(ALL_AXES, None),
        P(),
        P(),
        P(ENC, None),
        P(),
        P(ALL_AXES, None, None),
    )
    return jax.shard_map(
        local,
        mesh=fine,
        in_specs=placed,
        out_specs=(P(ALL_AXES, None, None), P(), P(), P(), P(ENC, None)),
        check_vma=False,
    )
```

```python
import functools

import jax
import jax.numpy as jnp
from jax import lax
from jax.experimental import pallas as pl
from jax.experimental.pallas import tpu as pltpu
from jax.sharding import Mesh
from jax.sharding import PartitionSpec as P

inv_root_two = 0.7071067811865476
inv_root_tau = 0.3989422804014327

MEL = 128
D2 = 640
ROWS = 80
LANES = 128
HOLDERS = 4
BLOCKS = 4
WIDE = 384
CLIPS = 16
HALF = 8
STEPS = CLIPS * HALF
SLOTS = 2 * CLIPS
PAY = 26
CHIPS = 8
PACK = 896
HALF_ROWS = 8 * ROWS
MIB = 1024 * 1024
ALL_AXES = ("xh", "y", "c", "zh", "zl", "xl")
ENC = ("xh", "y", "c")
F32 = jnp.float32
BF16 = jnp.bfloat16


def gelu_both(values):
    cdf = 0.5 * (1.0 + lax.erf(values * inv_root_two))
    return values * cdf, cdf + values * jnp.exp(-0.5 * values * values) * inv_root_tau


def shift_down(values):
    rows, width = values.shape
    t = lax.broadcasted_iota(jnp.int32, (rows, width), 0) & (HALF - 1)
    clips = values.reshape(rows // HALF, HALF, width)
    moved = pltpu.roll(clips, 1, 1).reshape(rows, width)
    return jnp.where(t == 0, 0.0, moved)


def shift_up(values):
    rows, width = values.shape
    t = lax.broadcasted_iota(jnp.int32, (rows, width), 0) & (HALF - 1)
    clips = values.reshape(rows // HALF, HALF, width)
    moved = pltpu.roll(clips, HALF - 1, 1).reshape(rows, width)
    return jnp.where(t == HALF - 1, 0.0, moved)


def dot(left, right):
    return jnp.dot(left, right, preferred_element_type=F32)


def dot_nt(left, right):
    return lax.dot_general(left, right, (((1,), (1,)), ((), ())), preferred_element_type=F32)


def dot_tn(left, right):
    return lax.dot_general(left, right, (((0,), (0,)), ((), ())), preferred_element_type=F32)


def stack_weights(refs, w2_ref):
    @pl.when(pl.program_id(0) == 0)
    def _():
        for block, ref in enumerate(refs):
            w2_ref[block * ROWS : (block + 1) * ROWS, :] = ref[...]
        w2_ref[BLOCKS * ROWS :, :] = jnp.zeros((WIDE - BLOCKS * ROWS, 3 * D2), BF16)


def prepare_kernel(length_ref, mel_ref, pay_ref):
    clip = lax.broadcasted_iota(jnp.int32, (CLIPS, MEL), 0)
    length = jnp.zeros((CLIPS, MEL), F32)
    for index in range(CLIPS):
        length = jnp.where(clip == index, length_ref[index].astype(F32), length)
    for target in range(HOLDERS):
        pay_ref[target, :CLIPS] = mel_ref[...]
        pay_ref[target, CLIPS] = length.astype(BF16)
        pay_ref[target, CLIPS + 1 :] = jnp.zeros((PAY - CLIPS - 1, 2 * HALF, MEL), BF16)


def columns_kernel(where_ref, weight_ref, bias_ref, w1_ref, b1_ref, picked):
    picked[...] = jnp.zeros_like(picked)
    b1_ref[...] = jnp.zeros_like(b1_ref)
    for block, flip in enumerate((0, 1, 2 * HOLDERS, 2 * HOLDERS + 1)):
        first = (where_ref[3] ^ flip) * ROWS
        start = pl.multiple_of(jnp.minimum((first >> 7) << 7, 16 * ROWS - 2 * LANES), LANES)
        shift = (2 * LANES - (first - start)) & (2 * LANES - 1)
        lanes = slice(block * ROWS, (block + 1) * ROWS)
        window = weight_ref[:, pl.ds(start, 2 * LANES)].astype(F32)
        picked[:, lanes] = pltpu.roll(window, shift, 1)[:, :ROWS]
        window = jnp.broadcast_to(bias_ref[:, pl.ds(start, 2 * LANES)], (8, 2 * LANES))
        b1_ref[:, lanes] = pltpu.roll(window, shift, 1)[0:1, :ROWS]
    w1_ref[...] = picked[...].astype(BF16)


def forward_kernel(
    pay_ref, w1_ref, b1_ref, own_ref, side_ref, far_ref, both_ref, part_ref, cols_ref, act_ref, slope_ref, w2_ref,
    frames_ref,
):
    stack_weights((own_ref, side_ref, far_ref, both_ref), w2_ref)
    spread = (
        lax.broadcasted_iota(jnp.int32, (STEPS, CLIPS), 0) >> 3
        == lax.broadcasted_iota(jnp.int32, (STEPS, CLIPS), 1)
    ).astype(F32).astype(BF16)
    length = dot(spread, pay_ref[0, CLIPS])
    frames_ref[...] = pay_ref[0, :CLIPS].astype(F32).reshape(2 * STEPS, MEL)
    t = (lax.broadcasted_iota(jnp.int32, (STEPS, LANES), 0) & (HALF - 1)).astype(F32)
    live_even, live_odd = 2.0 * t < length, 2.0 * t + 1.0 < length
    even = jnp.where(live_even, frames_ref[pl.ds(0, STEPS, 2), :], 0.0)
    odd = jnp.where(live_odd, frames_ref[pl.ds(1, STEPS, 2), :], 0.0)
    cols_ref[0, :, :LANES] = shift_down(odd).astype(BF16)
    cols_ref[0, :, LANES : 2 * LANES] = even.astype(BF16)
    cols_ref[0, :, 2 * LANES : 3 * LANES] = odd.astype(BF16)
    cols_ref[0, :, 3 * LANES :] = shift_up(even).astype(BF16)
    bias = b1_ref[...]
    mask_even = jnp.where(live_even, 1.0, 0.0)
    mask_odd = jnp.where(live_odd, 1.0, 0.0)
    mask_even = jnp.concatenate([mask_even] * (WIDE // LANES), axis=1)
    mask_odd = jnp.concatenate([mask_odd] * (WIDE // LANES), axis=1)
    act, slope = gelu_both(dot(cols_ref[0, :, : 3 * LANES], w1_ref[...]) + bias)
    act_even = (act * mask_even).astype(BF16)
    slope_ref[0, 0] = slope * mask_even
    act, slope = gelu_both(dot(cols_ref[0, :, LANES:], w1_ref[...]) + bias)
    act = act * mask_odd
    act_odd = act.astype(BF16)
    slope_ref[0, 1] = slope * mask_odd
    act_prior = shift_down(act).astype(BF16)
    act_ref[0, 0] = act_prior
    act_ref[0, 1] = act_even
    act_ref[0, 2] = act_odd
    total = dot(act_prior, w2_ref[:, :D2])
    total = total + dot(act_even, w2_ref[:, D2 : 2 * D2])
    total = total + dot(act_odd, w2_ref[:, 2 * D2 :])
    part_ref[0] = total.astype(BF16)


def middle_kernel(part_ref, grad_ref, b2_ref, length_ref, rep_ref, feature_ref):
    pre = part_ref[0].astype(F32)
    for source in range(1, HOLDERS):
        pre = pre + part_ref[source].astype(F32)
    pre = pre + b2_ref[...]
    t = (lax.broadcasted_iota(jnp.int32, (STEPS, 1), 0) & (HALF - 1)).astype(F32)
    live = jnp.where(2.0 * t < length_ref[...], 1.0, 0.0)
    value, slope = gelu_both(pre)
    features = (value * live).astype(BF16)
    second_grad = (grad_ref[...].astype(F32) * slope * live).astype(BF16)
    for target in range(HOLDERS):
        rep_ref[target] = second_grad
    feature_ref[...] = features


def place_kernel(where_ref, feature_ref, owner_col_ref, owner_row_ref, same_ref, cross_ref):
    here = lax.broadcasted_iota(jnp.int32, (STEPS, STEPS), 0)
    there = lax.broadcasted_iota(jnp.int32, (STEPS, STEPS), 1)
    same = (owner_col_ref[...] == owner_row_ref[...]) & ((here >> 3) < (there >> 3))
    same = same & ((here & (HALF - 1)) == 0)
    rank = jnp.sum(jnp.where(same, 1.0, 0.0), axis=0, keepdims=True)
    place = lax.broadcasted_iota(jnp.int32, (1, STEPS), 1) & (HALF - 1)
    place = (owner_row_ref[...] * 2 + rank.astype(jnp.int32)) * HALF + place
    wanted = lax.broadcasted_iota(jnp.int32, (SLOTS * HALF, STEPS), 0) == place
    placed = dot(jnp.where(wanted, 1.0, 0.0).astype(BF16), feature_ref[...])
    first = where_ref[2] == 0
    for chip in range(CHIPS):
        for tile in range(D2 // LANES):
            rows, columns = slice(tile * 16, (tile + 1) * 16), slice(tile * LANES, (tile + 1) * LANES)
            left = placed[chip * 32 : chip * 32 + 16, columns]
            right = placed[chip * 32 + 16 : chip * 32 + 32, columns]
            same_ref[chip, rows, :] = jnp.where(first, left, right).astype(BF16)
            cross_ref[chip, rows, :] = jnp.where(first, right, left).astype(BF16)


def backward_kernel(
    where_ref, grad_ref, own_ref, side_ref, far_ref, both_ref, cols_ref, act_ref, slope_ref, keep_ref, send_ref,
    w2_ref, conv2_sum, conv1_sum, bias1_sum, bias2_sum,
):
    stack_weights((own_ref, side_ref, far_ref, both_ref), w2_ref)
    step = pl.program_id(0)

    @pl.when(step == 0)
    def _():
        conv2_sum[...] = jnp.zeros_like(conv2_sum)
        conv1_sum[...] = jnp.zeros_like(conv1_sum)
        bias1_sum[...] = jnp.zeros_like(bias1_sum)
        bias2_sum[...] = jnp.zeros_like(bias2_sum)

    rows = 2 * STEPS
    grad = grad_ref[...].reshape(rows, D2)
    bias2_sum[...] += jnp.sum(grad.astype(F32), axis=0, keepdims=True)
    even = dot_nt(grad, w2_ref[:, D2 : 2 * D2])
    odd = dot_nt(grad, w2_ref[:, 2 * D2 :]) + shift_up(dot_nt(grad, w2_ref[:, :D2]))
    even = (even * slope_ref[:, 0].reshape(rows, WIDE)).astype(BF16)
    odd = (odd * slope_ref[:, 1].reshape(rows, WIDE)).astype(BF16)
    cols = cols_ref[...].reshape(rows, 4 * LANES)
    conv1_sum[...] += dot_tn(even, cols[:, : 3 * LANES]) + dot_tn(odd, cols[:, LANES:])
    bias1_sum[...] += jnp.sum(even.astype(F32) + odd.astype(F32), axis=0, keepdims=True)
    for tap in range(3):
        conv2_sum[:, tap * D2 : (tap + 1) * D2] += dot_tn(act_ref[:, tap].reshape(rows, WIDE), grad)

    @pl.when(step == pl.num_programs(0) - 1)
    def _():
        mine = where_ref[0]
        for block in range(BLOCKS):
            target = mine if block < 2 else 1 - mine
            out = keep_ref if block % 2 == 0 else send_ref
            first = block * ROWS
            for tile in range(15):
                half, spot = tile // 8, tile % 8
                piece = conv2_sum[first : first + ROWS, tile * LANES : (tile + 1) * LANES]
                out[target, half, spot * ROWS : (spot + 1) * ROWS, :] = piece.astype(out.dtype)
            out[target, 1, 7 * ROWS : 8 * ROWS, :] = jnp.zeros((ROWS, LANES), out.dtype)
            biases = [jnp.concatenate([bias1_sum[:, first : first + ROWS], jnp.zeros((1, LANES - ROWS), F32)], axis=1)]
            for tile in range(D2 // LANES):
                biases.append(bias2_sum[:, tile * LANES : (tile + 1) * LANES])
            biases.append(jnp.zeros((16 - len(biases), LANES), F32))
            biases = jnp.concatenate(biases, axis=0).astype(out.dtype)
            for half in range(2):
                for tile in range(3):
                    piece = conv1_sum[first : first + ROWS, tile * LANES : (tile + 1) * LANES]
                    out[target, half, (8 + tile) * ROWS : (9 + tile) * ROWS, :] = piece.astype(out.dtype)
                out[target, half, 11 * ROWS :, :] = biases


def sum_kernel(got_ref, out_ref):
    total = got_ref[0].astype(F32)
    for source in range(1, got_ref.shape[0]):
        total = total + got_ref[source].astype(F32)
    total = total.astype(BF16)
    if len(out_ref.shape) == 2:
        out_ref[...] = total
    else:
        for target in range(out_ref.shape[0]):
            out_ref[target] = total


def last_kernel(
    where_ref, got_ref, cross_ref, own_ref, other_ref, weight_ref, bias1_ref, bias2_ref, conv2_ref, packed_ref,
    whole, biases,
):
    step, core = pl.program_id(0), where_ref[2]
    rows = pl.ds(pl.multiple_of((step + 1) * ROWS, 16), ROWS)
    for chip in range(CHIPS):
        whole[pl.ds(pl.multiple_of((2 * chip + core) * ROWS, 16), ROWS), :] = got_ref[chip, rows, :]
        whole[pl.ds(pl.multiple_of((2 * chip + 1 - core) * ROWS, 16), ROWS), :] = cross_ref[chip, rows, :]
    for block in range(10):
        columns = slice(block * LANES, (block + 1) * LANES)
        weight_ref[:, columns] = whole[columns, :].T.astype(F32)

    @pl.when(step == 0)
    def _():
        for chip in range(CHIPS):
            biases[2 * chip + core] = got_ref[chip, 5 * ROWS :, :].astype(F32)
            biases[2 * chip + 1 - core] = cross_ref[chip, 5 * ROWS :, :].astype(F32)
            left = pl.ds(pl.multiple_of(chip * 32 + 16 * core, 16), 16)
            right = pl.ds(pl.multiple_of(chip * 32 + 16 - 16 * core, 16), 16)
            for tile in range(D2 // LANES):
                columns = slice(tile * LANES, (tile + 1) * LANES)
                packed_ref[left, columns] = got_ref[chip, tile * 16 : (tile + 1) * 16, :]
                packed_ref[right, columns] = cross_ref[chip, 4 * ROWS + tile * 16 : 4 * ROWS + (tile + 1) * 16, :]
        bias1 = jnp.concatenate([biases[source, 0:1, :ROWS] for source in range(16)], axis=1)
        bias1_ref[...] = bias1.reshape(16 * ROWS)
        bias2 = jnp.concatenate([biases[0, 1 + tile : 2 + tile, :] for tile in range(D2 // LANES)], axis=1)
        bias2_ref[...] = bias2.reshape(D2)
        lower = where_ref[1] == 0
        for tile in range(15):
            half, spot = tile // 8, tile % 8
            rows = slice(spot * ROWS, (spot + 1) * ROWS)
            own, other = own_ref[rows, :].astype(F32), other_ref[rows, :].astype(F32)
            picked = jnp.where(lower, own, other) if half == 0 else jnp.where(lower, other, own)
            conv2_ref[:, tile * LANES : (tile + 1) * LANES] = picked


def exchange(values, axes):
    return lax.all_to_all(values, axes, split_axis=0, concat_axis=0, tiled=True)


def spread_to(values, count):
    return jnp.broadcast_to(values[None], (count,) + values.shape)


def vmem():
    return pl.BlockSpec(memory_space=pltpu.VMEM)


def params(mib, *semantics):
    return pltpu.CompilerParams(vmem_limit_bytes=mib * MIB, dimension_semantics=semantics or None)


def local(mel, lengths, routes, conv1_weight, conv1_bias, conv2_weight, conv2_bias, out_grad):
    x_hi, y, core = lax.axis_index("xh"), lax.axis_index("y"), lax.axis_index("c")
    where = jnp.stack([x_hi, lax.axis_index("xl"), core, (x_hi * HOLDERS + y) * 2 + core]).astype(jnp.int32)

    def shape(*dims, dtype=BF16):
        return jax.ShapeDtypeStruct(dims, dtype)

    def from_hbm(values):
        return pltpu.with_memory_space_constraint(values, pltpu.HBM)

    def in_hbm(*dims, dtype=BF16):
        return pltpu.HBM(dims, dtype)

    pay = pl.pallas_call(
        prepare_kernel,
        in_specs=[pl.BlockSpec(memory_space=pltpu.SMEM), vmem()],
        out_specs=vmem(),
        out_shape=in_hbm(HOLDERS, PAY, 2 * HALF, MEL),
        compiler_params=params(60),
        name="mel_payload",
    )(lengths, mel)
    got_pay = exchange(pay, "y")
    cores = [(0, 1), (1, 0)]
    far_weight = lax.ppermute(conv2_weight, ("xh", "xl"), [(0, 3), (3, 0), (1, 2), (2, 1)])
    pay = pl.pallas_call(
        prepare_kernel,
        in_specs=[pl.BlockSpec(memory_space=pltpu.SMEM), vmem()],
        out_specs=vmem(),
        out_shape=in_hbm(HOLDERS, PAY, 2 * HALF, MEL),
        compiler_params=params(60),
        name="mel_payload",
    )(lengths, mel)
    got_pay = exchange(pay, "y")
    weights = [
        conv2_weight,
        lax.ppermute(conv2_weight, "c", [(0, 1), (1, 0)]),
        lax.ppermute(conv2_weight, ("xh", "xl"), [(0, 3), (3, 0), (1, 2), (2, 1)]),
        lax.ppermute(conv2_weight, ("xh", "c", "xl"), [(i, 7 - i) for i in range(8)]),
    ]

    w1, b1 = pl.pallas_call(
        columns_kernel,
        in_specs=[pl.BlockSpec(memory_space=pltpu.SMEM), vmem(), vmem()],
        out_specs=[vmem()] * 2,
        out_shape=[shape(3 * MEL, WIDE), shape(1, WIDE, dtype=F32)],
        scratch_shapes=[pltpu.VMEM((3 * MEL, WIDE), F32)],
        compiler_params=params(10),
        name="conv1_columns",
    )(where, conv1_weight, conv1_bias[None])
    own_weight, b1 = lax.optimization_barrier((conv2_weight, b1))
    far_weight, b1 = lax.optimization_barrier((far_weight, b1))
    weights = [
        conv2_weight,
        lax.ppermute(own_weight, "c", cores),
        far_weight,
        lax.ppermute(far_weight, "c", cores),
    ]

    pair = lambda i: (i, 0, 0)
    pair4 = lambda i: (i, 0, 0, 0)
    parts, cols, acts, slopes = pl.pallas_call(
        forward_kernel,
        grid=(HOLDERS,),
        in_specs=[
            pl.BlockSpec((1, PAY, 2 * HALF, MEL), pair4),
            *[vmem()] * (2 + BLOCKS),
        ],
        out_specs=[
            pl.BlockSpec((1, STEPS, D2), pair),
            pl.BlockSpec((1, STEPS, 4 * LANES), pair),
            pl.BlockSpec((1, 3, STEPS, WIDE), pair4),
            pl.BlockSpec((1, 2, STEPS, WIDE), pair4),
        ],
        out_shape=[
            in_hbm(HOLDERS, STEPS, D2),
            in_hbm(HOLDERS, STEPS, 4 * LANES),
            in_hbm(HOLDERS, 3, STEPS, WIDE),
            in_hbm(HOLDERS, 2, STEPS, WIDE, dtype=F32),
        ],
        scratch_shapes=[pltpu.VMEM((WIDE, 3 * D2), BF16), pltpu.VMEM((2 * STEPS, MEL), F32)],
        compiler_params=params(20, "arbitrary"),
        name="stem_forward",
    )(got_pay, w1, b1, *weights)

    got_parts = exchange(parts, "y")
    owner = jnp.repeat(routes[:, 0], HALF)
    rep, features = pl.pallas_call(
        middle_kernel,
        in_specs=[vmem()] * 4,
        out_specs=[vmem()] * 2,
        out_shape=[in_hbm(HOLDERS, STEPS, D2), shape(STEPS, D2)],
        compiler_params=params(10),
        name="stem_middle",
    )(
        got_parts,
        from_hbm(out_grad.reshape(STEPS, D2)),
        conv2_bias[None],
        from_hbm(jnp.repeat(lengths.astype(F32), HALF)[:, None]),
    )
    got_grad = exchange(rep, "y")
    same, cross = pl.pallas_call(
        place_kernel,
        in_specs=[pl.BlockSpec(memory_space=pltpu.SMEM), vmem(), vmem(), vmem()],
        out_specs=[vmem()] * 2,
        out_shape=[shape(CHIPS, ROWS, LANES)] * 2,
        compiler_params=params(10),
        name="features_place",
    )(where, features, owner[:, None], owner[None])
    got_grad, same = lax.optimization_barrier((got_grad, same))

    keep, send = pl.pallas_call(
        backward_kernel,
        grid=(HOLDERS // 2,),
        in_specs=[
            pl.BlockSpec(memory_space=pltpu.SMEM),
            pl.BlockSpec((2, STEPS, D2), pair),
            *[vmem()] * BLOCKS,
            pl.BlockSpec((2, STEPS, 4 * LANES), pair),
            pl.BlockSpec((2, 3, STEPS, WIDE), pair4),
            pl.BlockSpec((2, 2, STEPS, WIDE), pair4),
        ],
        out_specs=[vmem()] * 2,
        out_shape=[shape(2, 2, PACK, LANES, dtype=F32), shape(2, 2, PACK, LANES)],
        scratch_shapes=[
            pltpu.VMEM((WIDE, 3 * D2), BF16),
            pltpu.VMEM((WIDE, 3 * D2), F32),
            pltpu.VMEM((WIDE, 3 * LANES), F32),
            pltpu.VMEM((1, WIDE), F32),
            pltpu.VMEM((1, D2), F32),
        ],
        compiler_params=params(32, "arbitrary"),
        name="stem_backward",
    )(where, got_grad, *weights, from_hbm(cols), from_hbm(acts), from_hbm(slopes))
    got = lax.ppermute(send, "c", cores)
    quarters = exchange((keep + got.astype(F32)).astype(BF16).reshape(4, PACK, LANES), ("xh", "xl"))

    def summed(values, *dims):
        return pl.pallas_call(
            sum_kernel,
            in_specs=[vmem()],
            out_specs=vmem(),
            out_shape=shape(*dims),
            compiler_params=params(8),
            name="gradient_sum",
        )(values)

    half = summed(quarters, PACK, LANES)
    quarter = PACK // 4
    near = summed(exchange(half.reshape(4, quarter, LANES), "zl"), 4, quarter, LANES)
    far = summed(exchange(near, "zh"), 4, quarter, LANES)
    half = exchange(far, "zl").reshape(PACK, LANES)
    own = half[:HALF_ROWS]
    other = lax.ppermute(own, "xl", [(0, 1), (1, 0)])
    conv1 = spread_to(half[HALF_ROWS:], CHIPS)
    got = exchange(jnp.concatenate([same, conv1[:, : 3 * ROWS], cross, conv1[:, 3 * ROWS :]], axis=1), ("xh", "y"))
    got, other = lax.optimization_barrier((got, other))
    got_cross = lax.ppermute(got, "c", cores)
    weight_grad, bias_grad, second_bias_grad, conv2_rows_grad, packed = pl.pallas_call(
        last_kernel,
        grid=(3,),
        in_specs=[
            pl.BlockSpec(memory_space=pltpu.SMEM),
            *[vmem()] * 4,
        ],
        out_specs=[
            pl.BlockSpec((LANES, 16 * ROWS), lambda i: (i, 0)),
            pl.BlockSpec((16 * ROWS,), lambda i: (0,)),
            pl.BlockSpec((D2,), lambda i: (0,)),
            pl.BlockSpec((ROWS, 3 * D2), lambda i: (0, 0)),
            pl.BlockSpec((SLOTS * HALF, D2), lambda i: (0, 0)),
        ],
        out_shape=[
            shape(3 * MEL, 16 * ROWS, dtype=F32),
            shape(16 * ROWS, dtype=F32),
            shape(D2, dtype=F32),
            shape(ROWS, 3 * D2, dtype=F32),
            shape(SLOTS * HALF, D2),
        ],
        scratch_shapes=[pltpu.VMEM((16 * ROWS, LANES), BF16), pltpu.VMEM((16, 16, LANES), F32)],
        compiler_params=params(16, "arbitrary"),
        name="gradient_unpack",
    )(where, got, got_cross, own, other)
    return packed.reshape(SLOTS, HALF, D2), weight_grad, bias_grad, second_bias_grad, conv2_rows_grad


def solution(mesh):
    fine = Mesh(mesh.devices.reshape(2, 4, 2, 4, 4, 2), ALL_AXES)
    placed = (
        P(ALL_AXES, None, None),
        P(ALL_AXES),
        P(ALL_AXES, None),
        P(),
        P(),
        P(ENC, None),
        P(),
        P(ALL_AXES, None, None),
    )
    return jax.shard_map(
        local,
        mesh=fine,
        in_specs=placed,
        out_specs=(P(ALL_AXES, None, None), P(), P(), P(), P(ENC, None)),
        check_vma=False,
    )
```

```python
import functools

import jax
import jax.numpy as jnp
from jax import lax
from jax.experimental import pallas as pl
from jax.experimental.pallas import tpu as pltpu
from jax.sharding import Mesh
from jax.sharding import PartitionSpec as P

inv_root_two = 0.7071067811865476
inv_root_tau = 0.3989422804014327

MEL = 128
D2 = 640
ROWS = 80
LANES = 128
HOLDERS = 4
BLOCKS = 4
WIDE = 384
CLIPS = 16
HALF = 8
STEPS = CLIPS * HALF
SLOTS = 2 * CLIPS
PAY = 26
CHIPS = 8
DEAD = -1e30
PACK = 896
HALF_ROWS = 8 * ROWS
MIB = 1024 * 1024
ALL_AXES = ("xh", "y", "c", "zh", "zl", "xl")
ENC = ("xh", "y", "c")
F32 = jnp.float32
BF16 = jnp.bfloat16


def gelu_value(values):
    return values * (0.5 * (1.0 + lax.erf(values * inv_root_two)))


def gelu_both(values):
    cdf = 0.5 * (1.0 + lax.erf(values * inv_root_two))
    return values * cdf, cdf + values * jnp.exp(-0.5 * values * values) * inv_root_tau


def shift_down(values):
    rows, width = values.shape
    t = lax.broadcasted_iota(jnp.int32, (rows, width), 0) & (HALF - 1)
    clips = values.reshape(rows // HALF, HALF, width)
    moved = pltpu.roll(clips, 1, 1).reshape(rows, width)
    return jnp.where(t == 0, 0.0, moved)


def shift_up(values):
    rows, width = values.shape
    t = lax.broadcasted_iota(jnp.int32, (rows, width), 0) & (HALF - 1)
    clips = values.reshape(rows // HALF, HALF, width)
    moved = pltpu.roll(clips, HALF - 1, 1).reshape(rows, width)
    return jnp.where(t == HALF - 1, 0.0, moved)


def dot(left, right):
    return jnp.dot(left, right, preferred_element_type=F32)


def dot_nt(left, right):
    return lax.dot_general(left, right, (((1,), (1,)), ((), ())), preferred_element_type=F32)


def dot_tn(left, right):
    return lax.dot_general(left, right, (((0,), (0,)), ((), ())), preferred_element_type=F32)


def stack_weights(refs, w2_ref):
    @pl.when(pl.program_id(0) == 0)
    def _():
        for block, ref in enumerate(refs):
            w2_ref[block * ROWS : (block + 1) * ROWS, :] = ref[...]
        w2_ref[BLOCKS * ROWS :, :] = jnp.zeros((WIDE - BLOCKS * ROWS, 3 * D2), BF16)


def prepare_kernel(length_ref, mel_ref, pay_ref):
    clip = lax.broadcasted_iota(jnp.int32, (CLIPS, MEL), 0)
    length = jnp.zeros((CLIPS, MEL), F32)
    for index in range(CLIPS):
        length = jnp.where(clip == index, length_ref[index].astype(F32), length)
    for target in range(HOLDERS):
        pay_ref[target, :CLIPS] = mel_ref[...]
        pay_ref[target, CLIPS] = length.astype(BF16)
        pay_ref[target, CLIPS + 1 :] = jnp.zeros((PAY - CLIPS - 1, 2 * HALF, MEL), BF16)


def columns_kernel(where_ref, weight_ref, bias_ref, w1_ref, b1_ref, picked):
    picked[...] = jnp.zeros_like(picked)
    b1_ref[...] = jnp.zeros_like(b1_ref)
    for block, flip in enumerate((0, 1, 2 * HOLDERS, 2 * HOLDERS + 1)):
        first = (where_ref[3] ^ flip) * ROWS
        start = pl.multiple_of(jnp.minimum((first >> 7) << 7, 16 * ROWS - 2 * LANES), LANES)
        shift = (2 * LANES - (first - start)) & (2 * LANES - 1)
        lanes = slice(block * ROWS, (block + 1) * ROWS)
        window = weight_ref[:, pl.ds(start, 2 * LANES)].astype(F32)
        picked[:, lanes] = pltpu.roll(window, shift, 1)[:, :ROWS]
        window = jnp.broadcast_to(bias_ref[pl.ds(start, 2 * LANES)].reshape(1, 2 * LANES), (8, 2 * LANES))
        b1_ref[:, lanes] = pltpu.roll(window, shift, 1)[0:1, :ROWS]
    w1_ref[...] = picked[...].astype(BF16)


def forward_kernel(
    pay_ref, w1_ref, b1_ref, own_ref, side_ref, far_ref, both_ref, part_ref, cols_ref, act_ref, pre_ref, w2_ref,
    frames_ref,
):
    stack_weights((own_ref, side_ref, far_ref, both_ref), w2_ref)
    spread = (
        lax.broadcasted_iota(jnp.int32, (STEPS, CLIPS), 0) >> 3
        == lax.broadcasted_iota(jnp.int32, (STEPS, CLIPS), 1)
    ).astype(F32).astype(BF16)
    length = dot(spread, pay_ref[0, CLIPS])
    frames_ref[...] = pay_ref[0, :CLIPS].astype(F32).reshape(2 * STEPS, MEL)
    t = (lax.broadcasted_iota(jnp.int32, (STEPS, LANES), 0) & (HALF - 1)).astype(F32)
    live_even, live_odd = 2.0 * t < length, 2.0 * t + 1.0 < length
    even = jnp.where(live_even, frames_ref[pl.ds(0, STEPS, 2), :], 0.0)
    odd = jnp.where(live_odd, frames_ref[pl.ds(1, STEPS, 2), :], 0.0)
    cols_ref[0, :, :LANES] = shift_down(odd).astype(BF16)
    cols_ref[0, :, LANES : 2 * LANES] = even.astype(BF16)
    cols_ref[0, :, 2 * LANES : 3 * LANES] = odd.astype(BF16)
    cols_ref[0, :, 3 * LANES :] = shift_up(even).astype(BF16)
    bias = b1_ref[...]
    live_even = jnp.concatenate([live_even] * (WIDE // LANES), axis=1)
    live_odd = jnp.concatenate([live_odd] * (WIDE // LANES), axis=1)
    pre = dot(cols_ref[0, :, : 3 * LANES], w1_ref[...]) + bias
    pre_ref[0, 0] = jnp.where(live_even, pre, DEAD)
    act_even = jnp.where(live_even, gelu_value(pre), 0.0).astype(BF16)
    pre = dot(cols_ref[0, :, LANES:], w1_ref[...]) + bias
    pre_ref[0, 1] = jnp.where(live_odd, pre, DEAD)
    act = jnp.where(live_odd, gelu_value(pre), 0.0)
    act_odd = act.astype(BF16)
    act_prior = shift_down(act).astype(BF16)
    act_ref[0, 0] = act_prior
    act_ref[0, 1] = act_even
    act_ref[0, 2] = act_odd
    total = dot(act_prior, w2_ref[:, :D2])
    total = total + dot(act_even, w2_ref[:, D2 : 2 * D2])
    total = total + dot(act_odd, w2_ref[:, 2 * D2 :])
    part_ref[0] = total.astype(BF16)


def slope_kernel(pre_ref, act_ref, slope_ref, turned_ref):
    pre = pre_ref[0].reshape(2 * STEPS, WIDE)
    slope = jnp.where(pre > 0.5 * DEAD, gelu_both(pre)[1], 0.0)
    slope_ref[0] = slope.reshape(2, STEPS, WIDE)
    for tap in range(3):
        turned_ref[tap] = act_ref[0, tap].T


def middle_kernel(
    where_ref, part_ref, grad_ref, b2_ref, length_ref, owner_col_ref, owner_row_ref, rep_ref, same_ref, cross_ref
):
    pre = part_ref[0].astype(F32)
    for source in range(1, HOLDERS):
        pre = pre + part_ref[source].astype(F32)
    pre = pre + b2_ref[...]
    t = (lax.broadcasted_iota(jnp.int32, (STEPS, 1), 0) & (HALF - 1)).astype(F32)
    live = jnp.where(2.0 * t < length_ref[...], 1.0, 0.0)
    value, slope = gelu_both(pre)
    features = (value * live).astype(BF16)
    second_grad = (grad_ref[...].astype(F32) * slope * live).astype(BF16)
    for target in range(HOLDERS):
        rep_ref[target] = second_grad
    here = lax.broadcasted_iota(jnp.int32, (STEPS, STEPS), 0)
    there = lax.broadcasted_iota(jnp.int32, (STEPS, STEPS), 1)
    same = (owner_col_ref[...] == owner_row_ref[...]) & ((here >> 3) < (there >> 3))
    same = same & ((here & (HALF - 1)) == 0)
    rank = jnp.sum(jnp.where(same, 1.0, 0.0), axis=0, keepdims=True)
    place = lax.broadcasted_iota(jnp.int32, (1, STEPS), 1) & (HALF - 1)
    place = (owner_row_ref[...] * 2 + rank.astype(jnp.int32)) * HALF + place
    wanted = lax.broadcasted_iota(jnp.int32, (SLOTS * HALF, STEPS), 0) == place
    placed = dot(jnp.where(wanted, 1.0, 0.0).astype(BF16), features)
    first = where_ref[2] == 0
    for chip in range(CHIPS):
        for tile in range(D2 // LANES):
            rows, columns = slice(tile * 16, (tile + 1) * 16), slice(tile * LANES, (tile + 1) * LANES)
            left = placed[chip * 32 : chip * 32 + 16, columns]
            right = placed[chip * 32 + 16 : chip * 32 + 32, columns]
            same_ref[chip, rows, :] = jnp.where(first, left, right).astype(BF16)
            cross_ref[chip, rows, :] = jnp.where(first, right, left).astype(BF16)


def backward_kernel(
    where_ref, grad_ref, own_ref, side_ref, far_ref, both_ref, cols_ref, act_ref, slope_ref, keep_ref, send_ref,
    w2_ref, conv2_sum, conv1_sum, bias1_sum, bias2_sum,
):
    stack_weights((own_ref, side_ref, far_ref, both_ref), w2_ref)
    step = pl.program_id(0)

    @pl.when(step == 0)
    def _():
        conv2_sum[...] = jnp.zeros_like(conv2_sum)
        conv1_sum[...] = jnp.zeros_like(conv1_sum)
        bias1_sum[...] = jnp.zeros_like(bias1_sum)
        bias2_sum[...] = jnp.zeros_like(bias2_sum)

    rows = 2 * STEPS
    grad = grad_ref[...].reshape(rows, D2)
    bias2_sum[...] += jnp.sum(grad.astype(F32), axis=0, keepdims=True)
    even = dot_nt(grad, w2_ref[:, D2 : 2 * D2])
    odd = dot_nt(grad, w2_ref[:, 2 * D2 :]) + shift_up(dot_nt(grad, w2_ref[:, :D2]))
    even = (even * slope_ref[:, 0].reshape(rows, WIDE)).astype(BF16)
    odd = (odd * slope_ref[:, 1].reshape(rows, WIDE)).astype(BF16)
    cols = cols_ref[...].reshape(rows, 4 * LANES)
    conv1_sum[...] += dot_tn(even, cols[:, : 3 * LANES]) + dot_tn(odd, cols[:, LANES:])
    bias1_sum[...] += jnp.sum(even.astype(F32) + odd.astype(F32), axis=0, keepdims=True)
    for tap in range(3):
        conv2_sum[:, tap * D2 : (tap + 1) * D2] += dot(act_ref[tap], grad)

    @pl.when(step == pl.num_programs(0) - 1)
    def _():
        mine = where_ref[0]
        for block in range(BLOCKS):
            target = mine if block < 2 else 1 - mine
            out = keep_ref if block % 2 == 0 else send_ref
            first = block * ROWS
            for tile in range(15):
                half, spot = tile // 8, tile % 8
                piece = conv2_sum[first : first + ROWS, tile * LANES : (tile + 1) * LANES]
                out[target, half, spot * ROWS : (spot + 1) * ROWS, :] = piece.astype(out.dtype)
            out[target, 1, 7 * ROWS : 8 * ROWS, :] = jnp.zeros((ROWS, LANES), out.dtype)
            biases = [jnp.concatenate([bias1_sum[:, first : first + ROWS], jnp.zeros((1, LANES - ROWS), F32)], axis=1)]
            for tile in range(D2 // LANES):
                biases.append(bias2_sum[:, tile * LANES : (tile + 1) * LANES])
            biases.append(jnp.zeros((16 - len(biases), LANES), F32))
            biases = jnp.concatenate(biases, axis=0).astype(out.dtype)
            for half in range(2):
                for tile in range(3):
                    piece = conv1_sum[first : first + ROWS, tile * LANES : (tile + 1) * LANES]
                    out[target, half, (8 + tile) * ROWS : (9 + tile) * ROWS, :] = piece.astype(out.dtype)
                out[target, half, 11 * ROWS :, :] = biases


def sum_kernel(got_ref, out_ref):
    total = got_ref[0].astype(F32)
    for source in range(1, got_ref.shape[0]):
        total = total + got_ref[source].astype(F32)
    total = total.astype(BF16)
    if len(out_ref.shape) == 2:
        out_ref[...] = total
    else:
        for target in range(out_ref.shape[0]):
            out_ref[target] = total


def pairs_kernel(own_ref, near_ref, far_ref, both_ref, out_ref):
    own, near, far, both = (ref[...].astype(F32) for ref in (own_ref, near_ref, far_ref, both_ref))
    total = ((own + near) + (far + both)).astype(BF16)
    for target in range(out_ref.shape[0]):
        out_ref[target] = total


def last_kernel(
    where_ref, got_ref, cross_ref, own_ref, other_ref, weight_ref, bias1_ref, bias2_ref, conv2_ref, packed_ref,
    whole, biases,
):
    step, core = pl.program_id(0), where_ref[2]
    rows = pl.ds(pl.multiple_of((step + 1) * ROWS, 16), ROWS)
    for chip in range(CHIPS):
        whole[pl.ds(pl.multiple_of((2 * chip + core) * ROWS, 16), ROWS), :] = got_ref[chip, rows, :]
        whole[pl.ds(pl.multiple_of((2 * chip + 1 - core) * ROWS, 16), ROWS), :] = cross_ref[chip, rows, :]
    for block in range(10):
        columns = slice(block * LANES, (block + 1) * LANES)
        weight_ref[:, columns] = whole[columns, :].T.astype(F32)

    @pl.when(step == 0)
    def _():
        for chip in range(CHIPS):
            biases[2 * chip + core] = got_ref[chip, 5 * ROWS :, :].astype(F32)
            biases[2 * chip + 1 - core] = cross_ref[chip, 5 * ROWS :, :].astype(F32)
            left = pl.ds(pl.multiple_of(chip * 32 + 16 * core, 16), 16)
            right = pl.ds(pl.multiple_of(chip * 32 + 16 - 16 * core, 16), 16)
            for tile in range(D2 // LANES):
                columns = slice(tile * LANES, (tile + 1) * LANES)
                packed_ref[left, columns] = got_ref[chip, tile * 16 : (tile + 1) * 16, :]
                packed_ref[right, columns] = cross_ref[chip, 4 * ROWS + tile * 16 : 4 * ROWS + (tile + 1) * 16, :]
        bias1 = jnp.concatenate([biases[source, 0:1, :ROWS] for source in range(16)], axis=1)
        bias1_ref[...] = bias1.reshape(16 * ROWS)
        bias2 = jnp.concatenate([biases[0, 1 + tile : 2 + tile, :] for tile in range(D2 // LANES)], axis=1)
        bias2_ref[...] = bias2.reshape(D2)
        lower = where_ref[1] == 0
        for tile in range(15):
            half, spot = tile // 8, tile % 8
            rows = slice(spot * ROWS, (spot + 1) * ROWS)
            own, other = own_ref[rows, :].astype(F32), other_ref[rows, :].astype(F32)
            picked = jnp.where(lower, own, other) if half == 0 else jnp.where(lower, other, own)
            conv2_ref[:, tile * LANES : (tile + 1) * LANES] = picked


def exchange(values, axes):
    return lax.all_to_all(values, axes, split_axis=0, concat_axis=0, tiled=True)


def spread_to(values, count):
    return jnp.broadcast_to(values[None], (count,) + values.shape)


def vmem():
    return pl.BlockSpec(memory_space=pltpu.VMEM)


def params(mib, *semantics):
    return pltpu.CompilerParams(vmem_limit_bytes=mib * MIB, dimension_semantics=semantics or None)


def local(mel, lengths, routes, conv1_weight, conv1_bias, conv2_weight, conv2_bias, out_grad):
    x_hi, y, core = lax.axis_index("xh"), lax.axis_index("y"), lax.axis_index("c")
    where = jnp.stack([x_hi, lax.axis_index("xl"), core, (x_hi * HOLDERS + y) * 2 + core]).astype(jnp.int32)

    def shape(*dims, dtype=BF16):
        return jax.ShapeDtypeStruct(dims, dtype)

    def from_hbm(values):
        return pltpu.with_memory_space_constraint(values, pltpu.HBM)

    def in_hbm(*dims, dtype=BF16):
        return pltpu.HBM(dims, dtype)

    pay = pl.pallas_call(
        prepare_kernel,
        in_specs=[pl.BlockSpec(memory_space=pltpu.SMEM), vmem()],
        out_specs=vmem(),
        out_shape=in_hbm(HOLDERS, PAY, 2 * HALF, MEL),
        compiler_params=params(60),
        name="mel_payload",
    )(lengths, mel)
    got_pay = exchange(pay, "y")
    cores = [(0, 1), (1, 0)]
    far_weight = lax.ppermute(conv2_weight, ("xh", "xl"), [(0, 3), (3, 0), (1, 2), (2, 1)])
    pay = pl.pallas_call(
        prepare_kernel,
        in_specs=[pl.BlockSpec(memory_space=pltpu.SMEM), vmem()],
        out_specs=vmem(),
        out_shape=in_hbm(HOLDERS, PAY, 2 * HALF, MEL),
        compiler_params=params(60),
        name="mel_payload",
    )(lengths, mel)
    got_pay = exchange(pay, "y")
    weights = [
        conv2_weight,
        lax.ppermute(conv2_weight, "c", [(0, 1), (1, 0)]),
        lax.ppermute(conv2_weight, ("xh", "xl"), [(0, 3), (3, 0), (1, 2), (2, 1)]),
        lax.ppermute(conv2_weight, ("xh", "c", "xl"), [(i, 7 - i) for i in range(8)]),
    ]

    w1, b1 = pl.pallas_call(
        columns_kernel,
        in_specs=[pl.BlockSpec(memory_space=pltpu.SMEM), vmem(), vmem()],
        out_specs=[vmem()] * 2,
        out_shape=[shape(3 * MEL, WIDE), shape(1, WIDE, dtype=F32)],
        scratch_shapes=[pltpu.VMEM((3 * MEL, WIDE), F32)],
        compiler_params=params(10),
        name="conv1_columns",
    )(where, conv1_weight, conv1_bias)
    own_weight, place = lax.optimization_barrier((conv2_weight, where))
    far_weight, place = lax.optimization_barrier((far_weight, place))
    weights = [
        conv2_weight,
        lax.ppermute(own_weight, "c", cores),
        far_weight,
        lax.ppermute(far_weight, "c", cores),
    ]

    pair = lambda i: (i, 0, 0)
    pair4 = lambda i: (i, 0, 0, 0)
    parts, cols, acts, pres = pl.pallas_call(
        forward_kernel,
        grid=(HOLDERS,),
        in_specs=[
            pl.BlockSpec((1, PAY, 2 * HALF, MEL), pair4),
            *[vmem()] * (2 + BLOCKS),
        ],
        out_specs=[
            pl.BlockSpec((1, STEPS, D2), pair),
            pl.BlockSpec((1, STEPS, 4 * LANES), pair),
            pl.BlockSpec((1, 3, STEPS, WIDE), pair4),
            pl.BlockSpec((1, 2, STEPS, WIDE), pair4),
        ],
        out_shape=[
            in_hbm(HOLDERS, STEPS, D2),
            in_hbm(HOLDERS, STEPS, 4 * LANES),
            in_hbm(HOLDERS, 3, STEPS, WIDE),
            in_hbm(HOLDERS, 2, STEPS, WIDE, dtype=F32),
        ],
        scratch_shapes=[pltpu.VMEM((WIDE, 3 * D2), BF16), pltpu.VMEM((2 * STEPS, MEL), F32)],
        compiler_params=params(20, "arbitrary"),
        name="stem_forward",
    )(got_pay, w1, b1, *weights)

    got_parts = exchange(parts, "y")
    slopes, turned = pl.pallas_call(
        slope_kernel,
        grid=(HOLDERS,),
        in_specs=[pl.BlockSpec((1, 2, STEPS, WIDE), pair4), pl.BlockSpec((1, 3, STEPS, WIDE), pair4)],
        out_specs=[pl.BlockSpec((1, 2, STEPS, WIDE), pair4), pl.BlockSpec((3, WIDE, STEPS), lambda i: (0, 0, i))],
        out_shape=[in_hbm(HOLDERS, 2, STEPS, WIDE, dtype=F32), in_hbm(3, WIDE, HOLDERS * STEPS)],
        compiler_params=params(20, "arbitrary"),
        name="stem_slopes",
    )(from_hbm(pres), from_hbm(acts))
    got_parts, slopes, turned = lax.optimization_barrier((got_parts, slopes, turned))
    owner = jnp.repeat(routes[:, 0], HALF)
    rep, same, cross = pl.pallas_call(
        middle_kernel,
        in_specs=[pl.BlockSpec(memory_space=pltpu.SMEM)] + [vmem()] * 6,
        out_specs=[vmem()] * 3,
        out_shape=[in_hbm(HOLDERS, STEPS, D2), shape(CHIPS, ROWS, LANES), shape(CHIPS, ROWS, LANES)],
        compiler_params=params(10),
        name="stem_middle",
    )(
        where,
        got_parts,
        from_hbm(out_grad.reshape(STEPS, D2)),
        conv2_bias[None],
        from_hbm(jnp.repeat(lengths.astype(F32), HALF)[:, None]),
        owner[:, None],
        owner[None],
    )
    got_grad = exchange(rep, "y")

    keep, send = pl.pallas_call(
        backward_kernel,
        grid=(HOLDERS // 2,),
        in_specs=[
            pl.BlockSpec(memory_space=pltpu.SMEM),
            pl.BlockSpec((2, STEPS, D2), pair),
            *[vmem()] * BLOCKS,
            pl.BlockSpec((2, STEPS, 4 * LANES), pair),
            pl.BlockSpec((3, WIDE, 2 * STEPS), lambda i: (0, 0, i)),
            pl.BlockSpec((2, 2, STEPS, WIDE), pair4),
        ],
        out_specs=[vmem()] * 2,
        out_shape=[shape(2, 2, PACK, LANES, dtype=F32), shape(2, 2, PACK, LANES)],
        scratch_shapes=[
            pltpu.VMEM((WIDE, 3 * D2), BF16),
            pltpu.VMEM((WIDE, 3 * D2), F32),
            pltpu.VMEM((WIDE, 3 * LANES), F32),
            pltpu.VMEM((1, WIDE), F32),
            pltpu.VMEM((1, D2), F32),
        ],
        compiler_params=params(32, "arbitrary"),
        name="stem_backward",
    )(where, got_grad, *weights, from_hbm(cols), from_hbm(turned), from_hbm(slopes))
    got = lax.ppermute(send, "c", cores)
    quarters = exchange((keep + got.astype(F32)).astype(BF16).reshape(4, PACK, LANES), ("xh", "xl"))

    def summed(values, *dims):
        return pl.pallas_call(
            sum_kernel,
            in_specs=[vmem()],
            out_specs=vmem(),
            out_shape=shape(*dims),
            compiler_params=params(8),
            name="gradient_sum",
        )(values)

    half = summed(quarters, PACK, LANES)
    quarter = PACK // 4
    near = summed(exchange(half.reshape(4, quarter, LANES), "zl"), quarter, LANES)
    far = {flip: lax.ppermute(near, "zh", [(i, i ^ flip) for i in range(4)]) for flip in (2, 3, 1)}
    far = pl.pallas_call(
        pairs_kernel,
        in_specs=[vmem()] * 4,
        out_specs=vmem(),
        out_shape=shape(4, quarter, LANES),
        compiler_params=params(8),
        name="gradient_pairs",
    )(near, far[1], far[2], far[3])
    half = exchange(far, "zl").reshape(PACK, LANES)
    own = half[:HALF_ROWS]
    other = lax.ppermute(own, "xl", [(0, 1), (1, 0)])
    conv1 = spread_to(half[HALF_ROWS:], CHIPS)
    got = exchange(jnp.concatenate([same, conv1[:, : 3 * ROWS], cross, conv1[:, 3 * ROWS :]], axis=1), ("xh", "y"))
    got, other = lax.optimization_barrier((got, other))
    got_cross = lax.ppermute(got, "c", cores)
    weight_grad, bias_grad, second_bias_grad, conv2_rows_grad, packed = pl.pallas_call(
        last_kernel,
        grid=(3,),
        in_specs=[
            pl.BlockSpec(memory_space=pltpu.SMEM),
            *[vmem()] * 4,
        ],
        out_specs=[
            pl.BlockSpec((LANES, 16 * ROWS), lambda i: (i, 0)),
            pl.BlockSpec((16 * ROWS,), lambda i: (0,)),
            pl.BlockSpec((D2,), lambda i: (0,)),
            pl.BlockSpec((ROWS, 3 * D2), lambda i: (0, 0)),
            pl.BlockSpec((SLOTS * HALF, D2), lambda i: (0, 0)),
        ],
        out_shape=[
            shape(3 * MEL, 16 * ROWS, dtype=F32),
            shape(16 * ROWS, dtype=F32),
            shape(D2, dtype=F32),
            shape(ROWS, 3 * D2, dtype=F32),
            shape(SLOTS * HALF, D2),
        ],
        scratch_shapes=[pltpu.VMEM((16 * ROWS, LANES), BF16), pltpu.VMEM((16, 16, LANES), F32)],
        compiler_params=params(16, "arbitrary"),
        name="gradient_unpack",
    )(where, got, got_cross, own, other)
    return packed.reshape(SLOTS, HALF, D2), weight_grad, bias_grad, second_bias_grad, conv2_rows_grad


def solution(mesh):
    fine = Mesh(mesh.devices.reshape(2, 4, 2, 4, 4, 2), ALL_AXES)
    placed = (
        P(ALL_AXES, None, None),
        P(ALL_AXES),
        P(ALL_AXES, None),
        P(),
        P(),
        P(ENC, None),
        P(),
        P(ALL_AXES, None, None),
    )
    return jax.shard_map(
        local,
        mesh=fine,
        in_specs=placed,
        out_specs=(P(ALL_AXES, None, None), P(), P(), P(), P(ENC, None)),
        check_vma=False,
    )
```

```python
import functools

import jax
import jax.numpy as jnp
from jax import lax
from jax.experimental import pallas as pl
from jax.experimental.pallas import tpu as pltpu
from jax.sharding import Mesh
from jax.sharding import PartitionSpec as P

inv_root_two = 0.7071067811865476
inv_root_tau = 0.3989422804014327

MEL = 128
D2 = 640
ROWS = 80
LANES = 128
HOLDERS = 4
BLOCKS = 4
WIDE = 384
CLIPS = 16
HALF = 8
STEPS = CLIPS * HALF
SLOTS = 2 * CLIPS
PAY = 26
CHIPS = 8
PACK = 896
HALF_ROWS = 8 * ROWS
MIB = 1024 * 1024
ALL_AXES = ("xh", "y", "c", "zh", "zl", "xl")
ENC = ("xh", "y", "c")
F32 = jnp.float32
BF16 = jnp.bfloat16


def gelu_value(values):
    return values * (0.5 * (1.0 + lax.erf(values * inv_root_two)))


def gelu_both(values):
    cdf = 0.5 * (1.0 + lax.erf(values * inv_root_two))
    return values * cdf, cdf + values * jnp.exp(-0.5 * values * values) * inv_root_tau


def shift_down(values):
    rows, width = values.shape
    t = lax.broadcasted_iota(jnp.int32, (rows, width), 0) & (HALF - 1)
    clips = values.reshape(rows // HALF, HALF, width)
    moved = pltpu.roll(clips, 1, 1).reshape(rows, width)
    return jnp.where(t == 0, 0.0, moved)


def shift_up(values):
    rows, width = values.shape
    t = lax.broadcasted_iota(jnp.int32, (rows, width), 0) & (HALF - 1)
    clips = values.reshape(rows // HALF, HALF, width)
    moved = pltpu.roll(clips, HALF - 1, 1).reshape(rows, width)
    return jnp.where(t == HALF - 1, 0.0, moved)


def dot(left, right):
    return jnp.dot(left, right, preferred_element_type=F32)


def dot_nt(left, right):
    return lax.dot_general(left, right, (((1,), (1,)), ((), ())), preferred_element_type=F32)


def dot_tn(left, right):
    return lax.dot_general(left, right, (((0,), (0,)), ((), ())), preferred_element_type=F32)


def stack_weights(refs, w2_ref):
    for block, ref in enumerate(refs):
        w2_ref[block * ROWS : (block + 1) * ROWS, :] = ref[...]
    w2_ref[BLOCKS * ROWS :, :] = jnp.zeros((WIDE - BLOCKS * ROWS, 3 * D2), BF16)


def prepare_kernel(length_ref, mel_ref, pay_ref):
    clip = lax.broadcasted_iota(jnp.int32, (CLIPS, MEL), 0)
    length = jnp.zeros((CLIPS, MEL), F32)
    for index in range(CLIPS):
        length = jnp.where(clip == index, length_ref[index].astype(F32), length)
    for target in range(HOLDERS):
        pay_ref[target, :CLIPS] = mel_ref[...]
        pay_ref[target, CLIPS] = length.astype(BF16)
        pay_ref[target, CLIPS + 1 :] = jnp.zeros((PAY - CLIPS - 1, 2 * HALF, MEL), BF16)


def columns_kernel(where_ref, weight_ref, bias_ref, w1_ref, b1_ref, picked):
    picked[...] = jnp.zeros_like(picked)
    b1_ref[...] = jnp.zeros_like(b1_ref)
    for block, flip in enumerate((0, 1, 2 * HOLDERS, 2 * HOLDERS + 1)):
        first = (where_ref[3] ^ flip) * ROWS
        start = pl.multiple_of(jnp.minimum((first >> 7) << 7, 16 * ROWS - 2 * LANES), LANES)
        shift = (2 * LANES - (first - start)) & (2 * LANES - 1)
        lanes = slice(block * ROWS, (block + 1) * ROWS)
        window = weight_ref[:, pl.ds(start, 2 * LANES)].astype(F32)
        picked[:, lanes] = pltpu.roll(window, shift, 1)[:, :ROWS]
        window = jnp.broadcast_to(bias_ref[pl.ds(start, 2 * LANES)].reshape(1, 2 * LANES), (8, 2 * LANES))
        b1_ref[:, lanes] = pltpu.roll(window, shift, 1)[0:1, :ROWS]
    w1_ref[...] = picked[...].astype(BF16)


def first_conv(pay_ref, w1_ref, b1_ref, cols_ref, frames_ref):
    sources = pay_ref.shape[0]
    spread = (
        lax.broadcasted_iota(jnp.int32, (STEPS, CLIPS), 0) >> 3
        == lax.broadcasted_iota(jnp.int32, (STEPS, CLIPS), 1)
    ).astype(F32).astype(BF16)
    t = (lax.broadcasted_iota(jnp.int32, (STEPS, LANES), 0) & (HALF - 1)).astype(F32)
    lives_even, lives_odd = [], []
    for source in range(sources):
        rows = slice(source * STEPS, (source + 1) * STEPS)
        length = dot(spread, pay_ref[source, CLIPS])
        frames_ref[source] = pay_ref[source, :CLIPS].astype(F32).reshape(2 * STEPS, MEL)
        live_even, live_odd = 2.0 * t < length, 2.0 * t + 1.0 < length
        even = jnp.where(live_even, frames_ref[source, pl.ds(0, STEPS, 2), :], 0.0)
        odd = jnp.where(live_odd, frames_ref[source, pl.ds(1, STEPS, 2), :], 0.0)
        cols_ref[rows, :LANES] = shift_down(odd).astype(BF16)
        cols_ref[rows, LANES : 2 * LANES] = even.astype(BF16)
        cols_ref[rows, 2 * LANES : 3 * LANES] = odd.astype(BF16)
        cols_ref[rows, 3 * LANES :] = shift_up(even).astype(BF16)
        lives_even.append(jnp.concatenate([live_even] * (WIDE // LANES), axis=1))
        lives_odd.append(jnp.concatenate([live_odd] * (WIDE // LANES), axis=1))
    cols = jnp.concatenate([cols_ref[:, : 3 * LANES], cols_ref[:, LANES:]], axis=0)
    pre = dot(cols, w1_ref[...]) + b1_ref[...]
    half = sources * STEPS
    return pre[:half], pre[half:], jnp.concatenate(lives_even, axis=0), jnp.concatenate(lives_odd, axis=0)


def forward_kernel(
    pay_ref, w1_ref, b1_ref, own_ref, side_ref, far_ref, both_ref, part_ref, w2_ref, cols_ref, frames_ref
):
    @pl.when(pl.program_id(0) == 0)
    def _():
        stack_weights((own_ref, side_ref, far_ref, both_ref), w2_ref)

    pre_even, pre_odd, live_even, live_odd = first_conv(pay_ref, w1_ref, b1_ref, cols_ref, frames_ref)
    odd = jnp.where(live_odd, gelu_value(pre_odd), 0.0)
    total = dot(odd.astype(BF16), w2_ref[:, 2 * D2 :]) + dot(shift_down(odd).astype(BF16), w2_ref[:, :D2])
    even = jnp.where(live_even, gelu_value(pre_even), 0.0)
    total = total + dot(even.astype(BF16), w2_ref[:, D2 : 2 * D2])
    part_ref[...] = total.astype(BF16).reshape(part_ref.shape)


def slope_kernel(pay_ref, w1_ref, b1_ref, cols_ref, slope_ref, turned_ref, frames_ref):
    pre_even, pre_odd, live_even, live_odd = first_conv(pay_ref, w1_ref, b1_ref, cols_ref, frames_ref)
    value, slope = gelu_both(pre_odd)
    odd = jnp.where(live_odd, value, 0.0)
    slope_ref[1] = jnp.where(live_odd, slope, 0.0)
    turned_ref[0] = shift_down(odd).astype(BF16).T
    turned_ref[2] = odd.astype(BF16).T
    value, slope = gelu_both(pre_even)
    slope_ref[0] = jnp.where(live_even, slope, 0.0)
    turned_ref[1] = jnp.where(live_even, value, 0.0).astype(BF16).T


def middle_kernel(
    where_ref, part_ref, grad_ref, b2_ref, length_ref, owner_col_ref, owner_row_ref, rep_ref, same_ref, cross_ref
):
    pre = part_ref[0].astype(F32)
    for source in range(1, HOLDERS):
        pre = pre + part_ref[source].astype(F32)
    pre = pre + b2_ref[...]
    t = (lax.broadcasted_iota(jnp.int32, (STEPS, 1), 0) & (HALF - 1)).astype(F32)
    live = jnp.where(2.0 * t < length_ref[...], 1.0, 0.0)
    value, slope = gelu_both(pre)
    features = (value * live).astype(BF16)
    second_grad = (grad_ref[...].astype(F32) * slope * live).astype(BF16)
    for target in range(HOLDERS):
        rep_ref[target] = second_grad
    here = lax.broadcasted_iota(jnp.int32, (STEPS, STEPS), 0)
    there = lax.broadcasted_iota(jnp.int32, (STEPS, STEPS), 1)
    same = (owner_col_ref[...] == owner_row_ref[...]) & ((here >> 3) < (there >> 3))
    same = same & ((here & (HALF - 1)) == 0)
    rank = jnp.sum(jnp.where(same, 1.0, 0.0), axis=0, keepdims=True)
    place = lax.broadcasted_iota(jnp.int32, (1, STEPS), 1) & (HALF - 1)
    place = (owner_row_ref[...] * 2 + rank.astype(jnp.int32)) * HALF + place
    wanted = lax.broadcasted_iota(jnp.int32, (SLOTS * HALF, STEPS), 0) == place
    placed = dot(jnp.where(wanted, 1.0, 0.0).astype(BF16), features)
    first = where_ref[2] == 0
    for chip in range(CHIPS):
        for tile in range(D2 // LANES):
            rows, columns = slice(tile * 16, (tile + 1) * 16), slice(tile * LANES, (tile + 1) * LANES)
            left = placed[chip * 32 : chip * 32 + 16, columns]
            right = placed[chip * 32 + 16 : chip * 32 + 32, columns]
            same_ref[chip, rows, :] = jnp.where(first, left, right).astype(BF16)
            cross_ref[chip, rows, :] = jnp.where(first, right, left).astype(BF16)


def backward_kernel(
    where_ref, grad_ref, own_ref, side_ref, far_ref, both_ref, cols_ref, turned_ref, slope_ref, keep_ref, send_ref,
    w2_ref, conv_sum, cols_here, cols_done,
):
    cols_copy = pltpu.make_async_copy(cols_ref, cols_here, cols_done)
    cols_copy.start()
    stack_weights((own_ref, side_ref, far_ref, both_ref), w2_ref)
    mine = where_ref[0]
    grad = grad_ref[...].reshape(HOLDERS * STEPS, D2)
    places = []
    for block in range(BLOCKS):
        places.append((keep_ref if block % 2 == 0 else send_ref, mine if block < 2 else 1 - mine, block * ROWS))

    for tap in range(3):
        conv_sum[...] = dot(turned_ref[tap], grad)
        for out, target, first in places:
            for column in range(D2 // LANES):
                tile = tap * (D2 // LANES) + column
                piece = conv_sum[first : first + ROWS, column * LANES : (column + 1) * LANES]
                out[target, tile // 8, (tile % 8) * ROWS : (tile % 8 + 1) * ROWS, :] = piece.astype(out.dtype)

    even = dot_nt(grad, w2_ref[:, D2 : 2 * D2])
    even = (even * slope_ref[0]).astype(BF16)
    odd = dot_nt(grad, w2_ref[:, 2 * D2 :]) + shift_up(dot_nt(grad, w2_ref[:, :D2]))
    odd = (odd * slope_ref[1]).astype(BF16)
    cols_copy.wait()
    cols = cols_here[...]
    conv_sum[:, : 3 * LANES] = dot_tn(even, cols[:, : 3 * LANES]) + dot_tn(odd, cols[:, LANES:])
    bias1 = jnp.sum(even.astype(F32) + odd.astype(F32), axis=0, keepdims=True)
    bias2 = jnp.sum(grad.astype(F32), axis=0, keepdims=True)
    for out, target, first in places:
        out[target, 1, 7 * ROWS : 8 * ROWS, :] = jnp.zeros((ROWS, LANES), out.dtype)
        biases = [jnp.concatenate([bias1[:, first : first + ROWS], jnp.zeros((1, LANES - ROWS), F32)], axis=1)]
        for tile in range(D2 // LANES):
            biases.append(bias2[:, tile * LANES : (tile + 1) * LANES])
        biases.append(jnp.zeros((16 - len(biases), LANES), F32))
        biases = jnp.concatenate(biases, axis=0).astype(out.dtype)
        for half in range(2):
            for tile in range(3):
                piece = conv_sum[first : first + ROWS, tile * LANES : (tile + 1) * LANES]
                out[target, half, (8 + tile) * ROWS : (9 + tile) * ROWS, :] = piece.astype(out.dtype)
            out[target, half, 11 * ROWS :, :] = biases


def sum_kernel(got_ref, out_ref):
    total = got_ref[0].astype(F32)
    for source in range(1, got_ref.shape[0]):
        total = total + got_ref[source].astype(F32)
    total = total.astype(BF16)
    if len(out_ref.shape) == 2:
        out_ref[...] = total
    else:
        for target in range(out_ref.shape[0]):
            out_ref[target] = total


def pairs_kernel(own_ref, near_ref, both_ref, far_ref, out_ref):
    own, near, far, both = (ref[...].astype(F32) for ref in (own_ref, near_ref, far_ref, both_ref))
    total = ((own + near) + (far + both)).astype(BF16)
    for target in range(out_ref.shape[0]):
        out_ref[target] = total


def last_kernel(
    where_ref, got_ref, cross_ref, own_ref, other_ref, weight_ref, bias1_ref, bias2_ref, conv2_ref, packed_ref,
    whole, biases,
):
    step, core = pl.program_id(0), where_ref[2]
    rows = pl.ds(pl.multiple_of((step + 1) * ROWS, 16), ROWS)
    for chip in range(CHIPS):
        whole[pl.ds(pl.multiple_of((2 * chip + core) * ROWS, 16), ROWS), :] = got_ref[chip, rows, :]
        whole[pl.ds(pl.multiple_of((2 * chip + 1 - core) * ROWS, 16), ROWS), :] = cross_ref[chip, rows, :]
    for block in range(10):
        columns = slice(block * LANES, (block + 1) * LANES)
        weight_ref[:, columns] = whole[columns, :].T.astype(F32)

    @pl.when(step == 0)
    def _():
        for chip in range(CHIPS):
            biases[2 * chip + core] = got_ref[chip, 5 * ROWS :, :].astype(F32)
            biases[2 * chip + 1 - core] = cross_ref[chip, 5 * ROWS :, :].astype(F32)
            left = pl.ds(pl.multiple_of(chip * 32 + 16 * core, 16), 16)
            right = pl.ds(pl.multiple_of(chip * 32 + 16 - 16 * core, 16), 16)
            for tile in range(D2 // LANES):
                columns = slice(tile * LANES, (tile + 1) * LANES)
                packed_ref[left, columns] = got_ref[chip, tile * 16 : (tile + 1) * 16, :]
                packed_ref[right, columns] = cross_ref[chip, 4 * ROWS + tile * 16 : 4 * ROWS + (tile + 1) * 16, :]
        bias1 = jnp.concatenate([biases[source, 0:1, :ROWS] for source in range(16)], axis=1)
        bias1_ref[...] = bias1.reshape(16 * ROWS)
        bias2 = jnp.concatenate([biases[0, 1 + tile : 2 + tile, :] for tile in range(D2 // LANES)], axis=1)
        bias2_ref[...] = bias2.reshape(D2)
        lower = where_ref[1] == 0
        for tile in range(15):
            half, spot = tile // 8, tile % 8
            rows = slice(spot * ROWS, (spot + 1) * ROWS)
            own, other = own_ref[rows, :].astype(F32), other_ref[rows, :].astype(F32)
            picked = jnp.where(lower, own, other) if half == 0 else jnp.where(lower, other, own)
            conv2_ref[:, tile * LANES : (tile + 1) * LANES] = picked


def exchange(values, axes):
    return lax.all_to_all(values, axes, split_axis=0, concat_axis=0, tiled=True)


def spread_to(values, count):
    return jnp.broadcast_to(values[None], (count,) + values.shape)


def vmem():
    return pl.BlockSpec(memory_space=pltpu.VMEM)


def params(mib, *semantics):
    return pltpu.CompilerParams(vmem_limit_bytes=mib * MIB, dimension_semantics=semantics or None)


def local(mel, lengths, routes, conv1_weight, conv1_bias, conv2_weight, conv2_bias, out_grad):
    x_hi, y, core = lax.axis_index("xh"), lax.axis_index("y"), lax.axis_index("c")
    where = jnp.stack([x_hi, lax.axis_index("xl"), core, (x_hi * HOLDERS + y) * 2 + core]).astype(jnp.int32)

    def shape(*dims, dtype=BF16):
        return jax.ShapeDtypeStruct(dims, dtype)

    def from_hbm(values):
        return pltpu.with_memory_space_constraint(values, pltpu.HBM)

    def in_hbm(*dims, dtype=BF16):
        return pltpu.HBM(dims, dtype)

    pay = pl.pallas_call(
        prepare_kernel,
        in_specs=[pl.BlockSpec(memory_space=pltpu.SMEM), vmem()],
        out_specs=vmem(),
        out_shape=in_hbm(HOLDERS, PAY, 2 * HALF, MEL),
        compiler_params=params(60),
        name="mel_payload",
    )(lengths, mel)
    got_pay = exchange(pay, "y")
    cores = [(0, 1), (1, 0)]
    far_weight = lax.ppermute(conv2_weight, ("xh", "xl"), [(0, 3), (3, 0), (1, 2), (2, 1)])
    pay = pl.pallas_call(
        prepare_kernel,
        in_specs=[pl.BlockSpec(memory_space=pltpu.SMEM), vmem()],
        out_specs=vmem(),
        out_shape=in_hbm(HOLDERS, PAY, 2 * HALF, MEL),
        compiler_params=params(60),
        name="mel_payload",
    )(lengths, mel)
    got_pay = exchange(pay, "y")
    weights = [
        conv2_weight,
        lax.ppermute(conv2_weight, "c", [(0, 1), (1, 0)]),
        lax.ppermute(conv2_weight, ("xh", "xl"), [(0, 3), (3, 0), (1, 2), (2, 1)]),
        lax.ppermute(conv2_weight, ("xh", "c", "xl"), [(i, 7 - i) for i in range(8)]),
    ]

    w1, b1 = pl.pallas_call(
        columns_kernel,
        in_specs=[pl.BlockSpec(memory_space=pltpu.SMEM), vmem(), vmem()],
        out_specs=[vmem()] * 2,
        out_shape=[shape(3 * MEL, WIDE), shape(1, WIDE, dtype=F32)],
        scratch_shapes=[pltpu.VMEM((3 * MEL, WIDE), F32)],
        compiler_params=params(10),
        name="conv1_columns",
    )(where, conv1_weight, from_hbm(conv1_bias))
    own_weight, place = lax.optimization_barrier((conv2_weight, where))
    far_weight, place = lax.optimization_barrier((far_weight, place))
    weights = [
        conv2_weight,
        lax.ppermute(own_weight, "c", cores),
        far_weight,
        lax.ppermute(far_weight, "c", cores),
    ]

    pair = lambda i: (i, 0, 0)
    pair4 = lambda i: (i, 0, 0, 0)
    rows, some = HOLDERS * STEPS, 2 * STEPS
    frames = (2, 2 * STEPS, MEL)
    pay_spec = pl.BlockSpec((2, PAY, 2 * HALF, MEL), pair4)
    parts = pl.pallas_call(
        forward_kernel,
        grid=(HOLDERS // 2,),
        in_specs=[pay_spec, *[vmem()] * (2 + BLOCKS)],
        out_specs=pl.BlockSpec((2, STEPS, D2), pair),
        out_shape=in_hbm(HOLDERS, STEPS, D2),
        scratch_shapes=[
            pltpu.VMEM((WIDE, 3 * D2), BF16),
            pltpu.VMEM((some, 4 * LANES), BF16),
            pltpu.VMEM(frames, F32),
        ],
        compiler_params=params(20, "arbitrary"),
        name="stem_forward",
    )(got_pay, w1, b1, *weights)

    got_parts = exchange(parts, "y")
    cols, slopes, turned = pl.pallas_call(
        slope_kernel,
        grid=(HOLDERS // 2,),
        in_specs=[pay_spec, vmem(), vmem()],
        out_specs=[
            pl.BlockSpec((some, 4 * LANES), lambda i: (i, 0)),
            pl.BlockSpec((2, some, WIDE), lambda i: (0, i, 0)),
            pl.BlockSpec((3, WIDE, some), lambda i: (0, 0, i)),
        ],
        out_shape=[in_hbm(rows, 4 * LANES), shape(2, rows, WIDE, dtype=F32), shape(3, WIDE, rows)],
        scratch_shapes=[pltpu.VMEM(frames, F32)],
        compiler_params=params(20, "arbitrary"),
        name="stem_slopes",
    )(got_pay, w1, b1)
    got_parts, slopes, turned = lax.optimization_barrier((got_parts, slopes, turned))
    owner = jnp.repeat(routes[:, 0], HALF)
    rep, same, cross = pl.pallas_call(
        middle_kernel,
        in_specs=[pl.BlockSpec(memory_space=pltpu.SMEM)] + [vmem()] * 6,
        out_specs=[vmem()] * 3,
        out_shape=[in_hbm(HOLDERS, STEPS, D2), shape(CHIPS, ROWS, LANES), shape(CHIPS, ROWS, LANES)],
        compiler_params=params(10),
        name="stem_middle",
    )(
        where,
        got_parts,
        from_hbm(out_grad.reshape(STEPS, D2)),
        conv2_bias[None],
        from_hbm(jnp.repeat(lengths.astype(F32), HALF)[:, None]),
        owner[:, None],
        owner[None],
    )
    got_grad = exchange(rep, "y")

    keep, send = pl.pallas_call(
        backward_kernel,
        in_specs=[
            pl.BlockSpec(memory_space=pltpu.SMEM),
            *[vmem()] * (1 + BLOCKS),
            pl.BlockSpec(memory_space=pl.ANY),
            vmem(),
            vmem(),
        ],
        out_specs=[vmem()] * 2,
        out_shape=[shape(2, 2, PACK, LANES, dtype=F32), shape(2, 2, PACK, LANES)],
        scratch_shapes=[
            pltpu.VMEM((WIDE, 3 * D2), BF16),
            pltpu.VMEM((WIDE, D2), F32),
            pltpu.VMEM((rows, 4 * LANES), BF16),
            pltpu.SemaphoreType.DMA,
        ],
        compiler_params=params(32),
        name="stem_backward",
    )(where, got_grad, *weights, from_hbm(cols), turned, slopes)
    got = lax.ppermute(send, "c", cores)
    quarters = exchange((keep + got.astype(F32)).astype(BF16).reshape(4, PACK, LANES), ("xh", "xl"))

    def summed(values, *dims):
        return pl.pallas_call(
            sum_kernel,
            in_specs=[vmem()],
            out_specs=vmem(),
            out_shape=shape(*dims),
            compiler_params=params(8),
            name="gradient_sum",
        )(values)

    half = summed(quarters, PACK, LANES)
    quarter = PACK // 4
    near = summed(exchange(half.reshape(4, quarter, LANES), "zl"), quarter, LANES)
    far = {flip: lax.ppermute(near, "zh", [(i, i ^ flip) for i in range(4)]) for flip in (2, 3, 1)}
    far = pl.pallas_call(
        pairs_kernel,
        in_specs=[vmem()] * 4,
        out_specs=vmem(),
        out_shape=shape(4, quarter, LANES),
        compiler_params=params(8),
        name="gradient_pairs",
    )(near, far[1], far[3], far[2])
    half = exchange(far, "zl").reshape(PACK, LANES)
    own = half[:HALF_ROWS]
    other = lax.ppermute(own, "xl", [(0, 1), (1, 0)])
    conv1 = spread_to(half[HALF_ROWS:], CHIPS)
    got = exchange(jnp.concatenate([same, conv1[:, : 3 * ROWS], cross, conv1[:, 3 * ROWS :]], axis=1), ("xh", "y"))
    got, other = lax.optimization_barrier((got, other))
    got_cross = lax.ppermute(got, "c", cores)
    weight_grad, bias_grad, second_bias_grad, conv2_rows_grad, packed = pl.pallas_call(
        last_kernel,
        grid=(3,),
        in_specs=[
            pl.BlockSpec(memory_space=pltpu.SMEM),
            *[vmem()] * 4,
        ],
        out_specs=[
            pl.BlockSpec((LANES, 16 * ROWS), lambda i: (i, 0)),
            pl.BlockSpec((16 * ROWS,), lambda i: (0,)),
            pl.BlockSpec((D2,), lambda i: (0,)),
            pl.BlockSpec((ROWS, 3 * D2), lambda i: (0, 0)),
            pl.BlockSpec((SLOTS * HALF, D2), lambda i: (0, 0)),
        ],
        out_shape=[
            shape(3 * MEL, 16 * ROWS, dtype=F32),
            shape(16 * ROWS, dtype=F32),
            shape(D2, dtype=F32),
            shape(ROWS, 3 * D2, dtype=F32),
            shape(SLOTS * HALF, D2),
        ],
        scratch_shapes=[pltpu.VMEM((16 * ROWS, LANES), BF16), pltpu.VMEM((16, 16, LANES), F32)],
        compiler_params=params(16, "arbitrary"),
        name="gradient_unpack",
    )(where, got, got_cross, own, other)
    return packed.reshape(SLOTS, HALF, D2), weight_grad, bias_grad, second_bias_grad, conv2_rows_grad


def solution(mesh):
    fine = Mesh(mesh.devices.reshape(2, 4, 2, 4, 4, 2), ALL_AXES)
    placed = (
        P(ALL_AXES, None, None),
        P(ALL_AXES),
        P(ALL_AXES, None),
        P(),
        P(),
        P(ENC, None),
        P(),
        P(ALL_AXES, None, None),
    )
    return jax.shard_map(
        local,
        mesh=fine,
        in_specs=placed,
        out_specs=(P(ALL_AXES, None, None), P(), P(), P(), P(ENC, None)),
        check_vma=False,
    )
```

```python
import functools

import jax
import jax.numpy as jnp
from jax import lax
from jax.experimental import pallas as pl
from jax.experimental.pallas import tpu as pltpu
from jax.sharding import Mesh
from jax.sharding import PartitionSpec as P

inv_root_two = 0.7071067811865476
inv_root_tau = 0.3989422804014327

MEL = 128
D2 = 640
ROWS = 80
LANES = 128
HOLDERS = 4
BLOCKS = 4
WIDE = 384
CLIPS = 16
HALF = 8
STEPS = CLIPS * HALF
SLOTS = 2 * CLIPS
PAY = 26
CHIPS = 8
PACK = 896
HALF_ROWS = 8 * ROWS
MIB = 1024 * 1024
ALL_AXES = ("xh", "y", "c", "zh", "zl", "xl")
ENC = ("xh", "y", "c")
F32 = jnp.float32
BF16 = jnp.bfloat16


def gelu_value(values):
    return values * (0.5 * (1.0 + lax.erf(values * inv_root_two)))


def gelu_both(values):
    cdf = 0.5 * (1.0 + lax.erf(values * inv_root_two))
    return values * cdf, cdf + values * jnp.exp(-0.5 * values * values) * inv_root_tau


def shift_down(values):
    rows, width = values.shape
    t = lax.broadcasted_iota(jnp.int32, (rows, width), 0) & (HALF - 1)
    clips = values.reshape(rows // HALF, HALF, width)
    moved = pltpu.roll(clips, 1, 1).reshape(rows, width)
    return jnp.where(t == 0, 0.0, moved)


def shift_up(values):
    rows, width = values.shape
    t = lax.broadcasted_iota(jnp.int32, (rows, width), 0) & (HALF - 1)
    clips = values.reshape(rows // HALF, HALF, width)
    moved = pltpu.roll(clips, HALF - 1, 1).reshape(rows, width)
    return jnp.where(t == HALF - 1, 0.0, moved)


def dot(left, right):
    return jnp.dot(left, right, preferred_element_type=F32)


def dot_nt(left, right):
    return lax.dot_general(left, right, (((1,), (1,)), ((), ())), preferred_element_type=F32)


def dot_tn(left, right):
    return lax.dot_general(left, right, (((0,), (0,)), ((), ())), preferred_element_type=F32)


def weight_copies(refs, w2_ref, done):
    return [
        pltpu.make_async_copy(ref, w2_ref.at[block * ROWS : (block + 1) * ROWS], done.at[block])
        for block, ref in enumerate(refs)
    ]


def prepare_kernel(length_ref, mel_ref, pay_ref, length_here, mel_done, length_done):
    mel_copies = [
        pltpu.make_async_copy(mel_ref, pay_ref.at[target, :CLIPS], mel_done.at[target]) for target in range(HOLDERS)
    ]
    for copy in mel_copies:
        copy.start()
    clip = lax.broadcasted_iota(jnp.int32, (CLIPS, MEL), 0)
    length = jnp.zeros((CLIPS, MEL), F32)
    for index in range(CLIPS):
        length = jnp.where(clip == index, length_ref[index].astype(F32), length)
    slots = length_here.shape[0]
    for slot in range(slots):
        length_here[slot] = length.astype(BF16)
    length_copies = [
        pltpu.make_async_copy(length_here, pay_ref.at[target, CLIPS:], length_done.at[target])
        for target in range(HOLDERS)
    ]
    for copy in length_copies:
        copy.start()
    for copy in mel_copies + length_copies:
        copy.wait()


def columns_kernel(where_ref, weight_ref, bias_ref, w1_ref, b1_ref, picked):
    picked[...] = jnp.zeros_like(picked)
    b1_ref[...] = jnp.zeros_like(b1_ref)
    for block, flip in enumerate((0, 1, 2 * HOLDERS, 2 * HOLDERS + 1)):
        first = (where_ref[3] ^ flip) * ROWS
        start = pl.multiple_of(jnp.minimum((first >> 7) << 7, 16 * ROWS - 2 * LANES), LANES)
        shift = (2 * LANES - (first - start)) & (2 * LANES - 1)
        lanes = slice(block * ROWS, (block + 1) * ROWS)
        window = weight_ref[:, pl.ds(start, 2 * LANES)].astype(F32)
        picked[:, lanes] = pltpu.roll(window, shift, 1)[:, :ROWS]
        window = jnp.broadcast_to(bias_ref[pl.ds(start, 2 * LANES)].reshape(1, 2 * LANES), (8, 2 * LANES))
        b1_ref[:, lanes] = pltpu.roll(window, shift, 1)[0:1, :ROWS]
    w1_ref[...] = picked[...].astype(BF16)


def first_conv(pay_ref, w1_ref, b1_ref, cols_ref, frames_ref):
    sources = pay_ref.shape[0]
    spread = (
        lax.broadcasted_iota(jnp.int32, (STEPS, CLIPS), 0) >> 3
        == lax.broadcasted_iota(jnp.int32, (STEPS, CLIPS), 1)
    ).astype(F32).astype(BF16)
    t = (lax.broadcasted_iota(jnp.int32, (STEPS, LANES), 0) & (HALF - 1)).astype(F32)
    lives_even, lives_odd = [], []
    for source in range(sources):
        rows = slice(source * STEPS, (source + 1) * STEPS)
        length = dot(spread, pay_ref[source, CLIPS])
        frames_ref[source] = pay_ref[source, :CLIPS].astype(F32).reshape(2 * STEPS, MEL)
        live_even, live_odd = 2.0 * t < length, 2.0 * t + 1.0 < length
        even = jnp.where(live_even, frames_ref[source, pl.ds(0, STEPS, 2), :], 0.0)
        odd = jnp.where(live_odd, frames_ref[source, pl.ds(1, STEPS, 2), :], 0.0)
        cols_ref[rows, :LANES] = shift_down(odd).astype(BF16)
        cols_ref[rows, LANES : 2 * LANES] = even.astype(BF16)
        cols_ref[rows, 2 * LANES : 3 * LANES] = odd.astype(BF16)
        cols_ref[rows, 3 * LANES :] = shift_up(even).astype(BF16)
        lives_even.append(jnp.concatenate([live_even] * (WIDE // LANES), axis=1))
        lives_odd.append(jnp.concatenate([live_odd] * (WIDE // LANES), axis=1))
    cols = jnp.concatenate([cols_ref[:, : 3 * LANES], cols_ref[:, LANES:]], axis=0)
    pre = dot(cols, w1_ref[...]) + b1_ref[...]
    half = sources * STEPS
    return pre[:half], pre[half:], jnp.concatenate(lives_even, axis=0), jnp.concatenate(lives_odd, axis=0)


def forward_kernel(
    pay_ref, w1_ref, b1_ref, own_ref, side_ref, far_ref, both_ref, part_ref, w2_ref, cols_ref, frames_ref, done
):
    copies = weight_copies((own_ref, side_ref, far_ref, both_ref), w2_ref, done)

    @pl.when(pl.program_id(0) == 0)
    def _():
        for copy in copies:
            copy.start()
        w2_ref[BLOCKS * ROWS :, :] = jnp.zeros((WIDE - BLOCKS * ROWS, 3 * D2), BF16)

    pre_even, pre_odd, live_even, live_odd = first_conv(pay_ref, w1_ref, b1_ref, cols_ref, frames_ref)

    @pl.when(pl.program_id(0) == 0)
    def _():
        for copy in copies:
            copy.wait()

    odd = jnp.where(live_odd, gelu_value(pre_odd), 0.0)
    total = dot(odd.astype(BF16), w2_ref[:, 2 * D2 :]) + dot(shift_down(odd).astype(BF16), w2_ref[:, :D2])
    even = jnp.where(live_even, gelu_value(pre_even), 0.0)
    total = total + dot(even.astype(BF16), w2_ref[:, D2 : 2 * D2])
    part_ref[...] = total.astype(BF16).reshape(part_ref.shape)


def slope_kernel(
    pay_ref, w1_ref, b1_ref, grad_ref, column_ref, row_ref,
    cols_ref, slope_ref, turned_ref, live_grad_ref, wanted_ref, frames_ref,
):
    pre_even, pre_odd, live_even, live_odd = first_conv(pay_ref, w1_ref, b1_ref, cols_ref, frames_ref)
    value, slope = gelu_both(pre_odd)
    odd = jnp.where(live_odd, value, 0.0)
    slope_ref[1] = jnp.where(live_odd, slope, 0.0)
    turned_ref[0] = shift_down(odd).astype(BF16).T
    turned_ref[2] = odd.astype(BF16).T
    value, slope = gelu_both(pre_even)
    slope_ref[0] = jnp.where(live_even, slope, 0.0)
    turned_ref[1] = jnp.where(live_even, value, 0.0).astype(BF16).T

    @pl.when(pl.program_id(0) == 0)
    def _():
        t = (lax.broadcasted_iota(jnp.int32, (STEPS, 1), 0) & (HALF - 1)).astype(F32)
        length = (column_ref[...] & 31).astype(F32)
        live_grad_ref[...] = jnp.where(2.0 * t < length, grad_ref[...].astype(F32), 0.0).astype(BF16)
        here = lax.broadcasted_iota(jnp.int32, (STEPS, STEPS), 0)
        there = lax.broadcasted_iota(jnp.int32, (STEPS, STEPS), 1)
        owner = row_ref[...] >> 5
        same = ((column_ref[...] >> 5) == owner) & ((here >> 3) < (there >> 3))
        same = same & ((here & (HALF - 1)) == 0)
        rank = jnp.sum(jnp.where(same, 1.0, 0.0), axis=0, keepdims=True)
        place = lax.broadcasted_iota(jnp.int32, (1, STEPS), 1) & (HALF - 1)
        place = (owner * 2 + rank.astype(jnp.int32)) * HALF + place
        wanted = lax.broadcasted_iota(jnp.int32, (SLOTS * HALF, STEPS), 0) == place
        t = (lax.broadcasted_iota(jnp.int32, (1, STEPS), 1) & (HALF - 1)).astype(F32)
        wanted = wanted & (2.0 * t < (row_ref[...] & 31).astype(F32))
        wanted_ref[...] = jnp.where(wanted, 1.0, 0.0).astype(BF16)


def middle_kernel(
    where_ref, part_ref, b2_ref, live_grad_ref, wanted_ref, rep_ref, same_ref, cross_ref, live_grad_here, done
):
    copy = pltpu.make_async_copy(live_grad_ref, live_grad_here, done)
    copy.start()
    pre = part_ref[0].astype(F32)
    for source in range(1, HOLDERS):
        pre = pre + part_ref[source].astype(F32)
    value, slope = gelu_both(pre + b2_ref[...])
    copy.wait()
    second_grad = (live_grad_here[...].astype(F32) * slope).astype(BF16)
    for target in range(HOLDERS):
        rep_ref[target] = second_grad
    placed = dot(wanted_ref[...], value.astype(BF16))
    first = where_ref[2] == 0
    for chip in range(CHIPS):
        for tile in range(D2 // LANES):
            rows, columns = slice(tile * 16, (tile + 1) * 16), slice(tile * LANES, (tile + 1) * LANES)
            left = placed[chip * 32 : chip * 32 + 16, columns]
            right = placed[chip * 32 + 16 : chip * 32 + 32, columns]
            same_ref[chip, rows, :] = jnp.where(first, left, right).astype(BF16)
            cross_ref[chip, rows, :] = jnp.where(first, right, left).astype(BF16)


def backward_kernel(
    where_ref, grad_ref, own_ref, side_ref, far_ref, both_ref, cols_ref, turned_ref, slope_ref, keep_ref, send_ref,
    w2_ref, conv_sum, cols_here, weights_done, cols_done,
):
    copies = weight_copies((own_ref, side_ref, far_ref, both_ref), w2_ref, weights_done)
    copies.append(pltpu.make_async_copy(cols_ref, cols_here, cols_done))
    for copy in copies:
        copy.start()
    w2_ref[BLOCKS * ROWS :, :] = jnp.zeros((WIDE - BLOCKS * ROWS, 3 * D2), BF16)
    mine = where_ref[0]
    grad = grad_ref[...].reshape(HOLDERS * STEPS, D2)
    places = []
    for block in range(BLOCKS):
        places.append((keep_ref if block % 2 == 0 else send_ref, mine if block < 2 else 1 - mine, block * ROWS))

    for tap in range(3):
        conv_sum[...] = dot(turned_ref[tap], grad)
        for out, target, first in places:
            for column in range(D2 // LANES):
                tile = tap * (D2 // LANES) + column
                piece = conv_sum[first : first + ROWS, column * LANES : (column + 1) * LANES]
                out[target, tile // 8, (tile % 8) * ROWS : (tile % 8 + 1) * ROWS, :] = piece.astype(out.dtype)

    for copy in copies:
        copy.wait()
    even = dot_nt(grad, w2_ref[:, D2 : 2 * D2])
    even = (even * slope_ref[0]).astype(BF16)
    odd = dot_nt(grad, w2_ref[:, 2 * D2 :]) + shift_up(dot_nt(grad, w2_ref[:, :D2]))
    odd = (odd * slope_ref[1]).astype(BF16)
    cols = cols_here[...]
    conv_sum[:, : 3 * LANES] = dot_tn(even, cols[:, : 3 * LANES]) + dot_tn(odd, cols[:, LANES:])
    bias1 = jnp.sum(even.astype(F32) + odd.astype(F32), axis=0, keepdims=True)
    bias2 = jnp.sum(grad.astype(F32), axis=0, keepdims=True)
    for out, target, first in places:
        out[target, 1, 7 * ROWS : 8 * ROWS, :] = jnp.zeros((ROWS, LANES), out.dtype)
        biases = [jnp.concatenate([bias1[:, first : first + ROWS], jnp.zeros((1, LANES - ROWS), F32)], axis=1)]
        for tile in range(D2 // LANES):
            biases.append(bias2[:, tile * LANES : (tile + 1) * LANES])
        biases.append(jnp.zeros((16 - len(biases), LANES), F32))
        biases = jnp.concatenate(biases, axis=0).astype(out.dtype)
        for half in range(2):
            for tile in range(3):
                piece = conv_sum[first : first + ROWS, tile * LANES : (tile + 1) * LANES]
                out[target, half, (8 + tile) * ROWS : (9 + tile) * ROWS, :] = piece.astype(out.dtype)
            out[target, half, 11 * ROWS :, :] = biases


def sum_kernel(got_ref, out_ref):
    total = got_ref[0].astype(F32)
    for source in range(1, got_ref.shape[0]):
        total = total + got_ref[source].astype(F32)
    total = total.astype(BF16)
    if len(out_ref.shape) == 2:
        out_ref[...] = total
    else:
        for target in range(out_ref.shape[0]):
            out_ref[target] = total


def pairs_kernel(own_ref, near_ref, both_ref, far_ref, out_ref):
    own, near, far, both = (ref[...].astype(F32) for ref in (own_ref, near_ref, far_ref, both_ref))
    total = ((own + near) + (far + both)).astype(BF16)
    for target in range(out_ref.shape[0]):
        out_ref[target] = total


def last_kernel(
    where_ref, got_ref, cross_ref, weight_ref, bias1_ref, bias2_ref, packed_ref, whole, biases,
):
    step, core = pl.program_id(0), where_ref[2]
    rows = pl.ds(pl.multiple_of((step + 1) * ROWS, 16), ROWS)
    for chip in range(CHIPS):
        whole[pl.ds(pl.multiple_of((2 * chip + core) * ROWS, 16), ROWS), :] = got_ref[chip, rows, :]
        whole[pl.ds(pl.multiple_of((2 * chip + 1 - core) * ROWS, 16), ROWS), :] = cross_ref[chip, rows, :]
    for block in range(10):
        columns = slice(block * LANES, (block + 1) * LANES)
        weight_ref[:, columns] = whole[columns, :].T.astype(F32)

    @pl.when(step == 0)
    def _():
        for chip in range(CHIPS):
            biases[2 * chip + core] = got_ref[chip, 5 * ROWS :, :].astype(F32)
            biases[2 * chip + 1 - core] = cross_ref[chip, 5 * ROWS :, :].astype(F32)
            left = pl.ds(pl.multiple_of(chip * 32 + 16 * core, 16), 16)
            right = pl.ds(pl.multiple_of(chip * 32 + 16 - 16 * core, 16), 16)
            for tile in range(D2 // LANES):
                columns = slice(tile * LANES, (tile + 1) * LANES)
                packed_ref[left, columns] = got_ref[chip, tile * 16 : (tile + 1) * 16, :]
                packed_ref[right, columns] = cross_ref[chip, 4 * ROWS + tile * 16 : 4 * ROWS + (tile + 1) * 16, :]
        bias1 = jnp.concatenate([biases[source, 0:1, :ROWS] for source in range(16)], axis=1)
        bias1_ref[...] = bias1.reshape(16 * ROWS)
        bias2 = jnp.concatenate([biases[0, 1 + tile : 2 + tile, :] for tile in range(D2 // LANES)], axis=1)
        bias2_ref[...] = bias2.reshape(D2)


def unpack_kernel(where_ref, own_ref, other_ref, conv2_ref):
    lower = where_ref[1] == 0
    for tile in range(15):
        half, spot = tile // 8, tile % 8
        rows = slice(spot * ROWS, (spot + 1) * ROWS)
        own, other = own_ref[rows, :].astype(F32), other_ref[rows, :].astype(F32)
        picked = jnp.where(lower, own, other) if half == 0 else jnp.where(lower, other, own)
        conv2_ref[:, tile * LANES : (tile + 1) * LANES] = picked


def exchange(values, axes):
    return lax.all_to_all(values, axes, split_axis=0, concat_axis=0, tiled=True)


def spread_to(values, count):
    return jnp.broadcast_to(values[None], (count,) + values.shape)


def vmem():
    return pl.BlockSpec(memory_space=pltpu.VMEM)


def params(mib, *semantics):
    return pltpu.CompilerParams(vmem_limit_bytes=mib * MIB, dimension_semantics=semantics or None)


def local(mel, lengths, routes, conv1_weight, conv1_bias, conv2_weight, conv2_bias, out_grad):
    x_hi, y, core = lax.axis_index("xh"), lax.axis_index("y"), lax.axis_index("c")
    where = jnp.stack([x_hi, lax.axis_index("xl"), core, (x_hi * HOLDERS + y) * 2 + core]).astype(jnp.int32)

    def shape(*dims, dtype=BF16):
        return jax.ShapeDtypeStruct(dims, dtype)

    def from_hbm(values):
        return pltpu.with_memory_space_constraint(values, pltpu.HBM)

    def in_hbm(*dims, dtype=BF16):
        return pltpu.HBM(dims, dtype)

    pay = pl.pallas_call(
        prepare_kernel,
        in_specs=[pl.BlockSpec(memory_space=pltpu.SMEM), pl.BlockSpec(memory_space=pl.ANY)],
        out_specs=pl.BlockSpec(memory_space=pl.ANY),
        out_shape=in_hbm(HOLDERS, PAY, 2 * HALF, MEL),
        scratch_shapes=[
            pltpu.VMEM((PAY - CLIPS, 2 * HALF, MEL), BF16),
            pltpu.SemaphoreType.DMA((HOLDERS,)),
            pltpu.SemaphoreType.DMA((HOLDERS,)),
        ],
        compiler_params=params(60),
        name="mel_payload",
    )(lengths, from_hbm(mel))
    got_pay = exchange(pay, "y")
    cores = [(0, 1), (1, 0)]
    far_weight = lax.ppermute(conv2_weight, ("xh", "xl"), [(0, 3), (3, 0), (1, 2), (2, 1)])

    w1, b1 = pl.pallas_call(
        columns_kernel,
        in_specs=[pl.BlockSpec(memory_space=pltpu.SMEM), vmem(), vmem()],
        out_specs=[vmem()] * 2,
        out_shape=[shape(3 * MEL, WIDE), shape(1, WIDE, dtype=F32)],
        scratch_shapes=[pltpu.VMEM((3 * MEL, WIDE), F32)],
        compiler_params=params(10),
        name="conv1_columns",
    )(where, conv1_weight, from_hbm(conv1_bias))
    own_weight, place = lax.optimization_barrier((conv2_weight, where))
    far_weight, place = lax.optimization_barrier((far_weight, place))
    weights = [
        conv2_weight,
        lax.ppermute(own_weight, "c", cores),
        far_weight,
        lax.ppermute(far_weight, "c", cores),
    ]

    pair = lambda i: (i, 0, 0)
    pair4 = lambda i: (i, 0, 0, 0)
    rows, some = HOLDERS * STEPS, 2 * STEPS
    frames = (2, 2 * STEPS, MEL)
    pay_spec = pl.BlockSpec((2, PAY, 2 * HALF, MEL), pair4)
    parts = pl.pallas_call(
        forward_kernel,
        grid=(HOLDERS // 2,),
        in_specs=[pay_spec, vmem(), vmem(), *[pl.BlockSpec(memory_space=pl.ANY)] * BLOCKS],
        out_specs=pl.BlockSpec((2, STEPS, D2), pair),
        out_shape=in_hbm(HOLDERS, STEPS, D2),
        scratch_shapes=[
            pltpu.VMEM((WIDE, 3 * D2), BF16),
            pltpu.VMEM((some, 4 * LANES), BF16),
            pltpu.VMEM(frames, F32),
            pltpu.SemaphoreType.DMA((BLOCKS,)),
        ],
        compiler_params=params(20, "arbitrary"),
        name="stem_forward",
    )(got_pay, w1, b1, *weights)

    got_parts = exchange(parts, "y")
    code = jnp.repeat(routes[:, 0] * 32 + lengths, HALF)
    cols, slopes, turned, live_grad, wanted = pl.pallas_call(
        slope_kernel,
        grid=(HOLDERS // 2,),
        in_specs=[pay_spec, *[vmem()] * 5],
        out_specs=[
            pl.BlockSpec((some, 4 * LANES), lambda i: (i, 0)),
            pl.BlockSpec((2, some, WIDE), lambda i: (0, i, 0)),
            pl.BlockSpec((3, WIDE, some), lambda i: (0, 0, i)),
            vmem(),
            vmem(),
        ],
        out_shape=[
            in_hbm(rows, 4 * LANES),
            shape(2, rows, WIDE, dtype=F32),
            shape(3, WIDE, rows),
            in_hbm(STEPS, D2),
            shape(SLOTS * HALF, STEPS),
        ],
        scratch_shapes=[pltpu.VMEM(frames, F32)],
        compiler_params=params(20, "arbitrary"),
        name="stem_slopes",
    )(got_pay, w1, b1, from_hbm(out_grad.reshape(STEPS, D2)), code[:, None], code[None])
    got_parts, slopes, turned = lax.optimization_barrier((got_parts, slopes, turned))
    rep, same, cross = pl.pallas_call(
        middle_kernel,
        in_specs=[pl.BlockSpec(memory_space=pltpu.SMEM), vmem(), vmem(), pl.BlockSpec(memory_space=pl.ANY), vmem()],
        out_specs=[vmem()] * 3,
        out_shape=[shape(HOLDERS, STEPS, D2), shape(CHIPS, ROWS, LANES), shape(CHIPS, ROWS, LANES)],
        scratch_shapes=[pltpu.VMEM((STEPS, D2), BF16), pltpu.SemaphoreType.DMA],
        compiler_params=params(10),
        name="stem_middle",
    )(where, got_parts, conv2_bias[None], from_hbm(live_grad), wanted)
    got_grad = exchange(rep, "y")

    keep, send = pl.pallas_call(
        backward_kernel,
        in_specs=[
            pl.BlockSpec(memory_space=pltpu.SMEM),
            vmem(),
            *[pl.BlockSpec(memory_space=pl.ANY)] * (BLOCKS + 1),
            vmem(),
            vmem(),
        ],
        out_specs=[vmem()] * 2,
        out_shape=[shape(2, 2, PACK, LANES, dtype=F32), shape(2, 2, PACK, LANES)],
        scratch_shapes=[
            pltpu.VMEM((WIDE, 3 * D2), BF16),
            pltpu.VMEM((WIDE, D2), F32),
            pltpu.VMEM((rows, 4 * LANES), BF16),
            pltpu.SemaphoreType.DMA((BLOCKS,)),
            pltpu.SemaphoreType.DMA,
        ],
        compiler_params=params(32),
        name="stem_backward",
    )(where, got_grad, *[from_hbm(weight) for weight in weights], from_hbm(cols), turned, slopes)
    got = lax.ppermute(send, "c", cores)
    quarters = exchange((keep + got.astype(F32)).astype(BF16).reshape(4, PACK, LANES), ("xh", "xl"))

    def summed(values, *dims):
        return pl.pallas_call(
            sum_kernel,
            in_specs=[vmem()],
            out_specs=vmem(),
            out_shape=shape(*dims),
            compiler_params=params(8),
            name="gradient_sum",
        )(values)

    half = summed(quarters, PACK, LANES)
    quarter = PACK // 4
    near = summed(exchange(half.reshape(4, quarter, LANES), "zl"), quarter, LANES)
    far = {flip: lax.ppermute(near, "zh", [(i, i ^ flip) for i in range(4)]) for flip in (2, 3, 1)}
    far = pl.pallas_call(
        pairs_kernel,
        in_specs=[vmem()] * 4,
        out_specs=vmem(),
        out_shape=shape(4, quarter, LANES),
        compiler_params=params(8),
        name="gradient_pairs",
    )(near, far[1], far[3], far[2])
    half = exchange(far, "zl").reshape(PACK, LANES)
    own = half[:HALF_ROWS]
    other = lax.ppermute(own, "xl", [(0, 1), (1, 0)])
    conv1 = spread_to(half[HALF_ROWS:], CHIPS)
    got = exchange(jnp.concatenate([same, conv1[:, : 3 * ROWS], cross, conv1[:, 3 * ROWS :]], axis=1), ("xh", "y"))
    got, other = lax.optimization_barrier((got, other))
    got_cross = lax.ppermute(got, "c", cores)
    conv2_rows_grad = pl.pallas_call(
        unpack_kernel,
        in_specs=[pl.BlockSpec(memory_space=pltpu.SMEM), vmem(), vmem()],
        out_specs=vmem(),
        out_shape=in_hbm(ROWS, 3 * D2, dtype=F32),
        compiler_params=params(8),
        name="conv2_unpack",
    )(where, own, other)
    weight_grad, bias_grad, second_bias_grad, packed = pl.pallas_call(
        last_kernel,
        grid=(3,),
        in_specs=[
            pl.BlockSpec(memory_space=pltpu.SMEM),
            vmem(),
            vmem(),
        ],
        out_specs=[
            pl.BlockSpec((LANES, 16 * ROWS), lambda i: (i, 0)),
            pl.BlockSpec((16 * ROWS,), lambda i: (0,)),
            pl.BlockSpec((D2,), lambda i: (0,)),
            pl.BlockSpec((SLOTS * HALF, D2), lambda i: (0, 0)),
        ],
        out_shape=[
            shape(3 * MEL, 16 * ROWS, dtype=F32),
            shape(16 * ROWS, dtype=F32),
            shape(D2, dtype=F32),
            shape(SLOTS * HALF, D2),
        ],
        scratch_shapes=[pltpu.VMEM((16 * ROWS, LANES), BF16), pltpu.VMEM((16, 16, LANES), F32)],
        compiler_params=params(16, "arbitrary"),
        name="gradient_unpack",
    )(where, got, got_cross)
    return packed.reshape(SLOTS, HALF, D2), weight_grad, bias_grad, second_bias_grad, conv2_rows_grad


def solution(mesh):
    fine = Mesh(mesh.devices.reshape(2, 4, 2, 4, 4, 2), ALL_AXES)
    placed = (
        P(ALL_AXES, None, None),
        P(ALL_AXES),
        P(ALL_AXES, None),
        P(),
        P(),
        P(ENC, None),
        P(),
        P(ALL_AXES, None, None),
    )
    return jax.shard_map(
        local,
        mesh=fine,
        in_specs=placed,
        out_specs=(P(ALL_AXES, None, None), P(), P(), P(), P(ENC, None)),
        check_vma=False,
    )
```

```python
import functools

import jax
import jax.numpy as jnp
from jax import lax
from jax.experimental import pallas as pl
from jax.experimental.pallas import tpu as pltpu
from jax.sharding import Mesh
from jax.sharding import PartitionSpec as P

inv_root_two = 0.7071067811865476
inv_root_tau = 0.3989422804014327

MEL = 128
D2 = 640
ROWS = 80
LANES = 128
HOLDERS = 4
BLOCKS = 4
WIDE = 384
CLIPS = 16
HALF = 8
STEPS = CLIPS * HALF
SLOTS = 2 * CLIPS
PAY = 26
CHIPS = 8
PACK = 896
HALF_ROWS = 8 * ROWS
MIB = 1024 * 1024
ALL_AXES = ("xh", "y", "c", "zh", "zl", "xl")
ENC = ("xh", "y", "c")
F32 = jnp.float32
BF16 = jnp.bfloat16


def gelu_value(values):
    return values * (0.5 * (1.0 + lax.erf(values * inv_root_two)))


def gelu_both(values):
    cdf = 0.5 * (1.0 + lax.erf(values * inv_root_two))
    return values * cdf, cdf + values * jnp.exp(-0.5 * values * values) * inv_root_tau


def shift_down(values):
    rows, width = values.shape
    t = lax.broadcasted_iota(jnp.int32, (rows, width), 0) & (HALF - 1)
    clips = values.reshape(rows // HALF, HALF, width)
    moved = pltpu.roll(clips, 1, 1).reshape(rows, width)
    return jnp.where(t == 0, 0.0, moved)


def shift_up(values):
    rows, width = values.shape
    t = lax.broadcasted_iota(jnp.int32, (rows, width), 0) & (HALF - 1)
    clips = values.reshape(rows // HALF, HALF, width)
    moved = pltpu.roll(clips, HALF - 1, 1).reshape(rows, width)
    return jnp.where(t == HALF - 1, 0.0, moved)


def dot(left, right):
    return jnp.dot(left, right, preferred_element_type=F32)


def dot_nt(left, right):
    return lax.dot_general(left, right, (((1,), (1,)), ((), ())), preferred_element_type=F32)


def dot_tn(left, right):
    return lax.dot_general(left, right, (((0,), (0,)), ((), ())), preferred_element_type=F32)


def stack_weights(refs, w2_ref):
    for block, ref in enumerate(refs):
        w2_ref[block * ROWS : (block + 1) * ROWS, :] = ref[...]
    w2_ref[BLOCKS * ROWS :, :] = jnp.zeros((WIDE - BLOCKS * ROWS, 3 * D2), BF16)


def prepare_kernel(length_ref, mel_ref, pay_ref):
    clip = lax.broadcasted_iota(jnp.int32, (CLIPS, MEL), 0)
    length = jnp.zeros((CLIPS, MEL), F32)
    for index in range(CLIPS):
        length = jnp.where(clip == index, length_ref[index].astype(F32), length)
    for target in range(HOLDERS):
        pay_ref[target, :CLIPS] = mel_ref[...]
        pay_ref[target, CLIPS] = length.astype(BF16)
        pay_ref[target, CLIPS + 1 :] = jnp.zeros((PAY - CLIPS - 1, 2 * HALF, MEL), BF16)


def columns_kernel(where_ref, weight_ref, bias_ref, w1_ref, b1_ref, picked):
    picked[...] = jnp.zeros_like(picked)
    b1_ref[...] = jnp.zeros_like(b1_ref)
    for block, flip in enumerate((0, 1, 2 * HOLDERS, 2 * HOLDERS + 1)):
        first = (where_ref[3] ^ flip) * ROWS
        start = pl.multiple_of(jnp.minimum((first >> 7) << 7, 16 * ROWS - 2 * LANES), LANES)
        shift = (2 * LANES - (first - start)) & (2 * LANES - 1)
        lanes = slice(block * ROWS, (block + 1) * ROWS)
        window = weight_ref[:, pl.ds(start, 2 * LANES)].astype(F32)
        picked[:, lanes] = pltpu.roll(window, shift, 1)[:, :ROWS]
        window = jnp.broadcast_to(bias_ref[pl.ds(start, 2 * LANES)].reshape(1, 2 * LANES), (8, 2 * LANES))
        b1_ref[:, lanes] = pltpu.roll(window, shift, 1)[0:1, :ROWS]
    w1_ref[...] = picked[...].astype(BF16)


def first_conv(pay_ref, w1_ref, b1_ref, cols_ref, frames_ref):
    sources = pay_ref.shape[0]
    spread = (
        lax.broadcasted_iota(jnp.int32, (STEPS, CLIPS), 0) >> 3
        == lax.broadcasted_iota(jnp.int32, (STEPS, CLIPS), 1)
    ).astype(F32).astype(BF16)
    t = (lax.broadcasted_iota(jnp.int32, (STEPS, LANES), 0) & (HALF - 1)).astype(F32)
    lives_even, lives_odd = [], []
    for source in range(sources):
        rows = slice(source * STEPS, (source + 1) * STEPS)
        length = dot(spread, pay_ref[source, CLIPS])
        frames_ref[source] = pay_ref[source, :CLIPS].astype(F32).reshape(2 * STEPS, MEL)
        live_even, live_odd = 2.0 * t < length, 2.0 * t + 1.0 < length
        even = jnp.where(live_even, frames_ref[source, pl.ds(0, STEPS, 2), :], 0.0)
        odd = jnp.where(live_odd, frames_ref[source, pl.ds(1, STEPS, 2), :], 0.0)
        cols_ref[rows, :LANES] = shift_down(odd).astype(BF16)
        cols_ref[rows, LANES : 2 * LANES] = even.astype(BF16)
        cols_ref[rows, 2 * LANES : 3 * LANES] = odd.astype(BF16)
        cols_ref[rows, 3 * LANES :] = shift_up(even).astype(BF16)
        lives_even.append(jnp.concatenate([live_even] * (WIDE // LANES), axis=1))
        lives_odd.append(jnp.concatenate([live_odd] * (WIDE // LANES), axis=1))
    cols = jnp.concatenate([cols_ref[:, : 3 * LANES], cols_ref[:, LANES:]], axis=0)
    pre = dot(cols, w1_ref[...]) + b1_ref[...]
    half = sources * STEPS
    return pre[:half], pre[half:], jnp.concatenate(lives_even, axis=0), jnp.concatenate(lives_odd, axis=0)


def forward_kernel(
    pay_ref, w1_ref, b1_ref, own_ref, side_ref, far_ref, both_ref, part_ref, w2_ref, cols_ref, frames_ref
):
    @pl.when(pl.program_id(0) == 0)
    def _():
        stack_weights((own_ref, side_ref, far_ref, both_ref), w2_ref)

    pre_even, pre_odd, live_even, live_odd = first_conv(pay_ref, w1_ref, b1_ref, cols_ref, frames_ref)
    odd = jnp.where(live_odd, gelu_value(pre_odd), 0.0)
    total = dot(odd.astype(BF16), w2_ref[:, 2 * D2 :]) + dot(shift_down(odd).astype(BF16), w2_ref[:, :D2])
    even = jnp.where(live_even, gelu_value(pre_even), 0.0)
    total = total + dot(even.astype(BF16), w2_ref[:, D2 : 2 * D2])
    part_ref[...] = total.astype(BF16).reshape(part_ref.shape)


def slope_kernel(
    pay_ref, w1_ref, b1_ref, grad_ref, column_ref, row_ref,
    cols_ref, slope_ref, turned_ref, live_grad_ref, wanted_ref, frames_ref,
):
    pre_even, pre_odd, live_even, live_odd = first_conv(pay_ref, w1_ref, b1_ref, cols_ref, frames_ref)
    value, slope = gelu_both(pre_odd)
    odd = jnp.where(live_odd, value, 0.0)
    slope_ref[1] = jnp.where(live_odd, slope, 0.0)
    turned_ref[0] = shift_down(odd).astype(BF16).T
    turned_ref[2] = odd.astype(BF16).T
    value, slope = gelu_both(pre_even)
    slope_ref[0] = jnp.where(live_even, slope, 0.0)
    turned_ref[1] = jnp.where(live_even, value, 0.0).astype(BF16).T

    @pl.when(pl.program_id(0) == 0)
    def _():
        t = (lax.broadcasted_iota(jnp.int32, (STEPS, 1), 0) & (HALF - 1)).astype(F32)
        length = (column_ref[...] & 31).astype(F32)
        live_grad_ref[...] = jnp.where(2.0 * t < length, grad_ref[...].astype(F32), 0.0).astype(BF16)
        here = lax.broadcasted_iota(jnp.int32, (STEPS, STEPS), 0)
        there = lax.broadcasted_iota(jnp.int32, (STEPS, STEPS), 1)
        owner = row_ref[...] >> 5
        same = ((column_ref[...] >> 5) == owner) & ((here >> 3) < (there >> 3))
        same = same & ((here & (HALF - 1)) == 0)
        rank = jnp.sum(jnp.where(same, 1.0, 0.0), axis=0, keepdims=True)
        place = lax.broadcasted_iota(jnp.int32, (1, STEPS), 1) & (HALF - 1)
        place = (owner * 2 + rank.astype(jnp.int32)) * HALF + place
        wanted = lax.broadcasted_iota(jnp.int32, (SLOTS * HALF, STEPS), 0) == place
        t = (lax.broadcasted_iota(jnp.int32, (1, STEPS), 1) & (HALF - 1)).astype(F32)
        wanted = wanted & (2.0 * t < (row_ref[...] & 31).astype(F32))
        wanted_ref[...] = jnp.where(wanted, 1.0, 0.0).astype(BF16)


def middle_kernel(
    where_ref, part_ref, b2_ref, live_grad_ref, wanted_ref, rep_ref, same_ref, cross_ref, live_grad_here, done
):
    copy = pltpu.make_async_copy(live_grad_ref, live_grad_here, done)
    copy.start()
    pre = part_ref[0].astype(F32)
    for source in range(1, HOLDERS):
        pre = pre + part_ref[source].astype(F32)
    value, slope = gelu_both(pre + b2_ref[...])
    copy.wait()
    second_grad = (live_grad_here[...].astype(F32) * slope).astype(BF16)
    for target in range(HOLDERS):
        rep_ref[target] = second_grad
    placed = dot(wanted_ref[...], value.astype(BF16))
    first = where_ref[2] == 0
    for chip in range(CHIPS):
        for tile in range(D2 // LANES):
            rows, columns = slice(tile * 16, (tile + 1) * 16), slice(tile * LANES, (tile + 1) * LANES)
            left = placed[chip * 32 : chip * 32 + 16, columns]
            right = placed[chip * 32 + 16 : chip * 32 + 32, columns]
            same_ref[chip, rows, :] = jnp.where(first, left, right).astype(BF16)
            cross_ref[chip, rows, :] = jnp.where(first, right, left).astype(BF16)


def backward_kernel(
    where_ref, grad_ref, own_ref, side_ref, far_ref, both_ref, cols_ref, turned_ref, slope_ref, keep_ref, send_ref,
    w2_ref, conv_sum, cols_here, cols_done,
):
    cols_copy = pltpu.make_async_copy(cols_ref, cols_here, cols_done)
    cols_copy.start()
    stack_weights((own_ref, side_ref, far_ref, both_ref), w2_ref)
    mine = where_ref[0]
    grad = grad_ref[...].reshape(HOLDERS * STEPS, D2)
    places = []
    for block in range(BLOCKS):
        places.append((keep_ref if block % 2 == 0 else send_ref, mine if block < 2 else 1 - mine, block * ROWS))

    for tap in range(3):
        conv_sum[...] = dot(turned_ref[tap], grad)
        for out, target, first in places:
            for column in range(D2 // LANES):
                tile = tap * (D2 // LANES) + column
                piece = conv_sum[first : first + ROWS, column * LANES : (column + 1) * LANES]
                out[target, tile // 8, (tile % 8) * ROWS : (tile % 8 + 1) * ROWS, :] = piece.astype(out.dtype)

    even = dot_nt(grad, w2_ref[:, D2 : 2 * D2])
    even = (even * slope_ref[0]).astype(BF16)
    odd = dot_nt(grad, w2_ref[:, 2 * D2 :]) + shift_up(dot_nt(grad, w2_ref[:, :D2]))
    odd = (odd * slope_ref[1]).astype(BF16)
    cols_copy.wait()
    cols = cols_here[...]
    conv_sum[:, : 3 * LANES] = dot_tn(even, cols[:, : 3 * LANES]) + dot_tn(odd, cols[:, LANES:])
    bias1 = jnp.sum(even.astype(F32) + odd.astype(F32), axis=0, keepdims=True)
    bias2 = jnp.sum(grad.astype(F32), axis=0, keepdims=True)
    for out, target, first in places:
        out[target, 1, 7 * ROWS : 8 * ROWS, :] = jnp.zeros((ROWS, LANES), out.dtype)
        biases = [jnp.concatenate([bias1[:, first : first + ROWS], jnp.zeros((1, LANES - ROWS), F32)], axis=1)]
        for tile in range(D2 // LANES):
            biases.append(bias2[:, tile * LANES : (tile + 1) * LANES])
        biases.append(jnp.zeros((16 - len(biases), LANES), F32))
        biases = jnp.concatenate(biases, axis=0).astype(out.dtype)
        for half in range(2):
            for tile in range(3):
                piece = conv_sum[first : first + ROWS, tile * LANES : (tile + 1) * LANES]
                out[target, half, (8 + tile) * ROWS : (9 + tile) * ROWS, :] = piece.astype(out.dtype)
            out[target, half, 11 * ROWS :, :] = biases


def sum_kernel(got_ref, out_ref):
    total = got_ref[0].astype(F32)
    for source in range(1, got_ref.shape[0]):
        total = total + got_ref[source].astype(F32)
    total = total.astype(BF16)
    if len(out_ref.shape) == 2:
        out_ref[...] = total
    else:
        for target in range(out_ref.shape[0]):
            out_ref[target] = total


def pairs_kernel(own_ref, near_ref, both_ref, far_ref, out_ref):
    own, near, far, both = (ref[...].astype(F32) for ref in (own_ref, near_ref, far_ref, both_ref))
    total = ((own + near) + (far + both)).astype(BF16)
    for target in range(out_ref.shape[0]):
        out_ref[target] = total


def last_kernel(
    where_ref, got_ref, cross_ref, weight_ref, bias1_ref, bias2_ref, packed_ref, whole, biases,
):
    step, core = pl.program_id(0), where_ref[2]
    rows = pl.ds(pl.multiple_of((step + 1) * ROWS, 16), ROWS)
    for chip in range(CHIPS):
        whole[pl.ds(pl.multiple_of((2 * chip + core) * ROWS, 16), ROWS), :] = got_ref[chip, rows, :]
        whole[pl.ds(pl.multiple_of((2 * chip + 1 - core) * ROWS, 16), ROWS), :] = cross_ref[chip, rows, :]
    for block in range(10):
        columns = slice(block * LANES, (block + 1) * LANES)
        weight_ref[:, columns] = whole[columns, :].T.astype(F32)

    @pl.when(step == 0)
    def _():
        for chip in range(CHIPS):
            biases[2 * chip + core] = got_ref[chip, 5 * ROWS :, :].astype(F32)
            biases[2 * chip + 1 - core] = cross_ref[chip, 5 * ROWS :, :].astype(F32)
            left = pl.ds(pl.multiple_of(chip * 32 + 16 * core, 16), 16)
            right = pl.ds(pl.multiple_of(chip * 32 + 16 - 16 * core, 16), 16)
            for tile in range(D2 // LANES):
                columns = slice(tile * LANES, (tile + 1) * LANES)
                packed_ref[left, columns] = got_ref[chip, tile * 16 : (tile + 1) * 16, :]
                packed_ref[right, columns] = cross_ref[chip, 4 * ROWS + tile * 16 : 4 * ROWS + (tile + 1) * 16, :]
        bias1 = jnp.concatenate([biases[source, 0:1, :ROWS] for source in range(16)], axis=1)
        bias1_ref[...] = bias1.reshape(16 * ROWS)
        bias2 = jnp.concatenate([biases[0, 1 + tile : 2 + tile, :] for tile in range(D2 // LANES)], axis=1)
        bias2_ref[...] = bias2.reshape(D2)


def unpack_kernel(where_ref, own_ref, other_ref, conv2_ref):
    lower = where_ref[1] == 0
    for tile in range(15):
        half, spot = tile // 8, tile % 8
        rows = slice(spot * ROWS, (spot + 1) * ROWS)
        own, other = own_ref[rows, :].astype(F32), other_ref[rows, :].astype(F32)
        picked = jnp.where(lower, own, other) if half == 0 else jnp.where(lower, other, own)
        conv2_ref[:, tile * LANES : (tile + 1) * LANES] = picked


def exchange(values, axes):
    return lax.all_to_all(values, axes, split_axis=0, concat_axis=0, tiled=True)


def spread_to(values, count):
    return jnp.broadcast_to(values[None], (count,) + values.shape)


def vmem():
    return pl.BlockSpec(memory_space=pltpu.VMEM)


def params(mib, *semantics):
    return pltpu.CompilerParams(vmem_limit_bytes=mib * MIB, dimension_semantics=semantics or None)


def local(mel, lengths, routes, conv1_weight, conv1_bias, conv2_weight, conv2_bias, out_grad):
    x_hi, y, core = lax.axis_index("xh"), lax.axis_index("y"), lax.axis_index("c")
    where = jnp.stack([x_hi, lax.axis_index("xl"), core, (x_hi * HOLDERS + y) * 2 + core]).astype(jnp.int32)

    def shape(*dims, dtype=BF16):
        return jax.ShapeDtypeStruct(dims, dtype)

    def from_hbm(values):
        return pltpu.with_memory_space_constraint(values, pltpu.HBM)

    def in_hbm(*dims, dtype=BF16):
        return pltpu.HBM(dims, dtype)

    pay = pl.pallas_call(
        prepare_kernel,
        in_specs=[pl.BlockSpec(memory_space=pltpu.SMEM), vmem()],
        out_specs=vmem(),
        out_shape=in_hbm(HOLDERS, PAY, 2 * HALF, MEL),
        compiler_params=params(60),
        name="mel_payload",
    )(lengths, mel)
    got_pay = exchange(pay, "y")
    cores = [(0, 1), (1, 0)]
    far_weight = lax.ppermute(conv2_weight, ("xh", "xl"), [(0, 3), (3, 0), (1, 2), (2, 1)])

    w1, b1 = pl.pallas_call(
        columns_kernel,
        in_specs=[pl.BlockSpec(memory_space=pltpu.SMEM), vmem(), vmem()],
        out_specs=[vmem()] * 2,
        out_shape=[shape(3 * MEL, WIDE), shape(1, WIDE, dtype=F32)],
        scratch_shapes=[pltpu.VMEM((3 * MEL, WIDE), F32)],
        compiler_params=params(10),
        name="conv1_columns",
    )(where, conv1_weight, from_hbm(conv1_bias))
    own_weight, place = lax.optimization_barrier((conv2_weight, where))
    far_weight, place = lax.optimization_barrier((far_weight, place))
    weights = [
        conv2_weight,
        lax.ppermute(own_weight, "c", cores),
        far_weight,
        lax.ppermute(far_weight, "c", cores),
    ]

    pair = lambda i: (i, 0, 0)
    pair4 = lambda i: (i, 0, 0, 0)
    rows, some = HOLDERS * STEPS, 2 * STEPS
    frames = (2, 2 * STEPS, MEL)
    pay_spec = pl.BlockSpec((2, PAY, 2 * HALF, MEL), pair4)
    parts = pl.pallas_call(
        forward_kernel,
        grid=(HOLDERS // 2,),
        in_specs=[pay_spec, *[vmem()] * (2 + BLOCKS)],
        out_specs=pl.BlockSpec((2, STEPS, D2), pair),
        out_shape=in_hbm(HOLDERS, STEPS, D2),
        scratch_shapes=[
            pltpu.VMEM((WIDE, 3 * D2), BF16),
            pltpu.VMEM((some, 4 * LANES), BF16),
            pltpu.VMEM(frames, F32),
        ],
        compiler_params=params(20, "arbitrary"),
        name="stem_forward",
    )(got_pay, w1, b1, *weights)

    got_parts = exchange(parts, "y")
    code = jnp.repeat(routes[:, 0] * 32 + lengths, HALF)
    cols, slopes, turned, live_grad, wanted = pl.pallas_call(
        slope_kernel,
        grid=(HOLDERS // 2,),
        in_specs=[pay_spec, *[vmem()] * 5],
        out_specs=[
            pl.BlockSpec((some, 4 * LANES), lambda i: (i, 0)),
            pl.BlockSpec((2, some, WIDE), lambda i: (0, i, 0)),
            pl.BlockSpec((3, WIDE, some), lambda i: (0, 0, i)),
            vmem(),
            vmem(),
        ],
        out_shape=[
            in_hbm(rows, 4 * LANES),
            shape(2, rows, WIDE, dtype=F32),
            shape(3, WIDE, rows),
            in_hbm(STEPS, D2),
            shape(SLOTS * HALF, STEPS),
        ],
        scratch_shapes=[pltpu.VMEM(frames, F32)],
        compiler_params=params(20, "arbitrary"),
        name="stem_slopes",
    )(got_pay, w1, b1, from_hbm(out_grad.reshape(STEPS, D2)), code[:, None], code[None])
    got_parts, slopes, turned = lax.optimization_barrier((got_parts, slopes, turned))
    rep, same, cross = pl.pallas_call(
        middle_kernel,
        in_specs=[pl.BlockSpec(memory_space=pltpu.SMEM), vmem(), vmem(), pl.BlockSpec(memory_space=pl.ANY), vmem()],
        out_specs=[vmem()] * 3,
        out_shape=[shape(HOLDERS, STEPS, D2), shape(CHIPS, ROWS, LANES), shape(CHIPS, ROWS, LANES)],
        scratch_shapes=[pltpu.VMEM((STEPS, D2), BF16), pltpu.SemaphoreType.DMA],
        compiler_params=params(10),
        name="stem_middle",
    )(where, got_parts, conv2_bias[None], from_hbm(live_grad), wanted)
    got_grad = exchange(rep, "y")

    keep, send = pl.pallas_call(
        backward_kernel,
        in_specs=[
            pl.BlockSpec(memory_space=pltpu.SMEM),
            *[vmem()] * (1 + BLOCKS),
            pl.BlockSpec(memory_space=pl.ANY),
            vmem(),
            vmem(),
        ],
        out_specs=[vmem()] * 2,
        out_shape=[shape(2, 2, PACK, LANES, dtype=F32), shape(2, 2, PACK, LANES)],
        scratch_shapes=[
            pltpu.VMEM((WIDE, 3 * D2), BF16),
            pltpu.VMEM((WIDE, D2), F32),
            pltpu.VMEM((rows, 4 * LANES), BF16),
            pltpu.SemaphoreType.DMA,
        ],
        compiler_params=params(32),
        name="stem_backward",
    )(where, got_grad, *weights, from_hbm(cols), turned, slopes)
    got = lax.ppermute(send, "c", cores)
    quarters = exchange((keep + got.astype(F32)).astype(BF16).reshape(4, PACK, LANES), ("xh", "xl"))

    def summed(values, *dims):
        return pl.pallas_call(
            sum_kernel,
            in_specs=[vmem()],
            out_specs=vmem(),
            out_shape=shape(*dims),
            compiler_params=params(8),
            name="gradient_sum",
        )(values)

    half = summed(quarters, PACK, LANES)
    quarter = PACK // 4
    near = summed(exchange(half.reshape(4, quarter, LANES), "zl"), quarter, LANES)
    far = {flip: lax.ppermute(near, "zh", [(i, i ^ flip) for i in range(4)]) for flip in (2, 3, 1)}
    far = pl.pallas_call(
        pairs_kernel,
        in_specs=[vmem()] * 4,
        out_specs=vmem(),
        out_shape=shape(4, quarter, LANES),
        compiler_params=params(8),
        name="gradient_pairs",
    )(near, far[1], far[3], far[2])
    half = exchange(far, "zl").reshape(PACK, LANES)
    own = half[:HALF_ROWS]
    other = lax.ppermute(own, "xl", [(0, 1), (1, 0)])
    conv1 = spread_to(half[HALF_ROWS:], CHIPS)
    got = exchange(jnp.concatenate([same, conv1[:, : 3 * ROWS], cross, conv1[:, 3 * ROWS :]], axis=1), ("xh", "y"))
    got, other = lax.optimization_barrier((got, other))
    got_cross = lax.ppermute(got, "c", cores)
    conv2_rows_grad = pl.pallas_call(
        unpack_kernel,
        in_specs=[pl.BlockSpec(memory_space=pltpu.SMEM), vmem(), vmem()],
        out_specs=vmem(),
        out_shape=in_hbm(ROWS, 3 * D2, dtype=F32),
        compiler_params=params(8),
        name="conv2_unpack",
    )(where, own, other)
    weight_grad, bias_grad, second_bias_grad, packed = pl.pallas_call(
        last_kernel,
        grid=(3,),
        in_specs=[
            pl.BlockSpec(memory_space=pltpu.SMEM),
            vmem(),
            vmem(),
        ],
        out_specs=[
            pl.BlockSpec((LANES, 16 * ROWS), lambda i: (i, 0)),
            pl.BlockSpec((16 * ROWS,), lambda i: (0,)),
            pl.BlockSpec((D2,), lambda i: (0,)),
            pl.BlockSpec((SLOTS * HALF, D2), lambda i: (0, 0)),
        ],
        out_shape=[
            shape(3 * MEL, 16 * ROWS, dtype=F32),
            shape(16 * ROWS, dtype=F32),
            shape(D2, dtype=F32),
            shape(SLOTS * HALF, D2),
        ],
        scratch_shapes=[pltpu.VMEM((16 * ROWS, LANES), BF16), pltpu.VMEM((16, 16, LANES), F32)],
        compiler_params=params(16, "arbitrary"),
        name="gradient_unpack",
    )(where, got, got_cross)
    return packed.reshape(SLOTS, HALF, D2), weight_grad, bias_grad, second_bias_grad, conv2_rows_grad


def solution(mesh):
    fine = Mesh(mesh.devices.reshape(2, 4, 2, 4, 4, 2), ALL_AXES)
    placed = (
        P(ALL_AXES, None, None),
        P(ALL_AXES),
        P(ALL_AXES, None),
        P(),
        P(),
        P(ENC, None),
        P(),
        P(ALL_AXES, None, None),
    )
    return jax.shard_map(
        local,
        mesh=fine,
        in_specs=placed,
        out_specs=(P(ALL_AXES, None, None), P(), P(), P(), P(ENC, None)),
        check_vma=False,
    )
```

```python
import functools

import jax
import jax.numpy as jnp
from jax import lax
from jax.experimental import pallas as pl
from jax.experimental.pallas import tpu as pltpu
from jax.sharding import Mesh
from jax.sharding import PartitionSpec as P

inv_root_two = 0.7071067811865476
inv_root_tau = 0.3989422804014327

MEL = 128
D2 = 640
ROWS = 80
LANES = 128
HOLDERS = 4
BLOCKS = 4
WIDE = 384
CLIPS = 16
HALF = 8
STEPS = CLIPS * HALF
SLOTS = 2 * CLIPS
PAY = 26
CHIPS = 8
PACK = 896
HALF_ROWS = 8 * ROWS
MIB = 1024 * 1024
ALL_AXES = ("xh", "y", "c", "zh", "zl", "xl")
ENC = ("xh", "y", "c")
F32 = jnp.float32
BF16 = jnp.bfloat16


def gelu_value(values):
    return values * (0.5 * (1.0 + lax.erf(values * inv_root_two)))


def gelu_both(values):
    cdf = 0.5 * (1.0 + lax.erf(values * inv_root_two))
    return values * cdf, cdf + values * jnp.exp(-0.5 * values * values) * inv_root_tau


def shift_down(values):
    rows, width = values.shape
    t = lax.broadcasted_iota(jnp.int32, (rows, width), 0) & (HALF - 1)
    clips = values.reshape(rows // HALF, HALF, width)
    moved = pltpu.roll(clips, 1, 1).reshape(rows, width)
    return jnp.where(t == 0, 0.0, moved)


def shift_up(values):
    rows, width = values.shape
    t = lax.broadcasted_iota(jnp.int32, (rows, width), 0) & (HALF - 1)
    clips = values.reshape(rows // HALF, HALF, width)
    moved = pltpu.roll(clips, HALF - 1, 1).reshape(rows, width)
    return jnp.where(t == HALF - 1, 0.0, moved)


def dot(left, right):
    return jnp.dot(left, right, preferred_element_type=F32)


def dot_nt(left, right):
    return lax.dot_general(left, right, (((1,), (1,)), ((), ())), preferred_element_type=F32)


def dot_tn(left, right):
    return lax.dot_general(left, right, (((0,), (0,)), ((), ())), preferred_element_type=F32)


def stack_weights(refs, w2_ref):
    for block, ref in enumerate(refs):
        w2_ref[block * ROWS : (block + 1) * ROWS, :] = ref[...]
    w2_ref[BLOCKS * ROWS :, :] = jnp.zeros((WIDE - BLOCKS * ROWS, 3 * D2), BF16)


def prepare_kernel(length_ref, mel_ref, pay_ref):
    clip = lax.broadcasted_iota(jnp.int32, (CLIPS, MEL), 0)
    length = jnp.zeros((CLIPS, MEL), F32)
    for index in range(CLIPS):
        length = jnp.where(clip == index, length_ref[index].astype(F32), length)
    for target in range(HOLDERS):
        pay_ref[target, :CLIPS] = mel_ref[...]
        pay_ref[target, CLIPS] = length.astype(BF16)
        pay_ref[target, CLIPS + 1 :] = jnp.zeros((PAY - CLIPS - 1, 2 * HALF, MEL), BF16)


def columns_kernel(where_ref, weight_ref, bias_ref, w1_ref, b1_ref, picked):
    picked[...] = jnp.zeros_like(picked)
    b1_ref[...] = jnp.zeros_like(b1_ref)
    for block, flip in enumerate((0, 1, 2 * HOLDERS, 2 * HOLDERS + 1)):
        first = (where_ref[3] ^ flip) * ROWS
        start = pl.multiple_of(jnp.minimum((first >> 7) << 7, 16 * ROWS - 2 * LANES), LANES)
        shift = (2 * LANES - (first - start)) & (2 * LANES - 1)
        lanes = slice(block * ROWS, (block + 1) * ROWS)
        window = weight_ref[:, pl.ds(start, 2 * LANES)].astype(F32)
        picked[:, lanes] = pltpu.roll(window, shift, 1)[:, :ROWS]
        window = jnp.broadcast_to(bias_ref[pl.ds(start, 2 * LANES)].reshape(1, 2 * LANES), (8, 2 * LANES))
        b1_ref[:, lanes] = pltpu.roll(window, shift, 1)[0:1, :ROWS]
    w1_ref[...] = picked[...].astype(BF16)


def first_conv(pay_ref, w1_ref, b1_ref, cols_ref, frames_ref):
    sources = pay_ref.shape[0]
    spread = (
        lax.broadcasted_iota(jnp.int32, (STEPS, CLIPS), 0) >> 3
        == lax.broadcasted_iota(jnp.int32, (STEPS, CLIPS), 1)
    ).astype(F32).astype(BF16)
    t = (lax.broadcasted_iota(jnp.int32, (STEPS, LANES), 0) & (HALF - 1)).astype(F32)
    lives_even, lives_odd = [], []
    for source in range(sources):
        rows = slice(source * STEPS, (source + 1) * STEPS)
        length = dot(spread, pay_ref[source, CLIPS])
        frames_ref[source] = pay_ref[source, :CLIPS].astype(F32).reshape(2 * STEPS, MEL)
        live_even, live_odd = 2.0 * t < length, 2.0 * t + 1.0 < length
        even = jnp.where(live_even, frames_ref[source, pl.ds(0, STEPS, 2), :], 0.0)
        odd = jnp.where(live_odd, frames_ref[source, pl.ds(1, STEPS, 2), :], 0.0)
        cols_ref[rows, :LANES] = shift_down(odd).astype(BF16)
        cols_ref[rows, LANES : 2 * LANES] = even.astype(BF16)
        cols_ref[rows, 2 * LANES : 3 * LANES] = odd.astype(BF16)
        cols_ref[rows, 3 * LANES :] = shift_up(even).astype(BF16)
        lives_even.append(jnp.concatenate([live_even] * (WIDE // LANES), axis=1))
        lives_odd.append(jnp.concatenate([live_odd] * (WIDE // LANES), axis=1))
    cols = jnp.concatenate([cols_ref[:, : 3 * LANES], cols_ref[:, LANES:]], axis=0)
    pre = dot(cols, w1_ref[...]) + b1_ref[...]
    half = sources * STEPS
    return pre[:half], pre[half:], jnp.concatenate(lives_even, axis=0), jnp.concatenate(lives_odd, axis=0)


def forward_kernel(
    pay_ref, w1_ref, b1_ref, own_ref, side_ref, far_ref, both_ref, part_ref, w2_ref, cols_ref, frames_ref
):
    @pl.when(pl.program_id(0) == 0)
    def _():
        stack_weights((own_ref, side_ref, far_ref, both_ref), w2_ref)

    pre_even, pre_odd, live_even, live_odd = first_conv(pay_ref, w1_ref, b1_ref, cols_ref, frames_ref)
    odd = jnp.where(live_odd, gelu_value(pre_odd), 0.0)
    total = dot(odd.astype(BF16), w2_ref[:, 2 * D2 :]) + dot(shift_down(odd).astype(BF16), w2_ref[:, :D2])
    even = jnp.where(live_even, gelu_value(pre_even), 0.0)
    total = total + dot(even.astype(BF16), w2_ref[:, D2 : 2 * D2])
    part_ref[...] = total.astype(BF16).reshape(part_ref.shape)


def slope_kernel(
    pay_ref, w1_ref, b1_ref, grad_ref, column_ref, row_ref,
    cols_ref, slope_ref, turned_ref, live_grad_ref, wanted_ref, frames_ref,
):
    pre_even, pre_odd, live_even, live_odd = first_conv(pay_ref, w1_ref, b1_ref, cols_ref, frames_ref)
    value, slope = gelu_both(pre_odd)
    odd = jnp.where(live_odd, value, 0.0)
    slope_ref[1] = jnp.where(live_odd, slope, 0.0)
    turned_ref[0] = shift_down(odd).astype(BF16).T
    turned_ref[2] = odd.astype(BF16).T
    value, slope = gelu_both(pre_even)
    slope_ref[0] = jnp.where(live_even, slope, 0.0)
    turned_ref[1] = jnp.where(live_even, value, 0.0).astype(BF16).T

    @pl.when(pl.program_id(0) == 0)
    def _():
        t = (lax.broadcasted_iota(jnp.int32, (STEPS, 1), 0) & (HALF - 1)).astype(F32)
        length = (column_ref[...] & 31).astype(F32)
        live_grad_ref[...] = jnp.where(2.0 * t < length, grad_ref[...].astype(F32), 0.0).astype(BF16)
        here = lax.broadcasted_iota(jnp.int32, (STEPS, STEPS), 0)
        there = lax.broadcasted_iota(jnp.int32, (STEPS, STEPS), 1)
        owner = row_ref[...] >> 5
        same = ((column_ref[...] >> 5) == owner) & ((here >> 3) < (there >> 3))
        same = same & ((here & (HALF - 1)) == 0)
        rank = jnp.sum(jnp.where(same, 1.0, 0.0), axis=0, keepdims=True)
        place = lax.broadcasted_iota(jnp.int32, (1, STEPS), 1) & (HALF - 1)
        place = (owner * 2 + rank.astype(jnp.int32)) * HALF + place
        wanted = lax.broadcasted_iota(jnp.int32, (SLOTS * HALF, STEPS), 0) == place
        t = (lax.broadcasted_iota(jnp.int32, (1, STEPS), 1) & (HALF - 1)).astype(F32)
        wanted = wanted & (2.0 * t < (row_ref[...] & 31).astype(F32))
        wanted_ref[...] = jnp.where(wanted, 1.0, 0.0).astype(BF16)


def middle_kernel(
    where_ref, part_ref, b2_ref, live_grad_ref, wanted_ref, rep_ref, same_ref, cross_ref, live_grad_here, done
):
    copy = pltpu.make_async_copy(live_grad_ref, live_grad_here, done)
    copy.start()
    pre = part_ref[0].astype(F32)
    for source in range(1, HOLDERS):
        pre = pre + part_ref[source].astype(F32)
    value, slope = gelu_both(pre + b2_ref[...])
    copy.wait()
    second_grad = (live_grad_here[...].astype(F32) * slope).astype(BF16)
    for target in range(HOLDERS):
        rep_ref[target] = second_grad
    placed = dot(wanted_ref[...], value.astype(BF16))
    first = where_ref[2] == 0
    for chip in range(CHIPS):
        for tile in range(D2 // LANES):
            rows, columns = slice(tile * 16, (tile + 1) * 16), slice(tile * LANES, (tile + 1) * LANES)
            left = placed[chip * 32 : chip * 32 + 16, columns]
            right = placed[chip * 32 + 16 : chip * 32 + 32, columns]
            same_ref[chip, rows, :] = jnp.where(first, left, right).astype(BF16)
            cross_ref[chip, rows, :] = jnp.where(first, right, left).astype(BF16)


def backward_kernel(
    where_ref, grad_ref, own_ref, side_ref, far_ref, both_ref, cols_ref, turned_ref, slope_ref, keep_ref, send_ref,
    w2_ref, conv_sum, cols_here, cols_done,
):
    cols_copy = pltpu.make_async_copy(cols_ref, cols_here, cols_done)
    cols_copy.start()
    stack_weights((own_ref, side_ref, far_ref, both_ref), w2_ref)
    mine = where_ref[0]
    grad = grad_ref[...].reshape(HOLDERS * STEPS, D2)
    places = []
    for block in range(BLOCKS):
        places.append((keep_ref if block % 2 == 0 else send_ref, mine if block < 2 else 1 - mine, block * ROWS))

    for tap in range(3):
        conv_sum[...] = dot(turned_ref[tap], grad)
        for out, target, first in places:
            for column in range(D2 // LANES):
                tile = tap * (D2 // LANES) + column
                piece = conv_sum[first : first + ROWS, column * LANES : (column + 1) * LANES]
                out[target, tile // 8, (tile % 8) * ROWS : (tile % 8 + 1) * ROWS, :] = piece.astype(out.dtype)

    even = dot_nt(grad, w2_ref[:, D2 : 2 * D2])
    even = (even * slope_ref[0]).astype(BF16)
    odd = dot_nt(grad, w2_ref[:, 2 * D2 :]) + shift_up(dot_nt(grad, w2_ref[:, :D2]))
    odd = (odd * slope_ref[1]).astype(BF16)
    cols_copy.wait()
    cols = cols_here[...]
    conv_sum[:, : 3 * LANES] = dot_tn(even, cols[:, : 3 * LANES]) + dot_tn(odd, cols[:, LANES:])
    bias1 = jnp.sum(even.astype(F32) + odd.astype(F32), axis=0, keepdims=True)
    bias2 = jnp.sum(grad.astype(F32), axis=0, keepdims=True)
    for out, target, first in places:
        out[target, 1, 7 * ROWS : 8 * ROWS, :] = jnp.zeros((ROWS, LANES), out.dtype)
        biases = [jnp.concatenate([bias1[:, first : first + ROWS], jnp.zeros((1, LANES - ROWS), F32)], axis=1)]
        for tile in range(D2 // LANES):
            biases.append(bias2[:, tile * LANES : (tile + 1) * LANES])
        biases.append(jnp.zeros((16 - len(biases), LANES), F32))
        biases = jnp.concatenate(biases, axis=0).astype(out.dtype)
        for half in range(2):
            for tile in range(3):
                piece = conv_sum[first : first + ROWS, tile * LANES : (tile + 1) * LANES]
                out[target, half, (8 + tile) * ROWS : (9 + tile) * ROWS, :] = piece.astype(out.dtype)
            out[target, half, 11 * ROWS :, :] = biases


def sum_kernel(got_ref, out_ref):
    total = got_ref[0].astype(F32)
    for source in range(1, got_ref.shape[0]):
        total = total + got_ref[source].astype(F32)
    total = total.astype(BF16)
    if len(out_ref.shape) == 2:
        out_ref[...] = total
    else:
        for target in range(out_ref.shape[0]):
            out_ref[target] = total


def pair_kernel(own_ref, other_ref, out_ref):
    total = (own_ref[...].astype(F32) + other_ref[...].astype(F32)).astype(BF16)
    if len(out_ref.shape) == 2:
        out_ref[...] = total
    else:
        for target in range(out_ref.shape[0]):
            out_ref[target] = total


def last_kernel(
    where_ref, got_ref, cross_ref, weight_ref, bias1_ref, bias2_ref, packed_ref, whole, biases,
):
    step, core = pl.program_id(0), where_ref[2]
    rows = pl.ds(pl.multiple_of((step + 1) * ROWS, 16), ROWS)
    for chip in range(CHIPS):
        whole[pl.ds(pl.multiple_of((2 * chip + core) * ROWS, 16), ROWS), :] = got_ref[chip, rows, :]
        whole[pl.ds(pl.multiple_of((2 * chip + 1 - core) * ROWS, 16), ROWS), :] = cross_ref[chip, rows, :]
    for block in range(10):
        columns = slice(block * LANES, (block + 1) * LANES)
        weight_ref[:, columns] = whole[columns, :].T.astype(F32)

    @pl.when(step == 0)
    def _():
        for chip in range(CHIPS):
            biases[2 * chip + core] = got_ref[chip, 5 * ROWS :, :].astype(F32)
            biases[2 * chip + 1 - core] = cross_ref[chip, 5 * ROWS :, :].astype(F32)
            left = pl.ds(pl.multiple_of(chip * 32 + 16 * core, 16), 16)
            right = pl.ds(pl.multiple_of(chip * 32 + 16 - 16 * core, 16), 16)
            for tile in range(D2 // LANES):
                columns = slice(tile * LANES, (tile + 1) * LANES)
                packed_ref[left, columns] = got_ref[chip, tile * 16 : (tile + 1) * 16, :]
                packed_ref[right, columns] = cross_ref[chip, 4 * ROWS + tile * 16 : 4 * ROWS + (tile + 1) * 16, :]
        bias1 = jnp.concatenate([biases[source, 0:1, :ROWS] for source in range(16)], axis=1)
        bias1_ref[...] = bias1.reshape(16 * ROWS)
        bias2 = jnp.concatenate([biases[0, 1 + tile : 2 + tile, :] for tile in range(D2 // LANES)], axis=1)
        bias2_ref[...] = bias2.reshape(D2)


def unpack_kernel(where_ref, own_ref, other_ref, conv2_ref):
    lower = where_ref[1] == 0
    for tile in range(15):
        half, spot = tile // 8, tile % 8
        rows = slice(spot * ROWS, (spot + 1) * ROWS)
        own, other = own_ref[rows, :].astype(F32), other_ref[rows, :].astype(F32)
        picked = jnp.where(lower, own, other) if half == 0 else jnp.where(lower, other, own)
        conv2_ref[:, tile * LANES : (tile + 1) * LANES] = picked


def exchange(values, axes):
    return lax.all_to_all(values, axes, split_axis=0, concat_axis=0, tiled=True)


def spread_to(values, count):
    return jnp.broadcast_to(values[None], (count,) + values.shape)


def vmem():
    return pl.BlockSpec(memory_space=pltpu.VMEM)


def params(mib, *semantics):
    return pltpu.CompilerParams(vmem_limit_bytes=mib * MIB, dimension_semantics=semantics or None)


def local(mel, lengths, routes, conv1_weight, conv1_bias, conv2_weight, conv2_bias, out_grad):
    x_hi, y, core = lax.axis_index("xh"), lax.axis_index("y"), lax.axis_index("c")
    where = jnp.stack([x_hi, lax.axis_index("xl"), core, (x_hi * HOLDERS + y) * 2 + core]).astype(jnp.int32)

    def shape(*dims, dtype=BF16):
        return jax.ShapeDtypeStruct(dims, dtype)

    def from_hbm(values):
        return pltpu.with_memory_space_constraint(values, pltpu.HBM)

    def in_hbm(*dims, dtype=BF16):
        return pltpu.HBM(dims, dtype)

    pay = pl.pallas_call(
        prepare_kernel,
        in_specs=[pl.BlockSpec(memory_space=pltpu.SMEM), vmem()],
        out_specs=vmem(),
        out_shape=in_hbm(HOLDERS, PAY, 2 * HALF, MEL),
        compiler_params=params(60),
        name="mel_payload",
    )(lengths, mel)
    got_pay = exchange(pay, "y")
    cores = [(0, 1), (1, 0)]
    far_weight = lax.ppermute(conv2_weight, ("xh", "xl"), [(0, 3), (3, 0), (1, 2), (2, 1)])

    w1, b1 = pl.pallas_call(
        columns_kernel,
        in_specs=[pl.BlockSpec(memory_space=pltpu.SMEM), vmem(), vmem()],
        out_specs=[vmem()] * 2,
        out_shape=[shape(3 * MEL, WIDE), shape(1, WIDE, dtype=F32)],
        scratch_shapes=[pltpu.VMEM((3 * MEL, WIDE), F32)],
        compiler_params=params(10),
        name="conv1_columns",
    )(where, conv1_weight, from_hbm(conv1_bias))
    own_weight, place = lax.optimization_barrier((conv2_weight, where))
    far_weight, place = lax.optimization_barrier((far_weight, place))
    weights = [
        conv2_weight,
        lax.ppermute(own_weight, "c", cores),
        far_weight,
        lax.ppermute(far_weight, "c", cores),
    ]

    pair = lambda i: (i, 0, 0)
    pair4 = lambda i: (i, 0, 0, 0)
    rows, some = HOLDERS * STEPS, 2 * STEPS
    frames = (2, 2 * STEPS, MEL)
    pay_spec = pl.BlockSpec((2, PAY, 2 * HALF, MEL), pair4)
    parts = pl.pallas_call(
        forward_kernel,
        grid=(HOLDERS // 2,),
        in_specs=[pay_spec, *[vmem()] * (2 + BLOCKS)],
        out_specs=pl.BlockSpec((2, STEPS, D2), pair),
        out_shape=in_hbm(HOLDERS, STEPS, D2),
        scratch_shapes=[
            pltpu.VMEM((WIDE, 3 * D2), BF16),
            pltpu.VMEM((some, 4 * LANES), BF16),
            pltpu.VMEM(frames, F32),
        ],
        compiler_params=params(20, "arbitrary"),
        name="stem_forward",
    )(got_pay, w1, b1, *weights)

    got_parts = exchange(parts, "y")
    code = jnp.repeat(routes[:, 0] * 32 + lengths, HALF)
    cols, slopes, turned, live_grad, wanted = pl.pallas_call(
        slope_kernel,
        grid=(HOLDERS // 2,),
        in_specs=[pay_spec, *[vmem()] * 5],
        out_specs=[
            pl.BlockSpec((some, 4 * LANES), lambda i: (i, 0)),
            pl.BlockSpec((2, some, WIDE), lambda i: (0, i, 0)),
            pl.BlockSpec((3, WIDE, some), lambda i: (0, 0, i)),
            vmem(),
            vmem(),
        ],
        out_shape=[
            in_hbm(rows, 4 * LANES),
            shape(2, rows, WIDE, dtype=F32),
            shape(3, WIDE, rows),
            in_hbm(STEPS, D2),
            shape(SLOTS * HALF, STEPS),
        ],
        scratch_shapes=[pltpu.VMEM(frames, F32)],
        compiler_params=params(20, "arbitrary"),
        name="stem_slopes",
    )(got_pay, w1, b1, from_hbm(out_grad.reshape(STEPS, D2)), code[:, None], code[None])
    got_parts, slopes, turned = lax.optimization_barrier((got_parts, slopes, turned))
    rep, same, cross = pl.pallas_call(
        middle_kernel,
        in_specs=[pl.BlockSpec(memory_space=pltpu.SMEM), vmem(), vmem(), pl.BlockSpec(memory_space=pl.ANY), vmem()],
        out_specs=[vmem()] * 3,
        out_shape=[shape(HOLDERS, STEPS, D2), shape(CHIPS, ROWS, LANES), shape(CHIPS, ROWS, LANES)],
        scratch_shapes=[pltpu.VMEM((STEPS, D2), BF16), pltpu.SemaphoreType.DMA],
        compiler_params=params(10),
        name="stem_middle",
    )(where, got_parts, conv2_bias[None], from_hbm(live_grad), wanted)
    got_grad = exchange(rep, "y")

    keep, send = pl.pallas_call(
        backward_kernel,
        in_specs=[
            pl.BlockSpec(memory_space=pltpu.SMEM),
            *[vmem()] * (1 + BLOCKS),
            pl.BlockSpec(memory_space=pl.ANY),
            vmem(),
            vmem(),
        ],
        out_specs=[vmem()] * 2,
        out_shape=[shape(2, 2, PACK, LANES, dtype=F32), shape(2, 2, PACK, LANES)],
        scratch_shapes=[
            pltpu.VMEM((WIDE, 3 * D2), BF16),
            pltpu.VMEM((WIDE, D2), F32),
            pltpu.VMEM((rows, 4 * LANES), BF16),
            pltpu.SemaphoreType.DMA,
        ],
        compiler_params=params(32),
        name="stem_backward",
    )(where, got_grad, *weights, from_hbm(cols), turned, slopes)
    got = lax.ppermute(send, "c", cores)
    quarters = exchange((keep + got.astype(F32)).astype(BF16).reshape(4, PACK, LANES), ("xh", "xl"))

    def summed(values, *dims):
        return pl.pallas_call(
            sum_kernel,
            in_specs=[vmem()],
            out_specs=vmem(),
            out_shape=shape(*dims),
            compiler_params=params(8),
            name="gradient_sum",
        )(values)

    half = summed(quarters, PACK, LANES)
    quarter = PACK // 4
    near = summed(exchange(half.reshape(4, quarter, LANES), "zl"), quarter, LANES)

    def with_group(values, flip, *dims):
        return pl.pallas_call(
            pair_kernel,
            in_specs=[vmem()] * 2,
            out_specs=vmem(),
            out_shape=shape(*dims),
            compiler_params=params(8),
            name="gradient_pair",
        )(values, lax.ppermute(values, "zh", [(i, i ^ flip) for i in range(4)]))

    far = with_group(with_group(near, 1, quarter, LANES), 3, 4, quarter, LANES)
    half = exchange(far, "zl").reshape(PACK, LANES)
    own = half[:HALF_ROWS]
    other = lax.ppermute(own, "xl", [(0, 1), (1, 0)])
    conv1 = spread_to(half[HALF_ROWS:], CHIPS)
    got = exchange(jnp.concatenate([same, conv1[:, : 3 * ROWS], cross, conv1[:, 3 * ROWS :]], axis=1), ("xh", "y"))
    got, other = lax.optimization_barrier((got, other))
    got_cross = lax.ppermute(got, "c", cores)
    conv2_rows_grad = pl.pallas_call(
        unpack_kernel,
        in_specs=[pl.BlockSpec(memory_space=pltpu.SMEM), vmem(), vmem()],
        out_specs=vmem(),
        out_shape=in_hbm(ROWS, 3 * D2, dtype=F32),
        compiler_params=params(8),
        name="conv2_unpack",
    )(where, own, other)
    weight_grad, bias_grad, second_bias_grad, packed = pl.pallas_call(
        last_kernel,
        grid=(3,),
        in_specs=[
            pl.BlockSpec(memory_space=pltpu.SMEM),
            vmem(),
            vmem(),
        ],
        out_specs=[
            pl.BlockSpec((LANES, 16 * ROWS), lambda i: (i, 0)),
            pl.BlockSpec((16 * ROWS,), lambda i: (0,)),
            pl.BlockSpec((D2,), lambda i: (0,)),
            pl.BlockSpec((SLOTS * HALF, D2), lambda i: (0, 0)),
        ],
        out_shape=[
            shape(3 * MEL, 16 * ROWS, dtype=F32),
            shape(16 * ROWS, dtype=F32),
            shape(D2, dtype=F32),
            shape(SLOTS * HALF, D2),
        ],
        scratch_shapes=[pltpu.VMEM((16 * ROWS, LANES), BF16), pltpu.VMEM((16, 16, LANES), F32)],
        compiler_params=params(16, "arbitrary"),
        name="gradient_unpack",
    )(where, got, got_cross)
    return packed.reshape(SLOTS, HALF, D2), weight_grad, bias_grad, second_bias_grad, conv2_rows_grad


def solution(mesh):
    fine = Mesh(mesh.devices.reshape(2, 4, 2, 4, 4, 2), ALL_AXES)
    placed = (
        P(ALL_AXES, None, None),
        P(ALL_AXES),
        P(ALL_AXES, None),
        P(),
        P(),
        P(ENC, None),
        P(),
        P(ALL_AXES, None, None),
    )
    return jax.shard_map(
        local,
        mesh=fine,
        in_specs=placed,
        out_specs=(P(ALL_AXES, None, None), P(), P(), P(), P(ENC, None)),
        check_vma=False,
    )
```

```python
import functools

import jax
import jax.numpy as jnp
from jax import lax
from jax.experimental import pallas as pl
from jax.experimental.pallas import tpu as pltpu
from jax.sharding import Mesh
from jax.sharding import PartitionSpec as P

inv_root_two = 0.7071067811865476
inv_root_tau = 0.3989422804014327

MEL = 128
D2 = 640
ROWS = 80
LANES = 128
HOLDERS = 4
BLOCKS = 4
WIDE = 384
CLIPS = 16
HALF = 8
STEPS = CLIPS * HALF
SLOTS = 2 * CLIPS
PAY = 26
CHIPS = 8
PACK = 896
HALF_ROWS = 8 * ROWS
MIB = 1024 * 1024
ALL_AXES = ("xh", "y", "c", "zh", "zl", "xl")
ENC = ("xh", "y", "c")
F32 = jnp.float32
BF16 = jnp.bfloat16


def gelu_value(values):
    return values * (0.5 * (1.0 + lax.erf(values * inv_root_two)))


def gelu_both(values):
    cdf = 0.5 * (1.0 + lax.erf(values * inv_root_two))
    return values * cdf, cdf + values * jnp.exp(-0.5 * values * values) * inv_root_tau


def shift_down(values):
    rows, width = values.shape
    t = lax.broadcasted_iota(jnp.int32, (rows, width), 0) & (HALF - 1)
    clips = values.reshape(rows // HALF, HALF, width)
    moved = pltpu.roll(clips, 1, 1).reshape(rows, width)
    return jnp.where(t == 0, 0.0, moved)


def shift_up(values):
    rows, width = values.shape
    t = lax.broadcasted_iota(jnp.int32, (rows, width), 0) & (HALF - 1)
    clips = values.reshape(rows // HALF, HALF, width)
    moved = pltpu.roll(clips, HALF - 1, 1).reshape(rows, width)
    return jnp.where(t == HALF - 1, 0.0, moved)


def dot(left, right):
    return jnp.dot(left, right, preferred_element_type=F32)


def dot_nt(left, right):
    return lax.dot_general(left, right, (((1,), (1,)), ((), ())), preferred_element_type=F32)


def dot_tn(left, right):
    return lax.dot_general(left, right, (((0,), (0,)), ((), ())), preferred_element_type=F32)


def stack_weights(refs, w2_ref):
    for block, ref in enumerate(refs):
        w2_ref[block * ROWS : (block + 1) * ROWS, :] = ref[...]
    w2_ref[BLOCKS * ROWS :, :] = jnp.zeros((WIDE - BLOCKS * ROWS, 3 * D2), BF16)


def prepare_kernel(length_ref, mel_ref, pay_ref):
    clip = lax.broadcasted_iota(jnp.int32, (CLIPS, MEL), 0)
    length = jnp.zeros((CLIPS, MEL), F32)
    for index in range(CLIPS):
        length = jnp.where(clip == index, length_ref[index].astype(F32), length)
    for target in range(HOLDERS):
        pay_ref[target, :CLIPS] = mel_ref[...]
        pay_ref[target, CLIPS] = length.astype(BF16)
        pay_ref[target, CLIPS + 1 :] = jnp.zeros((PAY - CLIPS - 1, 2 * HALF, MEL), BF16)


def columns_kernel(where_ref, weight_ref, bias_ref, w1_ref, b1_ref, picked):
    picked[...] = jnp.zeros_like(picked)
    b1_ref[...] = jnp.zeros_like(b1_ref)
    for block, flip in enumerate((0, 1, 2 * HOLDERS, 2 * HOLDERS + 1)):
        first = (where_ref[3] ^ flip) * ROWS
        start = pl.multiple_of(jnp.minimum((first >> 7) << 7, 16 * ROWS - 2 * LANES), LANES)
        shift = (2 * LANES - (first - start)) & (2 * LANES - 1)
        lanes = slice(block * ROWS, (block + 1) * ROWS)
        window = weight_ref[:, pl.ds(start, 2 * LANES)].astype(F32)
        picked[:, lanes] = pltpu.roll(window, shift, 1)[:, :ROWS]
        window = jnp.broadcast_to(bias_ref[pl.ds(start, 2 * LANES)].reshape(1, 2 * LANES), (8, 2 * LANES))
        b1_ref[:, lanes] = pltpu.roll(window, shift, 1)[0:1, :ROWS]
    w1_ref[...] = picked[...].astype(BF16)


def first_conv(pay_ref, w1_ref, b1_ref, cols_ref, frames_ref):
    sources = pay_ref.shape[0]
    spread = (
        lax.broadcasted_iota(jnp.int32, (STEPS, CLIPS), 0) >> 3
        == lax.broadcasted_iota(jnp.int32, (STEPS, CLIPS), 1)
    ).astype(F32).astype(BF16)
    t = (lax.broadcasted_iota(jnp.int32, (STEPS, LANES), 0) & (HALF - 1)).astype(F32)
    lives_even, lives_odd = [], []
    for source in range(sources):
        rows = slice(source * STEPS, (source + 1) * STEPS)
        length = dot(spread, pay_ref[source, CLIPS])
        frames_ref[source] = pay_ref[source, :CLIPS].astype(F32).reshape(2 * STEPS, MEL)
        live_even, live_odd = 2.0 * t < length, 2.0 * t + 1.0 < length
        even = jnp.where(live_even, frames_ref[source, pl.ds(0, STEPS, 2), :], 0.0)
        odd = jnp.where(live_odd, frames_ref[source, pl.ds(1, STEPS, 2), :], 0.0)
        cols_ref[rows, :LANES] = shift_down(odd).astype(BF16)
        cols_ref[rows, LANES : 2 * LANES] = even.astype(BF16)
        cols_ref[rows, 2 * LANES : 3 * LANES] = odd.astype(BF16)
        cols_ref[rows, 3 * LANES :] = shift_up(even).astype(BF16)
        lives_even.append(jnp.concatenate([live_even] * (WIDE // LANES), axis=1))
        lives_odd.append(jnp.concatenate([live_odd] * (WIDE // LANES), axis=1))
    cols = jnp.concatenate([cols_ref[:, : 3 * LANES], cols_ref[:, LANES:]], axis=0)
    pre = dot(cols, w1_ref[...]) + b1_ref[...]
    half = sources * STEPS
    return pre[:half], pre[half:], jnp.concatenate(lives_even, axis=0), jnp.concatenate(lives_odd, axis=0)


def forward_kernel(
    pay_ref, w1_ref, b1_ref, own_ref, side_ref, far_ref, both_ref, part_ref, w2_ref, cols_ref, frames_ref
):
    @pl.when(pl.program_id(0) == 0)
    def _():
        stack_weights((own_ref, side_ref, far_ref, both_ref), w2_ref)

    pre_even, pre_odd, live_even, live_odd = first_conv(pay_ref, w1_ref, b1_ref, cols_ref, frames_ref)
    odd = jnp.where(live_odd, gelu_value(pre_odd), 0.0)
    total = dot(odd.astype(BF16), w2_ref[:, 2 * D2 :]) + dot(shift_down(odd).astype(BF16), w2_ref[:, :D2])
    even = jnp.where(live_even, gelu_value(pre_even), 0.0)
    total = total + dot(even.astype(BF16), w2_ref[:, D2 : 2 * D2])
    part_ref[...] = total.astype(BF16).reshape(part_ref.shape)


def slope_kernel(
    pay_ref, w1_ref, b1_ref, grad_ref, column_ref, row_ref,
    cols_ref, slope_ref, turned_ref, live_grad_ref, wanted_ref, frames_ref,
):
    pre_even, pre_odd, live_even, live_odd = first_conv(pay_ref, w1_ref, b1_ref, cols_ref, frames_ref)
    value, slope = gelu_both(pre_odd)
    odd = jnp.where(live_odd, value, 0.0)
    slope_ref[1] = jnp.where(live_odd, slope, 0.0)
    turned_ref[0] = shift_down(odd).astype(BF16).T
    turned_ref[2] = odd.astype(BF16).T
    value, slope = gelu_both(pre_even)
    slope_ref[0] = jnp.where(live_even, slope, 0.0)
    turned_ref[1] = jnp.where(live_even, value, 0.0).astype(BF16).T

    @pl.when(pl.program_id(0) == 0)
    def _():
        t = (lax.broadcasted_iota(jnp.int32, (STEPS, 1), 0) & (HALF - 1)).astype(F32)
        length = (column_ref[...] & 31).astype(F32)
        live_grad_ref[...] = jnp.where(2.0 * t < length, grad_ref[...].astype(F32), 0.0).astype(BF16)
        here = lax.broadcasted_iota(jnp.int32, (STEPS, STEPS), 0)
        there = lax.broadcasted_iota(jnp.int32, (STEPS, STEPS), 1)
        owner = row_ref[...] >> 5
        same = ((column_ref[...] >> 5) == owner) & ((here >> 3) < (there >> 3))
        same = same & ((here & (HALF - 1)) == 0)
        rank = jnp.sum(jnp.where(same, 1.0, 0.0), axis=0, keepdims=True)
        place = lax.broadcasted_iota(jnp.int32, (1, STEPS), 1) & (HALF - 1)
        place = (owner * 2 + rank.astype(jnp.int32)) * HALF + place
        wanted = lax.broadcasted_iota(jnp.int32, (SLOTS * HALF, STEPS), 0) == place
        t = (lax.broadcasted_iota(jnp.int32, (1, STEPS), 1) & (HALF - 1)).astype(F32)
        wanted = wanted & (2.0 * t < (row_ref[...] & 31).astype(F32))
        wanted_ref[...] = jnp.where(wanted, 1.0, 0.0).astype(BF16)


def middle_kernel(
    where_ref, part_ref, b2_ref, live_grad_ref, wanted_ref, rep_ref, same_ref, cross_ref, live_grad_here, done
):
    copy = pltpu.make_async_copy(live_grad_ref, live_grad_here, done)
    copy.start()
    pre = part_ref[0].astype(F32)
    for source in range(1, HOLDERS):
        pre = pre + part_ref[source].astype(F32)
    value, slope = gelu_both(pre + b2_ref[...])
    copy.wait()
    second_grad = (live_grad_here[...].astype(F32) * slope).astype(BF16)
    for target in range(HOLDERS):
        rep_ref[target] = second_grad
    placed = dot(wanted_ref[...], value.astype(BF16))
    first = where_ref[2] == 0
    for chip in range(CHIPS):
        for tile in range(D2 // LANES):
            rows, columns = slice(tile * 16, (tile + 1) * 16), slice(tile * LANES, (tile + 1) * LANES)
            left = placed[chip * 32 : chip * 32 + 16, columns]
            right = placed[chip * 32 + 16 : chip * 32 + 32, columns]
            same_ref[chip, rows, :] = jnp.where(first, left, right).astype(BF16)
            cross_ref[chip, rows, :] = jnp.where(first, right, left).astype(BF16)


def backward_kernel(
    where_ref, grad_ref, own_ref, side_ref, far_ref, both_ref, cols_ref, turned_ref, slope_ref, keep_ref, send_ref,
    w2_ref, conv_sum, cols_here, cols_done,
):
    cols_copy = pltpu.make_async_copy(cols_ref, cols_here, cols_done)
    cols_copy.start()
    stack_weights((own_ref, side_ref, far_ref, both_ref), w2_ref)
    mine = where_ref[0]
    grad = grad_ref[...].reshape(HOLDERS * STEPS, D2)
    places = []
    for block in range(BLOCKS):
        places.append((keep_ref if block % 2 == 0 else send_ref, mine if block < 2 else 1 - mine, block * ROWS))

    for tap in range(3):
        conv_sum[...] = dot(turned_ref[tap], grad)
        for out, target, first in places:
            for column in range(D2 // LANES):
                tile = tap * (D2 // LANES) + column
                piece = conv_sum[first : first + ROWS, column * LANES : (column + 1) * LANES]
                out[target, tile // 8, (tile % 8) * ROWS : (tile % 8 + 1) * ROWS, :] = piece.astype(out.dtype)

    even = dot_nt(grad, w2_ref[:, D2 : 2 * D2])
    even = (even * slope_ref[0]).astype(BF16)
    odd = dot_nt(grad, w2_ref[:, 2 * D2 :]) + shift_up(dot_nt(grad, w2_ref[:, :D2]))
    odd = (odd * slope_ref[1]).astype(BF16)
    cols_copy.wait()
    cols = cols_here[...]
    conv_sum[:, : 3 * LANES] = dot_tn(even, cols[:, : 3 * LANES]) + dot_tn(odd, cols[:, LANES:])
    bias1 = jnp.sum(even.astype(F32) + odd.astype(F32), axis=0, keepdims=True)
    bias2 = jnp.sum(grad.astype(F32), axis=0, keepdims=True)
    for out, target, first in places:
        out[target, 1, 7 * ROWS : 8 * ROWS, :] = jnp.zeros((ROWS, LANES), out.dtype)
        biases = [jnp.concatenate([bias1[:, first : first + ROWS], jnp.zeros((1, LANES - ROWS), F32)], axis=1)]
        for tile in range(D2 // LANES):
            biases.append(bias2[:, tile * LANES : (tile + 1) * LANES])
        biases.append(jnp.zeros((16 - len(biases), LANES), F32))
        biases = jnp.concatenate(biases, axis=0).astype(out.dtype)
        for half in range(2):
            for tile in range(3):
                piece = conv_sum[first : first + ROWS, tile * LANES : (tile + 1) * LANES]
                out[target, half, (8 + tile) * ROWS : (9 + tile) * ROWS, :] = piece.astype(out.dtype)
            out[target, half, 11 * ROWS :, :] = biases


def sum_kernel(got_ref, out_ref):
    total = got_ref[0].astype(F32)
    for source in range(1, got_ref.shape[0]):
        total = total + got_ref[source].astype(F32)
    out_ref[...] = total.astype(BF16)


def split_kernel(got_ref, conv2_ref, conv1_ref):
    total = got_ref[0].astype(F32)
    for source in range(1, got_ref.shape[0]):
        total = total + got_ref[source].astype(F32)
    conv2_ref[...] = total[:HALF_ROWS].astype(BF16)
    conv1_ref[...] = total[HALF_ROWS:].astype(BF16)


def pair_kernel(own_ref, other_ref, out_ref):
    out_ref[...] = (own_ref[...].astype(F32) + other_ref[...].astype(F32)).astype(BF16)


def last_kernel(
    where_ref, got_ref, cross_ref, weight_ref, bias1_ref, bias2_ref, packed_ref, whole, biases,
):
    step, core = pl.program_id(0), where_ref[2]
    rows = pl.ds(pl.multiple_of((step + 1) * ROWS, 16), ROWS)
    for chip in range(CHIPS):
        whole[pl.ds(pl.multiple_of((2 * chip + core) * ROWS, 16), ROWS), :] = got_ref[chip, rows, :]
        whole[pl.ds(pl.multiple_of((2 * chip + 1 - core) * ROWS, 16), ROWS), :] = cross_ref[chip, rows, :]
    for block in range(10):
        columns = slice(block * LANES, (block + 1) * LANES)
        weight_ref[:, columns] = whole[columns, :].T.astype(F32)

    @pl.when(step == 0)
    def _():
        for chip in range(CHIPS):
            biases[2 * chip + core] = got_ref[chip, 5 * ROWS :, :].astype(F32)
            biases[2 * chip + 1 - core] = cross_ref[chip, 5 * ROWS :, :].astype(F32)
            left = pl.ds(pl.multiple_of(chip * 32 + 16 * core, 16), 16)
            right = pl.ds(pl.multiple_of(chip * 32 + 16 - 16 * core, 16), 16)
            for tile in range(D2 // LANES):
                columns = slice(tile * LANES, (tile + 1) * LANES)
                packed_ref[left, columns] = got_ref[chip, tile * 16 : (tile + 1) * 16, :]
                packed_ref[right, columns] = cross_ref[chip, 4 * ROWS + tile * 16 : 4 * ROWS + (tile + 1) * 16, :]
        bias1 = jnp.concatenate([biases[source, 0:1, :ROWS] for source in range(16)], axis=1)
        bias1_ref[...] = bias1.reshape(16 * ROWS)
        bias2 = jnp.concatenate([biases[0, 1 + tile : 2 + tile, :] for tile in range(D2 // LANES)], axis=1)
        bias2_ref[...] = bias2.reshape(D2)


def unpack_kernel(where_ref, own_ref, first_ref, second_ref, third_ref, conv2_ref):
    for flip, ref in enumerate((own_ref, first_ref, second_ref, third_ref)):
        for side in range(2):
            for spot in range(2):
                tile = 8 * (where_ref[1] ^ side) + 2 * (where_ref[4] ^ flip) + spot
                rows = slice((2 * side + spot) * ROWS, (2 * side + spot + 1) * ROWS)

                @pl.when(tile < 15)
                def _(ref=ref, rows=rows, tile=tile):
                    lanes = pl.ds(pl.multiple_of(tile * LANES, LANES), LANES)
                    conv2_ref[:, lanes] = ref[rows, :].astype(F32)


def exchange(values, axes):
    return lax.all_to_all(values, axes, split_axis=0, concat_axis=0, tiled=True)


def spread_to(values, count):
    return jnp.broadcast_to(values[None], (count,) + values.shape)


def vmem():
    return pl.BlockSpec(memory_space=pltpu.VMEM)


def params(mib, *semantics):
    return pltpu.CompilerParams(vmem_limit_bytes=mib * MIB, dimension_semantics=semantics or None)


def local(mel, lengths, routes, conv1_weight, conv1_bias, conv2_weight, conv2_bias, out_grad):
    x_hi, y, core = lax.axis_index("xh"), lax.axis_index("y"), lax.axis_index("c")
    where = jnp.stack([x_hi, lax.axis_index("xl"), core, (x_hi * HOLDERS + y) * 2 + core, lax.axis_index("zl")])
    where = where.astype(jnp.int32)

    def shape(*dims, dtype=BF16):
        return jax.ShapeDtypeStruct(dims, dtype)

    def from_hbm(values):
        return pltpu.with_memory_space_constraint(values, pltpu.HBM)

    def in_hbm(*dims, dtype=BF16):
        return pltpu.HBM(dims, dtype)

    pay = pl.pallas_call(
        prepare_kernel,
        in_specs=[pl.BlockSpec(memory_space=pltpu.SMEM), vmem()],
        out_specs=vmem(),
        out_shape=in_hbm(HOLDERS, PAY, 2 * HALF, MEL),
        compiler_params=params(60),
        name="mel_payload",
    )(lengths, mel)
    got_pay = exchange(pay, "y")
    cores = [(0, 1), (1, 0)]
    far_weight = lax.ppermute(conv2_weight, ("xh", "xl"), [(0, 3), (3, 0), (1, 2), (2, 1)])

    w1, b1 = pl.pallas_call(
        columns_kernel,
        in_specs=[pl.BlockSpec(memory_space=pltpu.SMEM), vmem(), vmem()],
        out_specs=[vmem()] * 2,
        out_shape=[shape(3 * MEL, WIDE), shape(1, WIDE, dtype=F32)],
        scratch_shapes=[pltpu.VMEM((3 * MEL, WIDE), F32)],
        compiler_params=params(10),
        name="conv1_columns",
    )(where, conv1_weight, from_hbm(conv1_bias))
    own_weight, place = lax.optimization_barrier((conv2_weight, where))
    far_weight, place = lax.optimization_barrier((far_weight, place))
    weights = [
        conv2_weight,
        lax.ppermute(own_weight, "c", cores),
        far_weight,
        lax.ppermute(far_weight, "c", cores),
    ]

    pair = lambda i: (i, 0, 0)
    pair4 = lambda i: (i, 0, 0, 0)
    rows, some = HOLDERS * STEPS, 2 * STEPS
    frames = (2, 2 * STEPS, MEL)
    pay_spec = pl.BlockSpec((2, PAY, 2 * HALF, MEL), pair4)
    parts = pl.pallas_call(
        forward_kernel,
        grid=(HOLDERS // 2,),
        in_specs=[pay_spec, *[vmem()] * (2 + BLOCKS)],
        out_specs=pl.BlockSpec((2, STEPS, D2), pair),
        out_shape=in_hbm(HOLDERS, STEPS, D2),
        scratch_shapes=[
            pltpu.VMEM((WIDE, 3 * D2), BF16),
            pltpu.VMEM((some, 4 * LANES), BF16),
            pltpu.VMEM(frames, F32),
        ],
        compiler_params=params(20, "arbitrary"),
        name="stem_forward",
    )(got_pay, w1, b1, *weights)

    got_parts = exchange(parts, "y")
    code = jnp.repeat(routes[:, 0] * 32 + lengths, HALF)
    cols, slopes, turned, live_grad, wanted = pl.pallas_call(
        slope_kernel,
        grid=(HOLDERS // 2,),
        in_specs=[pay_spec, *[vmem()] * 5],
        out_specs=[
            pl.BlockSpec((some, 4 * LANES), lambda i: (i, 0)),
            pl.BlockSpec((2, some, WIDE), lambda i: (0, i, 0)),
            pl.BlockSpec((3, WIDE, some), lambda i: (0, 0, i)),
            vmem(),
            vmem(),
        ],
        out_shape=[
            in_hbm(rows, 4 * LANES),
            shape(2, rows, WIDE, dtype=F32),
            shape(3, WIDE, rows),
            in_hbm(STEPS, D2),
            shape(SLOTS * HALF, STEPS),
        ],
        scratch_shapes=[pltpu.VMEM(frames, F32)],
        compiler_params=params(20, "arbitrary"),
        name="stem_slopes",
    )(got_pay, w1, b1, from_hbm(out_grad.reshape(STEPS, D2)), code[:, None], code[None])
    got_parts, slopes, turned = lax.optimization_barrier((got_parts, slopes, turned))
    rep, same, cross = pl.pallas_call(
        middle_kernel,
        in_specs=[pl.BlockSpec(memory_space=pltpu.SMEM), vmem(), vmem(), pl.BlockSpec(memory_space=pl.ANY), vmem()],
        out_specs=[vmem()] * 3,
        out_shape=[shape(HOLDERS, STEPS, D2), shape(CHIPS, ROWS, LANES), shape(CHIPS, ROWS, LANES)],
        scratch_shapes=[pltpu.VMEM((STEPS, D2), BF16), pltpu.SemaphoreType.DMA],
        compiler_params=params(10),
        name="stem_middle",
    )(where, got_parts, conv2_bias[None], from_hbm(live_grad), wanted)
    got_grad = exchange(rep, "y")

    keep, send = pl.pallas_call(
        backward_kernel,
        in_specs=[
            pl.BlockSpec(memory_space=pltpu.SMEM),
            *[vmem()] * (1 + BLOCKS),
            pl.BlockSpec(memory_space=pl.ANY),
            vmem(),
            vmem(),
        ],
        out_specs=[vmem()] * 2,
        out_shape=[shape(2, 2, PACK, LANES, dtype=F32), shape(2, 2, PACK, LANES)],
        scratch_shapes=[
            pltpu.VMEM((WIDE, 3 * D2), BF16),
            pltpu.VMEM((WIDE, D2), F32),
            pltpu.VMEM((rows, 4 * LANES), BF16),
            pltpu.SemaphoreType.DMA,
        ],
        compiler_params=params(32),
        name="stem_backward",
    )(where, got_grad, *weights, from_hbm(cols), turned, slopes)
    got = lax.ppermute(send, "c", cores)
    quarters = exchange((keep + got.astype(F32)).astype(BF16).reshape(4, PACK, LANES), ("xh", "xl"))

    def with_other(values, axis, flip):
        return pl.pallas_call(
            pair_kernel,
            in_specs=[vmem()] * 2,
            out_specs=vmem(),
            out_shape=shape(*values.shape),
            compiler_params=params(8),
            name="gradient_pair",
        )(values, lax.ppermute(values, axis, [(i, i ^ flip) for i in range(4)]))

    conv2, conv1 = pl.pallas_call(
        split_kernel,
        in_specs=[vmem()],
        out_specs=[vmem()] * 2,
        out_shape=[shape(HALF_ROWS, LANES), shape(PACK - HALF_ROWS, LANES)],
        compiler_params=params(8),
        name="gradient_sum",
    )(quarters)
    quarter = HALF_ROWS // 4
    conv2 = exchange(conv2.reshape(4, quarter, LANES), "zl")
    conv2 = pl.pallas_call(
        sum_kernel,
        in_specs=[vmem()],
        out_specs=vmem(),
        out_shape=shape(quarter, LANES),
        compiler_params=params(8),
        name="gradient_sum",
    )(conv2)
    conv1 = with_other(with_other(conv1, "zl", 1), "zl", 2)
    conv2 = with_other(with_other(conv2, "zh", 1), "zh", 3)
    conv1 = with_other(with_other(conv1, "zh", 1), "zh", 3)
    conv2 = jnp.concatenate([conv2, lax.ppermute(conv2, "xl", [(0, 1), (1, 0)])], axis=0)
    conv2, conv1 = lax.optimization_barrier((conv2, conv1))
    others = [lax.ppermute(conv2, "zl", [(i, i ^ flip) for i in range(4)]) for flip in (1, 2, 3)]
    conv1 = spread_to(conv1, CHIPS)
    got = exchange(jnp.concatenate([same, conv1[:, : 3 * ROWS], cross, conv1[:, 3 * ROWS :]], axis=1), ("xh", "y"))
    got, *others = lax.optimization_barrier((got, *others))
    got_cross = lax.ppermute(got, "c", cores)
    conv2_rows_grad = pl.pallas_call(
        unpack_kernel,
        in_specs=[pl.BlockSpec(memory_space=pltpu.SMEM), *[vmem()] * 4],
        out_specs=vmem(),
        out_shape=in_hbm(ROWS, 3 * D2, dtype=F32),
        compiler_params=params(8),
        name="conv2_unpack",
    )(where, conv2, *others)
    weight_grad, bias_grad, second_bias_grad, packed = pl.pallas_call(
        last_kernel,
        grid=(3,),
        in_specs=[
            pl.BlockSpec(memory_space=pltpu.SMEM),
            vmem(),
            vmem(),
        ],
        out_specs=[
            pl.BlockSpec((LANES, 16 * ROWS), lambda i: (i, 0)),
            pl.BlockSpec((16 * ROWS,), lambda i: (0,)),
            pl.BlockSpec((D2,), lambda i: (0,)),
            pl.BlockSpec((SLOTS * HALF, D2), lambda i: (0, 0)),
        ],
        out_shape=[
            shape(3 * MEL, 16 * ROWS, dtype=F32),
            shape(16 * ROWS, dtype=F32),
            shape(D2, dtype=F32),
            shape(SLOTS * HALF, D2),
        ],
        scratch_shapes=[pltpu.VMEM((16 * ROWS, LANES), BF16), pltpu.VMEM((16, 16, LANES), F32)],
        compiler_params=params(16, "arbitrary"),
        name="gradient_unpack",
    )(where, got, got_cross)
    return packed.reshape(SLOTS, HALF, D2), weight_grad, bias_grad, second_bias_grad, conv2_rows_grad


def solution(mesh):
    fine = Mesh(mesh.devices.reshape(2, 4, 2, 4, 4, 2), ALL_AXES)
    placed = (
        P(ALL_AXES, None, None),
        P(ALL_AXES),
        P(ALL_AXES, None),
        P(),
        P(),
        P(ENC, None),
        P(),
        P(ALL_AXES, None, None),
    )
    return jax.shard_map(
        local,
        mesh=fine,
        in_specs=placed,
        out_specs=(P(ALL_AXES, None, None), P(), P(), P(), P(ENC, None)),
        check_vma=False,
    )
```

```python
import functools

import jax
import jax.numpy as jnp
from jax import lax
from jax.experimental import pallas as pl
from jax.experimental.pallas import tpu as pltpu
from jax.sharding import Mesh
from jax.sharding import PartitionSpec as P

inv_root_two = 0.7071067811865476
inv_root_tau = 0.3989422804014327

MEL = 128
D2 = 640
ROWS = 80
LANES = 128
HOLDERS = 4
BLOCKS = 4
WIDE = 384
CLIPS = 16
HALF = 8
STEPS = CLIPS * HALF
SLOTS = 2 * CLIPS
PAY = 26
CHIPS = 8
PACK = 896
HALF_ROWS = 8 * ROWS
MIB = 1024 * 1024
ALL_AXES = ("xh", "y", "c", "zh", "zl", "xl")
ENC = ("xh", "y", "c")
F32 = jnp.float32
BF16 = jnp.bfloat16


def gelu_value(values):
    return values * (0.5 * (1.0 + lax.erf(values * inv_root_two)))


def gelu_both(values):
    cdf = 0.5 * (1.0 + lax.erf(values * inv_root_two))
    return values * cdf, cdf + values * jnp.exp(-0.5 * values * values) * inv_root_tau


def shift_down(values):
    rows, width = values.shape
    t = lax.broadcasted_iota(jnp.int32, (rows, width), 0) & (HALF - 1)
    clips = values.reshape(rows // HALF, HALF, width)
    moved = pltpu.roll(clips, 1, 1).reshape(rows, width)
    return jnp.where(t == 0, 0.0, moved)


def shift_up(values):
    rows, width = values.shape
    t = lax.broadcasted_iota(jnp.int32, (rows, width), 0) & (HALF - 1)
    clips = values.reshape(rows // HALF, HALF, width)
    moved = pltpu.roll(clips, HALF - 1, 1).reshape(rows, width)
    return jnp.where(t == HALF - 1, 0.0, moved)


def dot(left, right):
    return jnp.dot(left, right, preferred_element_type=F32)


def dot_nt(left, right):
    return lax.dot_general(left, right, (((1,), (1,)), ((), ())), preferred_element_type=F32)


def dot_tn(left, right):
    return lax.dot_general(left, right, (((0,), (0,)), ((), ())), preferred_element_type=F32)


def prepare_kernel(length_ref, mel_ref, pay_ref, slots, mel_done, pay_done):
    mel_copy = pltpu.make_async_copy(mel_ref, slots.at[:CLIPS], mel_done)
    mel_copy.start()
    clip = lax.broadcasted_iota(jnp.int32, (CLIPS, MEL), 0)
    length = jnp.zeros((CLIPS, MEL), F32)
    for index in range(CLIPS):
        length = jnp.where(clip == index, length_ref[index].astype(F32), length)
    for slot in range(CLIPS, PAY):
        slots[slot] = length.astype(BF16)
    mel_copy.wait()
    copies = [pltpu.make_async_copy(slots, pay_ref.at[target], pay_done.at[target]) for target in range(HOLDERS)]
    for copy in copies:
        copy.start()
    for copy in copies:
        copy.wait()


def pick_columns(where_ref, weight_ref, bias_ref, w1_ref, b1_ref, picked):
    picked[...] = jnp.zeros_like(picked)
    b1_ref[...] = jnp.zeros_like(b1_ref)
    for block, flip in enumerate((0, 1, 2 * HOLDERS, 2 * HOLDERS + 1)):
        first = (where_ref[3] ^ flip) * ROWS
        start = pl.multiple_of(jnp.minimum((first >> 7) << 7, 16 * ROWS - 2 * LANES), LANES)
        shift = (2 * LANES - (first - start)) & (2 * LANES - 1)
        lanes = slice(block * ROWS, (block + 1) * ROWS)
        window = weight_ref[:, pl.ds(start, 2 * LANES)].astype(F32)
        picked[:, lanes] = pltpu.roll(window, shift, 1)[:, :ROWS]
        window = jnp.broadcast_to(bias_ref[pl.ds(start, 2 * LANES)].reshape(1, 2 * LANES), (8, 2 * LANES))
        b1_ref[:, lanes] = pltpu.roll(window, shift, 1)[0:1, :ROWS]
    w1_ref[...] = picked[...].astype(BF16)


def first_conv(pay_ref, w1_ref, b1_ref, cols_ref, frames_ref):
    sources = pay_ref.shape[0]
    spread = (
        lax.broadcasted_iota(jnp.int32, (STEPS, CLIPS), 0) >> 3
        == lax.broadcasted_iota(jnp.int32, (STEPS, CLIPS), 1)
    ).astype(F32).astype(BF16)
    t = (lax.broadcasted_iota(jnp.int32, (STEPS, LANES), 0) & (HALF - 1)).astype(F32)
    lives_even, lives_odd = [], []
    for source in range(sources):
        rows = slice(source * STEPS, (source + 1) * STEPS)
        length = dot(spread, pay_ref[source, CLIPS])
        frames_ref[source] = pay_ref[source, :CLIPS].astype(F32).reshape(2 * STEPS, MEL)
        live_even, live_odd = 2.0 * t < length, 2.0 * t + 1.0 < length
        even = jnp.where(live_even, frames_ref[source, pl.ds(0, STEPS, 2), :], 0.0)
        odd = jnp.where(live_odd, frames_ref[source, pl.ds(1, STEPS, 2), :], 0.0)
        cols_ref[rows, :LANES] = shift_down(odd).astype(BF16)
        cols_ref[rows, LANES : 2 * LANES] = even.astype(BF16)
        cols_ref[rows, 2 * LANES : 3 * LANES] = odd.astype(BF16)
        cols_ref[rows, 3 * LANES :] = shift_up(even).astype(BF16)
        lives_even.append(jnp.concatenate([live_even] * (WIDE // LANES), axis=1))
        lives_odd.append(jnp.concatenate([live_odd] * (WIDE // LANES), axis=1))
    cols = jnp.concatenate([cols_ref[:, : 3 * LANES], cols_ref[:, LANES:]], axis=0)
    pre = dot(cols, w1_ref[...]) + b1_ref[...]
    half = sources * STEPS
    return pre[:half], pre[half:], jnp.concatenate(lives_even, axis=0), jnp.concatenate(lives_odd, axis=0)


def forward_kernel(
    where_ref, pay_ref, weight_ref, bias_ref, own_ref, side_ref, far_ref, both_ref, part_ref,
    w2_ref, cols_ref, frames_ref, w1_ref, b1_ref, picked, own_done,
):
    own_copy = pltpu.make_async_copy(own_ref, w2_ref.at[:ROWS], own_done)

    @pl.when(pl.program_id(0) == 0)
    def _():
        own_copy.start()
        pick_columns(where_ref, weight_ref, bias_ref, w1_ref, b1_ref, picked)
        for block, ref in enumerate((side_ref, far_ref, both_ref)):
            w2_ref[(block + 1) * ROWS : (block + 2) * ROWS, :] = ref[...]
        w2_ref[BLOCKS * ROWS :, :] = jnp.zeros((WIDE - BLOCKS * ROWS, 3 * D2), BF16)
        own_copy.wait()

    pre_even, pre_odd, live_even, live_odd = first_conv(pay_ref, w1_ref, b1_ref, cols_ref, frames_ref)
    odd = jnp.where(live_odd, gelu_value(pre_odd), 0.0)
    total = dot(odd.astype(BF16), w2_ref[:, 2 * D2 :]) + dot(shift_down(odd).astype(BF16), w2_ref[:, :D2])
    even = jnp.where(live_even, gelu_value(pre_even), 0.0)
    total = total + dot(even.astype(BF16), w2_ref[:, D2 : 2 * D2])
    part_ref[...] = total.astype(BF16).reshape(part_ref.shape)


def slope_kernel(
    where_ref, pay_ref, weight_ref, bias_ref, grad_ref, column_ref, row_ref,
    cols_ref, slope_ref, turned_ref, live_grad_ref, wanted_ref, frames_ref, w1_ref, b1_ref, picked,
):
    @pl.when(pl.program_id(0) == 0)
    def _():
        pick_columns(where_ref, weight_ref, bias_ref, w1_ref, b1_ref, picked)

    pre_even, pre_odd, live_even, live_odd = first_conv(pay_ref, w1_ref, b1_ref, cols_ref, frames_ref)
    value, slope = gelu_both(pre_odd)
    odd = jnp.where(live_odd, value, 0.0)
    slope_ref[1] = jnp.where(live_odd, slope, 0.0)
    turned_ref[0] = shift_down(odd).astype(BF16).T
    turned_ref[2] = odd.astype(BF16).T
    value, slope = gelu_both(pre_even)
    slope_ref[0] = jnp.where(live_even, slope, 0.0)
    turned_ref[1] = jnp.where(live_even, value, 0.0).astype(BF16).T

    @pl.when(pl.program_id(0) == 0)
    def _():
        t = (lax.broadcasted_iota(jnp.int32, (STEPS, 1), 0) & (HALF - 1)).astype(F32)
        length = (column_ref[...] & 31).astype(F32)
        live_grad_ref[...] = jnp.where(2.0 * t < length, grad_ref[...].astype(F32), 0.0).astype(BF16)
        here = lax.broadcasted_iota(jnp.int32, (STEPS, STEPS), 0)
        there = lax.broadcasted_iota(jnp.int32, (STEPS, STEPS), 1)
        owner = row_ref[...] >> 5
        same = ((column_ref[...] >> 5) == owner) & ((here >> 3) < (there >> 3))
        same = same & ((here & (HALF - 1)) == 0)
        rank = jnp.sum(jnp.where(same, 1.0, 0.0), axis=0, keepdims=True)
        place = lax.broadcasted_iota(jnp.int32, (1, STEPS), 1) & (HALF - 1)
        place = (owner * 2 + rank.astype(jnp.int32)) * HALF + place
        wanted = lax.broadcasted_iota(jnp.int32, (SLOTS * HALF, STEPS), 0) == place
        t = (lax.broadcasted_iota(jnp.int32, (1, STEPS), 1) & (HALF - 1)).astype(F32)
        wanted = wanted & (2.0 * t < (row_ref[...] & 31).astype(F32))
        wanted_ref[...] = jnp.where(wanted, 1.0, 0.0).astype(BF16)


def middle_kernel(
    where_ref, part_ref, b2_ref, live_grad_ref, wanted_ref, rep_ref, same_ref, cross_ref, live_grad_here, done
):
    copy = pltpu.make_async_copy(live_grad_ref, live_grad_here, done)
    copy.start()
    pre = part_ref[0].astype(F32)
    for source in range(1, HOLDERS):
        pre = pre + part_ref[source].astype(F32)
    value, slope = gelu_both(pre + b2_ref[...])
    copy.wait()
    second_grad = (live_grad_here[...].astype(F32) * slope).astype(BF16)
    for target in range(HOLDERS):
        rep_ref[target] = second_grad
    placed = dot(wanted_ref[...], value.astype(BF16))
    first = where_ref[2] == 0
    for chip in range(CHIPS):
        for tile in range(D2 // LANES):
            rows, columns = slice(tile * 16, (tile + 1) * 16), slice(tile * LANES, (tile + 1) * LANES)
            left = placed[chip * 32 : chip * 32 + 16, columns]
            right = placed[chip * 32 + 16 : chip * 32 + 32, columns]
            same_ref[chip, rows, :] = jnp.where(first, left, right).astype(BF16)
            cross_ref[chip, rows, :] = jnp.where(first, right, left).astype(BF16)


def backward_kernel(
    where_ref, grad_ref, own_ref, side_ref, far_ref, both_ref, cols_ref, turned_ref, slope_ref, keep_ref, send_ref,
    w2_ref, conv_sum, cols_here, cols_done, both_done,
):
    cols_copy = pltpu.make_async_copy(cols_ref, cols_here, cols_done)
    cols_copy.start()
    both_copy = pltpu.make_async_copy(both_ref, w2_ref.at[3 * ROWS : 4 * ROWS], both_done)
    both_copy.start()
    for block, ref in enumerate((own_ref, side_ref, far_ref)):
        w2_ref[block * ROWS : (block + 1) * ROWS, :] = ref[...]
    w2_ref[BLOCKS * ROWS :, :] = jnp.zeros((WIDE - BLOCKS * ROWS, 3 * D2), BF16)
    mine = where_ref[0]
    grad = grad_ref[...].reshape(HOLDERS * STEPS, D2)
    places = []
    for block in range(BLOCKS):
        places.append((keep_ref if block % 2 == 0 else send_ref, mine if block < 2 else 1 - mine, block * ROWS))

    for tap in range(3):
        conv_sum[...] = dot(turned_ref[tap], grad)
        for out, target, first in places:
            for column in range(D2 // LANES):
                tile = tap * (D2 // LANES) + column
                piece = conv_sum[first : first + ROWS, column * LANES : (column + 1) * LANES]
                out[target, tile // 8, (tile % 8) * ROWS : (tile % 8 + 1) * ROWS, :] = piece.astype(out.dtype)

    both_copy.wait()
    even = dot_nt(grad, w2_ref[:, D2 : 2 * D2])
    even = (even * slope_ref[0]).astype(BF16)
    odd = dot_nt(grad, w2_ref[:, 2 * D2 :]) + shift_up(dot_nt(grad, w2_ref[:, :D2]))
    odd = (odd * slope_ref[1]).astype(BF16)
    cols_copy.wait()
    cols = cols_here[...]
    conv_sum[:, : 3 * LANES] = dot_tn(even, cols[:, : 3 * LANES]) + dot_tn(odd, cols[:, LANES:])
    bias1 = jnp.sum(even.astype(F32) + odd.astype(F32), axis=0, keepdims=True)
    bias2 = jnp.sum(grad.astype(F32), axis=0, keepdims=True)
    for out, target, first in places:
        out[target, 1, 7 * ROWS : 8 * ROWS, :] = jnp.zeros((ROWS, LANES), out.dtype)
        biases = [jnp.concatenate([bias1[:, first : first + ROWS], jnp.zeros((1, LANES - ROWS), F32)], axis=1)]
        for tile in range(D2 // LANES):
            biases.append(bias2[:, tile * LANES : (tile + 1) * LANES])
        biases.append(jnp.zeros((16 - len(biases), LANES), F32))
        biases = jnp.concatenate(biases, axis=0).astype(out.dtype)
        for half in range(2):
            for tile in range(3):
                piece = conv_sum[first : first + ROWS, tile * LANES : (tile + 1) * LANES]
                out[target, half, (8 + tile) * ROWS : (9 + tile) * ROWS, :] = piece.astype(out.dtype)
            out[target, half, 11 * ROWS :, :] = biases


def sum_kernel(got_ref, out_ref):
    total = got_ref[0].astype(F32)
    for source in range(1, got_ref.shape[0]):
        total = total + got_ref[source].astype(F32)
    total = total.astype(BF16)
    if len(out_ref.shape) == 2:
        out_ref[...] = total
    else:
        for target in range(out_ref.shape[0]):
            out_ref[target] = total


def pair_kernel(own_ref, other_ref, out_ref):
    total = (own_ref[...].astype(F32) + other_ref[...].astype(F32)).astype(BF16)
    if len(out_ref.shape) == 2:
        out_ref[...] = total
    else:
        for target in range(out_ref.shape[0]):
            out_ref[target] = total


def last_kernel(
    where_ref, got_ref, cross_ref, weight_ref, bias1_ref, bias2_ref, packed_ref, whole, biases,
):
    step, core = pl.program_id(0), where_ref[2]
    rows = pl.ds(pl.multiple_of((step + 1) * ROWS, 16), ROWS)
    for chip in range(CHIPS):
        whole[pl.ds(pl.multiple_of((2 * chip + core) * ROWS, 16), ROWS), :] = got_ref[chip, rows, :]
        whole[pl.ds(pl.multiple_of((2 * chip + 1 - core) * ROWS, 16), ROWS), :] = cross_ref[chip, rows, :]
    for block in range(10):
        columns = slice(block * LANES, (block + 1) * LANES)
        weight_ref[:, columns] = whole[columns, :].T.astype(F32)

    @pl.when(step == 0)
    def _():
        for chip in range(CHIPS):
            biases[2 * chip + core] = got_ref[chip, 5 * ROWS :, :].astype(F32)
            biases[2 * chip + 1 - core] = cross_ref[chip, 5 * ROWS :, :].astype(F32)
            left = pl.ds(pl.multiple_of(chip * 32 + 16 * core, 16), 16)
            right = pl.ds(pl.multiple_of(chip * 32 + 16 - 16 * core, 16), 16)
            for tile in range(D2 // LANES):
                columns = slice(tile * LANES, (tile + 1) * LANES)
                packed_ref[left, columns] = got_ref[chip, tile * 16 : (tile + 1) * 16, :]
                packed_ref[right, columns] = cross_ref[chip, 4 * ROWS + tile * 16 : 4 * ROWS + (tile + 1) * 16, :]
        bias1 = jnp.concatenate([biases[source, 0:1, :ROWS] for source in range(16)], axis=1)
        bias1_ref[...] = bias1.reshape(16 * ROWS)
        bias2 = jnp.concatenate([biases[0, 1 + tile : 2 + tile, :] for tile in range(D2 // LANES)], axis=1)
        bias2_ref[...] = bias2.reshape(D2)


def unpack_kernel(where_ref, own_ref, other_ref, conv2_ref):
    lower = where_ref[1] == 0
    for tile in range(15):
        half, spot = tile // 8, tile % 8
        rows = slice(spot * ROWS, (spot + 1) * ROWS)
        own, other = own_ref[rows, :].astype(F32), other_ref[rows, :].astype(F32)
        picked = jnp.where(lower, own, other) if half == 0 else jnp.where(lower, other, own)
        conv2_ref[:, tile * LANES : (tile + 1) * LANES] = picked


def exchange(values, axes):
    return lax.all_to_all(values, axes, split_axis=0, concat_axis=0, tiled=True)


def spread_to(values, count):
    return jnp.broadcast_to(values[None], (count,) + values.shape)


def vmem():
    return pl.BlockSpec(memory_space=pltpu.VMEM)


def params(mib, *semantics):
    return pltpu.CompilerParams(vmem_limit_bytes=mib * MIB, dimension_semantics=semantics or None)


def local(mel, lengths, routes, conv1_weight, conv1_bias, conv2_weight, conv2_bias, out_grad):
    x_hi, y, core = lax.axis_index("xh"), lax.axis_index("y"), lax.axis_index("c")
    where = jnp.stack([x_hi, lax.axis_index("xl"), core, (x_hi * HOLDERS + y) * 2 + core]).astype(jnp.int32)

    def shape(*dims, dtype=BF16):
        return jax.ShapeDtypeStruct(dims, dtype)

    def from_hbm(values):
        return pltpu.with_memory_space_constraint(values, pltpu.HBM)

    def in_hbm(*dims, dtype=BF16):
        return pltpu.HBM(dims, dtype)

    pay = pl.pallas_call(
        prepare_kernel,
        in_specs=[pl.BlockSpec(memory_space=pltpu.SMEM), pl.BlockSpec(memory_space=pl.ANY)],
        out_specs=pl.BlockSpec(memory_space=pl.ANY),
        out_shape=in_hbm(HOLDERS, PAY, 2 * HALF, MEL),
        scratch_shapes=[
            pltpu.VMEM((PAY, 2 * HALF, MEL), BF16),
            pltpu.SemaphoreType.DMA,
            pltpu.SemaphoreType.DMA((HOLDERS,)),
        ],
        compiler_params=params(60),
        name="mel_payload",
    )(lengths, from_hbm(mel))
    got_pay = exchange(pay, "y")
    cores = [(0, 1), (1, 0)]
    far_weight = lax.ppermute(conv2_weight, ("xh", "xl"), [(0, 3), (3, 0), (1, 2), (2, 1)])

    own_weight, place = lax.optimization_barrier((conv2_weight, where))
    far_weight, place = lax.optimization_barrier((far_weight, place))
    weights = [
        conv2_weight,
        lax.ppermute(own_weight, "c", cores),
        far_weight,
        lax.ppermute(far_weight, "c", cores),
    ]

    pair = lambda i: (i, 0, 0)
    pair4 = lambda i: (i, 0, 0, 0)
    rows, some = HOLDERS * STEPS, 2 * STEPS
    frames = (2, 2 * STEPS, MEL)
    pay_spec = pl.BlockSpec((2, PAY, 2 * HALF, MEL), pair4)
    smem = pl.BlockSpec(memory_space=pltpu.SMEM)
    columns = [
        pltpu.VMEM((3 * MEL, WIDE), BF16),
        pltpu.VMEM((1, WIDE), F32),
        pltpu.VMEM((3 * MEL, WIDE), F32),
    ]
    parts = pl.pallas_call(
        forward_kernel,
        grid=(HOLDERS // 2,),
        in_specs=[smem, pay_spec, vmem(), vmem(), pl.BlockSpec(memory_space=pl.ANY), *[vmem()] * (BLOCKS - 1)],
        out_specs=pl.BlockSpec((2, STEPS, D2), pair),
        out_shape=in_hbm(HOLDERS, STEPS, D2),
        scratch_shapes=[
            pltpu.VMEM((WIDE, 3 * D2), BF16),
            pltpu.VMEM((some, 4 * LANES), BF16),
            pltpu.VMEM(frames, F32),
            *columns,
            pltpu.SemaphoreType.DMA,
        ],
        compiler_params=params(20, "arbitrary"),
        name="stem_forward",
    )(where, got_pay, conv1_weight, from_hbm(conv1_bias), from_hbm(conv2_weight), *weights[1:])

    got_parts = exchange(parts, "y")
    code = jnp.repeat(routes[:, 0] * 32 + lengths, HALF)
    cols, slopes, turned, live_grad, wanted = pl.pallas_call(
        slope_kernel,
        grid=(HOLDERS // 2,),
        in_specs=[smem, pay_spec, *[vmem()] * 5],
        out_specs=[
            pl.BlockSpec((some, 4 * LANES), lambda i: (i, 0)),
            pl.BlockSpec((2, some, WIDE), lambda i: (0, i, 0)),
            pl.BlockSpec((3, WIDE, some), lambda i: (0, 0, i)),
            vmem(),
            vmem(),
        ],
        out_shape=[
            in_hbm(rows, 4 * LANES),
            shape(2, rows, WIDE, dtype=F32),
            shape(3, WIDE, rows),
            in_hbm(STEPS, D2),
            shape(SLOTS * HALF, STEPS),
        ],
        scratch_shapes=[pltpu.VMEM(frames, F32), *columns],
        compiler_params=params(20, "arbitrary"),
        name="stem_slopes",
    )(where, got_pay, from_hbm(conv1_weight), from_hbm(conv1_bias), from_hbm(out_grad.reshape(STEPS, D2)), code[:, None], code[None])
    got_parts, slopes, turned = lax.optimization_barrier((got_parts, slopes, turned))
    rep, same, cross = pl.pallas_call(
        middle_kernel,
        in_specs=[pl.BlockSpec(memory_space=pltpu.SMEM), vmem(), vmem(), pl.BlockSpec(memory_space=pl.ANY), vmem()],
        out_specs=[vmem()] * 3,
        out_shape=[shape(HOLDERS, STEPS, D2), shape(CHIPS, ROWS, LANES), shape(CHIPS, ROWS, LANES)],
        scratch_shapes=[pltpu.VMEM((STEPS, D2), BF16), pltpu.SemaphoreType.DMA],
        compiler_params=params(10),
        name="stem_middle",
    )(where, got_parts, conv2_bias[None], from_hbm(live_grad), wanted)
    got_grad = exchange(rep, "y")

    keep, send = pl.pallas_call(
        backward_kernel,
        in_specs=[
            pl.BlockSpec(memory_space=pltpu.SMEM),
            *[vmem()] * BLOCKS,
            pl.BlockSpec(memory_space=pl.ANY),
            pl.BlockSpec(memory_space=pl.ANY),
            vmem(),
            vmem(),
        ],
        out_specs=[vmem()] * 2,
        out_shape=[shape(2, 2, PACK, LANES, dtype=F32), shape(2, 2, PACK, LANES)],
        scratch_shapes=[
            pltpu.VMEM((WIDE, 3 * D2), BF16),
            pltpu.VMEM((WIDE, D2), F32),
            pltpu.VMEM((rows, 4 * LANES), BF16),
            pltpu.SemaphoreType.DMA,
            pltpu.SemaphoreType.DMA,
        ],
        compiler_params=params(32),
        name="stem_backward",
    )(where, got_grad, *weights[:3], from_hbm(weights[3]), from_hbm(cols), turned, slopes)
    got = lax.ppermute(send, "c", cores)
    quarters = exchange((keep + got.astype(F32)).astype(BF16).reshape(4, PACK, LANES), ("xh", "xl"))

    def summed(values, *dims):
        return pl.pallas_call(
            sum_kernel,
            in_specs=[vmem()],
            out_specs=vmem(),
            out_shape=shape(*dims),
            compiler_params=params(8),
            name="gradient_sum",
        )(values)

    half = summed(quarters, PACK, LANES)
    quarter = PACK // 4
    near = summed(exchange(half.reshape(4, quarter, LANES), "zl"), quarter, LANES)

    def with_group(values, flip, *dims):
        return pl.pallas_call(
            pair_kernel,
            in_specs=[vmem()] * 2,
            out_specs=vmem(),
            out_shape=shape(*dims),
            compiler_params=params(8),
            name="gradient_pair",
        )(values, lax.ppermute(values, "zh", [(i, i ^ flip) for i in range(4)]))

    far = with_group(with_group(near, 1, quarter, LANES), 3, 4, quarter, LANES)
    half = exchange(far, "zl").reshape(PACK, LANES)
    own = half[:HALF_ROWS]
    other = lax.ppermute(own, "xl", [(0, 1), (1, 0)])
    conv1 = spread_to(half[HALF_ROWS:], CHIPS)
    got = exchange(jnp.concatenate([same, conv1[:, : 3 * ROWS], cross, conv1[:, 3 * ROWS :]], axis=1), ("xh", "y"))
    got, other = lax.optimization_barrier((got, other))
    got_cross = lax.ppermute(got, "c", cores)
    conv2_rows_grad = pl.pallas_call(
        unpack_kernel,
        in_specs=[pl.BlockSpec(memory_space=pltpu.SMEM), vmem(), vmem()],
        out_specs=vmem(),
        out_shape=in_hbm(ROWS, 3 * D2, dtype=F32),
        compiler_params=params(8),
        name="conv2_unpack",
    )(where, own, other)
    weight_grad, bias_grad, second_bias_grad, packed = pl.pallas_call(
        last_kernel,
        grid=(3,),
        in_specs=[
            pl.BlockSpec(memory_space=pltpu.SMEM),
            vmem(),
            vmem(),
        ],
        out_specs=[
            pl.BlockSpec((LANES, 16 * ROWS), lambda i: (i, 0)),
            pl.BlockSpec((16 * ROWS,), lambda i: (0,)),
            pl.BlockSpec((D2,), lambda i: (0,)),
            pl.BlockSpec((SLOTS * HALF, D2), lambda i: (0, 0)),
        ],
        out_shape=[
            shape(3 * MEL, 16 * ROWS, dtype=F32),
            shape(16 * ROWS, dtype=F32),
            shape(D2, dtype=F32),
            shape(SLOTS * HALF, D2),
        ],
        scratch_shapes=[pltpu.VMEM((16 * ROWS, LANES), BF16), pltpu.VMEM((16, 16, LANES), F32)],
        compiler_params=params(16, "arbitrary"),
        name="gradient_unpack",
    )(where, got, got_cross)
    return packed.reshape(SLOTS, HALF, D2), weight_grad, bias_grad, second_bias_grad, conv2_rows_grad


def solution(mesh):
    fine = Mesh(mesh.devices.reshape(2, 4, 2, 4, 4, 2), ALL_AXES)
    placed = (
        P(ALL_AXES, None, None),
        P(ALL_AXES),
        P(ALL_AXES, None),
        P(),
        P(),
        P(ENC, None),
        P(),
        P(ALL_AXES, None, None),
    )
    return jax.shard_map(
        local,
        mesh=fine,
        in_specs=placed,
        out_specs=(P(ALL_AXES, None, None), P(), P(), P(), P(ENC, None)),
        check_vma=False,
    )
```

```python
import functools

import jax
import jax.numpy as jnp
from jax import lax
from jax.experimental import pallas as pl
from jax.experimental.pallas import tpu as pltpu
from jax.sharding import Mesh
from jax.sharding import PartitionSpec as P

inv_root_two = 0.7071067811865476
inv_root_tau = 0.3989422804014327

MEL = 128
D2 = 640
ROWS = 80
LANES = 128
HOLDERS = 4
BLOCKS = 4
WIDE = 384
CLIPS = 16
HALF = 8
STEPS = CLIPS * HALF
SLOTS = 2 * CLIPS
PAY = 26
CHIPS = 8
PACK = 896
HALF_ROWS = 8 * ROWS
MIB = 1024 * 1024
ALL_AXES = ("xh", "y", "c", "zh", "zl", "xl")
ENC = ("xh", "y", "c")
F32 = jnp.float32
BF16 = jnp.bfloat16


def gelu_value(values):
    return values * (0.5 * (1.0 + lax.erf(values * inv_root_two)))


def gelu_both(values):
    cdf = 0.5 * (1.0 + lax.erf(values * inv_root_two))
    return values * cdf, cdf + values * jnp.exp(-0.5 * values * values) * inv_root_tau


def shift_down(values):
    rows, width = values.shape
    t = lax.broadcasted_iota(jnp.int32, (rows, width), 0) & (HALF - 1)
    clips = values.reshape(rows // HALF, HALF, width)
    moved = pltpu.roll(clips, 1, 1).reshape(rows, width)
    return jnp.where(t == 0, 0.0, moved)


def shift_up(values):
    rows, width = values.shape
    t = lax.broadcasted_iota(jnp.int32, (rows, width), 0) & (HALF - 1)
    clips = values.reshape(rows // HALF, HALF, width)
    moved = pltpu.roll(clips, HALF - 1, 1).reshape(rows, width)
    return jnp.where(t == HALF - 1, 0.0, moved)


def dot(left, right):
    return jnp.dot(left, right, preferred_element_type=F32)


def dot_nt(left, right):
    return lax.dot_general(left, right, (((1,), (1,)), ((), ())), preferred_element_type=F32)


def dot_tn(left, right):
    return lax.dot_general(left, right, (((0,), (0,)), ((), ())), preferred_element_type=F32)


def stack_weights(refs, w2_ref):
    for block, ref in enumerate(refs):
        w2_ref[block * ROWS : (block + 1) * ROWS, :] = ref[...]
    w2_ref[BLOCKS * ROWS :, :] = jnp.zeros((WIDE - BLOCKS * ROWS, 3 * D2), BF16)


def prepare_kernel(length_ref, mel_ref, pay_ref):
    clip = lax.broadcasted_iota(jnp.int32, (CLIPS, MEL), 0)
    length = jnp.zeros((CLIPS, MEL), F32)
    for index in range(CLIPS):
        length = jnp.where(clip == index, length_ref[index].astype(F32), length)
    for target in range(HOLDERS):
        pay_ref[target, :CLIPS] = mel_ref[...]
        pay_ref[target, CLIPS] = length.astype(BF16)
        pay_ref[target, CLIPS + 1 :] = jnp.zeros((PAY - CLIPS - 1, 2 * HALF, MEL), BF16)


def columns_kernel(where_ref, weight_ref, bias_ref, w1_ref, b1_ref, picked):
    picked[...] = jnp.zeros_like(picked)
    b1_ref[...] = jnp.zeros_like(b1_ref)
    for block, flip in enumerate((0, 1, 2 * HOLDERS, 2 * HOLDERS + 1)):
        first = (where_ref[3] ^ flip) * ROWS
        start = pl.multiple_of(jnp.minimum((first >> 7) << 7, 16 * ROWS - 2 * LANES), LANES)
        shift = (2 * LANES - (first - start)) & (2 * LANES - 1)
        lanes = slice(block * ROWS, (block + 1) * ROWS)
        window = weight_ref[:, pl.ds(start, 2 * LANES)].astype(F32)
        picked[:, lanes] = pltpu.roll(window, shift, 1)[:, :ROWS]
        window = jnp.broadcast_to(bias_ref[pl.ds(start, 2 * LANES)].reshape(1, 2 * LANES), (8, 2 * LANES))
        b1_ref[:, lanes] = pltpu.roll(window, shift, 1)[0:1, :ROWS]
    w1_ref[...] = picked[...].astype(BF16)


def first_conv(pay_ref, w1_ref, b1_ref, cols_ref, frames_ref):
    sources = pay_ref.shape[0]
    spread = (
        lax.broadcasted_iota(jnp.int32, (STEPS, CLIPS), 0) >> 3
        == lax.broadcasted_iota(jnp.int32, (STEPS, CLIPS), 1)
    ).astype(F32).astype(BF16)
    t = (lax.broadcasted_iota(jnp.int32, (STEPS, LANES), 0) & (HALF - 1)).astype(F32)
    lives_even, lives_odd = [], []
    for source in range(sources):
        rows = slice(source * STEPS, (source + 1) * STEPS)
        length = dot(spread, pay_ref[source, CLIPS])
        frames_ref[source] = pay_ref[source, :CLIPS].astype(F32).reshape(2 * STEPS, MEL)
        live_even, live_odd = 2.0 * t < length, 2.0 * t + 1.0 < length
        even = jnp.where(live_even, frames_ref[source, pl.ds(0, STEPS, 2), :], 0.0)
        odd = jnp.where(live_odd, frames_ref[source, pl.ds(1, STEPS, 2), :], 0.0)
        cols_ref[rows, :LANES] = shift_down(odd).astype(BF16)
        cols_ref[rows, LANES : 2 * LANES] = even.astype(BF16)
        cols_ref[rows, 2 * LANES : 3 * LANES] = odd.astype(BF16)
        cols_ref[rows, 3 * LANES :] = shift_up(even).astype(BF16)
        lives_even.append(jnp.concatenate([live_even] * (WIDE // LANES), axis=1))
        lives_odd.append(jnp.concatenate([live_odd] * (WIDE // LANES), axis=1))
    cols = jnp.concatenate([cols_ref[:, : 3 * LANES], cols_ref[:, LANES:]], axis=0)
    pre = dot(cols, w1_ref[...]) + b1_ref[...]
    half = sources * STEPS
    return pre[:half], pre[half:], jnp.concatenate(lives_even, axis=0), jnp.concatenate(lives_odd, axis=0)


def forward_kernel(
    pay_ref, w1_ref, b1_ref, own_ref, side_ref, far_ref, both_ref, part_ref, w2_ref, cols_ref, frames_ref
):
    @pl.when(pl.program_id(0) == 0)
    def _():
        stack_weights((own_ref, side_ref, far_ref, both_ref), w2_ref)

    pre_even, pre_odd, live_even, live_odd = first_conv(pay_ref, w1_ref, b1_ref, cols_ref, frames_ref)
    odd = jnp.where(live_odd, gelu_value(pre_odd), 0.0)
    total = dot(odd.astype(BF16), w2_ref[:, 2 * D2 :]) + dot(shift_down(odd).astype(BF16), w2_ref[:, :D2])
    even = jnp.where(live_even, gelu_value(pre_even), 0.0)
    total = total + dot(even.astype(BF16), w2_ref[:, D2 : 2 * D2])
    part_ref[...] = total.astype(BF16).reshape(part_ref.shape)


def slope_kernel(
    pay_ref, w1_ref, b1_ref, grad_ref, column_ref, row_ref,
    slope_ref, turned_ref, live_grad_ref, wanted_ref, frames_ref, cols_ref,
):
    pre_even, pre_odd, live_even, live_odd = first_conv(pay_ref, w1_ref, b1_ref, cols_ref, frames_ref)
    some = pre_odd.shape[0]
    lanes = pl.ds(pl.multiple_of(pl.program_id(0) * some, some), some)
    turned_ref[pl.ds(pl.multiple_of(3 * WIDE + pl.program_id(0) * some, some // 2), some), :] = cols_ref[...]
    value, slope = gelu_both(pre_odd)
    odd = jnp.where(live_odd, value, 0.0)
    slope_ref[1] = jnp.where(live_odd, slope, 0.0)
    turned_ref[:WIDE, lanes] = shift_down(odd).astype(BF16).T
    turned_ref[2 * WIDE : 3 * WIDE, lanes] = odd.astype(BF16).T
    value, slope = gelu_both(pre_even)
    slope_ref[0] = jnp.where(live_even, slope, 0.0)
    turned_ref[WIDE : 2 * WIDE, lanes] = jnp.where(live_even, value, 0.0).astype(BF16).T

    @pl.when(pl.program_id(0) == 0)
    def _():
        t = (lax.broadcasted_iota(jnp.int32, (STEPS, 1), 0) & (HALF - 1)).astype(F32)
        length = (column_ref[...] & 31).astype(F32)
        live_grad_ref[...] = jnp.where(2.0 * t < length, grad_ref[...].astype(F32), 0.0).astype(BF16)
        here = lax.broadcasted_iota(jnp.int32, (STEPS, STEPS), 0)
        there = lax.broadcasted_iota(jnp.int32, (STEPS, STEPS), 1)
        owner = row_ref[...] >> 5
        same = ((column_ref[...] >> 5) == owner) & ((here >> 3) < (there >> 3))
        same = same & ((here & (HALF - 1)) == 0)
        rank = jnp.sum(jnp.where(same, 1.0, 0.0), axis=0, keepdims=True)
        place = lax.broadcasted_iota(jnp.int32, (1, STEPS), 1) & (HALF - 1)
        place = (owner * 2 + rank.astype(jnp.int32)) * HALF + place
        wanted = lax.broadcasted_iota(jnp.int32, (SLOTS * HALF, STEPS), 0) == place
        t = (lax.broadcasted_iota(jnp.int32, (1, STEPS), 1) & (HALF - 1)).astype(F32)
        wanted = wanted & (2.0 * t < (row_ref[...] & 31).astype(F32))
        wanted_ref[...] = jnp.where(wanted, 1.0, 0.0).astype(BF16)


def middle_kernel(
    where_ref, part_ref, b2_ref, live_grad_ref, wanted_ref, rep_ref, same_ref, cross_ref, live_grad_here, done
):
    copy = pltpu.make_async_copy(live_grad_ref, live_grad_here, done)
    copy.start()
    pre = part_ref[0].astype(F32)
    for source in range(1, HOLDERS):
        pre = pre + part_ref[source].astype(F32)
    value, slope = gelu_both(pre + b2_ref[...])
    copy.wait()
    second_grad = (live_grad_here[...].astype(F32) * slope).astype(BF16)
    for target in range(HOLDERS):
        rep_ref[target] = second_grad
    placed = dot(wanted_ref[...], value.astype(BF16))
    first = where_ref[2] == 0
    for chip in range(CHIPS):
        for tile in range(D2 // LANES):
            rows, columns = slice(tile * 16, (tile + 1) * 16), slice(tile * LANES, (tile + 1) * LANES)
            left = placed[chip * 32 : chip * 32 + 16, columns]
            right = placed[chip * 32 + 16 : chip * 32 + 32, columns]
            same_ref[chip, rows, :] = jnp.where(first, left, right).astype(BF16)
            cross_ref[chip, rows, :] = jnp.where(first, right, left).astype(BF16)


def backward_kernel(
    where_ref, grad_ref, own_ref, side_ref, far_ref, both_ref, turned_ref, slope_ref, keep_ref, send_ref,
    w2_ref, conv_sum,
):
    stack_weights((own_ref, side_ref, far_ref, both_ref), w2_ref)
    mine = where_ref[0]
    grad = grad_ref[...].reshape(HOLDERS * STEPS, D2)
    places = []
    for block in range(BLOCKS):
        places.append((keep_ref if block % 2 == 0 else send_ref, mine if block < 2 else 1 - mine, block * ROWS))

    for tap in range(3):
        conv_sum[...] = dot(turned_ref[tap * WIDE : (tap + 1) * WIDE, :], grad)
        for out, target, first in places:
            for column in range(D2 // LANES):
                tile = tap * (D2 // LANES) + column
                piece = conv_sum[first : first + ROWS, column * LANES : (column + 1) * LANES]
                out[target, tile // 8, (tile % 8) * ROWS : (tile % 8 + 1) * ROWS, :] = piece.astype(out.dtype)

    even = dot_nt(grad, w2_ref[:, D2 : 2 * D2])
    even = (even * slope_ref[0]).astype(BF16)
    odd = dot_nt(grad, w2_ref[:, 2 * D2 :]) + shift_up(dot_nt(grad, w2_ref[:, :D2]))
    odd = (odd * slope_ref[1]).astype(BF16)
    cols = turned_ref[3 * WIDE :, :]
    conv_sum[:, : 3 * LANES] = dot_tn(even, cols[:, : 3 * LANES]) + dot_tn(odd, cols[:, LANES:])
    bias1 = jnp.sum(even.astype(F32) + odd.astype(F32), axis=0, keepdims=True)
    bias2 = jnp.sum(grad.astype(F32), axis=0, keepdims=True)
    for out, target, first in places:
        out[target, 1, 7 * ROWS : 8 * ROWS, :] = jnp.zeros((ROWS, LANES), out.dtype)
        biases = [jnp.concatenate([bias1[:, first : first + ROWS], jnp.zeros((1, LANES - ROWS), F32)], axis=1)]
        for tile in range(D2 // LANES):
            biases.append(bias2[:, tile * LANES : (tile + 1) * LANES])
        biases.append(jnp.zeros((16 - len(biases), LANES), F32))
        biases = jnp.concatenate(biases, axis=0).astype(out.dtype)
        for half in range(2):
            for tile in range(3):
                piece = conv_sum[first : first + ROWS, tile * LANES : (tile + 1) * LANES]
                out[target, half, (8 + tile) * ROWS : (9 + tile) * ROWS, :] = piece.astype(out.dtype)
            out[target, half, 11 * ROWS :, :] = biases


def sum_kernel(got_ref, out_ref):
    total = got_ref[0].astype(F32)
    for source in range(1, got_ref.shape[0]):
        total = total + got_ref[source].astype(F32)
    total = total.astype(BF16)
    if len(out_ref.shape) == 2:
        out_ref[...] = total
    else:
        for target in range(out_ref.shape[0]):
            out_ref[target] = total


def pair_kernel(own_ref, other_ref, out_ref):
    total = (own_ref[...].astype(F32) + other_ref[...].astype(F32)).astype(BF16)
    if len(out_ref.shape) == 2:
        out_ref[...] = total
    else:
        for target in range(out_ref.shape[0]):
            out_ref[target] = total


def last_kernel(
    where_ref, got_ref, cross_ref, weight_ref, bias1_ref, bias2_ref, packed_ref, whole, biases,
):
    step, core = pl.program_id(0), where_ref[2]
    rows = pl.ds(pl.multiple_of((step + 1) * ROWS, 16), ROWS)
    for chip in range(CHIPS):
        whole[pl.ds(pl.multiple_of((2 * chip + core) * ROWS, 16), ROWS), :] = got_ref[chip, rows, :]
        whole[pl.ds(pl.multiple_of((2 * chip + 1 - core) * ROWS, 16), ROWS), :] = cross_ref[chip, rows, :]
    for block in range(10):
        columns = slice(block * LANES, (block + 1) * LANES)
        weight_ref[:, columns] = whole[columns, :].T.astype(F32)

    @pl.when(step == 0)
    def _():
        for chip in range(CHIPS):
            biases[2 * chip + core] = got_ref[chip, 5 * ROWS :, :].astype(F32)
            biases[2 * chip + 1 - core] = cross_ref[chip, 5 * ROWS :, :].astype(F32)
            left = pl.ds(pl.multiple_of(chip * 32 + 16 * core, 16), 16)
            right = pl.ds(pl.multiple_of(chip * 32 + 16 - 16 * core, 16), 16)
            for tile in range(D2 // LANES):
                columns = slice(tile * LANES, (tile + 1) * LANES)
                packed_ref[left, columns] = got_ref[chip, tile * 16 : (tile + 1) * 16, :]
                packed_ref[right, columns] = cross_ref[chip, 4 * ROWS + tile * 16 : 4 * ROWS + (tile + 1) * 16, :]
        bias1 = jnp.concatenate([biases[source, 0:1, :ROWS] for source in range(16)], axis=1)
        bias1_ref[...] = bias1.reshape(16 * ROWS)
        bias2 = jnp.concatenate([biases[0, 1 + tile : 2 + tile, :] for tile in range(D2 // LANES)], axis=1)
        bias2_ref[...] = bias2.reshape(D2)


def unpack_kernel(where_ref, own_ref, other_ref, conv2_ref):
    lower = where_ref[1] == 0
    for tile in range(15):
        half, spot = tile // 8, tile % 8
        rows = slice(spot * ROWS, (spot + 1) * ROWS)
        own, other = own_ref[rows, :].astype(F32), other_ref[rows, :].astype(F32)
        picked = jnp.where(lower, own, other) if half == 0 else jnp.where(lower, other, own)
        conv2_ref[:, tile * LANES : (tile + 1) * LANES] = picked


def exchange(values, axes):
    return lax.all_to_all(values, axes, split_axis=0, concat_axis=0, tiled=True)


def spread_to(values, count):
    return jnp.broadcast_to(values[None], (count,) + values.shape)


def vmem():
    return pl.BlockSpec(memory_space=pltpu.VMEM)


def params(mib, *semantics):
    return pltpu.CompilerParams(vmem_limit_bytes=mib * MIB, dimension_semantics=semantics or None)


def local(mel, lengths, routes, conv1_weight, conv1_bias, conv2_weight, conv2_bias, out_grad):
    x_hi, y, core = lax.axis_index("xh"), lax.axis_index("y"), lax.axis_index("c")
    where = jnp.stack([x_hi, lax.axis_index("xl"), core, (x_hi * HOLDERS + y) * 2 + core]).astype(jnp.int32)

    def shape(*dims, dtype=BF16):
        return jax.ShapeDtypeStruct(dims, dtype)

    def from_hbm(values):
        return pltpu.with_memory_space_constraint(values, pltpu.HBM)

    def in_hbm(*dims, dtype=BF16):
        return pltpu.HBM(dims, dtype)

    pay = pl.pallas_call(
        prepare_kernel,
        in_specs=[pl.BlockSpec(memory_space=pltpu.SMEM), vmem()],
        out_specs=vmem(),
        out_shape=in_hbm(HOLDERS, PAY, 2 * HALF, MEL),
        compiler_params=params(60),
        name="mel_payload",
    )(lengths, mel)
    got_pay = exchange(pay, "y")
    cores = [(0, 1), (1, 0)]
    far_weight = lax.ppermute(conv2_weight, ("xh", "xl"), [(0, 3), (3, 0), (1, 2), (2, 1)])

    w1, b1 = pl.pallas_call(
        columns_kernel,
        in_specs=[pl.BlockSpec(memory_space=pltpu.SMEM), vmem(), vmem()],
        out_specs=[vmem()] * 2,
        out_shape=[shape(3 * MEL, WIDE), shape(1, WIDE, dtype=F32)],
        scratch_shapes=[pltpu.VMEM((3 * MEL, WIDE), F32)],
        compiler_params=params(10),
        name="conv1_columns",
    )(where, conv1_weight, from_hbm(conv1_bias))
    own_weight, place = lax.optimization_barrier((conv2_weight, where))
    far_weight, place = lax.optimization_barrier((far_weight, place))
    weights = [
        conv2_weight,
        lax.ppermute(own_weight, "c", cores),
        far_weight,
        lax.ppermute(far_weight, "c", cores),
    ]

    pair = lambda i: (i, 0, 0)
    pair4 = lambda i: (i, 0, 0, 0)
    rows, some = HOLDERS * STEPS, 2 * STEPS
    frames = (2, 2 * STEPS, MEL)
    pay_spec = pl.BlockSpec((2, PAY, 2 * HALF, MEL), pair4)
    parts = pl.pallas_call(
        forward_kernel,
        grid=(HOLDERS // 2,),
        in_specs=[pay_spec, *[vmem()] * (2 + BLOCKS)],
        out_specs=pl.BlockSpec((2, STEPS, D2), pair),
        out_shape=in_hbm(HOLDERS, STEPS, D2),
        scratch_shapes=[
            pltpu.VMEM((WIDE, 3 * D2), BF16),
            pltpu.VMEM((some, 4 * LANES), BF16),
            pltpu.VMEM(frames, F32),
        ],
        compiler_params=params(20, "arbitrary"),
        name="stem_forward",
    )(got_pay, w1, b1, *weights)

    got_parts = exchange(parts, "y")
    code = jnp.repeat(routes[:, 0] * 32 + lengths, HALF)
    slopes, turned, live_grad, wanted = pl.pallas_call(
        slope_kernel,
        grid=(HOLDERS // 2,),
        in_specs=[pay_spec, *[vmem()] * 5],
        out_specs=[pl.BlockSpec((2, some, WIDE), lambda i: (0, i, 0)), vmem(), vmem(), vmem()],
        out_shape=[
            shape(2, rows, WIDE, dtype=F32),
            shape(3 * WIDE + rows, rows),
            in_hbm(STEPS, D2),
            shape(SLOTS * HALF, STEPS),
        ],
        scratch_shapes=[pltpu.VMEM(frames, F32), pltpu.VMEM((some, 4 * LANES), BF16)],
        compiler_params=params(20, "arbitrary"),
        name="stem_slopes",
    )(got_pay, w1, b1, from_hbm(out_grad.reshape(STEPS, D2)), code[:, None], code[None])
    got_parts, slopes, turned = lax.optimization_barrier((got_parts, slopes, turned))
    rep, same, cross = pl.pallas_call(
        middle_kernel,
        in_specs=[pl.BlockSpec(memory_space=pltpu.SMEM), vmem(), vmem(), pl.BlockSpec(memory_space=pl.ANY), vmem()],
        out_specs=[vmem()] * 3,
        out_shape=[shape(HOLDERS, STEPS, D2), shape(CHIPS, ROWS, LANES), shape(CHIPS, ROWS, LANES)],
        scratch_shapes=[pltpu.VMEM((STEPS, D2), BF16), pltpu.SemaphoreType.DMA],
        compiler_params=params(10),
        name="stem_middle",
    )(where, got_parts, conv2_bias[None], from_hbm(live_grad), wanted)
    got_grad = exchange(rep, "y")

    keep, send = pl.pallas_call(
        backward_kernel,
        in_specs=[
            pl.BlockSpec(memory_space=pltpu.SMEM),
            *[vmem()] * (3 + BLOCKS),
        ],
        out_specs=[vmem()] * 2,
        out_shape=[shape(2, 2, PACK, LANES, dtype=F32), shape(2, 2, PACK, LANES)],
        scratch_shapes=[
            pltpu.VMEM((WIDE, 3 * D2), BF16),
            pltpu.VMEM((WIDE, D2), F32),
        ],
        compiler_params=params(32),
        name="stem_backward",
    )(where, got_grad, *weights, turned, slopes)
    got = lax.ppermute(send, "c", cores)
    quarters = exchange((keep + got.astype(F32)).astype(BF16).reshape(4, PACK, LANES), ("xh", "xl"))

    def summed(values, *dims):
        return pl.pallas_call(
            sum_kernel,
            in_specs=[vmem()],
            out_specs=vmem(),
            out_shape=shape(*dims),
            compiler_params=params(8),
            name="gradient_sum",
        )(values)

    half = summed(quarters, PACK, LANES)
    quarter = PACK // 4
    near = summed(exchange(half.reshape(4, quarter, LANES), "zl"), quarter, LANES)

    def with_group(values, flip, *dims):
        return pl.pallas_call(
            pair_kernel,
            in_specs=[vmem()] * 2,
            out_specs=vmem(),
            out_shape=shape(*dims),
            compiler_params=params(8),
            name="gradient_pair",
        )(values, lax.ppermute(values, "zh", [(i, i ^ flip) for i in range(4)]))

    far = with_group(with_group(near, 1, quarter, LANES), 3, 4, quarter, LANES)
    half = exchange(far, "zl").reshape(PACK, LANES)
    own = half[:HALF_ROWS]
    other = lax.ppermute(own, "xl", [(0, 1), (1, 0)])
    conv1 = spread_to(half[HALF_ROWS:], CHIPS)
    got = exchange(jnp.concatenate([same, conv1[:, : 3 * ROWS], cross, conv1[:, 3 * ROWS :]], axis=1), ("xh", "y"))
    got, other = lax.optimization_barrier((got, other))
    got_cross = lax.ppermute(got, "c", cores)
    conv2_rows_grad = pl.pallas_call(
        unpack_kernel,
        in_specs=[pl.BlockSpec(memory_space=pltpu.SMEM), vmem(), vmem()],
        out_specs=vmem(),
        out_shape=in_hbm(ROWS, 3 * D2, dtype=F32),
        compiler_params=params(8),
        name="conv2_unpack",
    )(where, own, other)
    weight_grad, bias_grad, second_bias_grad, packed = pl.pallas_call(
        last_kernel,
        grid=(3,),
        in_specs=[
            pl.BlockSpec(memory_space=pltpu.SMEM),
            vmem(),
            vmem(),
        ],
        out_specs=[
            pl.BlockSpec((LANES, 16 * ROWS), lambda i: (i, 0)),
            pl.BlockSpec((16 * ROWS,), lambda i: (0,)),
            pl.BlockSpec((D2,), lambda i: (0,)),
            pl.BlockSpec((SLOTS * HALF, D2), lambda i: (0, 0)),
        ],
        out_shape=[
            shape(3 * MEL, 16 * ROWS, dtype=F32),
            shape(16 * ROWS, dtype=F32),
            shape(D2, dtype=F32),
            shape(SLOTS * HALF, D2),
        ],
        scratch_shapes=[pltpu.VMEM((16 * ROWS, LANES), BF16), pltpu.VMEM((16, 16, LANES), F32)],
        compiler_params=params(16, "arbitrary"),
        name="gradient_unpack",
    )(where, got, got_cross)
    return packed.reshape(SLOTS, HALF, D2), weight_grad, bias_grad, second_bias_grad, conv2_rows_grad


def solution(mesh):
    fine = Mesh(mesh.devices.reshape(2, 4, 2, 4, 4, 2), ALL_AXES)
    placed = (
        P(ALL_AXES, None, None),
        P(ALL_AXES),
        P(ALL_AXES, None),
        P(),
        P(),
        P(ENC, None),
        P(),
        P(ALL_AXES, None, None),
    )
    return jax.shard_map(
        local,
        mesh=fine,
        in_specs=placed,
        out_specs=(P(ALL_AXES, None, None), P(), P(), P(), P(ENC, None)),
        check_vma=False,
    )
```

```python
import functools

import jax
import jax.numpy as jnp
from jax import lax
from jax.experimental import pallas as pl
from jax.experimental.pallas import tpu as pltpu
from jax.sharding import Mesh
from jax.sharding import PartitionSpec as P

inv_root_two = 0.7071067811865476
inv_root_tau = 0.3989422804014327

MEL = 128
D2 = 640
ROWS = 80
LANES = 128
HOLDERS = 4
BLOCKS = 4
WIDE = 384
CLIPS = 16
HALF = 8
STEPS = CLIPS * HALF
SLOTS = 2 * CLIPS
PAY = 26
CHIPS = 8
PACK = 896
HALF_ROWS = 8 * ROWS
MIB = 1024 * 1024
ALL_AXES = ("xh", "y", "c", "zh", "zl", "xl")
ENC = ("xh", "y", "c")
F32 = jnp.float32
BF16 = jnp.bfloat16


def gelu_value(values):
    return values * (0.5 * (1.0 + lax.erf(values * inv_root_two)))


def gelu_both(values):
    cdf = 0.5 * (1.0 + lax.erf(values * inv_root_two))
    return values * cdf, cdf + values * jnp.exp(-0.5 * values * values) * inv_root_tau


def shift_down(values):
    rows, width = values.shape
    t = lax.broadcasted_iota(jnp.int32, (rows, width), 0) & (HALF - 1)
    clips = values.reshape(rows // HALF, HALF, width)
    moved = pltpu.roll(clips, 1, 1).reshape(rows, width)
    return jnp.where(t == 0, 0.0, moved)


def shift_up(values):
    rows, width = values.shape
    t = lax.broadcasted_iota(jnp.int32, (rows, width), 0) & (HALF - 1)
    clips = values.reshape(rows // HALF, HALF, width)
    moved = pltpu.roll(clips, HALF - 1, 1).reshape(rows, width)
    return jnp.where(t == HALF - 1, 0.0, moved)


def dot(left, right):
    return jnp.dot(left, right, preferred_element_type=F32)


def dot_nt(left, right):
    return lax.dot_general(left, right, (((1,), (1,)), ((), ())), preferred_element_type=F32)


def dot_tn(left, right):
    return lax.dot_general(left, right, (((0,), (0,)), ((), ())), preferred_element_type=F32)


def stack_weights(refs, w2_ref):
    for block, ref in enumerate(refs):
        w2_ref[block * ROWS : (block + 1) * ROWS, :] = ref[...]
    w2_ref[BLOCKS * ROWS :, :] = jnp.zeros((WIDE - BLOCKS * ROWS, 3 * D2), BF16)


def prepare_kernel(length_ref, mel_ref, pay_ref):
    clip = lax.broadcasted_iota(jnp.int32, (CLIPS, MEL), 0)
    length = jnp.zeros((CLIPS, MEL), F32)
    for index in range(CLIPS):
        length = jnp.where(clip == index, length_ref[index].astype(F32), length)
    for target in range(HOLDERS):
        pay_ref[target, :CLIPS] = mel_ref[...]
        pay_ref[target, CLIPS] = length.astype(BF16)
        pay_ref[target, CLIPS + 1 :] = jnp.zeros((PAY - CLIPS - 1, 2 * HALF, MEL), BF16)


def columns_kernel(where_ref, weight_ref, bias_ref, w1_ref, b1_ref, picked):
    picked[...] = jnp.zeros_like(picked)
    b1_ref[...] = jnp.zeros_like(b1_ref)
    for block, flip in enumerate((0, 1, 2 * HOLDERS, 2 * HOLDERS + 1)):
        first = (where_ref[3] ^ flip) * ROWS
        start = pl.multiple_of(jnp.minimum((first >> 7) << 7, 16 * ROWS - 2 * LANES), LANES)
        shift = (2 * LANES - (first - start)) & (2 * LANES - 1)
        lanes = slice(block * ROWS, (block + 1) * ROWS)
        window = weight_ref[:, pl.ds(start, 2 * LANES)].astype(F32)
        picked[:, lanes] = pltpu.roll(window, shift, 1)[:, :ROWS]
        window = jnp.broadcast_to(bias_ref[pl.ds(start, 2 * LANES)].reshape(1, 2 * LANES), (8, 2 * LANES))
        b1_ref[:, lanes] = pltpu.roll(window, shift, 1)[0:1, :ROWS]
    w1_ref[...] = picked[...].astype(BF16)


def first_conv(pay_ref, w1_ref, b1_ref, cols_ref, frames_ref):
    sources = pay_ref.shape[0]
    spread = (
        lax.broadcasted_iota(jnp.int32, (STEPS, CLIPS), 0) >> 3
        == lax.broadcasted_iota(jnp.int32, (STEPS, CLIPS), 1)
    ).astype(F32).astype(BF16)
    t = (lax.broadcasted_iota(jnp.int32, (STEPS, LANES), 0) & (HALF - 1)).astype(F32)
    lives_even, lives_odd = [], []
    for source in range(sources):
        rows = slice(source * STEPS, (source + 1) * STEPS)
        length = dot(spread, pay_ref[source, CLIPS])
        frames_ref[source] = pay_ref[source, :CLIPS].astype(F32).reshape(2 * STEPS, MEL)
        live_even, live_odd = 2.0 * t < length, 2.0 * t + 1.0 < length
        even = jnp.where(live_even, frames_ref[source, pl.ds(0, STEPS, 2), :], 0.0)
        odd = jnp.where(live_odd, frames_ref[source, pl.ds(1, STEPS, 2), :], 0.0)
        cols_ref[rows, :LANES] = shift_down(odd).astype(BF16)
        cols_ref[rows, LANES : 2 * LANES] = even.astype(BF16)
        cols_ref[rows, 2 * LANES : 3 * LANES] = odd.astype(BF16)
        cols_ref[rows, 3 * LANES :] = shift_up(even).astype(BF16)
        lives_even.append(jnp.concatenate([live_even] * (WIDE // LANES), axis=1))
        lives_odd.append(jnp.concatenate([live_odd] * (WIDE // LANES), axis=1))
    cols = jnp.concatenate([cols_ref[:, : 3 * LANES], cols_ref[:, LANES:]], axis=0)
    pre = dot(cols, w1_ref[...]) + b1_ref[...]
    half = sources * STEPS
    return pre[:half], pre[half:], jnp.concatenate(lives_even, axis=0), jnp.concatenate(lives_odd, axis=0)


def forward_kernel(
    pay_ref, w1_ref, b1_ref, own_ref, side_ref, far_ref, both_ref, grad_ref, column_ref, row_ref,
    part_ref, slope_ref, turned_ref, live_grad_ref, wanted_ref, w2_ref, cols_ref, frames_ref,
):
    @pl.when(pl.program_id(0) == 0)
    def _():
        stack_weights((own_ref, side_ref, far_ref, both_ref), w2_ref)

    pre_even, pre_odd, live_even, live_odd = first_conv(pay_ref, w1_ref, b1_ref, cols_ref, frames_ref)
    some = pre_odd.shape[0]
    lanes = pl.ds(pl.multiple_of(pl.program_id(0) * some, some), some)
    value, slope = gelu_both(pre_odd)
    value = jnp.where(live_odd, value, 0.0)
    odd, prior = value.astype(BF16), shift_down(value).astype(BF16)
    slope_ref[1] = jnp.where(live_odd, slope, 0.0)
    total = dot(odd, w2_ref[:, 2 * D2 :]) + dot(prior, w2_ref[:, :D2])
    value, slope = gelu_both(pre_even)
    even = jnp.where(live_even, value, 0.0).astype(BF16)
    slope_ref[0] = jnp.where(live_even, slope, 0.0)
    total = total + dot(even, w2_ref[:, D2 : 2 * D2])
    part_ref[...] = total.astype(BF16).reshape(part_ref.shape)
    turned_ref[pl.ds(pl.multiple_of(3 * WIDE + pl.program_id(0) * some, some // 2), some), :] = cols_ref[...]
    turned_ref[:WIDE, lanes] = prior.T
    turned_ref[WIDE : 2 * WIDE, lanes] = even.T
    turned_ref[2 * WIDE : 3 * WIDE, lanes] = odd.T

    @pl.when(pl.program_id(0) == 0)
    def _():
        t = (lax.broadcasted_iota(jnp.int32, (STEPS, 1), 0) & (HALF - 1)).astype(F32)
        length = (column_ref[...] & 31).astype(F32)
        live_grad_ref[...] = jnp.where(2.0 * t < length, grad_ref[...].astype(F32), 0.0).astype(BF16)
        here = lax.broadcasted_iota(jnp.int32, (STEPS, STEPS), 0)
        there = lax.broadcasted_iota(jnp.int32, (STEPS, STEPS), 1)
        owner = row_ref[...] >> 5
        same = ((column_ref[...] >> 5) == owner) & ((here >> 3) < (there >> 3))
        same = same & ((here & (HALF - 1)) == 0)
        rank = jnp.sum(jnp.where(same, 1.0, 0.0), axis=0, keepdims=True)
        place = lax.broadcasted_iota(jnp.int32, (1, STEPS), 1) & (HALF - 1)
        place = (owner * 2 + rank.astype(jnp.int32)) * HALF + place
        wanted = lax.broadcasted_iota(jnp.int32, (SLOTS * HALF, STEPS), 0) == place
        t = (lax.broadcasted_iota(jnp.int32, (1, STEPS), 1) & (HALF - 1)).astype(F32)
        wanted = wanted & (2.0 * t < (row_ref[...] & 31).astype(F32))
        wanted_ref[...] = jnp.where(wanted, 1.0, 0.0).astype(BF16)


def middle_kernel(
    where_ref, part_ref, b2_ref, live_grad_ref, wanted_ref, rep_ref, same_ref, cross_ref, live_grad_here, done
):
    copy = pltpu.make_async_copy(live_grad_ref, live_grad_here, done)
    copy.start()
    pre = part_ref[0].astype(F32)
    for source in range(1, HOLDERS):
        pre = pre + part_ref[source].astype(F32)
    value, slope = gelu_both(pre + b2_ref[...].reshape(1, D2))
    copy.wait()
    second_grad = (live_grad_here[...].astype(F32) * slope).astype(BF16)
    for target in range(HOLDERS):
        rep_ref[target] = second_grad
    placed = dot(wanted_ref[...], value.astype(BF16))
    first = where_ref[2] == 0
    for chip in range(CHIPS):
        for tile in range(D2 // LANES):
            rows, columns = slice(tile * 16, (tile + 1) * 16), slice(tile * LANES, (tile + 1) * LANES)
            left = placed[chip * 32 : chip * 32 + 16, columns]
            right = placed[chip * 32 + 16 : chip * 32 + 32, columns]
            same_ref[chip, rows, :] = jnp.where(first, left, right).astype(BF16)
            cross_ref[chip, rows, :] = jnp.where(first, right, left).astype(BF16)


def backward_kernel(
    where_ref, grad_ref, own_ref, side_ref, far_ref, both_ref, turned_ref, slope_ref, keep_ref, send_ref,
    w2_ref, conv_sum,
):
    stack_weights((own_ref, side_ref, far_ref, both_ref), w2_ref)
    mine = where_ref[0]
    grad = grad_ref[...].reshape(HOLDERS * STEPS, D2)
    places = []
    for block in range(BLOCKS):
        places.append((keep_ref if block % 2 == 0 else send_ref, mine if block < 2 else 1 - mine, block * ROWS))

    for tap in range(3):
        conv_sum[...] = dot(turned_ref[tap * WIDE : (tap + 1) * WIDE, :], grad)
        for out, target, first in places:
            for column in range(D2 // LANES):
                tile = tap * (D2 // LANES) + column
                piece = conv_sum[first : first + ROWS, column * LANES : (column + 1) * LANES]
                out[target, tile // 8, (tile % 8) * ROWS : (tile % 8 + 1) * ROWS, :] = piece.astype(out.dtype)

    even = dot_nt(grad, w2_ref[:, D2 : 2 * D2])
    even = (even * slope_ref[0]).astype(BF16)
    odd = dot_nt(grad, w2_ref[:, 2 * D2 :]) + shift_up(dot_nt(grad, w2_ref[:, :D2]))
    odd = (odd * slope_ref[1]).astype(BF16)
    cols = turned_ref[3 * WIDE :, :]
    conv_sum[:, : 3 * LANES] = dot_tn(even, cols[:, : 3 * LANES]) + dot_tn(odd, cols[:, LANES:])
    bias1 = jnp.sum(even.astype(F32) + odd.astype(F32), axis=0, keepdims=True)
    bias2 = jnp.sum(grad.astype(F32), axis=0, keepdims=True)
    for out, target, first in places:
        out[target, 1, 7 * ROWS : 8 * ROWS, :] = jnp.zeros((ROWS, LANES), out.dtype)
        biases = [jnp.concatenate([bias1[:, first : first + ROWS], jnp.zeros((1, LANES - ROWS), F32)], axis=1)]
        for tile in range(D2 // LANES):
            biases.append(bias2[:, tile * LANES : (tile + 1) * LANES])
        biases.append(jnp.zeros((16 - len(biases), LANES), F32))
        biases = jnp.concatenate(biases, axis=0).astype(out.dtype)
        for half in range(2):
            for tile in range(3):
                piece = conv_sum[first : first + ROWS, tile * LANES : (tile + 1) * LANES]
                out[target, half, (8 + tile) * ROWS : (9 + tile) * ROWS, :] = piece.astype(out.dtype)
            out[target, half, 11 * ROWS :, :] = biases


def sum_kernel(got_ref, out_ref):
    total = got_ref[0].astype(F32)
    for source in range(1, got_ref.shape[0]):
        total = total + got_ref[source].astype(F32)
    total = total.astype(BF16)
    if len(out_ref.shape) == 2:
        out_ref[...] = total
    else:
        for target in range(out_ref.shape[0]):
            out_ref[target] = total


def pair_kernel(own_ref, other_ref, out_ref):
    total = (own_ref[...].astype(F32) + other_ref[...].astype(F32)).astype(BF16)
    if len(out_ref.shape) == 2:
        out_ref[...] = total
    else:
        for target in range(out_ref.shape[0]):
            out_ref[target] = total


def last_kernel(
    where_ref, got_ref, cross_ref, weight_ref, bias1_ref, bias2_ref, packed_ref, whole, biases,
):
    step, core = pl.program_id(0), where_ref[2]
    rows = pl.ds(pl.multiple_of((step + 1) * ROWS, 16), ROWS)
    for chip in range(CHIPS):
        whole[pl.ds(pl.multiple_of((2 * chip + core) * ROWS, 16), ROWS), :] = got_ref[chip, rows, :]
        whole[pl.ds(pl.multiple_of((2 * chip + 1 - core) * ROWS, 16), ROWS), :] = cross_ref[chip, rows, :]
    for block in range(10):
        columns = slice(block * LANES, (block + 1) * LANES)
        weight_ref[:, columns] = whole[columns, :].T.astype(F32)

    @pl.when(step == 0)
    def _():
        for chip in range(CHIPS):
            biases[2 * chip + core] = got_ref[chip, 5 * ROWS :, :].astype(F32)
            biases[2 * chip + 1 - core] = cross_ref[chip, 5 * ROWS :, :].astype(F32)
            left = pl.ds(pl.multiple_of(chip * 32 + 16 * core, 16), 16)
            right = pl.ds(pl.multiple_of(chip * 32 + 16 - 16 * core, 16), 16)
            for tile in range(D2 // LANES):
                columns = slice(tile * LANES, (tile + 1) * LANES)
                packed_ref[left, columns] = got_ref[chip, tile * 16 : (tile + 1) * 16, :]
                packed_ref[right, columns] = cross_ref[chip, 4 * ROWS + tile * 16 : 4 * ROWS + (tile + 1) * 16, :]
        bias1 = jnp.concatenate([biases[source, 0:1, :ROWS] for source in range(16)], axis=1)
        bias1_ref[...] = bias1.reshape(16 * ROWS)
        bias2 = jnp.concatenate([biases[0, 1 + tile : 2 + tile, :] for tile in range(D2 // LANES)], axis=1)
        bias2_ref[...] = bias2.reshape(D2)


def unpack_kernel(where_ref, own_ref, other_ref, conv2_ref):
    lower = where_ref[1] == 0
    for tile in range(15):
        half, spot = tile // 8, tile % 8
        rows = slice(spot * ROWS, (spot + 1) * ROWS)
        own, other = own_ref[rows, :].astype(F32), other_ref[rows, :].astype(F32)
        picked = jnp.where(lower, own, other) if half == 0 else jnp.where(lower, other, own)
        conv2_ref[:, tile * LANES : (tile + 1) * LANES] = picked


def exchange(values, axes):
    return lax.all_to_all(values, axes, split_axis=0, concat_axis=0, tiled=True)


def spread_to(values, count):
    return jnp.broadcast_to(values[None], (count,) + values.shape)


def vmem():
    return pl.BlockSpec(memory_space=pltpu.VMEM)


def params(mib, *semantics):
    return pltpu.CompilerParams(vmem_limit_bytes=mib * MIB, dimension_semantics=semantics or None)


def local(mel, lengths, routes, conv1_weight, conv1_bias, conv2_weight, conv2_bias, out_grad):
    x_hi, y, core = lax.axis_index("xh"), lax.axis_index("y"), lax.axis_index("c")
    where = jnp.stack([x_hi, lax.axis_index("xl"), core, (x_hi * HOLDERS + y) * 2 + core]).astype(jnp.int32)

    def shape(*dims, dtype=BF16):
        return jax.ShapeDtypeStruct(dims, dtype)

    def from_hbm(values):
        return pltpu.with_memory_space_constraint(values, pltpu.HBM)

    def in_hbm(*dims, dtype=BF16):
        return pltpu.HBM(dims, dtype)

    pay = pl.pallas_call(
        prepare_kernel,
        in_specs=[pl.BlockSpec(memory_space=pltpu.SMEM), vmem()],
        out_specs=vmem(),
        out_shape=in_hbm(HOLDERS, PAY, 2 * HALF, MEL),
        compiler_params=params(60),
        name="mel_payload",
    )(lengths, mel)
    got_pay = exchange(pay, "y")
    cores = [(0, 1), (1, 0)]
    far_weight = lax.ppermute(conv2_weight, ("xh", "xl"), [(0, 3), (3, 0), (1, 2), (2, 1)])

    w1, b1 = pl.pallas_call(
        columns_kernel,
        in_specs=[pl.BlockSpec(memory_space=pltpu.SMEM), vmem(), vmem()],
        out_specs=[vmem()] * 2,
        out_shape=[shape(3 * MEL, WIDE), shape(1, WIDE, dtype=F32)],
        scratch_shapes=[pltpu.VMEM((3 * MEL, WIDE), F32)],
        compiler_params=params(10),
        name="conv1_columns",
    )(where, conv1_weight, from_hbm(conv1_bias))
    own_weight, place = lax.optimization_barrier((conv2_weight, where))
    far_weight, place = lax.optimization_barrier((far_weight, place))
    weights = [
        conv2_weight,
        lax.ppermute(own_weight, "c", cores),
        far_weight,
        lax.ppermute(far_weight, "c", cores),
    ]

    pair = lambda i: (i, 0, 0)
    pair4 = lambda i: (i, 0, 0, 0)
    rows, some = HOLDERS * STEPS, 2 * STEPS
    frames = (2, 2 * STEPS, MEL)
    pay_spec = pl.BlockSpec((2, PAY, 2 * HALF, MEL), pair4)
    code = jnp.repeat(routes[:, 0] * 32 + lengths, HALF)
    parts, slopes, turned, live_grad, wanted = pl.pallas_call(
        forward_kernel,
        grid=(HOLDERS // 2,),
        in_specs=[pay_spec, *[vmem()] * (5 + BLOCKS)],
        out_specs=[
            pl.BlockSpec((2, STEPS, D2), pair),
            pl.BlockSpec((2, some, WIDE), lambda i: (0, i, 0)),
            *[vmem()] * 3,
        ],
        out_shape=[
            shape(HOLDERS, STEPS, D2),
            shape(2, rows, WIDE, dtype=F32),
            shape(3 * WIDE + rows, rows),
            in_hbm(STEPS, D2),
            shape(SLOTS * HALF, STEPS),
        ],
        scratch_shapes=[
            pltpu.VMEM((WIDE, 3 * D2), BF16),
            pltpu.VMEM((some, 4 * LANES), BF16),
            pltpu.VMEM(frames, F32),
        ],
        compiler_params=params(24, "arbitrary"),
        name="stem_forward",
    )(got_pay, w1, b1, *weights, from_hbm(out_grad.reshape(STEPS, D2)), code[:, None], code[None])
    got_parts = exchange(parts, "y")
    rep, same, cross = pl.pallas_call(
        middle_kernel,
        in_specs=[pl.BlockSpec(memory_space=pltpu.SMEM), vmem(), vmem(), pl.BlockSpec(memory_space=pl.ANY), vmem()],
        out_specs=[vmem()] * 3,
        out_shape=[shape(HOLDERS, STEPS, D2), shape(CHIPS, ROWS, LANES), shape(CHIPS, ROWS, LANES)],
        scratch_shapes=[pltpu.VMEM((STEPS, D2), BF16), pltpu.SemaphoreType.DMA],
        compiler_params=params(10),
        name="stem_middle",
    )(where, got_parts, conv2_bias, from_hbm(live_grad), wanted)
    got_grad = exchange(rep, "y")

    keep, send = pl.pallas_call(
        backward_kernel,
        in_specs=[
            pl.BlockSpec(memory_space=pltpu.SMEM),
            *[vmem()] * (3 + BLOCKS),
        ],
        out_specs=[vmem()] * 2,
        out_shape=[shape(2, 2, PACK, LANES, dtype=F32), shape(2, 2, PACK, LANES)],
        scratch_shapes=[
            pltpu.VMEM((WIDE, 3 * D2), BF16),
            pltpu.VMEM((WIDE, D2), F32),
        ],
        compiler_params=params(32),
        name="stem_backward",
    )(where, got_grad, *weights, turned, slopes)
    got = lax.ppermute(send, "c", cores)
    quarters = exchange((keep + got.astype(F32)).astype(BF16).reshape(4, PACK, LANES), ("xh", "xl"))

    def summed(values, *dims):
        return pl.pallas_call(
            sum_kernel,
            in_specs=[vmem()],
            out_specs=vmem(),
            out_shape=shape(*dims),
            compiler_params=params(8),
            name="gradient_sum",
        )(values)

    half = summed(quarters, PACK, LANES)
    quarter = PACK // 4
    near = summed(exchange(half.reshape(4, quarter, LANES), "zl"), quarter, LANES)

    def with_group(values, flip, *dims):
        return pl.pallas_call(
            pair_kernel,
            in_specs=[vmem()] * 2,
            out_specs=vmem(),
            out_shape=shape(*dims),
            compiler_params=params(8),
            name="gradient_pair",
        )(values, lax.ppermute(values, "zh", [(i, i ^ flip) for i in range(4)]))

    far = with_group(with_group(near, 1, quarter, LANES), 3, 4, quarter, LANES)
    half = exchange(far, "zl").reshape(PACK, LANES)
    own = half[:HALF_ROWS]
    other = lax.ppermute(own, "xl", [(0, 1), (1, 0)])
    conv1 = spread_to(half[HALF_ROWS:], CHIPS)
    got = exchange(jnp.concatenate([same, conv1[:, : 3 * ROWS], cross, conv1[:, 3 * ROWS :]], axis=1), ("xh", "y"))
    got, other = lax.optimization_barrier((got, other))
    got_cross = lax.ppermute(got, "c", cores)
    conv2_rows_grad = pl.pallas_call(
        unpack_kernel,
        in_specs=[pl.BlockSpec(memory_space=pltpu.SMEM), vmem(), vmem()],
        out_specs=vmem(),
        out_shape=in_hbm(ROWS, 3 * D2, dtype=F32),
        compiler_params=params(8),
        name="conv2_unpack",
    )(where, own, other)
    weight_grad, bias_grad, second_bias_grad, packed = pl.pallas_call(
        last_kernel,
        grid=(3,),
        in_specs=[
            pl.BlockSpec(memory_space=pltpu.SMEM),
            vmem(),
            vmem(),
        ],
        out_specs=[
            pl.BlockSpec((LANES, 16 * ROWS), lambda i: (i, 0)),
            pl.BlockSpec((16 * ROWS,), lambda i: (0,)),
            pl.BlockSpec((D2,), lambda i: (0,)),
            pl.BlockSpec((SLOTS * HALF, D2), lambda i: (0, 0)),
        ],
        out_shape=[
            shape(3 * MEL, 16 * ROWS, dtype=F32),
            shape(16 * ROWS, dtype=F32),
            shape(D2, dtype=F32),
            shape(SLOTS * HALF, D2),
        ],
        scratch_shapes=[pltpu.VMEM((16 * ROWS, LANES), BF16), pltpu.VMEM((16, 16, LANES), F32)],
        compiler_params=params(16, "arbitrary"),
        name="gradient_unpack",
    )(where, got, got_cross)
    return packed.reshape(SLOTS, HALF, D2), weight_grad, bias_grad, second_bias_grad, conv2_rows_grad


def solution(mesh):
    fine = Mesh(mesh.devices.reshape(2, 4, 2, 4, 4, 2), ALL_AXES)
    placed = (
        P(ALL_AXES, None, None),
        P(ALL_AXES),
        P(ALL_AXES, None),
        P(),
        P(),
        P(ENC, None),
        P(),
        P(ALL_AXES, None, None),
    )
    return jax.shard_map(
        local,
        mesh=fine,
        in_specs=placed,
        out_specs=(P(ALL_AXES, None, None), P(), P(), P(), P(ENC, None)),
        check_vma=False,
    )
```

```python
import functools

import jax
import jax.numpy as jnp
from jax import lax
from jax.experimental import pallas as pl
from jax.experimental.pallas import tpu as pltpu
from jax.sharding import Mesh
from jax.sharding import PartitionSpec as P

inv_root_two = 0.7071067811865476
inv_root_tau = 0.3989422804014327

MEL = 128
D2 = 640
ROWS = 80
LANES = 128
HOLDERS = 4
BLOCKS = 4
WIDE = 384
CLIPS = 16
HALF = 8
STEPS = CLIPS * HALF
SLOTS = 2 * CLIPS
PAY = 26
CHIPS = 8
PACK = 896
HALF_ROWS = 8 * ROWS
MIB = 1024 * 1024
ALL_AXES = ("xh", "y", "c", "zh", "zl", "xl")
ENC = ("xh", "y", "c")
F32 = jnp.float32
BF16 = jnp.bfloat16


def gelu_value(values):
    return values * (0.5 * (1.0 + lax.erf(values * inv_root_two)))


def gelu_both(values):
    cdf = 0.5 * (1.0 + lax.erf(values * inv_root_two))
    return values * cdf, cdf + values * jnp.exp(-0.5 * values * values) * inv_root_tau


def shift_down(values):
    rows, width = values.shape
    t = lax.broadcasted_iota(jnp.int32, (rows, width), 0) & (HALF - 1)
    clips = values.reshape(rows // HALF, HALF, width)
    moved = pltpu.roll(clips, 1, 1).reshape(rows, width)
    return jnp.where(t == 0, 0.0, moved)


def shift_up(values):
    rows, width = values.shape
    t = lax.broadcasted_iota(jnp.int32, (rows, width), 0) & (HALF - 1)
    clips = values.reshape(rows // HALF, HALF, width)
    moved = pltpu.roll(clips, HALF - 1, 1).reshape(rows, width)
    return jnp.where(t == HALF - 1, 0.0, moved)


def dot(left, right):
    return jnp.dot(left, right, preferred_element_type=F32)


def dot_nt(left, right):
    return lax.dot_general(left, right, (((1,), (1,)), ((), ())), preferred_element_type=F32)


def dot_tn(left, right):
    return lax.dot_general(left, right, (((0,), (0,)), ((), ())), preferred_element_type=F32)


def stack_weights(refs, w2_ref):
    for block, ref in enumerate(refs):
        w2_ref[block * ROWS : (block + 1) * ROWS, :] = ref[...]
    w2_ref[BLOCKS * ROWS :, :] = jnp.zeros((WIDE - BLOCKS * ROWS, 3 * D2), BF16)


def prepare_kernel(length_ref, mel_ref, pay_ref):
    clip = lax.broadcasted_iota(jnp.int32, (CLIPS, MEL), 0)
    length = jnp.zeros((CLIPS, MEL), F32)
    for index in range(CLIPS):
        length = jnp.where(clip == index, length_ref[index].astype(F32), length)
    for target in range(HOLDERS):
        pay_ref[target, :CLIPS] = mel_ref[...]
        pay_ref[target, CLIPS] = length.astype(BF16)
        pay_ref[target, CLIPS + 1 :] = jnp.zeros((PAY - CLIPS - 1, 2 * HALF, MEL), BF16)


def columns_kernel(where_ref, weight_ref, bias_ref, w1_ref, b1_ref, picked):
    picked[...] = jnp.zeros_like(picked)
    b1_ref[...] = jnp.zeros_like(b1_ref)
    for block, flip in enumerate((0, 1, 2 * HOLDERS, 2 * HOLDERS + 1)):
        first = (where_ref[3] ^ flip) * ROWS
        start = pl.multiple_of(jnp.minimum((first >> 7) << 7, 16 * ROWS - 2 * LANES), LANES)
        shift = (2 * LANES - (first - start)) & (2 * LANES - 1)
        lanes = slice(block * ROWS, (block + 1) * ROWS)
        window = weight_ref[:, pl.ds(start, 2 * LANES)].astype(F32)
        picked[:, lanes] = pltpu.roll(window, shift, 1)[:, :ROWS]
        window = jnp.broadcast_to(bias_ref[pl.ds(start, 2 * LANES)].reshape(1, 2 * LANES), (8, 2 * LANES))
        b1_ref[:, lanes] = pltpu.roll(window, shift, 1)[0:1, :ROWS]
    w1_ref[...] = picked[...].astype(BF16)


def first_conv(pay_ref, w1_ref, b1_ref, cols_ref, frames_ref):
    sources = pay_ref.shape[0]
    spread = (
        lax.broadcasted_iota(jnp.int32, (STEPS, CLIPS), 0) >> 3
        == lax.broadcasted_iota(jnp.int32, (STEPS, CLIPS), 1)
    ).astype(F32).astype(BF16)
    t = (lax.broadcasted_iota(jnp.int32, (STEPS, LANES), 0) & (HALF - 1)).astype(F32)
    lives_even, lives_odd = [], []
    for source in range(sources):
        rows = slice(source * STEPS, (source + 1) * STEPS)
        length = dot(spread, pay_ref[source, CLIPS])
        frames_ref[source] = pay_ref[source, :CLIPS].astype(F32).reshape(2 * STEPS, MEL)
        live_even, live_odd = 2.0 * t < length, 2.0 * t + 1.0 < length
        even = jnp.where(live_even, frames_ref[source, pl.ds(0, STEPS, 2), :], 0.0)
        odd = jnp.where(live_odd, frames_ref[source, pl.ds(1, STEPS, 2), :], 0.0)
        cols_ref[rows, :LANES] = shift_down(odd).astype(BF16)
        cols_ref[rows, LANES : 2 * LANES] = even.astype(BF16)
        cols_ref[rows, 2 * LANES : 3 * LANES] = odd.astype(BF16)
        cols_ref[rows, 3 * LANES :] = shift_up(even).astype(BF16)
        lives_even.append(jnp.concatenate([live_even] * (WIDE // LANES), axis=1))
        lives_odd.append(jnp.concatenate([live_odd] * (WIDE // LANES), axis=1))
    cols = jnp.concatenate([cols_ref[:, : 3 * LANES], cols_ref[:, LANES:]], axis=0)
    pre = dot(cols, w1_ref[...]) + b1_ref[...]
    half = sources * STEPS
    return pre[:half], pre[half:], jnp.concatenate(lives_even, axis=0), jnp.concatenate(lives_odd, axis=0)


def forward_kernel(
    pay_ref, w1_ref, b1_ref, own_ref, side_ref, far_ref, both_ref, part_ref, w2_ref, cols_ref, frames_ref
):
    @pl.when(pl.program_id(0) == 0)
    def _():
        stack_weights((own_ref, side_ref, far_ref, both_ref), w2_ref)

    pre_even, pre_odd, live_even, live_odd = first_conv(pay_ref, w1_ref, b1_ref, cols_ref, frames_ref)
    odd = jnp.where(live_odd, gelu_value(pre_odd), 0.0)
    total = dot(odd.astype(BF16), w2_ref[:, 2 * D2 :]) + dot(shift_down(odd).astype(BF16), w2_ref[:, :D2])
    even = jnp.where(live_even, gelu_value(pre_even), 0.0)
    total = total + dot(even.astype(BF16), w2_ref[:, D2 : 2 * D2])
    part_ref[...] = total.astype(BF16).reshape(part_ref.shape)


def slope_kernel(
    pay_ref, w1_ref, b1_ref, grad_ref, column_ref, row_ref,
    slope_ref, turned_ref, live_grad_ref, wanted_ref, frames_ref, cols_ref,
):
    pre_even, pre_odd, live_even, live_odd = first_conv(pay_ref, w1_ref, b1_ref, cols_ref, frames_ref)
    some = pre_odd.shape[0]
    lanes = pl.ds(pl.multiple_of(pl.program_id(0) * some, some), some)
    turned_ref[pl.ds(pl.multiple_of(3 * WIDE + pl.program_id(0) * some, some // 2), some), :] = cols_ref[...]
    value, slope = gelu_both(pre_odd)
    odd = jnp.where(live_odd, value, 0.0)
    slope_ref[1] = jnp.where(live_odd, slope, 0.0)
    turned_ref[:WIDE, lanes] = shift_down(odd).astype(BF16).T
    turned_ref[2 * WIDE : 3 * WIDE, lanes] = odd.astype(BF16).T
    value, slope = gelu_both(pre_even)
    slope_ref[0] = jnp.where(live_even, slope, 0.0)
    turned_ref[WIDE : 2 * WIDE, lanes] = jnp.where(live_even, value, 0.0).astype(BF16).T

    @pl.when(pl.program_id(0) == 0)
    def _():
        t = (lax.broadcasted_iota(jnp.int32, (STEPS, 1), 0) & (HALF - 1)).astype(F32)
        length = (column_ref[...] & 31).astype(F32)
        live_grad_ref[...] = jnp.where(2.0 * t < length, grad_ref[...].astype(F32), 0.0).astype(BF16)
        here = lax.broadcasted_iota(jnp.int32, (STEPS, STEPS), 0)
        there = lax.broadcasted_iota(jnp.int32, (STEPS, STEPS), 1)
        owner = row_ref[...] >> 5
        same = ((column_ref[...] >> 5) == owner) & ((here >> 3) < (there >> 3))
        same = same & ((here & (HALF - 1)) == 0)
        rank = jnp.sum(jnp.where(same, 1.0, 0.0), axis=0, keepdims=True)
        place = lax.broadcasted_iota(jnp.int32, (1, STEPS), 1) & (HALF - 1)
        place = (owner * 2 + rank.astype(jnp.int32)) * HALF + place
        wanted = lax.broadcasted_iota(jnp.int32, (SLOTS * HALF, STEPS), 0) == place
        t = (lax.broadcasted_iota(jnp.int32, (1, STEPS), 1) & (HALF - 1)).astype(F32)
        wanted = wanted & (2.0 * t < (row_ref[...] & 31).astype(F32))
        wanted_ref[...] = jnp.where(wanted, 1.0, 0.0).astype(BF16)


def middle_kernel(
    where_ref, part_ref, b2_ref, live_grad_ref, wanted_ref, rep_ref, same_ref, cross_ref, live_grad_here, done
):
    copy = pltpu.make_async_copy(live_grad_ref, live_grad_here, done)
    copy.start()
    pre = part_ref[0].astype(F32)
    for source in range(1, HOLDERS):
        pre = pre + part_ref[source].astype(F32)
    value, slope = gelu_both(pre + b2_ref[...])
    copy.wait()
    second_grad = (live_grad_here[...].astype(F32) * slope).astype(BF16)
    for target in range(HOLDERS):
        rep_ref[target] = second_grad
    placed = dot(wanted_ref[...], value.astype(BF16))
    first = where_ref[2] == 0
    for chip in range(CHIPS):
        for tile in range(D2 // LANES):
            rows, columns = slice(tile * 16, (tile + 1) * 16), slice(tile * LANES, (tile + 1) * LANES)
            left = placed[chip * 32 : chip * 32 + 16, columns]
            right = placed[chip * 32 + 16 : chip * 32 + 32, columns]
            same_ref[chip, rows, :] = jnp.where(first, left, right).astype(BF16)
            cross_ref[chip, rows, :] = jnp.where(first, right, left).astype(BF16)


def backward_kernel(
    where_ref, grad_ref, own_ref, side_ref, far_ref, both_ref, turned_ref, slope_ref, out,
    w2_ref, conv_sum,
):
    stack_weights((own_ref, side_ref, far_ref, both_ref), w2_ref)
    mine, core = where_ref[0], where_ref[2]
    grad = grad_ref[...].reshape(HOLDERS * STEPS, D2)
    places = []
    for block in range(BLOCKS):
        to_core = core if block % 2 == 0 else 1 - core
        places.append((2 * to_core + (mine if block < 2 else 1 - mine), block * ROWS))

    for tap in range(3):
        conv_sum[...] = dot(turned_ref[tap * WIDE : (tap + 1) * WIDE, :], grad)
        for target, first in places:
            for column in range(D2 // LANES):
                tile = tap * (D2 // LANES) + column
                piece = conv_sum[first : first + ROWS, column * LANES : (column + 1) * LANES]
                out[target, tile // 8, (tile % 8) * ROWS : (tile % 8 + 1) * ROWS, :] = piece.astype(out.dtype)

    even = dot_nt(grad, w2_ref[:, D2 : 2 * D2])
    even = (even * slope_ref[0]).astype(BF16)
    odd = dot_nt(grad, w2_ref[:, 2 * D2 :]) + shift_up(dot_nt(grad, w2_ref[:, :D2]))
    odd = (odd * slope_ref[1]).astype(BF16)
    cols = turned_ref[3 * WIDE :, :]
    conv_sum[:, : 3 * LANES] = dot_tn(even, cols[:, : 3 * LANES]) + dot_tn(odd, cols[:, LANES:])
    bias1 = jnp.sum(even.astype(F32) + odd.astype(F32), axis=0, keepdims=True)
    bias2 = jnp.sum(grad.astype(F32), axis=0, keepdims=True)
    for target, first in places:
        out[target, 1, 7 * ROWS : 8 * ROWS, :] = jnp.zeros((ROWS, LANES), out.dtype)
        biases = [jnp.concatenate([bias1[:, first : first + ROWS], jnp.zeros((1, LANES - ROWS), F32)], axis=1)]
        for tile in range(D2 // LANES):
            biases.append(bias2[:, tile * LANES : (tile + 1) * LANES])
        biases.append(jnp.zeros((16 - len(biases), LANES), F32))
        biases = jnp.concatenate(biases, axis=0).astype(out.dtype)
        for half in range(2):
            for tile in range(3):
                piece = conv_sum[first : first + ROWS, tile * LANES : (tile + 1) * LANES]
                out[target, half, (8 + tile) * ROWS : (9 + tile) * ROWS, :] = piece.astype(out.dtype)
            out[target, half, 11 * ROWS :, :] = biases


def sum_kernel(got_ref, out_ref):
    total = got_ref[0].astype(F32)
    for source in range(1, got_ref.shape[0]):
        total = total + got_ref[source].astype(F32)
    total = total.astype(BF16)
    if len(out_ref.shape) == 2:
        out_ref[...] = total
    else:
        for target in range(out_ref.shape[0]):
            out_ref[target] = total


def pair_kernel(own_ref, other_ref, out_ref):
    total = (own_ref[...].astype(F32) + other_ref[...].astype(F32)).astype(BF16)
    if len(out_ref.shape) == 2:
        out_ref[...] = total
    else:
        for target in range(out_ref.shape[0]):
            out_ref[target] = total


def last_kernel(
    where_ref, got_ref, cross_ref, weight_ref, bias1_ref, bias2_ref, packed_ref, whole, biases,
):
    step, core = pl.program_id(0), where_ref[2]
    rows = pl.ds(pl.multiple_of((step + 1) * ROWS, 16), ROWS)
    for chip in range(CHIPS):
        whole[pl.ds(pl.multiple_of((2 * chip + core) * ROWS, 16), ROWS), :] = got_ref[chip, rows, :]
        whole[pl.ds(pl.multiple_of((2 * chip + 1 - core) * ROWS, 16), ROWS), :] = cross_ref[chip, rows, :]
    for block in range(10):
        columns = slice(block * LANES, (block + 1) * LANES)
        weight_ref[:, columns] = whole[columns, :].T.astype(F32)

    @pl.when(step == 0)
    def _():
        for chip in range(CHIPS):
            biases[2 * chip + core] = got_ref[chip, 5 * ROWS :, :].astype(F32)
            biases[2 * chip + 1 - core] = cross_ref[chip, 5 * ROWS :, :].astype(F32)
            left = pl.ds(pl.multiple_of(chip * 32 + 16 * core, 16), 16)
            right = pl.ds(pl.multiple_of(chip * 32 + 16 - 16 * core, 16), 16)
            for tile in range(D2 // LANES):
                columns = slice(tile * LANES, (tile + 1) * LANES)
                packed_ref[left, columns] = got_ref[chip, tile * 16 : (tile + 1) * 16, :]
                packed_ref[right, columns] = cross_ref[chip, 4 * ROWS + tile * 16 : 4 * ROWS + (tile + 1) * 16, :]
        bias1 = jnp.concatenate([biases[source, 0:1, :ROWS] for source in range(16)], axis=1)
        bias1_ref[...] = bias1.reshape(16 * ROWS)
        bias2 = jnp.concatenate([biases[0, 1 + tile : 2 + tile, :] for tile in range(D2 // LANES)], axis=1)
        bias2_ref[...] = bias2.reshape(D2)


def unpack_kernel(where_ref, own_ref, other_ref, conv2_ref):
    lower = where_ref[1] == 0
    for tile in range(15):
        half, spot = tile // 8, tile % 8
        rows = slice(spot * ROWS, (spot + 1) * ROWS)
        own, other = own_ref[rows, :].astype(F32), other_ref[rows, :].astype(F32)
        picked = jnp.where(lower, own, other) if half == 0 else jnp.where(lower, other, own)
        conv2_ref[:, tile * LANES : (tile + 1) * LANES] = picked


def exchange(values, axes):
    return lax.all_to_all(values, axes, split_axis=0, concat_axis=0, tiled=True)


def spread_to(values, count):
    return jnp.broadcast_to(values[None], (count,) + values.shape)


def vmem():
    return pl.BlockSpec(memory_space=pltpu.VMEM)


def params(mib, *semantics):
    return pltpu.CompilerParams(vmem_limit_bytes=mib * MIB, dimension_semantics=semantics or None)


def local(mel, lengths, routes, conv1_weight, conv1_bias, conv2_weight, conv2_bias, out_grad):
    x_hi, y, core = lax.axis_index("xh"), lax.axis_index("y"), lax.axis_index("c")
    where = jnp.stack([x_hi, lax.axis_index("xl"), core, (x_hi * HOLDERS + y) * 2 + core]).astype(jnp.int32)

    def shape(*dims, dtype=BF16):
        return jax.ShapeDtypeStruct(dims, dtype)

    def from_hbm(values):
        return pltpu.with_memory_space_constraint(values, pltpu.HBM)

    def in_hbm(*dims, dtype=BF16):
        return pltpu.HBM(dims, dtype)

    pay = pl.pallas_call(
        prepare_kernel,
        in_specs=[pl.BlockSpec(memory_space=pltpu.SMEM), vmem()],
        out_specs=vmem(),
        out_shape=in_hbm(HOLDERS, PAY, 2 * HALF, MEL),
        compiler_params=params(60),
        name="mel_payload",
    )(lengths, mel)
    got_pay = exchange(pay, "y")
    cores = [(0, 1), (1, 0)]
    far_weight = lax.ppermute(conv2_weight, ("xh", "xl"), [(0, 3), (3, 0), (1, 2), (2, 1)])

    w1, b1 = pl.pallas_call(
        columns_kernel,
        in_specs=[pl.BlockSpec(memory_space=pltpu.SMEM), vmem(), vmem()],
        out_specs=[vmem()] * 2,
        out_shape=[shape(3 * MEL, WIDE), shape(1, WIDE, dtype=F32)],
        scratch_shapes=[pltpu.VMEM((3 * MEL, WIDE), F32)],
        compiler_params=params(10),
        name="conv1_columns",
    )(where, conv1_weight, from_hbm(conv1_bias))
    own_weight, place = lax.optimization_barrier((conv2_weight, where))
    far_weight, place = lax.optimization_barrier((far_weight, place))
    weights = [
        conv2_weight,
        lax.ppermute(own_weight, "c", cores),
        far_weight,
        lax.ppermute(far_weight, "c", cores),
    ]

    pair = lambda i: (i, 0, 0)
    pair4 = lambda i: (i, 0, 0, 0)
    rows, some = HOLDERS * STEPS, 2 * STEPS
    frames = (2, 2 * STEPS, MEL)
    pay_spec = pl.BlockSpec((2, PAY, 2 * HALF, MEL), pair4)
    parts = pl.pallas_call(
        forward_kernel,
        grid=(HOLDERS // 2,),
        in_specs=[pay_spec, *[vmem()] * (2 + BLOCKS)],
        out_specs=pl.BlockSpec((2, STEPS, D2), pair),
        out_shape=in_hbm(HOLDERS, STEPS, D2),
        scratch_shapes=[
            pltpu.VMEM((WIDE, 3 * D2), BF16),
            pltpu.VMEM((some, 4 * LANES), BF16),
            pltpu.VMEM(frames, F32),
        ],
        compiler_params=params(20, "arbitrary"),
        name="stem_forward",
    )(got_pay, w1, b1, *weights)

    got_parts = exchange(parts, "y")
    code = jnp.repeat(routes[:, 0] * 32 + lengths, HALF)
    slopes, turned, live_grad, wanted = pl.pallas_call(
        slope_kernel,
        grid=(HOLDERS // 2,),
        in_specs=[pay_spec, *[vmem()] * 5],
        out_specs=[pl.BlockSpec((2, some, WIDE), lambda i: (0, i, 0)), vmem(), vmem(), vmem()],
        out_shape=[
            shape(2, rows, WIDE, dtype=F32),
            shape(3 * WIDE + rows, rows),
            in_hbm(STEPS, D2),
            shape(SLOTS * HALF, STEPS),
        ],
        scratch_shapes=[pltpu.VMEM(frames, F32), pltpu.VMEM((some, 4 * LANES), BF16)],
        compiler_params=params(20, "arbitrary"),
        name="stem_slopes",
    )(got_pay, w1, b1, from_hbm(out_grad.reshape(STEPS, D2)), code[:, None], code[None])
    got_parts, slopes, turned = lax.optimization_barrier((got_parts, slopes, turned))
    rep, same, cross = pl.pallas_call(
        middle_kernel,
        in_specs=[pl.BlockSpec(memory_space=pltpu.SMEM), vmem(), vmem(), pl.BlockSpec(memory_space=pl.ANY), vmem()],
        out_specs=[vmem()] * 3,
        out_shape=[shape(HOLDERS, STEPS, D2), shape(CHIPS, ROWS, LANES), shape(CHIPS, ROWS, LANES)],
        scratch_shapes=[pltpu.VMEM((STEPS, D2), BF16), pltpu.SemaphoreType.DMA],
        compiler_params=params(10),
        name="stem_middle",
    )(where, got_parts, conv2_bias[None], from_hbm(live_grad), wanted)
    got_grad = exchange(rep, "y")

    pack = pl.pallas_call(
        backward_kernel,
        in_specs=[
            pl.BlockSpec(memory_space=pltpu.SMEM),
            *[vmem()] * (3 + BLOCKS),
        ],
        out_specs=vmem(),
        out_shape=shape(4, 2, PACK, LANES),
        scratch_shapes=[
            pltpu.VMEM((WIDE, 3 * D2), BF16),
            pltpu.VMEM((WIDE, D2), F32),
        ],
        compiler_params=params(32),
        name="stem_backward",
    )(where, got_grad, *weights, turned, slopes)
    def summed(values, *dims):
        return pl.pallas_call(
            sum_kernel,
            in_specs=[vmem()],
            out_specs=vmem(),
            out_shape=shape(*dims),
            compiler_params=params(8),
            name="gradient_sum",
        )(values)

    pack = summed(exchange(pack.reshape(2, 4 * PACK, LANES), "c"), 4 * PACK, LANES)
    half = summed(exchange(pack.reshape(4, PACK, LANES), ("xh", "xl")), PACK, LANES)
    quarter = PACK // 4
    near = summed(exchange(half.reshape(4, quarter, LANES), "zl"), quarter, LANES)

    def with_group(values, flip, *dims):
        return pl.pallas_call(
            pair_kernel,
            in_specs=[vmem()] * 2,
            out_specs=vmem(),
            out_shape=shape(*dims),
            compiler_params=params(8),
            name="gradient_pair",
        )(values, lax.ppermute(values, "zh", [(i, i ^ flip) for i in range(4)]))

    far = with_group(with_group(near, 1, quarter, LANES), 3, 4, quarter, LANES)
    half = exchange(far, "zl").reshape(PACK, LANES)
    own = half[:HALF_ROWS]
    other = lax.ppermute(own, "xl", [(0, 1), (1, 0)])
    conv1 = spread_to(half[HALF_ROWS:], CHIPS)
    got = exchange(jnp.concatenate([same, conv1[:, : 3 * ROWS], cross, conv1[:, 3 * ROWS :]], axis=1), ("xh", "y"))
    got, other = lax.optimization_barrier((got, other))
    got_cross = lax.ppermute(got, "c", cores)
    conv2_rows_grad = pl.pallas_call(
        unpack_kernel,
        in_specs=[pl.BlockSpec(memory_space=pltpu.SMEM), vmem(), vmem()],
        out_specs=vmem(),
        out_shape=in_hbm(ROWS, 3 * D2, dtype=F32),
        compiler_params=params(8),
        name="conv2_unpack",
    )(where, own, other)
    weight_grad, bias_grad, second_bias_grad, packed = pl.pallas_call(
        last_kernel,
        grid=(3,),
        in_specs=[
            pl.BlockSpec(memory_space=pltpu.SMEM),
            vmem(),
            vmem(),
        ],
        out_specs=[
            pl.BlockSpec((LANES, 16 * ROWS), lambda i: (i, 0)),
            pl.BlockSpec((16 * ROWS,), lambda i: (0,)),
            pl.BlockSpec((D2,), lambda i: (0,)),
            pl.BlockSpec((SLOTS * HALF, D2), lambda i: (0, 0)),
        ],
        out_shape=[
            shape(3 * MEL, 16 * ROWS, dtype=F32),
            shape(16 * ROWS, dtype=F32),
            shape(D2, dtype=F32),
            shape(SLOTS * HALF, D2),
        ],
        scratch_shapes=[pltpu.VMEM((16 * ROWS, LANES), BF16), pltpu.VMEM((16, 16, LANES), F32)],
        compiler_params=params(16, "arbitrary"),
        name="gradient_unpack",
    )(where, got, got_cross)
    return packed.reshape(SLOTS, HALF, D2), weight_grad, bias_grad, second_bias_grad, conv2_rows_grad


def solution(mesh):
    fine = Mesh(mesh.devices.reshape(2, 4, 2, 4, 4, 2), ALL_AXES)
    placed = (
        P(ALL_AXES, None, None),
        P(ALL_AXES),
        P(ALL_AXES, None),
        P(),
        P(),
        P(ENC, None),
        P(),
        P(ALL_AXES, None, None),
    )
    return jax.shard_map(
        local,
        mesh=fine,
        in_specs=placed,
        out_specs=(P(ALL_AXES, None, None), P(), P(), P(), P(ENC, None)),
        check_vma=False,
    )
```
